32 devices in a mesh: ctx: 4 (over x, core), ch: 8 (over z, y).
Axes of the slice: x: 2, y: 2, z: 4, core: 2. Of those that a mesh axis runs over, the one named last changes fastest.
Arguments:
- out_grad: bfloat16 [1024, 8192], P('ctx', 'ch'), may hold values from -6 to 6
- out_weight: bfloat16 [8192, 8192], P(None, 'ch'), may hold values from -0.09375 to 0.09375
- query_in: bfloat16 [1024, 8192], P('ctx', 'ch'), may hold values from -6 to 6
- conv_out: bfloat16 [1024, 8192], P('ctx', 'ch'), may hold values from -6 to 6
- residues: float32 [8192, 16], P('ch'), may hold values from -0.3 to 0.3
- decay_rates: float32 [8192, 16], P('ch'), may hold values from 0.96 to 1, as said below
Outputs:
- grad_query: bfloat16 [1024, 8192], P('ctx', 'ch')
- grad_input: bfloat16 [1024, 8192], P('ctx', 'ch')
The draws below stay inside these ranges and needn't reach their ends.
Inputs may be any that keep to these rules, and one draw needn't show every extreme that they name: `decay_rates`: each pole lies strictly below 1.
All inputs are finite; a program needn't handle non-finite values.
Results may differ from the reference program's by a relative error of at most 0.001.
Values may be sent and summed in bfloat16 or wider, within the bound.
No kernel may reach another device: no remote copies, remote signals or barrier semaphores. Data moves between devices by JAX's collectives and lax.ppermute only.
A program may use at most 256 MiB of HBM per device.

```python
import math
import jax
import jax.numpy as jnp
from jax import lax

D = 8192
N_MODES = 16
TOKENS = 1024


def draw_decay_rates(key, part):
    lowest = math.log(0.2 / TOKENS)
    highest = math.log(1.0 / 30.0)
    mixing = jax.random.uniform(key, (D, N_MODES), jnp.float32)
    return jnp.exp(-jnp.exp(lowest + mixing * (highest - lowest)))


def raised(values, rng, source, target, shards_of, factor):
    owner, partner = [(jnp.arange(values.shape[dim]) // (values.shape[dim] // shards_of)).reshape([-1 if axis == dim else 1 for axis in range(values.ndim)]) for dim in (source, target)]
    chosen = jax.random.permutation(rng, shards_of)[partner]
    strong = (owner == chosen) | (owner == (partner + shards_of // 2) % shards_of)
    return jnp.where(strong, factor * values, values)


def steps_of(key, dims, shards, smallest, high):
    factor_of = 1.0
    for axis_at, shards_of in shards:
        steps = jax.random.uniform(jax.random.fold_in(jax.random.fold_in(key, 6), axis_at), (shards_of,), jnp.float32, smallest / len(shards), high / len(shards))
        factor_of = factor_of * jnp.repeat(jnp.exp(steps), dims[axis_at] // shards_of).reshape((-1,) + (1,) * (len(dims) - 1 - axis_at))
    return factor_of


def gaussian(own_key, shape, scale, limit, shards=(), kind=jnp.bfloat16):
    result = jax.random.normal(own_key, shape, jnp.float32) * scale
    if len(shards) > 0:
        result = steps_of(own_key, shape, shards, -0.22, 0.18) * result
    return jnp.clip(result, min=-limit, max=limit).astype(kind)


def noise_with(stream_key, extent, deviation, limit, shards, heavy, dtype=jnp.bfloat16):
    array = deviation * jax.random.normal(stream_key, extent, jnp.float32)
    if shards:
        array = array * steps_of(stream_key, extent, shards, -0.22, 0.18)
    return jnp.clip(raised(array, jax.random.fold_in(stream_key, 3), *heavy), -limit, limit).astype(dtype)


def setup_inputs(seed: int = 0) -> dict:
    seeds = jax.random.split(jax.random.key(seed), 7)
    out_grad = gaussian(seeds[0], (TOKENS, D), 1.0, 6.0, ((0, 4), (1, 8)))
    out_weight = noise_with(seeds[1], (D, D), D ** -0.5, 0.09375, ((1, 8),), (1, 0, 8, 2.0))
    query_in = gaussian(seeds[2], (TOKENS, D), 1.0, 6.0, ((0, 4), (1, 8)))
    conv_out = gaussian(seeds[3], (TOKENS, D), 1.0, 6.0, ((0, 4), (1, 8)))
    residues = gaussian(seeds[4], (D, N_MODES), 0.05, 0.3, ((0, 8),), jnp.float32)
    decay_rates = draw_decay_rates(jax.random.fold_in(seeds[6], 71), 0)
    return {"out_grad": out_grad, "out_weight": out_weight, "query_in": query_in, "conv_out": conv_out, "residues": residues, "decay_rates": decay_rates}


def reference(out_grad, out_weight, query_in, conv_out, residues, decay_rates):
    grad_mix = jnp.dot(out_grad, out_weight.T, preferred_element_type=jnp.float32)
    grad_query = (grad_mix * conv_out.astype(jnp.float32)).astype(jnp.bfloat16)
    grad_conv = grad_mix * query_in.astype(jnp.float32)

    def backstep(adjoint, conv_row):
        adjoint = decay_rates * adjoint + conv_row[:, None]
        return adjoint, jnp.sum(residues * adjoint, axis=1)

    start_state = jnp.zeros(decay_rates.shape, jnp.float32)
    final_state, grad_rows = lax.scan(backstep, start_state, grad_conv, reverse=True)
    return grad_query, grad_rows.astype(jnp.bfloat16)
```

```python
import functools
import math

import jax
import jax.numpy as jnp
from jax import lax
from jax.experimental import pallas as pl
from jax.experimental.pallas import tpu as pltpu
from jax.sharding import PartitionSpec as P

GROUPS = 16
SPAN = 251 * math.log(2.0)
SHIFT = 125 * math.log(2.0)
SUBS = 1
VMEM = 24 * 1024 * 1024


def encode(acc, out_ref):
    rows, _ = acc.shape
    part = rows // GROUPS
    peaks = []
    for i in range(GROUPS):
        block = acc[i * part : (i + 1) * part, :]
        size = jnp.abs(block)
        peak = jnp.maximum(jnp.max(size, axis=0, keepdims=True) * 1.01, 1e-30)
        peak = peak.astype(jnp.bfloat16).astype(jnp.float32)
        code = jnp.exp(size * (SPAN / peak) - SHIFT)
        out_ref[i * part : (i + 1) * part, :] = jnp.where(block < 0, -code, code).astype(jnp.bfloat16)
        peaks.append(peak)
    out_ref[rows:, :] = jnp.concatenate(peaks, axis=0).astype(jnp.bfloat16)


def decode(ref, first, count):
    rows = ref.shape[0] - GROUPS
    part = rows // GROUPS
    peaks = ref[rows:, :].astype(jnp.float32) * (1.0 / SPAN)
    blocks = []
    for i in range(first // part, (first + count) // part):
        code = ref[i * part : (i + 1) * part, :].astype(jnp.float32)
        size = (jnp.log(jnp.abs(code)) + SHIFT) * peaks[i : i + 1, :]
        blocks.append(jnp.where(code < 0, -size, size))
    return jnp.concatenate(blocks, axis=0)


def product(w_ref, g_ref):
    return lax.dot_general(
        w_ref[...], g_ref[...], (((1,), (1,)), ((), ())), preferred_element_type=jnp.float32
    )


def first_kernel(_, w_ref, g_ref, out_ref):
    encode(product(w_ref, g_ref), out_ref)


def relay_kernel(_, w_ref, g_ref, near_ref, out_ref):
    rows = w_ref.shape[0]
    encode(product(w_ref, g_ref) + decode(near_ref, 0, rows), out_ref)


def keep_kernel(_, w_ref, g_ref, near_ref, out_ref):
    rows = w_ref.shape[0]
    out_ref[...] = product(w_ref, g_ref) + decode(near_ref, 0, rows)


def on_block(kernel, block, rows, weight, grad, near, coded):
    toks, depth = grad.shape
    whole = lambda shape: pl.BlockSpec(shape, lambda i, at: (0, 0))
    specs = [pl.BlockSpec((rows, depth), lambda i, at: (at[0], 0)), whole((toks, depth))]
    operands = [pltpu.with_memory_space_constraint(weight, pltpu.HBM), grad]
    if near is not None:
        specs.append(whole(near.shape))
        operands.append(near)
    out = (
        jax.ShapeDtypeStruct((rows + GROUPS, toks), jnp.bfloat16)
        if coded
        else jax.ShapeDtypeStruct((rows, toks), jnp.float32)
    )
    return pl.pallas_call(
        kernel,
        grid_spec=pltpu.PrefetchScalarGridSpec(
            num_scalar_prefetch=1, grid=(1,), in_specs=specs, out_specs=whole(out.shape)
        ),
        out_shape=out,
        compiler_params=pltpu.CompilerParams(vmem_limit_bytes=VMEM),
        cost_estimate=pl.CostEstimate(
            flops=2 * rows * depth * toks, bytes_accessed=2 * rows * (depth + toks), transcendentals=2 * rows * toks
        ),
    )(jnp.reshape(block, (1,)).astype(jnp.int32), *operands)


def steps_back(count, body, state, unroll):
    def some(i, state):
        for j in range(unroll):
            state = body(count - 1 - (i * unroll + j), state)
        return state

    return lax.fori_loop(0, count // unroll, some, state)


def gate_kernel(subs, far_count, *refs):
    accs, refs = refs[:subs], refs[subs:]
    fars, refs = refs[: subs * far_count], refs[subs * far_count :]
    query_ref, conv_ref, decay_ref, gq_ref, gc_ref, state_ref = refs
    toks, width = query_ref.shape
    modes, lines, lanes = decay_ref.shape
    rows = width // subs
    for line in range(lines):
        sub, first = divmod(line * lanes, rows)
        mix = accs[sub][first : first + lanes, :]
        for far in range(far_count):
            mix = mix + decode(fars[far * subs + sub], first, lanes)
        mix = mix.T
        at = slice(line * lanes, (line + 1) * lanes)
        gq_ref[:, at] = (mix * conv_ref[:, at].astype(jnp.float32)).astype(jnp.bfloat16)
        gc_ref[line * toks : (line + 1) * toks, :] = mix * query_ref[:, at].astype(jnp.float32)
    decay = [decay_ref[n] for n in range(modes)]

    def step(t, state):
        row = gc_ref[pl.ds(t, lines, stride=toks), :]
        return tuple(decay[n] * state[n] + row for n in range(modes))

    zero = jnp.zeros((lines, lanes), jnp.float32)
    state = steps_back(toks, step, (zero,) * modes, 8)
    for n in range(modes):
        state_ref[n] = state[n]


def gate(accs, fars, query_in, conv_out, decay):
    toks, width = query_in.shape
    modes, lines, lanes = decay.shape
    return pl.pallas_call(
        functools.partial(gate_kernel, len(accs), len(fars) // len(accs)),
        out_shape=(
            jax.ShapeDtypeStruct((toks, width), jnp.bfloat16),
            jax.ShapeDtypeStruct((lines * toks, lanes), jnp.float32),
            jax.ShapeDtypeStruct(decay.shape, jnp.float32),
        ),
        compiler_params=pltpu.CompilerParams(vmem_limit_bytes=VMEM),
        cost_estimate=pl.CostEstimate(
            flops=2 * modes * toks * width, bytes_accessed=16 * toks * width, transcendentals=3 * toks * width
        ),
    )(*accs, *fars, query_in, conv_out, decay)


def power(base, exponent):
    result = None
    while exponent:
        if exponent % 2:
            result = base if result is None else result * base
        base = base * base
        exponent //= 2
    return result


def scan_kernel(hops, gc_ref, *refs):
    laters, (decay_ref, residue_ref, out_ref, rows_ref) = refs[:hops], refs[hops:]
    toks, width = out_ref.shape
    modes, lines, lanes = decay_ref.shape
    decay = [decay_ref[n] for n in range(modes)]
    state = []
    for n in range(modes):
        group = power(decay[n], toks)
        total = laters[-1][n]
        for later in reversed(laters[:-1]):
            total = total * group + later[n]
        state.append(total)

    def step(t, state):
        at = pl.ds(t, lines, stride=toks)
        row = gc_ref[at, :]
        state = tuple(decay[n] * state[n] + row for n in range(modes))
        terms = [residue_ref[n] * state[n] for n in range(modes)]
        while len(terms) > 1:
            terms = [sum(terms[i : i + 2][1:], terms[i]) for i in range(0, len(terms), 2)]
        rows_ref[at, :] = terms[0]
        return state

    steps_back(toks, step, tuple(state), 8)
    for line in range(lines):
        out_ref[:, line * lanes : (line + 1) * lanes] = rows_ref[
            line * toks : (line + 1) * toks, :
        ].astype(jnp.bfloat16)


def scan(grad_conv, laters, decay, residues, toks):
    modes, lines, lanes = decay.shape
    return pl.pallas_call(
        functools.partial(scan_kernel, len(laters)),
        out_shape=jax.ShapeDtypeStruct((toks, lines * lanes), jnp.bfloat16),
        scratch_shapes=[pltpu.VMEM((lines * toks, lanes), jnp.float32)],
        compiler_params=pltpu.CompilerParams(vmem_limit_bytes=VMEM),
        cost_estimate=pl.CostEstimate(
            flops=4 * modes * toks * lines * lanes, bytes_accessed=6 * toks * lines * lanes, transcendentals=0
        ),
    )(grad_conv, *laters, decay, residues)


def local(out_grad, out_weight, query_in, conv_out, residues, decay_rates):
    toks, width = query_in.shape
    modes = decay_rates.shape[1]
    lanes = math.gcd(width, 128)
    by_mode = lambda values: values.T.reshape(modes, width // lanes, lanes)
    decay, residues = by_mode(decay_rates), by_mode(residues)

    pairs = lax.axis_size("ch") // 2
    place = lax.axis_index("ch")
    high, low = place // 2, place % 2
    rows = width // SUBS
    shifts = [pairs // 2] + [k for k in range(1, pairs) if k != pairs // 2] + [0]
    near_pairs = [(i, i ^ 1) for i in range(2 * pairs)]
    chunks = [(k, sub) for k in shifts for sub in range(SUBS)]

    def block_of(shift, sub, side):
        return (((high + shift) % pairs) * 2 + side) * SUBS + sub

    nears = {}
    for k, sub in chunks:
        coded = on_block(first_kernel, block_of(k, sub, 1 - low), rows, out_weight, out_grad, None, True)
        nears[k, sub] = lax.ppermute(coded, "ch", near_pairs)
    fars, accs = [], []
    for k, sub in chunks:
        block = block_of(k, sub, low)
        if k == 0:
            accs.append(on_block(keep_kernel, block, rows, out_weight, out_grad, nears[k, sub], False))
            continue
        coded = on_block(relay_kernel, block, rows, out_weight, out_grad, nears[k, sub], True)
        far_pairs = [(i, (i + 2 * k) % (2 * pairs)) for i in range(2 * pairs)]
        fars.append(lax.ppermute(coded, "ch", far_pairs))
    grad_query, grad_conv, state = gate(accs, fars, query_in, conv_out, decay)

    groups = lax.axis_size("ctx")
    laters = [
        lax.ppermute(state, "ctx", [(i, i - hop) for i in range(hop, groups)]) for hop in range(1, groups)
    ]
    grad_input = scan(grad_conv, laters, decay, residues, toks)
    return grad_query, grad_input


def solution(mesh):
    placed = (
        P("ctx", "ch"),
        P(None, "ch"),
        P("ctx", "ch"),
        P("ctx", "ch"),
        P("ch", None),
        P("ch", None),
    )
    return jax.shard_map(
        local,
        mesh=mesh,
        in_specs=placed,
        out_specs=(P("ctx", "ch"), P("ctx", "ch")),
        check_vma=False,
    )
```

```python
import functools
import math

import jax
import jax.numpy as jnp
from jax import lax
from jax.experimental import pallas as pl
from jax.experimental.pallas import tpu as pltpu
from jax.sharding import PartitionSpec as P

PEAKS = 16
SPAN = 251 * math.log(2.0)
SHIFT = 125 * math.log(2.0)
STEP = 256
VMEM = 24 * 1024 * 1024
QUICK = pl.CostEstimate(flops=0, bytes_accessed=1024, transcendentals=0)

ORDER = (
    (0, 0, 6), (1, 0, 6), (0, 0, 4), (0, 1, 4), (0, 0, 2), (1, 1, 4), (1, 0, 4), (0, 2, 0), (0, 1, 0),
    (1, 0, 2), (1, 2, 0), (0, 0, 0), (1, 1, 0), (1, 0, 0),
)


def part_of(rows):
    return max(rows // PEAKS, min(rows, 16))


def encode(block, part):
    codes, peaks = [], []
    for i in range(block.shape[0] // part):
        piece = block[i * part : (i + 1) * part, :]
        size = jnp.abs(piece)
        peak = jnp.maximum(jnp.max(size, axis=0, keepdims=True) * 1.01, 1e-30)
        peak = peak.astype(jnp.bfloat16).astype(jnp.float32)
        code = jnp.exp(size * (SPAN / peak) - SHIFT)
        codes.append(jnp.where(piece < 0, -code, code))
        peaks.append(peak)
    return jnp.concatenate(codes, axis=0).astype(jnp.bfloat16), peaks


def decode(ref, base, rows, first, count):
    part = part_of(rows)
    peaks = ref[base + rows : base + rows + PEAKS, :].astype(jnp.float32) * (1.0 / SPAN)
    blocks = []
    for i in range(first // part, (first + count) // part):
        code = ref[base + i * part : base + (i + 1) * part, :].astype(jnp.float32)
        size = (jnp.log(jnp.abs(code)) + SHIFT) * peaks[i : i + 1, :]
        blocks.append(jnp.where(code < 0, -size, size))
    return jnp.concatenate(blocks, axis=0)


def pinned(array):
    return pltpu.with_memory_space_constraint(array, pltpu.HBM)


def send_kernel(rows, starts, sources, coded, near, place_ref, w_ref, g_ref, *refs):
    near_refs, (out_ref, w_buf, g_buf, sems) = refs[:near], refs[near:]
    step = min(rows, STEP)
    place = place_ref[0]
    grad = pltpu.make_async_copy(g_ref, g_buf, sems.at[0])
    grad.start()
    copies = []
    for i, (block, offset, width) in enumerate(starts):
        first = pl.multiple_of((place ^ block) * width + offset, 16)
        for at in range(0, rows, step):
            copy = pltpu.make_async_copy(
                w_ref.at[pl.ds(first + at, step), :],
                w_buf.at[pl.ds(i * rows + at, step), :],
                sems.at[1 + len(copies)],
            )
            copy.start()
            copies.append(copy)
    grad.wait()
    part = part_of(rows)
    stride = rows + PEAKS if coded else rows
    copies = iter(copies)
    for i in range(len(starts)):
        peaks = []
        for at in range(0, rows, step):
            next(copies).wait()
            block = lax.dot_general(
                w_buf[i * rows + at : i * rows + at + step, :],
                g_buf[...],
                (((1,), (1,)), ((), ())),
                preferred_element_type=jnp.float32,
            )
            for source, base in sources[i]:
                block = block + decode(near_refs[source], base, rows, at, step)
            if coded:
                block, more = encode(block, part)
                peaks += more
            out_ref[i * stride + at : i * stride + at + step, :] = block
        if coded:
            toks = block.shape[1]
            if len(peaks) < PEAKS:
                peaks.append(jnp.zeros((PEAKS - len(peaks), toks), jnp.float32))
            out_ref[i * stride + rows : (i + 1) * stride, :] = jnp.concatenate(peaks, axis=0).astype(jnp.bfloat16)


def send(rows, starts, sources, coded, place, weight, grad, nears):
    toks, depth = grad.shape
    vmem = pl.BlockSpec(memory_space=pltpu.VMEM)
    high = pl.BlockSpec(memory_space=pltpu.HBM)
    count = len(starts) * (rows + PEAKS if coded else rows)
    steps = len(starts) * (rows // min(rows, STEP))
    work = len(starts) * rows
    return pl.pallas_call(
        functools.partial(send_kernel, rows, starts, sources, coded, len(nears)),
        in_specs=[pl.BlockSpec(memory_space=pltpu.SMEM), high, high] + [vmem] * len(nears),
        out_specs=vmem,
        out_shape=jax.ShapeDtypeStruct((count, toks), jnp.bfloat16 if coded else jnp.float32),
        scratch_shapes=[
            pltpu.VMEM((work, depth), jnp.bfloat16),
            pltpu.VMEM((toks, depth), jnp.bfloat16),
            pltpu.SemaphoreType.DMA((steps + 1,)),
        ],
        compiler_params=pltpu.CompilerParams(vmem_limit_bytes=VMEM),
        cost_estimate=QUICK,
    )(place, pinned(weight), pinned(grad), *nears)


def steps_back(count, body, state, unroll):
    def some(i, state):
        for j in range(unroll):
            state = body(count - 1 - (i * unroll + j), state)
        return state

    return lax.fori_loop(0, count // unroll, some, state)


def power(base, exponent):
    result = None
    while exponent:
        if exponent % 2:
            result = base if result is None else result * base
        base = base * base
        exponent //= 2
    return result


def segment_of(shape, segments):
    return lax.rem(lax.broadcasted_iota(jnp.int32, shape, 0), segments)


def rolled(value, by):
    by %= value.shape[0]
    return pltpu.roll(value, by, 0) if by else value


def gate_kernel(portion, rows, segments, fars, acc_ref, *refs):
    far_refs, refs = refs[: len(fars)], refs[len(fars) :]
    query_hbm, conv_hbm, decay_ref = refs[:3]
    out_hbm, gc_ref, state_ref, pack_ref, query_ref, conv_ref, gq_ref, sems = refs[-8:]
    columns = pl.ds(portion * rows, rows)
    loads = [
        pltpu.make_async_copy(query_hbm.at[:, columns], query_ref, sems.at[0]),
        pltpu.make_async_copy(conv_hbm.at[:, columns], conv_ref, sems.at[1]),
    ]
    for load in loads:
        load.start()
    toks = query_ref.shape[0]
    modes, sublanes, lanes = state_ref.shape
    mine = slice(portion * sublanes, (portion + 1) * sublanes)
    for line in range(rows // lanes):
        mix = acc_ref[line * lanes : (line + 1) * lanes, :]
        for ref, base in zip(far_refs, fars):
            mix = mix + decode(ref, base, rows, line * lanes, lanes)
        mix = mix.T
        if line == 0:
            for load in loads:
                load.wait()
        at = slice(line * lanes, (line + 1) * lanes)
        gq_ref[:, at] = (mix * conv_ref[:, at].astype(jnp.float32)).astype(jnp.bfloat16)
        gc_ref[line * toks : (line + 1) * toks, :] = mix * query_ref[:, at].astype(jnp.float32)
    store = pltpu.make_async_copy(gq_ref, out_hbm.at[:, columns], sems.at[2])
    store.start()
    decay = [decay_ref[n, mine] for n in range(modes)]
    span = toks // segments

    def step(t, state):
        row = gc_ref[pl.ds(t, sublanes, stride=span), :]
        return tuple(decay[n] * state[n] + row for n in range(modes))

    zero = jnp.zeros((sublanes, lanes), jnp.float32)
    state = steps_back(span, step, (zero,) * modes, 8)
    segment = segment_of((sublanes, lanes), segments)
    whole = []
    for n in range(modes):
        state_ref[n] = state[n]
        total = state[n]
        if segments > 1:
            factor = jnp.where(segment < segments - 1, power(decay[n], span), 0.0)
            for _ in range(segments - 1):
                total = state[n] + factor * rolled(total, -1)
        whole.append(total)
    for m in range(modes // segments):
        packed = whole[m * segments]
        for j in range(1, segments):
            packed = jnp.where(segment == j, rolled(whole[m * segments + j], j), packed)
        pack_ref[m] = packed
    store.wait()


def gate(portion, rows, segments, acc, fars, query_in, conv_out, decay, partial):
    toks, width = query_in.shape
    modes, sublanes, lanes = decay.shape
    sublanes = rows // lanes * segments
    vmem = pl.BlockSpec(memory_space=pltpu.VMEM)
    high = pl.BlockSpec(memory_space=pltpu.HBM)
    more = [] if partial is None else [partial]
    return pl.pallas_call(
        functools.partial(gate_kernel, portion, rows, segments, (0,) * len(fars)),
        in_specs=[vmem] * (1 + len(fars)) + [high, high, vmem] + [high] * len(more),
        out_specs=(high, vmem, vmem, vmem),
        out_shape=(
            jax.ShapeDtypeStruct((toks, width), jnp.bfloat16),
            jax.ShapeDtypeStruct((rows // lanes * toks, lanes), jnp.float32),
            jax.ShapeDtypeStruct((modes, sublanes, lanes), jnp.float32),
            jax.ShapeDtypeStruct((modes // segments, sublanes, lanes), jnp.float32),
        ),
        scratch_shapes=[pltpu.VMEM((toks, rows), jnp.bfloat16)] * 3 + [pltpu.SemaphoreType.DMA((3,))],
        input_output_aliases={4 + len(fars): 0} if more else {},
        compiler_params=pltpu.CompilerParams(vmem_limit_bytes=VMEM),
        cost_estimate=QUICK,
    )(acc, *fars, pinned(query_in), pinned(conv_out), decay, *more)


def scan_kernel(portion, segments, hops, gc_ref, state_ref, *refs):
    later_refs, refs = refs[:hops], refs[hops:]
    decay_ref, residue_ref = refs[:2]
    out_hbm, rows_ref, out_ref, sem = refs[-4:]
    toks, rows = out_ref.shape
    modes, sublanes, lanes = state_ref.shape
    mine = slice(portion * sublanes, (portion + 1) * sublanes)
    span = toks // segments
    segment = segment_of((sublanes, lanes), segments)
    decay = [decay_ref[n, mine] for n in range(modes)]
    start = []
    for n in range(modes):
        group = power(decay[n], span)
        whole = power(group, segments)
        m, j = divmod(n, segments)
        total = later_refs[-1][m]
        for ref in reversed(later_refs[:-1]):
            total = total * whole + ref[m]
        total = rolled(total, segments - 1 - j)
        for k in range(segments - 2, -1, -1):
            total = jnp.where(segment == k, rolled(state_ref[n] + group * total, -1), total)
        start.append(total)

    def step(t, state):
        at = pl.ds(t, sublanes, stride=span)
        row = gc_ref[at, :]
        state = tuple(decay[n] * state[n] + row for n in range(modes))
        terms = [residue_ref[n, mine] * state[n] for n in range(modes)]
        while len(terms) > 1:
            terms = [terms[i] + terms[i + 1] for i in range(0, len(terms), 2)]
        rows_ref[at, :] = terms[0]
        return state

    steps_back(span, step, tuple(start), 8)
    for line in range(rows // lanes):
        out_ref[:, line * lanes : (line + 1) * lanes] = rows_ref[
            line * toks : (line + 1) * toks, :
        ].astype(jnp.bfloat16)
    store = pltpu.make_async_copy(out_ref, out_hbm.at[:, pl.ds(portion * rows, rows)], sem)
    store.start()
    store.wait()


def scan(portion, rows, segments, grad_conv, state, laters, decay, residues, toks, width, partial):
    vmem = pl.BlockSpec(memory_space=pltpu.VMEM)
    high = pl.BlockSpec(memory_space=pltpu.HBM)
    more = [] if partial is None else [partial]
    return pl.pallas_call(
        functools.partial(scan_kernel, portion, segments, len(laters)),
        in_specs=[vmem] * (4 + len(laters)) + [high] * len(more),
        out_specs=high,
        out_shape=jax.ShapeDtypeStruct((toks, width), jnp.bfloat16),
        scratch_shapes=[
            pltpu.VMEM(grad_conv.shape, jnp.float32),
            pltpu.VMEM((toks, rows), jnp.bfloat16),
            pltpu.SemaphoreType.DMA,
        ],
        input_output_aliases={4 + len(laters): 0} if more else {},
        compiler_params=pltpu.CompilerParams(vmem_limit_bytes=VMEM),
        cost_estimate=QUICK,
    )(grad_conv, state, *laters, decay, residues, *more)


def local(out_grad, out_weight, query_in, conv_out, residues, decay_rates):
    toks, width = query_in.shape
    modes = decay_rates.shape[1]
    lanes = math.gcd(width, 128)
    size = lax.axis_size("ch")
    bits = [1 << i for i in range(size.bit_length() - 1)]
    place = jnp.reshape(lax.axis_index("ch"), (1,)).astype(jnp.int32)
    rows = width // 2
    lines = rows // lanes
    segments = 8 // lines
    by_mode = lambda values: jnp.repeat(values.T.reshape(modes, width // lanes, lanes), segments, axis=1)
    decay, residue = by_mode(decay_rates), by_mode(residues)

    order = ORDER
    if size != 8:
        order = [
            (p, s, block)
            for p in range(2)
            for s, bit in enumerate(bits)
            for block in sorted(range(0, size, 2 * bit), reverse=True)
        ]
    received = {}
    groups = lax.axis_size("ctx")
    last = None

    def after(value):
        return value if last is None else lax.optimization_barrier((value, last))[0]

    for p, s, block in order:
        bit = bits[s]
        nears = [received[p, i, block ^ bit] for i in range(s)]
        last = send(
            rows,
            ((block ^ bit, p * rows, width),),
            (tuple((i, 0) for i in range(s)),),
            True,
            after(place),
            out_weight,
            out_grad,
            nears,
        )
        received[p, s, block] = lax.ppermute(last, "ch", [(i, i ^ bit) for i in range(size)])

    states = []
    grad_query = grad_input = None
    for p in range(2):
        acc = send(
            rows, ((0, p * rows, width),), (((0, 0),),), False, after(place), out_weight, out_grad, [received[p, 0, 0]]
        )
        fars = [received[p, s, 0] for s in range(1, len(bits))]
        grad_query, grad_conv, state, packed = gate(
            p, rows, segments, acc, fars, query_in, conv_out, decay, grad_query
        )
        last = packed
        laters = [
            lax.ppermute(packed, "ctx", [(i, i - hop) for i in range(hop, groups)]) for hop in range(1, groups)
        ]
        states.append((grad_conv, state, laters))
    for p, (grad_conv, state, laters) in enumerate(states):
        grad_input = scan(
            p, rows, segments, grad_conv, state, laters, decay, residue, toks, width, grad_input
        )
    return grad_query, grad_input


def solution(mesh):
    placed = (
        P("ctx", "ch"),
        P(None, "ch"),
        P("ctx", "ch"),
        P("ctx", "ch"),
        P("ch", None),
        P("ch", None),
    )
    return jax.shard_map(
        local,
        mesh=mesh,
        in_specs=placed,
        out_specs=(P("ctx", "ch"), P("ctx", "ch")),
        check_vma=False,
    )
```

```python
import functools
import math

import jax
import jax.numpy as jnp
from jax import lax
from jax.experimental import pallas as pl
from jax.experimental.pallas import tpu as pltpu
from jax.sharding import PartitionSpec as P

PEAKS = 16
SPAN = 251 * math.log(2.0)
SHIFT = 125 * math.log(2.0)
STEP = 256
VMEM = 24 * 1024 * 1024
QUICK = pl.CostEstimate(flops=0, bytes_accessed=1024, transcendentals=0)

ORDER = (
    (0, 0, 6), (1, 0, 6), (0, 0, 4), (0, 1, 4), (0, 0, 2), (1, 1, 4), (1, 0, 4), (0, 2, 0), (0, 1, 0),
    (1, 0, 2), (1, 2, 0), (0, 0, 0), (1, 1, 0), (1, 0, 0),
)


def part_of(rows):
    return max(rows // PEAKS, min(rows, 16))


def encode(block, part):
    codes, peaks = [], []
    for i in range(block.shape[0] // part):
        piece = block[i * part : (i + 1) * part, :]
        size = jnp.abs(piece)
        peak = jnp.maximum(jnp.max(size, axis=0, keepdims=True) * 1.01, 1e-30)
        peak = peak.astype(jnp.bfloat16).astype(jnp.float32)
        code = jnp.exp(size * (SPAN / peak) - SHIFT)
        codes.append(jnp.where(piece < 0, -code, code))
        peaks.append(peak)
    return jnp.concatenate(codes, axis=0).astype(jnp.bfloat16), peaks


def decode(ref, base, rows, first, count):
    part = part_of(rows)
    peaks = ref[base + rows : base + rows + PEAKS, :].astype(jnp.float32) * (1.0 / SPAN)
    blocks = []
    for i in range(first // part, (first + count) // part):
        code = ref[base + i * part : base + (i + 1) * part, :].astype(jnp.float32)
        size = (jnp.log(jnp.abs(code)) + SHIFT) * peaks[i : i + 1, :]
        blocks.append(jnp.where(code < 0, -size, size))
    return jnp.concatenate(blocks, axis=0)


def pinned(array):
    return pltpu.with_memory_space_constraint(array, pltpu.HBM)


def send_kernel(rows, block, offset, width, sources, coded, place_ref, w_ref, turned_ref, *refs):
    near_refs, out_ref = refs[:sources], refs[sources]
    step = min(rows, STEP)
    first = (place_ref[0] ^ block) * width + offset
    part = part_of(rows)
    peaks = []
    for at in range(0, rows, step):
        total = jnp.dot(
            w_ref[pl.ds(pl.multiple_of(first + at, 16), step), :], turned_ref[...], preferred_element_type=jnp.float32
        )
        for near_ref in near_refs:
            total = total + decode(near_ref, 0, rows, at, step)
        if coded:
            total, more = encode(total, part)
            peaks += more
        out_ref[at : at + step, :] = total
    if coded:
        if len(peaks) < PEAKS:
            peaks.append(jnp.zeros((PEAKS - len(peaks), total.shape[1]), jnp.float32))
        out_ref[rows:, :] = jnp.concatenate(peaks, axis=0).astype(jnp.bfloat16)


def send(rows, block, offset, width, coded, place, weight, turned, nears):
    toks = turned.shape[1]
    vmem = pl.BlockSpec(memory_space=pltpu.VMEM)
    count = rows + PEAKS if coded else rows
    return pl.pallas_call(
        functools.partial(send_kernel, rows, block, offset, width, len(nears), coded),
        in_specs=[pl.BlockSpec(memory_space=pltpu.SMEM)] + [vmem] * (2 + len(nears)),
        out_specs=vmem,
        out_shape=jax.ShapeDtypeStruct((count, toks), jnp.bfloat16 if coded else jnp.float32),
        compiler_params=pltpu.CompilerParams(vmem_limit_bytes=VMEM),
        cost_estimate=QUICK,
    )(place, weight, turned, *nears)


def first_kernel(rows, block, offset, width, place_ref, w_hbm, g_hbm, out_ref, turned_ref, w_ref, g_ref, sems):
    step = min(rows, STEP)
    first = pl.multiple_of((place_ref[0] ^ block) * width + offset, 16)
    copies = [pltpu.make_async_copy(g_hbm, g_ref, sems.at[0])]
    for i, at in enumerate(range(0, rows, step)):
        copies.append(
            pltpu.make_async_copy(w_hbm.at[pl.ds(first + at, step), :], w_ref.at[pl.ds(at, step), :], sems.at[1 + i])
        )
    for copy in copies:
        copy.start()
    copies[0].wait()
    turned_ref[...] = g_ref[...].T
    part = part_of(rows)
    peaks = []
    for i, at in enumerate(range(0, rows, step)):
        copies[1 + i].wait()
        total = jnp.dot(w_ref[at : at + step, :], turned_ref[...], preferred_element_type=jnp.float32)
        total, more = encode(total, part)
        peaks += more
        out_ref[at : at + step, :] = total
    if len(peaks) < PEAKS:
        peaks.append(jnp.zeros((PEAKS - len(peaks), total.shape[1]), jnp.float32))
    out_ref[rows:, :] = jnp.concatenate(peaks, axis=0).astype(jnp.bfloat16)


def first_send(rows, block, offset, width, place, weight, grad):
    toks, depth = grad.shape
    vmem = pl.BlockSpec(memory_space=pltpu.VMEM)
    high = pl.BlockSpec(memory_space=pltpu.HBM)
    return pl.pallas_call(
        functools.partial(first_kernel, rows, block, offset, width),
        in_specs=[pl.BlockSpec(memory_space=pltpu.SMEM), high, high],
        out_specs=(vmem, vmem),
        out_shape=(
            jax.ShapeDtypeStruct((rows + PEAKS, toks), jnp.bfloat16),
            jax.ShapeDtypeStruct((depth, toks), jnp.bfloat16),
        ),
        scratch_shapes=[
            pltpu.VMEM((rows, depth), jnp.bfloat16),
            pltpu.VMEM((toks, depth), jnp.bfloat16),
            pltpu.SemaphoreType.DMA((1 + rows // min(rows, STEP),)),
        ],
        compiler_params=pltpu.CompilerParams(vmem_limit_bytes=VMEM),
        cost_estimate=QUICK,
    )(place, pinned(weight), pinned(grad))


def steps_back(count, body, state, unroll):
    def some(i, state):
        for j in range(unroll):
            state = body(count - 1 - (i * unroll + j), state)
        return state

    return lax.fori_loop(0, count // unroll, some, state)


def power(base, exponent):
    result = None
    while exponent:
        if exponent % 2:
            result = base if result is None else result * base
        base = base * base
        exponent //= 2
    return result


def segment_of(shape, segments):
    return lax.rem(lax.broadcasted_iota(jnp.int32, shape, 0), segments)


def rolled(value, by):
    by %= value.shape[0]
    return pltpu.roll(value, by, 0) if by else value


def gate_kernel(portion, rows, segments, fars, acc_ref, *refs):
    far_refs, refs = refs[: len(fars)], refs[len(fars) :]
    query_hbm, conv_hbm, decay_ref = refs[:3]
    out_hbm, gc_ref, state_ref, pack_ref, query_ref, conv_ref, gq_ref, sems = refs[-8:]
    columns = pl.ds(portion * rows, rows)
    loads = [
        pltpu.make_async_copy(query_hbm.at[:, columns], query_ref, sems.at[0]),
        pltpu.make_async_copy(conv_hbm.at[:, columns], conv_ref, sems.at[1]),
    ]
    for load in loads:
        load.start()
    toks = query_ref.shape[0]
    modes, sublanes, lanes = state_ref.shape
    mine = slice(portion * sublanes, (portion + 1) * sublanes)
    for line in range(rows // lanes):
        mix = acc_ref[line * lanes : (line + 1) * lanes, :]
        for ref, base in zip(far_refs, fars):
            mix = mix + decode(ref, base, rows, line * lanes, lanes)
        mix = mix.T
        if line == 0:
            for load in loads:
                load.wait()
        at = slice(line * lanes, (line + 1) * lanes)
        gq_ref[:, at] = (mix * conv_ref[:, at].astype(jnp.float32)).astype(jnp.bfloat16)
        gc_ref[line * toks : (line + 1) * toks, :] = mix * query_ref[:, at].astype(jnp.float32)
    store = pltpu.make_async_copy(gq_ref, out_hbm.at[:, columns], sems.at[2])
    store.start()
    decay = [decay_ref[n, mine] for n in range(modes)]
    span = toks // segments

    def step(t, state):
        row = gc_ref[pl.ds(t, sublanes, stride=span), :]
        return tuple(decay[n] * state[n] + row for n in range(modes))

    zero = jnp.zeros((sublanes, lanes), jnp.float32)
    state = steps_back(span, step, (zero,) * modes, 8)
    segment = segment_of((sublanes, lanes), segments)
    whole = []
    for n in range(modes):
        state_ref[n] = state[n]
        total = state[n]
        if segments > 1:
            factor = jnp.where(segment < segments - 1, power(decay[n], span), 0.0)
            for _ in range(segments - 1):
                total = state[n] + factor * rolled(total, -1)
        whole.append(total)
    for m in range(modes // segments):
        packed = whole[m * segments]
        for j in range(1, segments):
            packed = jnp.where(segment == j, rolled(whole[m * segments + j], j), packed)
        pack_ref[m] = packed
    store.wait()


def gate(portion, rows, segments, acc, fars, query_in, conv_out, decay, partial):
    toks, width = query_in.shape
    modes, sublanes, lanes = decay.shape
    sublanes = rows // lanes * segments
    vmem = pl.BlockSpec(memory_space=pltpu.VMEM)
    high = pl.BlockSpec(memory_space=pltpu.HBM)
    more = [] if partial is None else [partial]
    return pl.pallas_call(
        functools.partial(gate_kernel, portion, rows, segments, (0,) * len(fars)),
        in_specs=[vmem] * (1 + len(fars)) + [high, high, vmem] + [high] * len(more),
        out_specs=(high, vmem, vmem, vmem),
        out_shape=(
            jax.ShapeDtypeStruct((toks, width), jnp.bfloat16),
            jax.ShapeDtypeStruct((rows // lanes * toks, lanes), jnp.float32),
            jax.ShapeDtypeStruct((modes, sublanes, lanes), jnp.float32),
            jax.ShapeDtypeStruct((modes // segments, sublanes, lanes), jnp.float32),
        ),
        scratch_shapes=[pltpu.VMEM((toks, rows), jnp.bfloat16)] * 3 + [pltpu.SemaphoreType.DMA((3,))],
        input_output_aliases={4 + len(fars): 0} if more else {},
        compiler_params=pltpu.CompilerParams(vmem_limit_bytes=VMEM),
        cost_estimate=QUICK,
    )(acc, *fars, pinned(query_in), pinned(conv_out), decay, *more)


def scan_kernel(portion, segments, hops, gc_ref, state_ref, *refs):
    later_refs, refs = refs[:hops], refs[hops:]
    decay_ref, residue_ref = refs[:2]
    out_hbm, rows_ref, out_ref, sem = refs[-4:]
    toks, rows = out_ref.shape
    modes, sublanes, lanes = state_ref.shape
    mine = slice(portion * sublanes, (portion + 1) * sublanes)
    span = toks // segments
    segment = segment_of((sublanes, lanes), segments)
    decay = [decay_ref[n, mine] for n in range(modes)]
    start = []
    for n in range(modes):
        group = power(decay[n], span)
        whole = power(group, segments)
        m, j = divmod(n, segments)
        total = later_refs[-1][m]
        for ref in reversed(later_refs[:-1]):
            total = total * whole + ref[m]
        total = rolled(total, segments - 1 - j)
        for k in range(segments - 2, -1, -1):
            total = jnp.where(segment == k, rolled(state_ref[n] + group * total, -1), total)
        start.append(total)

    def step(t, state):
        at = pl.ds(t, sublanes, stride=span)
        row = gc_ref[at, :]
        state = tuple(decay[n] * state[n] + row for n in range(modes))
        terms = [residue_ref[n, mine] * state[n] for n in range(modes)]
        while len(terms) > 1:
            terms = [terms[i] + terms[i + 1] for i in range(0, len(terms), 2)]
        rows_ref[at, :] = terms[0]
        return state

    steps_back(span, step, tuple(start), 8)
    for line in range(rows // lanes):
        out_ref[:, line * lanes : (line + 1) * lanes] = rows_ref[
            line * toks : (line + 1) * toks, :
        ].astype(jnp.bfloat16)
    store = pltpu.make_async_copy(out_ref, out_hbm.at[:, pl.ds(portion * rows, rows)], sem)
    store.start()
    store.wait()


def scan(portion, rows, segments, grad_conv, state, laters, decay, residues, toks, width, partial):
    vmem = pl.BlockSpec(memory_space=pltpu.VMEM)
    high = pl.BlockSpec(memory_space=pltpu.HBM)
    more = [] if partial is None else [partial]
    return pl.pallas_call(
        functools.partial(scan_kernel, portion, segments, len(laters)),
        in_specs=[vmem] * (4 + len(laters)) + [high] * len(more),
        out_specs=high,
        out_shape=jax.ShapeDtypeStruct((toks, width), jnp.bfloat16),
        scratch_shapes=[
            pltpu.VMEM(grad_conv.shape, jnp.float32),
            pltpu.VMEM((toks, rows), jnp.bfloat16),
            pltpu.SemaphoreType.DMA,
        ],
        input_output_aliases={4 + len(laters): 0} if more else {},
        compiler_params=pltpu.CompilerParams(vmem_limit_bytes=VMEM),
        cost_estimate=QUICK,
    )(grad_conv, state, *laters, decay, residues, *more)


def local(out_grad, out_weight, query_in, conv_out, residues, decay_rates):
    toks, width = query_in.shape
    modes = decay_rates.shape[1]
    lanes = math.gcd(width, 128)
    size = lax.axis_size("ch")
    bits = [1 << i for i in range(size.bit_length() - 1)]
    place = jnp.reshape(lax.axis_index("ch"), (1,)).astype(jnp.int32)
    rows = width // 2
    lines = rows // lanes
    segments = 8 // lines
    by_mode = lambda values: jnp.repeat(values.T.reshape(modes, width // lanes, lanes), segments, axis=1)
    decay, residue = by_mode(decay_rates), by_mode(residues)

    order = ORDER
    if size != 8:
        order = [
            (p, s, block)
            for p in range(2)
            for s, bit in enumerate(bits)
            for block in sorted(range(0, size, 2 * bit), reverse=True)
        ]
    received = {}
    groups = lax.axis_size("ctx")
    last = None

    def after(value):
        return value if last is None else lax.optimization_barrier((value, last))[0]

    for p, s, block in order:
        bit = bits[s]
        if last is None:
            last, turned = first_send(rows, block ^ bit, p * rows, width, place, out_weight, out_grad)
        else:
            nears = [received[p, i, block ^ bit] for i in range(s)]
            last = send(rows, block ^ bit, p * rows, width, True, after(place), out_weight, turned, nears)
        received[p, s, block] = lax.ppermute(last, "ch", [(i, i ^ bit) for i in range(size)])

    states = []
    grad_query = grad_input = None
    for p in range(2):
        acc = send(rows, 0, p * rows, width, False, after(place), out_weight, turned, [received[p, 0, 0]])
        fars = [received[p, s, 0] for s in range(1, len(bits))]
        grad_query, grad_conv, state, packed = gate(
            p, rows, segments, acc, fars, query_in, conv_out, decay, grad_query
        )
        last = packed
        laters = [
            lax.ppermute(packed, "ctx", [(i, i - hop) for i in range(hop, groups)]) for hop in range(1, groups)
        ]
        states.append((grad_conv, state, laters))
    for p, (grad_conv, state, laters) in enumerate(states):
        grad_input = scan(
            p, rows, segments, grad_conv, state, laters, decay, residue, toks, width, grad_input
        )
    return grad_query, grad_input


def solution(mesh):
    placed = (
        P("ctx", "ch"),
        P(None, "ch"),
        P("ctx", "ch"),
        P("ctx", "ch"),
        P("ch", None),
        P("ch", None),
    )
    return jax.shard_map(
        local,
        mesh=mesh,
        in_specs=placed,
        out_specs=(P("ctx", "ch"), P("ctx", "ch")),
        check_vma=False,
    )
```

```python
import functools
import math

import jax
import jax.numpy as jnp
from jax import lax
from jax.experimental import pallas as pl
from jax.experimental.pallas import tpu as pltpu
from jax.sharding import PartitionSpec as P

PEAKS = 16
SPAN = 251 * math.log(2.0)
SHIFT = 125 * math.log(2.0)
STEP = 256
VMEM = 24 * 1024 * 1024
QUICK = pl.CostEstimate(flops=0, bytes_accessed=1024, transcendentals=0)

ORDER = (
    (0, 0, 6), (0, 0, 4), (0, 0, 2), (0, 1, 4), (1, 0, 6), (0, 0, 0), (0, 2, 0), (0, 1, 0), (1, 0, 4), (1, 1, 4),
    (1, 0, 2), (1, 0, 0), (0, "sum"), (0, "gate"), (0, "scan"), (1, 2, 0), (1, 1, 0), (0, "fix"), (1, "sum"),
    (1, "gate"), (1, "scan"), (1, "fix"),
)


def part_of(rows):
    return max(rows // PEAKS, min(rows, 16))


def encode(block, part):
    codes, peaks = [], []
    for i in range(block.shape[0] // part):
        piece = block[i * part : (i + 1) * part, :]
        size = jnp.abs(piece)
        peak = jnp.maximum(jnp.max(size, axis=0, keepdims=True) * 1.01, 1e-30)
        peak = peak.astype(jnp.bfloat16).astype(jnp.float32)
        code = jnp.exp(size * (SPAN / peak) - SHIFT)
        codes.append(jnp.where(piece < 0, -code, code))
        peaks.append(peak)
    return jnp.concatenate(codes, axis=0).astype(jnp.bfloat16), peaks


def decode(ref, base, rows, first, count):
    part = part_of(rows)
    peaks = ref[base + rows : base + rows + PEAKS, :].astype(jnp.float32) * (1.0 / SPAN)
    blocks = []
    for i in range(first // part, (first + count) // part):
        code = ref[base + i * part : base + (i + 1) * part, :].astype(jnp.float32)
        size = (jnp.log(jnp.abs(code)) + SHIFT) * peaks[i : i + 1, :]
        blocks.append(jnp.where(code < 0, -size, size))
    return jnp.concatenate(blocks, axis=0)


def pinned(array):
    return pltpu.with_memory_space_constraint(array, pltpu.HBM)


def send_kernel(rows, block, offset, width, sources, coded, place_ref, w_ref, turned_ref, *refs):
    near_refs, out_ref = refs[:sources], refs[sources]
    step = min(rows, STEP)
    first = (place_ref[0] ^ block) * width + offset
    part = part_of(rows)
    peaks = []
    for at in range(0, rows, step):
        total = jnp.dot(
            w_ref[pl.ds(pl.multiple_of(first + at, 16), step), :], turned_ref[...], preferred_element_type=jnp.float32
        )
        for near_ref in near_refs:
            total = total + decode(near_ref, 0, rows, at, step)
        if coded:
            total, more = encode(total, part)
            peaks += more
        out_ref[at : at + step, :] = total
    if coded:
        if len(peaks) < PEAKS:
            peaks.append(jnp.zeros((PEAKS - len(peaks), total.shape[1]), jnp.float32))
        out_ref[rows:, :] = jnp.concatenate(peaks, axis=0).astype(jnp.bfloat16)


def send(rows, block, offset, width, coded, place, weight, turned, nears):
    toks = turned.shape[1]
    vmem = pl.BlockSpec(memory_space=pltpu.VMEM)
    count = rows + PEAKS if coded else rows
    return pl.pallas_call(
        functools.partial(send_kernel, rows, block, offset, width, len(nears), coded),
        in_specs=[pl.BlockSpec(memory_space=pltpu.SMEM)] + [vmem] * (2 + len(nears)),
        out_specs=vmem,
        out_shape=jax.ShapeDtypeStruct((count, toks), jnp.bfloat16 if coded else jnp.float32),
        compiler_params=pltpu.CompilerParams(vmem_limit_bytes=VMEM),
        cost_estimate=QUICK,
    )(place, weight, turned, *nears)


def first_kernel(rows, block, offset, width, place_ref, w_hbm, g_hbm, out_ref, turned_ref, w_ref, g_ref, sems):
    step = min(rows, STEP)
    first = pl.multiple_of((place_ref[0] ^ block) * width + offset, 16)
    copies = [pltpu.make_async_copy(g_hbm, g_ref, sems.at[0])]
    for i, at in enumerate(range(0, rows, step)):
        copies.append(
            pltpu.make_async_copy(w_hbm.at[pl.ds(first + at, step), :], w_ref.at[pl.ds(at, step), :], sems.at[1 + i])
        )
    for copy in copies:
        copy.start()
    copies[0].wait()
    turned_ref[...] = g_ref[...].T
    part = part_of(rows)
    peaks = []
    for i, at in enumerate(range(0, rows, step)):
        copies[1 + i].wait()
        total = jnp.dot(w_ref[at : at + step, :], turned_ref[...], preferred_element_type=jnp.float32)
        total, more = encode(total, part)
        peaks += more
        out_ref[at : at + step, :] = total
    if len(peaks) < PEAKS:
        peaks.append(jnp.zeros((PEAKS - len(peaks), total.shape[1]), jnp.float32))
    out_ref[rows:, :] = jnp.concatenate(peaks, axis=0).astype(jnp.bfloat16)


def first_send(rows, block, offset, width, place, weight, grad):
    toks, depth = grad.shape
    vmem = pl.BlockSpec(memory_space=pltpu.VMEM)
    high = pl.BlockSpec(memory_space=pltpu.HBM)
    return pl.pallas_call(
        functools.partial(first_kernel, rows, block, offset, width),
        in_specs=[pl.BlockSpec(memory_space=pltpu.SMEM), high, high],
        out_specs=(vmem, vmem),
        out_shape=(
            jax.ShapeDtypeStruct((rows + PEAKS, toks), jnp.bfloat16),
            jax.ShapeDtypeStruct((depth, toks), jnp.bfloat16),
        ),
        scratch_shapes=[
            pltpu.VMEM((rows, depth), jnp.bfloat16),
            pltpu.VMEM((toks, depth), jnp.bfloat16),
            pltpu.SemaphoreType.DMA((1 + rows // min(rows, STEP),)),
        ],
        compiler_params=pltpu.CompilerParams(vmem_limit_bytes=VMEM),
        cost_estimate=QUICK,
    )(place, pinned(weight), pinned(grad))


def steps_back(count, body, state, unroll):
    def some(i, state):
        for j in range(unroll):
            state = body(count - 1 - (i * unroll + j), state)
        return state

    return lax.fori_loop(0, count // unroll, some, state)


def power(base, exponent):
    result = None
    while exponent:
        if exponent % 2:
            result = base if result is None else result * base
        base = base * base
        exponent //= 2
    return result


def segment_of(shape, segments):
    return lax.rem(lax.broadcasted_iota(jnp.int32, shape, 0), segments)


def rolled(value, by):
    by %= value.shape[0]
    return pltpu.roll(value, by, 0) if by else value


def gate_kernel(portion, rows, segments, fars, acc_ref, *refs):
    far_refs, refs = refs[: len(fars)], refs[len(fars) :]
    query_ref, conv_ref, decay_ref = refs[:3]
    out_hbm, gc_ref, state_ref, pack_ref, gq_ref, sem = refs[-6:]
    toks = query_ref.shape[0]
    modes, sublanes, lanes = state_ref.shape
    mine = slice(portion * sublanes, (portion + 1) * sublanes)
    for line in range(rows // lanes):
        mix = acc_ref[line * lanes : (line + 1) * lanes, :]
        for ref, base in zip(far_refs, fars):
            mix = mix + decode(ref, base, rows, line * lanes, lanes)
        mix = mix.T
        at = slice(line * lanes, (line + 1) * lanes)
        full = slice(portion * rows + line * lanes, portion * rows + (line + 1) * lanes)
        gq_ref[:, at] = (mix * conv_ref[:, full].astype(jnp.float32)).astype(jnp.bfloat16)
        gc_ref[line * toks : (line + 1) * toks, :] = mix * query_ref[:, full].astype(jnp.float32)
    store = pltpu.make_async_copy(gq_ref, out_hbm.at[:, pl.ds(portion * rows, rows)], sem)
    store.start()
    decay = [decay_ref[n, mine] for n in range(modes)]
    span = toks // segments

    def step(t, state):
        row = gc_ref[pl.ds(t, sublanes, stride=span), :]
        return tuple(decay[n] * state[n] + row for n in range(modes))

    zero = jnp.zeros((sublanes, lanes), jnp.float32)
    state = steps_back(span, step, (zero,) * modes, 8)
    segment = segment_of((sublanes, lanes), segments)
    whole = []
    for n in range(modes):
        state_ref[n] = state[n]
        total = state[n]
        if segments > 1:
            factor = jnp.where(segment < segments - 1, power(decay[n], span), 0.0)
            for _ in range(segments - 1):
                total = state[n] + factor * rolled(total, -1)
        whole.append(total)
    for m in range(modes // segments):
        packed = whole[m * segments]
        for j in range(1, segments):
            packed = jnp.where(segment == j, rolled(whole[m * segments + j], j), packed)
        pack_ref[m] = packed
    store.wait()


def gate(portion, rows, segments, acc, fars, query_in, conv_out, decay, partial):
    toks, width = query_in.shape
    modes, sublanes, lanes = decay.shape
    sublanes = rows // lanes * segments
    vmem = pl.BlockSpec(memory_space=pltpu.VMEM)
    high = pl.BlockSpec(memory_space=pltpu.HBM)
    more = [] if partial is None else [partial]
    return pl.pallas_call(
        functools.partial(gate_kernel, portion, rows, segments, (0,) * len(fars)),
        in_specs=[vmem] * (4 + len(fars)) + [high] * len(more),
        out_specs=(high, vmem, vmem, vmem),
        out_shape=(
            jax.ShapeDtypeStruct((toks, width), jnp.bfloat16),
            jax.ShapeDtypeStruct((rows // lanes * toks, lanes), jnp.float32),
            jax.ShapeDtypeStruct((modes, sublanes, lanes), jnp.float32),
            jax.ShapeDtypeStruct((modes // segments, sublanes, lanes), jnp.float32),
        ),
        scratch_shapes=[pltpu.VMEM((toks, rows), jnp.bfloat16), pltpu.SemaphoreType.DMA],
        input_output_aliases={4 + len(fars): 0} if more else {},
        compiler_params=pltpu.CompilerParams(vmem_limit_bytes=VMEM),
        cost_estimate=QUICK,
    )(acc, *fars, query_in, conv_out, decay, *more)


def summed(terms):
    while len(terms) > 1:
        terms = [terms[k] + terms[k + 1] if k + 1 < len(terms) else terms[k] for k in range(0, len(terms), 2)]
    return terms[0]


def scan_kernel(portion, segments, gc_ref, state_ref, decay_ref, residue_ref, rows_ref):
    modes, sublanes, lanes = state_ref.shape
    mine = slice(portion * sublanes, (portion + 1) * sublanes)
    span = gc_ref.shape[0] // sublanes
    segment = segment_of((sublanes, lanes), segments)
    decay = [decay_ref[n, mine] for n in range(modes)]
    start = []
    for n in range(modes):
        total = jnp.zeros((sublanes, lanes), jnp.float32)
        if segments > 1:
            group = power(decay[n], span)
            for k in range(segments - 2, -1, -1):
                total = jnp.where(segment == k, rolled(state_ref[n] + group * total, -1), total)
        start.append(total)

    def step(t, state):
        at = pl.ds(t, sublanes, stride=span)
        row = gc_ref[at, :]
        state = tuple(decay[n] * state[n] + row for n in range(modes))
        rows_ref[at, :] = summed([residue_ref[n, mine] * state[n] for n in range(modes)])
        return state

    steps_back(span, step, tuple(start), 8)


def scan(portion, segments, grad_conv, state, decay, residues):
    vmem = pl.BlockSpec(memory_space=pltpu.VMEM)
    return pl.pallas_call(
        functools.partial(scan_kernel, portion, segments),
        in_specs=[vmem] * 4,
        out_specs=vmem,
        out_shape=jax.ShapeDtypeStruct(grad_conv.shape, jnp.float32),
        compiler_params=pltpu.CompilerParams(vmem_limit_bytes=VMEM),
        cost_estimate=QUICK,
    )(grad_conv, state, decay, residues)


def fix_kernel(portion, segments, hops, rows_in_ref, *refs):
    later_refs, refs = refs[:hops], refs[hops:]
    decay_ref, residue_ref = refs[:2]
    out_hbm, rows_ref, out_ref, sem = refs[-4:]
    toks, rows = out_ref.shape
    sublanes, lanes = later_refs[0].shape[1:]
    modes = decay_ref.shape[0]
    mine = slice(portion * sublanes, (portion + 1) * sublanes)
    span = toks // segments
    segment = segment_of((sublanes, lanes), segments)
    decay = [decay_ref[n, mine] for n in range(modes)]
    start = []
    for n in range(modes):
        group = power(decay[n], span)
        m, j = divmod(n, segments)
        total = later_refs[-1][m]
        if hops > 1:
            whole = rolled(power(group, segments), 0)
            for ref in reversed(later_refs[:-1]):
                total = total * whole + ref[m]
        total = rolled(total, segments - 1 - j)
        for k in range(segments - 2, -1, -1):
            total = jnp.where(segment == k, rolled(group * total, -1), total)
        start.append(residue_ref[n, mine] * total)

    def step(t, state):
        at = pl.ds(t, sublanes, stride=span)
        state = tuple(decay[n] * state[n] for n in range(modes))
        rows_ref[at, :] = rows_in_ref[at, :] + summed(list(state))
        return state

    steps_back(span, step, tuple(start), 8)
    for line in range(rows // lanes):
        out_ref[:, line * lanes : (line + 1) * lanes] = rows_ref[
            line * toks : (line + 1) * toks, :
        ].astype(jnp.bfloat16)
    store = pltpu.make_async_copy(out_ref, out_hbm.at[:, pl.ds(portion * rows, rows)], sem)
    store.start()
    store.wait()


def fix(portion, rows, segments, scanned, laters, decay, residues, toks, width, partial):
    vmem = pl.BlockSpec(memory_space=pltpu.VMEM)
    high = pl.BlockSpec(memory_space=pltpu.HBM)
    more = [] if partial is None else [partial]
    return pl.pallas_call(
        functools.partial(fix_kernel, portion, segments, len(laters)),
        in_specs=[vmem] * (3 + len(laters)) + [high] * len(more),
        out_specs=high,
        out_shape=jax.ShapeDtypeStruct((toks, width), jnp.bfloat16),
        scratch_shapes=[
            pltpu.VMEM(scanned.shape, jnp.float32),
            pltpu.VMEM((toks, rows), jnp.bfloat16),
            pltpu.SemaphoreType.DMA,
        ],
        input_output_aliases={3 + len(laters): 0} if more else {},
        compiler_params=pltpu.CompilerParams(vmem_limit_bytes=VMEM),
        cost_estimate=QUICK,
    )(scanned, *laters, decay, residues, *more)


def local(out_grad, out_weight, query_in, conv_out, residues, decay_rates):
    toks, width = query_in.shape
    modes = decay_rates.shape[1]
    lanes = math.gcd(width, 128)
    size = lax.axis_size("ch")
    bits = [1 << i for i in range(size.bit_length() - 1)]
    place = jnp.reshape(lax.axis_index("ch"), (1,)).astype(jnp.int32)
    rows = width // 2
    lines = rows // lanes
    segments = 8 // lines
    by_mode = lambda values: jnp.repeat(values.T.reshape(modes, width // lanes, lanes), segments, axis=1)
    decay, residue = by_mode(decay_rates), by_mode(residues)

    order = ORDER
    if size != 8:
        order = [
            (p, s, block)
            for p in range(2)
            for s, bit in enumerate(bits)
            for block in sorted(range(0, size, 2 * bit), reverse=True)
        ] + [(p, kind) for kind in ("sum", "gate", "scan", "fix") for p in range(2)]
    groups = lax.axis_size("ctx")
    received, sums, gated, scanned, laters = {}, {}, {}, {}, {}
    grad_query = grad_input = last = None

    def after(value):
        return value if last is None else lax.optimization_barrier((value, last))[0]

    for p, s, *block in order:
        if s == "sum":
            last = sums[p] = send(rows, 0, p * rows, width, False, after(place), out_weight, turned, [received[p, 0, 0]])
        elif s == "gate":
            fars = [received[p, s, 0] for s in range(1, len(bits))]
            grad_query, grad_conv, state, packed = gate(
                p, rows, segments, after(sums[p]), fars, query_in, conv_out, decay, grad_query
            )
            last, gated[p] = packed, (grad_conv, state)
            laters[p] = [
                lax.ppermute(packed, "ctx", [(i, i - hop) for i in range(hop, groups)]) for hop in range(1, groups)
            ]
        elif s == "scan":
            last = scanned[p] = scan(p, segments, *gated[p], decay, residue)
        elif s == "fix":
            grad_input = fix(
                p, rows, segments, after(scanned[p]), laters[p], decay, residue, toks, width, grad_input
            )
        else:
            (block,), bit = block, bits[s]
            if last is None:
                last, turned = first_send(rows, block ^ bit, p * rows, width, place, out_weight, out_grad)
            else:
                nears = [received[p, i, block ^ bit] for i in range(s)]
                last = send(rows, block ^ bit, p * rows, width, True, after(place), out_weight, turned, nears)
            received[p, s, block] = lax.ppermute(last, "ch", [(i, i ^ bit) for i in range(size)])
    return grad_query, grad_input


def solution(mesh):
    placed = (
        P("ctx", "ch"),
        P(None, "ch"),
        P("ctx", "ch"),
        P("ctx", "ch"),
        P("ch", None),
        P("ch", None),
    )
    return jax.shard_map(
        local,
        mesh=mesh,
        in_specs=placed,
        out_specs=(P("ctx", "ch"), P("ctx", "ch")),
        check_vma=False,
    )
```

```python
import functools
import math

import jax
import jax.numpy as jnp
from jax import lax
from jax.experimental import pallas as pl
from jax.experimental.pallas import tpu as pltpu
from jax.sharding import PartitionSpec as P

PEAKS = 16
SPAN = 251 * math.log(2.0)
SHIFT = 125 * math.log(2.0)
STEP = 256
VMEM = 24 * 1024 * 1024
QUICK = pl.CostEstimate(flops=0, bytes_accessed=1024, transcendentals=0)

PORTIONS = (((0, 1, 2), 2, 0), ((0, 1, 2), 2, 1))
ORDER = (
    (0, 0, (6,)), (0, 0, (4,)), (1, 0, (2,)), (0, 0, (2,)), (0, 0, (0,)), (1, 0, (4,)), (1, 0, (6,)), (0, 1, (4,)),
    (0, 1, (0,)), (1, 0, (0,)), (1, 1, (4,)), (0, 2, (0,)), (1, 1, (0,)), (1, 2, (0,)), (0, "sum"), (0, "gate"),
    (1, "sum"), (0, "scan"), (1, "gate"), (1, "scan"), (0, "fix"), (1, "fix"),
)
GATHERED = (True, False)


def part_of(rows):
    return next(part for part in range(16, rows + 1, 16) if rows % part == 0 and rows // part <= PEAKS)


def step_of(rows):
    return next(step for step in (STEP, STEP // 2, rows) if rows % step == 0)


def encode(block, part):
    codes, peaks = [], []
    for i in range(block.shape[0] // part):
        piece = block[i * part : (i + 1) * part, :]
        size = jnp.abs(piece)
        peak = jnp.maximum(jnp.max(size, axis=0, keepdims=True) * 1.01, 1e-30)
        peak = peak.astype(jnp.bfloat16).astype(jnp.float32)
        code = jnp.exp(size * (SPAN / peak) - SHIFT)
        codes.append(jnp.where(piece < 0, -code, code))
        peaks.append(peak)
    return jnp.concatenate(codes, axis=0).astype(jnp.bfloat16), peaks


def decode(ref, base, rows, first, count):
    part = part_of(rows)
    peaks = ref[base + rows : base + rows + PEAKS, :].astype(jnp.float32) * (1.0 / SPAN)
    blocks = []
    for i in range(first // part, (first + count) // part):
        code = ref[base + i * part : base + (i + 1) * part, :].astype(jnp.float32)
        size = (jnp.log(jnp.abs(code)) + SHIFT) * peaks[i : i + 1, :]
        blocks.append(jnp.where(code < 0, -size, size))
    return jnp.concatenate(blocks, axis=0)


def pinned(array):
    return pltpu.with_memory_space_constraint(array, pltpu.HBM)


def send_kernel(items, coded, width, near, place_ref, w_ref, turned_ref, *refs):
    near_refs, out_ref = refs[:near], refs[near]
    base = 0
    for block, offset, rows, sources in items:
        step, part = step_of(rows), part_of(rows)
        first = (place_ref[0] ^ block) * width + offset
        peaks = []
        for at in range(0, rows, step):
            total = jnp.dot(
                w_ref[pl.ds(pl.multiple_of(first + at, 16), step), :],
                turned_ref[...],
                preferred_element_type=jnp.float32,
            )
            for source, start in sources:
                total = total + decode(near_refs[source], start, rows, at, step)
            if coded:
                total, more = encode(total, part)
                peaks += more
            out_ref[base + at : base + at + step, :] = total
        base += rows
        if coded:
            if len(peaks) < PEAKS:
                peaks.append(jnp.zeros((PEAKS - len(peaks), total.shape[1]), jnp.float32))
            out_ref[base : base + PEAKS, :] = jnp.concatenate(peaks, axis=0).astype(jnp.bfloat16)
            base += PEAKS


def send(items, coded, width, place, weight, turned, nears):
    toks = turned.shape[1]
    vmem = pl.BlockSpec(memory_space=pltpu.VMEM)
    count = sum(rows + PEAKS if coded else rows for _, _, rows, _ in items)
    return pl.pallas_call(
        functools.partial(send_kernel, items, coded, width, len(nears)),
        in_specs=[pl.BlockSpec(memory_space=pltpu.SMEM)] + [vmem] * (2 + len(nears)),
        out_specs=vmem,
        out_shape=jax.ShapeDtypeStruct((count, toks), jnp.bfloat16 if coded else jnp.float32),
        compiler_params=pltpu.CompilerParams(vmem_limit_bytes=VMEM),
        cost_estimate=QUICK,
    )(place, weight, turned, *nears)


def first_kernel(rows, block, offset, width, place_ref, w_hbm, g_hbm, out_ref, turned_ref, w_ref, g_ref, sems):
    step = step_of(rows)
    first = pl.multiple_of((place_ref[0] ^ block) * width + offset, 16)
    copies = [pltpu.make_async_copy(g_hbm, g_ref, sems.at[0])]
    for i, at in enumerate(range(0, rows, step)):
        copies.append(
            pltpu.make_async_copy(w_hbm.at[pl.ds(first + at, step), :], w_ref.at[pl.ds(at, step), :], sems.at[1 + i])
        )
    for copy in copies:
        copy.start()
    copies[0].wait()
    turned_ref[...] = g_ref[...].T
    part = part_of(rows)
    peaks = []
    for i, at in enumerate(range(0, rows, step)):
        copies[1 + i].wait()
        total = jnp.dot(w_ref[at : at + step, :], turned_ref[...], preferred_element_type=jnp.float32)
        total, more = encode(total, part)
        peaks += more
        out_ref[at : at + step, :] = total
    if len(peaks) < PEAKS:
        peaks.append(jnp.zeros((PEAKS - len(peaks), total.shape[1]), jnp.float32))
    out_ref[rows:, :] = jnp.concatenate(peaks, axis=0).astype(jnp.bfloat16)


def first_send(rows, block, offset, width, place, weight, grad):
    toks, depth = grad.shape
    vmem = pl.BlockSpec(memory_space=pltpu.VMEM)
    high = pl.BlockSpec(memory_space=pltpu.HBM)
    return pl.pallas_call(
        functools.partial(first_kernel, rows, block, offset, width),
        in_specs=[pl.BlockSpec(memory_space=pltpu.SMEM), high, high],
        out_specs=(vmem, vmem),
        out_shape=(
            jax.ShapeDtypeStruct((rows + PEAKS, toks), jnp.bfloat16),
            jax.ShapeDtypeStruct((depth, toks), jnp.bfloat16),
        ),
        scratch_shapes=[
            pltpu.VMEM((rows, depth), jnp.bfloat16),
            pltpu.VMEM((toks, depth), jnp.bfloat16),
            pltpu.SemaphoreType.DMA((1 + rows // step_of(rows),)),
        ],
        compiler_params=pltpu.CompilerParams(vmem_limit_bytes=VMEM),
        cost_estimate=QUICK,
    )(place, pinned(weight), pinned(grad))


def steps_back(count, body, state, unroll):
    def some(i, state):
        for j in range(unroll):
            state = body(count - 1 - (i * unroll + j), state)
        return state

    return lax.fori_loop(0, count // unroll, some, state)


def power(base, exponent):
    result = None
    while exponent:
        if exponent % 2:
            result = base if result is None else result * base
        base = base * base
        exponent //= 2
    return result


def segment_of(shape, segments):
    return lax.rem(lax.broadcasted_iota(jnp.int32, shape, 0), segments)


def rolled(value, by):
    by %= value.shape[0]
    return pltpu.roll(value, by, 0) if by else value


def gate_kernel(half, rows, segments, pieces, near, acc_ref, *refs):
    near_refs, refs = refs[:near], refs[near:]
    query_ref, conv_ref, decay_ref = refs[:3]
    out_hbm, gc_ref, state_ref, pack_ref, gq_ref, sem = refs[-6:]
    toks = query_ref.shape[0]
    modes, sublanes, lanes = state_ref.shape
    mine = slice(half * sublanes, (half + 1) * sublanes)
    for line in range(rows // lanes):
        mix = acc_ref[line * lanes : (line + 1) * lanes, :]
        first, count, sources = next(piece for piece in reversed(pieces) if piece[0] <= line * lanes)
        for source, start in sources:
            mix = mix + decode(near_refs[source], start, count, line * lanes - first, lanes)
        mix = mix.T
        at = slice(line * lanes, (line + 1) * lanes)
        full = slice(half * rows + line * lanes, half * rows + (line + 1) * lanes)
        gq_ref[:, at] = (mix * conv_ref[:, full].astype(jnp.float32)).astype(jnp.bfloat16)
        gc_ref[line * toks : (line + 1) * toks, :] = mix * query_ref[:, full].astype(jnp.float32)
    store = pltpu.make_async_copy(gq_ref, out_hbm.at[:, pl.ds(half * rows, rows)], sem)
    store.start()
    decay = [decay_ref[n, mine] for n in range(modes)]
    span = toks // segments

    def step(t, state):
        row = gc_ref[pl.ds(t, sublanes, stride=span), :]
        return tuple(decay[n] * state[n] + row for n in range(modes))

    zero = jnp.zeros((sublanes, lanes), jnp.float32)
    state = steps_back(span, step, (zero,) * modes, 8)
    segment = segment_of((sublanes, lanes), segments)
    whole = []
    for n in range(modes):
        state_ref[n] = state[n]
        total = state[n]
        if segments > 1:
            factor = jnp.where(segment < segments - 1, power(decay[n], span), 0.0)
            for _ in range(segments - 1):
                total = state[n] + factor * rolled(total, -1)
        whole.append(total)
    for m in range(modes // segments):
        packed = whole[m * segments]
        for j in range(1, segments):
            packed = jnp.where(segment == j, rolled(whole[m * segments + j], j), packed)
        for copy in range(pack_ref.shape[0]):
            pack_ref[copy, m] = packed
    store.wait()


def gate(half, rows, segments, copies, pieces, acc, nears, query_in, conv_out, decay, partial):
    toks, width = query_in.shape
    modes, sublanes, lanes = decay.shape
    sublanes = rows // lanes * segments
    vmem = pl.BlockSpec(memory_space=pltpu.VMEM)
    high = pl.BlockSpec(memory_space=pltpu.HBM)
    more = [] if partial is None else [partial]
    return pl.pallas_call(
        functools.partial(gate_kernel, half, rows, segments, pieces, len(nears)),
        in_specs=[vmem] * (4 + len(nears)) + [high] * len(more),
        out_specs=(high, vmem, vmem, vmem),
        out_shape=(
            jax.ShapeDtypeStruct((toks, width), jnp.bfloat16),
            jax.ShapeDtypeStruct((rows // lanes * toks, lanes), jnp.float32),
            jax.ShapeDtypeStruct((modes, sublanes, lanes), jnp.float32),
            jax.ShapeDtypeStruct((copies, modes // segments, sublanes, lanes), jnp.float32),
        ),
        scratch_shapes=[pltpu.VMEM((toks, rows), jnp.bfloat16), pltpu.SemaphoreType.DMA],
        input_output_aliases={4 + len(nears): 0} if more else {},
        compiler_params=pltpu.CompilerParams(vmem_limit_bytes=VMEM),
        cost_estimate=QUICK,
    )(acc, *nears, query_in, conv_out, decay, *more)


def summed(terms):
    while len(terms) > 1:
        terms = [terms[k] + terms[k + 1] if k + 1 < len(terms) else terms[k] for k in range(0, len(terms), 2)]
    return terms[0]


def scan_kernel(half, segments, gc_ref, state_ref, decay_ref, residue_ref, rows_ref):
    modes, sublanes, lanes = state_ref.shape
    mine = slice(half * sublanes, (half + 1) * sublanes)
    span = gc_ref.shape[0] // sublanes
    segment = segment_of((sublanes, lanes), segments)
    decay = [decay_ref[n, mine] for n in range(modes)]
    start = []
    for n in range(modes):
        total = jnp.zeros((sublanes, lanes), jnp.float32)
        if segments > 1:
            group = power(decay[n], span)
            for k in range(segments - 2, -1, -1):
                total = jnp.where(segment == k, rolled(state_ref[n] + group * total, -1), total)
        start.append(total)

    def step(t, state):
        at = pl.ds(t, sublanes, stride=span)
        row = gc_ref[at, :]
        state = tuple(decay[n] * state[n] + row for n in range(modes))
        rows_ref[at, :] = summed([residue_ref[n, mine] * state[n] for n in range(modes)])
        return state

    steps_back(span, step, tuple(start), 8)


def scan(half, segments, grad_conv, state, decay, residues):
    vmem = pl.BlockSpec(memory_space=pltpu.VMEM)
    return pl.pallas_call(
        functools.partial(scan_kernel, half, segments),
        in_specs=[vmem] * 4,
        out_specs=vmem,
        out_shape=jax.ShapeDtypeStruct(grad_conv.shape, jnp.float32),
        compiler_params=pltpu.CompilerParams(vmem_limit_bytes=VMEM),
        cost_estimate=QUICK,
    )(grad_conv, state, decay, residues)


def fix_kernel(half, segments, group_ref, rows_in_ref, states_ref, decay_ref, residue_ref, *refs):
    out_hbm, rows_ref, out_ref, sem = refs[-4:]
    toks, rows = out_ref.shape
    groups, _, sublanes, lanes = states_ref.shape
    modes = decay_ref.shape[0]
    mine = slice(half * sublanes, (half + 1) * sublanes)
    span = toks // segments
    segment = segment_of((sublanes, lanes), segments)
    decay = [decay_ref[n, mine] for n in range(modes)]
    start = []
    for n in range(modes):
        lap = power(decay[n], span)
        whole = power(lap, segments)
        m, j = divmod(n, segments)
        total = jnp.zeros((sublanes, lanes), jnp.float32)
        for group in range(groups - 1, 0, -1):
            state = rolled(states_ref[group, m], segments - 1 - j)
            total = jnp.where(group > group_ref[0], total * whole + state, total)
        for k in range(segments - 2, -1, -1):
            total = jnp.where(segment == k, rolled(lap * total, -1), total)
        start.append(residue_ref[n, mine] * total)

    def step(t, state):
        at = pl.ds(t, sublanes, stride=span)
        state = tuple(decay[n] * state[n] for n in range(modes))
        rows_ref[at, :] = rows_in_ref[at, :] + summed(list(state))
        return state

    steps_back(span, step, tuple(start), 8)
    for line in range(rows // lanes):
        out_ref[:, line * lanes : (line + 1) * lanes] = rows_ref[
            line * toks : (line + 1) * toks, :
        ].astype(jnp.bfloat16)
    store = pltpu.make_async_copy(out_ref, out_hbm.at[:, pl.ds(half * rows, rows)], sem)
    store.start()
    store.wait()


def fix(half, rows, segments, group, scanned, states, decay, residues, toks, width, partial):
    vmem = pl.BlockSpec(memory_space=pltpu.VMEM)
    high = pl.BlockSpec(memory_space=pltpu.HBM)
    more = [] if partial is None else [partial]
    return pl.pallas_call(
        functools.partial(fix_kernel, half, segments),
        in_specs=[pl.BlockSpec(memory_space=pltpu.SMEM)] + [vmem] * 4 + [high] * len(more),
        out_specs=high,
        out_shape=jax.ShapeDtypeStruct((toks, width), jnp.bfloat16),
        scratch_shapes=[
            pltpu.VMEM(scanned.shape, jnp.float32),
            pltpu.VMEM((toks, rows), jnp.bfloat16),
            pltpu.SemaphoreType.DMA,
        ],
        input_output_aliases={5: 0} if more else {},
        compiler_params=pltpu.CompilerParams(vmem_limit_bytes=VMEM),
        cost_estimate=QUICK,
    )(group, scanned, states, decay, residues, *more)


def local(out_grad, out_weight, query_in, conv_out, residues, decay_rates):
    toks, width = query_in.shape
    modes = decay_rates.shape[1]
    lanes = math.gcd(width, 128)
    size, groups = lax.axis_size("ch"), lax.axis_size("ctx")
    bits = [1 << i for i in range(size.bit_length() - 1)]
    place = jnp.reshape(lax.axis_index("ch"), (1,)).astype(jnp.int32)
    group = jnp.reshape(lax.axis_index("ctx"), (1,)).astype(jnp.int32)
    half_rows = width // 2
    lines = half_rows // lanes
    segments = 8 // lines
    by_mode = lambda values: jnp.repeat(values.T.reshape(modes, width // lanes, lanes), segments, axis=1)
    decay, residue = by_mode(decay_rates), by_mode(residues)

    portions, order = PORTIONS, ORDER
    if size != 8:
        portions = ((tuple(range(len(bits))), 2, 0), (tuple(range(len(bits))), 2, 1))
        order = [
            (p, s, (block,))
            for p in range(2)
            for s, bit in enumerate(bits)
            for block in sorted(range(0, size, 2 * bit), reverse=True)
        ] + [(p, kind) for kind in ("sum", "gate", "scan", "fix") for p in range(2)]
    offsets = [sum(width // part for _, part, _ in portions[:p]) for p in range(len(portions))]

    received, sums, gated, scanned, states = {}, {}, {}, {}, {}
    grad_query = grad_input = last = None

    def after(value):
        return value if last is None else lax.optimization_barrier((value, last))[0]

    def collect(wanted):
        arrays, places = [], []
        for key in wanted:
            array, start = received[key]
            index = next((i for i, known in enumerate(arrays) if known is array), len(arrays))
            if index == len(arrays):
                arrays.append(array)
            places.append((index, start))
        return arrays, places

    for p, s, *blocks in order:
        inside = [q for q, (_, _, half) in enumerate(portions) if half == p]
        if s == "sum":
            arrays, places = collect([(q, 0, 0) for q in inside])
            items = tuple((0, offsets[q], width // portions[q][1], (at,)) for q, at in zip(inside, places))
            last = sums[p] = send(items, False, width, after(place), out_weight, turned, arrays)
        elif s == "gate":
            later = range(1, len(bits))
            arrays, places = collect([(q, i, 0) for q in inside for i in later])
            pieces = tuple(
                (
                    offsets[q] - p * half_rows,
                    width // portions[q][1],
                    tuple(places[i * len(later) : (i + 1) * len(later)]),
                )
                for i, q in enumerate(inside)
            )
            copies = 1 if GATHERED[p] else groups
            grad_query, grad_conv, state, packed = gate(
                p, half_rows, segments, copies, pieces, after(sums[p]), arrays, query_in, conv_out, decay, grad_query
            )
            last, gated[p] = packed, (grad_conv, state)
            if GATHERED[p]:
                states[p] = lax.all_gather(packed, "ctx", tiled=True)
            else:
                states[p] = lax.all_to_all(packed, "ctx", 0, 0, tiled=True)
        elif s == "scan":
            last = scanned[p] = scan(p, segments, *gated[p], decay, residue)
        elif s == "fix":
            last = grad_input = fix(
                p, half_rows, segments, group, after(scanned[p]), states[p], decay, residue, toks, width, grad_input
            )
        else:
            route, part, _ = portions[p]
            rows, (blocks,) = width // part, blocks
            bit = bits[route[s]]
            if last is None:
                last, turned = first_send(rows, blocks[0] ^ bit, offsets[p], width, place, out_weight, out_grad)
            else:
                wanted = [(p, i, block ^ bit) for block in blocks for i in range(s)]
                arrays, places = collect(wanted)
                items = tuple(
                    (block ^ bit, offsets[p], rows, tuple(places[i * s : (i + 1) * s]))
                    for i, block in enumerate(blocks)
                )
                last = send(items, True, width, after(place), out_weight, turned, arrays)
            arrived = lax.ppermute(last, "ch", [(i, i ^ bit) for i in range(size)])
            for i, block in enumerate(blocks):
                received[p, s, block] = (arrived, i * (rows + PEAKS))
    return grad_query, grad_input


def solution(mesh):
    placed = (
        P("ctx", "ch"),
        P(None, "ch"),
        P("ctx", "ch"),
        P("ctx", "ch"),
        P("ch", None),
        P("ch", None),
    )
    return jax.shard_map(
        local,
        mesh=mesh,
        in_specs=placed,
        out_specs=(P("ctx", "ch"), P("ctx", "ch")),
        check_vma=False,
    )
```

```python
import functools
import math

import jax
import jax.numpy as jnp
from jax import lax
from jax.experimental import pallas as pl
from jax.experimental.pallas import tpu as pltpu
from jax.sharding import PartitionSpec as P

PEAKS = 16
SPAN = 251 * math.log(2.0)
SHIFT = 125 * math.log(2.0)
STEP = 256
VMEM = 24 * 1024 * 1024
QUICK = pl.CostEstimate(flops=0, bytes_accessed=1024, transcendentals=0)

PORTIONS = (((0, 1, 2), 2, 0), ((0, 1, 2), 4, 1), ((1, 0, 2), 4, 1))
ORDER = (
    (0, 0, (6,)), (1, 0, (4,)), (1, 0, (6,)), (2, 0, (5, 4, 1, 0)), (0, 0, (4, 2)), (0, 1, (4,)), (0, 0, (0,)),
    (1, 1, (4,)), (1, 0, (2,)), (2, 1, (4, 0)), (0, 1, (0,)), (0, 2, (0,)), (1, 1, (0,)), (0, "sum"), (1, 0, (0,)),
    (1, 2, (0,)), (0, "gate"), (2, 2, (0,)), (0, "scan"), (1, "sum"), (1, "gate"), (0, "fix"), (1, "scan"), (1, "fix"),
)


def part_of(rows, blocks):
    return next(part for part in range(16, rows + 1, 16) if rows % part == 0 and rows // part * blocks <= PEAKS)


def step_of(rows):
    return next(step for step in (STEP, STEP // 2, rows) if rows % step == 0)


def encode(block, part):
    codes, peaks = [], []
    for i in range(block.shape[0] // part):
        piece = block[i * part : (i + 1) * part, :]
        size = jnp.abs(piece)
        peak = jnp.maximum(jnp.max(size, axis=0, keepdims=True) * 1.01, 1e-30)
        peak = peak.astype(jnp.bfloat16).astype(jnp.float32)
        code = jnp.exp(size * (SPAN / peak) - SHIFT)
        codes.append(jnp.where(piece < 0, -code, code))
        peaks.append(peak)
    return jnp.concatenate(codes, axis=0).astype(jnp.bfloat16), peaks


def put_peaks(peaks, out_ref):
    if len(peaks) < PEAKS:
        peaks = peaks + [jnp.zeros((PEAKS - len(peaks), peaks[0].shape[1]), jnp.float32)]
    out_ref[out_ref.shape[0] - PEAKS :, :] = jnp.concatenate(peaks, axis=0).astype(jnp.bfloat16)


def decode(ref, place, first, count):
    start, peak, part = place
    peaks = ref[ref.shape[0] - PEAKS :, :].astype(jnp.float32) * (1.0 / SPAN)
    blocks = []
    for i in range(first // part, -(-(first + count) // part)):
        low, high = max(first, i * part), min(first + count, (i + 1) * part)
        code = ref[start + low : start + high, :].astype(jnp.float32)
        size = (jnp.log(jnp.abs(code)) + SHIFT) * peaks[peak + i : peak + i + 1, :]
        blocks.append(jnp.where(code < 0, -size, size))
    return jnp.concatenate(blocks, axis=0)


def pinned(array):
    return pltpu.with_memory_space_constraint(array, pltpu.HBM)


def send_kernel(items, coded, width, near, place_ref, w_ref, turned_ref, *refs):
    near_refs, out_ref = refs[:near], refs[near]
    base, peaks = 0, []
    for block, offset, rows, sources in items:
        step = step_of(rows)
        first = (place_ref[0] ^ block) * width + offset
        for at in range(0, rows, step):
            total = jnp.dot(
                w_ref[pl.ds(pl.multiple_of(first + at, 16), step), :],
                turned_ref[...],
                preferred_element_type=jnp.float32,
            )
            for source, place in sources:
                total = total + decode(near_refs[source], place, at, step)
            if coded:
                total, more = encode(total, part_of(rows, len(items)))
                peaks += more
            out_ref[base + at : base + at + step, :] = total
        base += rows
    if coded:
        put_peaks(peaks, out_ref)


def send(items, coded, width, place, weight, turned, nears):
    toks = turned.shape[1]
    vmem = pl.BlockSpec(memory_space=pltpu.VMEM)
    count = sum(rows for _, _, rows, _ in items) + (PEAKS if coded else 0)
    return pl.pallas_call(
        functools.partial(send_kernel, items, coded, width, len(nears)),
        in_specs=[pl.BlockSpec(memory_space=pltpu.SMEM)] + [vmem] * (2 + len(nears)),
        out_specs=vmem,
        out_shape=jax.ShapeDtypeStruct((count, toks), jnp.bfloat16 if coded else jnp.float32),
        compiler_params=pltpu.CompilerParams(vmem_limit_bytes=VMEM),
        cost_estimate=QUICK,
    )(place, weight, turned, *nears)


def first_kernel(items, width, place_ref, w_hbm, g_hbm, out_ref, turned_ref, w_ref, g_ref, sems):
    copies = [pltpu.make_async_copy(g_hbm, g_ref, sems.at[0])]
    base = 0
    for block, offset, rows, _ in items:
        step = step_of(rows)
        first = pl.multiple_of((place_ref[0] ^ block) * width + offset, 16)
        for at in range(0, rows, step):
            copies.append(
                pltpu.make_async_copy(
                    w_hbm.at[pl.ds(first + at, step), :], w_ref.at[pl.ds(base + at, step), :], sems.at[len(copies)]
                )
            )
        base += rows
    for copy in copies:
        copy.start()
    copies[0].wait()
    turned_ref[...] = g_ref[...].T
    base, peaks, waits = 0, [], iter(copies[1:])
    for _, _, rows, _ in items:
        step = step_of(rows)
        for at in range(base, base + rows, step):
            next(waits).wait()
            total = jnp.dot(w_ref[at : at + step, :], turned_ref[...], preferred_element_type=jnp.float32)
            total, more = encode(total, part_of(rows, len(items)))
            peaks += more
            out_ref[at : at + step, :] = total
        base += rows
    put_peaks(peaks, out_ref)


def first_send(items, width, place, weight, grad):
    toks, depth = grad.shape
    vmem = pl.BlockSpec(memory_space=pltpu.VMEM)
    high = pl.BlockSpec(memory_space=pltpu.HBM)
    count = sum(rows for _, _, rows, _ in items)
    steps = sum(rows // step_of(rows) for _, _, rows, _ in items)
    return pl.pallas_call(
        functools.partial(first_kernel, items, width),
        in_specs=[pl.BlockSpec(memory_space=pltpu.SMEM), high, high],
        out_specs=(vmem, vmem),
        out_shape=(
            jax.ShapeDtypeStruct((count + PEAKS, toks), jnp.bfloat16),
            jax.ShapeDtypeStruct((depth, toks), jnp.bfloat16),
        ),
        scratch_shapes=[
            pltpu.VMEM((count, depth), jnp.bfloat16),
            pltpu.VMEM((toks, depth), jnp.bfloat16),
            pltpu.SemaphoreType.DMA((1 + steps,)),
        ],
        compiler_params=pltpu.CompilerParams(vmem_limit_bytes=VMEM),
        cost_estimate=QUICK,
    )(place, pinned(weight), pinned(grad))


def steps_back(count, body, state, unroll):
    def some(i, state):
        for j in range(unroll):
            state = body(count - 1 - (i * unroll + j), state)
        return state

    return lax.fori_loop(0, count // unroll, some, state)


def power(base, exponent):
    result = None
    while exponent:
        if exponent % 2:
            result = base if result is None else result * base
        base = base * base
        exponent //= 2
    return result


def segment_of(shape, segments):
    return lax.rem(lax.broadcasted_iota(jnp.int32, shape, 0), segments)


def rolled(value, by):
    by %= value.shape[0]
    return pltpu.roll(value, by, 0) if by else value


def gate_kernel(half, rows, segments, pieces, near, acc_ref, *refs):
    near_refs, refs = refs[:near], refs[near:]
    query_ref, conv_ref, decay_ref = refs[:3]
    out_hbm, gc_ref, state_ref, pack_ref, gq_ref, sem = refs[-6:]
    toks = query_ref.shape[0]
    modes, sublanes, lanes = state_ref.shape
    mine = slice(half * sublanes, (half + 1) * sublanes)
    for line in range(rows // lanes):
        mix = acc_ref[line * lanes : (line + 1) * lanes, :]
        first, sources = next(piece for piece in reversed(pieces) if piece[0] <= line * lanes)
        for source, place in sources:
            mix = mix + decode(near_refs[source], place, line * lanes - first, lanes)
        mix = mix.T
        at = slice(line * lanes, (line + 1) * lanes)
        full = slice(half * rows + line * lanes, half * rows + (line + 1) * lanes)
        gq_ref[:, at] = (mix * conv_ref[:, full].astype(jnp.float32)).astype(jnp.bfloat16)
        gc_ref[line * toks : (line + 1) * toks, :] = mix * query_ref[:, full].astype(jnp.float32)
    store = pltpu.make_async_copy(gq_ref, out_hbm.at[:, pl.ds(half * rows, rows)], sem)
    store.start()
    decay = [decay_ref[n, mine] for n in range(modes)]
    span = toks // segments

    def step(t, state):
        row = gc_ref[pl.ds(t, sublanes, stride=span), :]
        return tuple(decay[n] * state[n] + row for n in range(modes))

    zero = jnp.zeros((sublanes, lanes), jnp.float32)
    state = steps_back(span, step, (zero,) * modes, 8)
    segment = segment_of((sublanes, lanes), segments)
    whole = []
    for n in range(modes):
        state_ref[n] = state[n]
        total = state[n]
        if segments > 1:
            factor = jnp.where(segment < segments - 1, power(decay[n], span), 0.0)
            for _ in range(segments - 1):
                total = state[n] + factor * rolled(total, -1)
        whole.append(total)
    for m in range(modes // segments):
        packed = whole[m * segments]
        for j in range(1, segments):
            packed = jnp.where(segment == j, rolled(whole[m * segments + j], j), packed)
        for copy in range(pack_ref.shape[0]):
            pack_ref[copy, m] = packed
    store.wait()


def gate(half, rows, segments, copies, pieces, acc, nears, query_in, conv_out, decay, partial):
    toks, width = query_in.shape
    modes, sublanes, lanes = decay.shape
    sublanes = rows // lanes * segments
    vmem = pl.BlockSpec(memory_space=pltpu.VMEM)
    high = pl.BlockSpec(memory_space=pltpu.HBM)
    more = [] if partial is None else [partial]
    return pl.pallas_call(
        functools.partial(gate_kernel, half, rows, segments, pieces, len(nears)),
        in_specs=[vmem] * (4 + len(nears)) + [high] * len(more),
        out_specs=(high, vmem, vmem, vmem),
        out_shape=(
            jax.ShapeDtypeStruct((toks, width), jnp.bfloat16),
            jax.ShapeDtypeStruct((rows // lanes * toks, lanes), jnp.float32),
            jax.ShapeDtypeStruct((modes, sublanes, lanes), jnp.float32),
            jax.ShapeDtypeStruct((copies, modes // segments, sublanes, lanes), jnp.float32),
        ),
        scratch_shapes=[pltpu.VMEM((toks, rows), jnp.bfloat16), pltpu.SemaphoreType.DMA],
        input_output_aliases={4 + len(nears): 0} if more else {},
        compiler_params=pltpu.CompilerParams(vmem_limit_bytes=VMEM),
        cost_estimate=QUICK,
    )(acc, *nears, query_in, conv_out, decay, *more)


def summed(terms):
    while len(terms) > 1:
        terms = [terms[k] + terms[k + 1] if k + 1 < len(terms) else terms[k] for k in range(0, len(terms), 2)]
    return terms[0]


def scan_kernel(half, segments, gc_ref, state_ref, decay_ref, residue_ref, rows_ref):
    modes, sublanes, lanes = state_ref.shape
    mine = slice(half * sublanes, (half + 1) * sublanes)
    span = gc_ref.shape[0] // sublanes
    segment = segment_of((sublanes, lanes), segments)
    decay = [decay_ref[n, mine] for n in range(modes)]
    start = []
    for n in range(modes):
        total = jnp.zeros((sublanes, lanes), jnp.float32)
        if segments > 1:
            group = power(decay[n], span)
            for k in range(segments - 2, -1, -1):
                total = jnp.where(segment == k, rolled(state_ref[n] + group * total, -1), total)
        start.append(total)

    def step(t, state):
        at = pl.ds(t, sublanes, stride=span)
        row = gc_ref[at, :]
        state = tuple(decay[n] * state[n] + row for n in range(modes))
        rows_ref[at, :] = summed([residue_ref[n, mine] * state[n] for n in range(modes)])
        return state

    steps_back(span, step, tuple(start), 8)


def scan(half, segments, grad_conv, state, decay, residues):
    vmem = pl.BlockSpec(memory_space=pltpu.VMEM)
    return pl.pallas_call(
        functools.partial(scan_kernel, half, segments),
        in_specs=[vmem] * 4,
        out_specs=vmem,
        out_shape=jax.ShapeDtypeStruct(grad_conv.shape, jnp.float32),
        compiler_params=pltpu.CompilerParams(vmem_limit_bytes=VMEM),
        cost_estimate=QUICK,
    )(grad_conv, state, decay, residues)


def fix_kernel(half, segments, group_ref, rows_in_ref, states_ref, decay_ref, residue_ref, *refs):
    out_hbm, rows_ref, out_ref, sem = refs[-4:]
    toks, rows = out_ref.shape
    groups, _, sublanes, lanes = states_ref.shape
    modes = decay_ref.shape[0]
    mine = slice(half * sublanes, (half + 1) * sublanes)
    span = toks // segments
    segment = segment_of((sublanes, lanes), segments)
    decay = [decay_ref[n, mine] for n in range(modes)]
    start = []
    for n in range(modes):
        lap = power(decay[n], span)
        whole = power(lap, segments)
        m, j = divmod(n, segments)
        total = jnp.zeros((sublanes, lanes), jnp.float32)
        for group in range(groups - 1, 0, -1):
            state = rolled(states_ref[group, m], segments - 1 - j)
            total = jnp.where(group > group_ref[0], total * whole + state, total)
        for k in range(segments - 2, -1, -1):
            total = jnp.where(segment == k, rolled(lap * total, -1), total)
        start.append(residue_ref[n, mine] * total)

    def step(t, state):
        at = pl.ds(t, sublanes, stride=span)
        state = tuple(decay[n] * state[n] for n in range(modes))
        rows_ref[at, :] = rows_in_ref[at, :] + summed(list(state))
        return state

    steps_back(span, step, tuple(start), 8)
    for line in range(rows // lanes):
        out_ref[:, line * lanes : (line + 1) * lanes] = rows_ref[
            line * toks : (line + 1) * toks, :
        ].astype(jnp.bfloat16)
    store = pltpu.make_async_copy(out_ref, out_hbm.at[:, pl.ds(half * rows, rows)], sem)
    store.start()
    store.wait()


def fix(half, rows, segments, group, scanned, states, decay, residues, toks, width, partial):
    vmem = pl.BlockSpec(memory_space=pltpu.VMEM)
    high = pl.BlockSpec(memory_space=pltpu.HBM)
    more = [] if partial is None else [partial]
    return pl.pallas_call(
        functools.partial(fix_kernel, half, segments),
        in_specs=[pl.BlockSpec(memory_space=pltpu.SMEM)] + [vmem] * 4 + [high] * len(more),
        out_specs=high,
        out_shape=jax.ShapeDtypeStruct((toks, width), jnp.bfloat16),
        scratch_shapes=[
            pltpu.VMEM(scanned.shape, jnp.float32),
            pltpu.VMEM((toks, rows), jnp.bfloat16),
            pltpu.SemaphoreType.DMA,
        ],
        input_output_aliases={5: 0} if more else {},
        compiler_params=pltpu.CompilerParams(vmem_limit_bytes=VMEM),
        cost_estimate=QUICK,
    )(group, scanned, states, decay, residues, *more)


def local(out_grad, out_weight, query_in, conv_out, residues, decay_rates):
    toks, width = query_in.shape
    modes = decay_rates.shape[1]
    lanes = math.gcd(width, 128)
    size, groups = lax.axis_size("ch"), lax.axis_size("ctx")
    bits = [1 << i for i in range(size.bit_length() - 1)]
    place = jnp.reshape(lax.axis_index("ch"), (1,)).astype(jnp.int32)
    group = jnp.reshape(lax.axis_index("ctx"), (1,)).astype(jnp.int32)
    half_rows = width // 2
    lines = half_rows // lanes
    segments = 8 // lines
    by_mode = lambda values: jnp.repeat(values.T.reshape(modes, width // lanes, lanes), segments, axis=1)
    decay, residue = by_mode(decay_rates), by_mode(residues)

    portions, order = PORTIONS, ORDER
    if size != 8:
        portions = ((tuple(range(len(bits))), 2, 0), (tuple(range(len(bits))), 2, 1))
        order = [
            (p, s, (block,))
            for p in range(2)
            for s, bit in enumerate(bits)
            for block in sorted(range(0, size, 2 * bit), reverse=True)
        ] + [(p, kind) for kind in ("sum", "gate", "scan", "fix") for p in range(2)]
    offsets = [sum(width // part for _, part, _ in portions[:p]) for p in range(len(portions))]

    received, sums, gated, scanned, states = {}, {}, {}, {}, {}
    grad_query = grad_input = last = None

    def after(value):
        return value if last is None else lax.optimization_barrier((value, last))[0]

    def collect(wanted):
        arrays, places = [], []
        for key in wanted:
            array, *place = received[key]
            index = next((i for i, known in enumerate(arrays) if known is array), len(arrays))
            if index == len(arrays):
                arrays.append(array)
            places.append((index, tuple(place)))
        return arrays, places

    for p, s, *blocks in order:
        inside = [q for q, (_, _, half) in enumerate(portions) if half == p]
        if s == "sum":
            arrays, places = collect([(q, 0, 0) for q in inside])
            items = tuple((0, offsets[q], width // portions[q][1], (at,)) for q, at in zip(inside, places))
            last = sums[p] = send(items, False, width, after(place), out_weight, turned, arrays)
        elif s == "gate":
            later = range(1, len(bits))
            arrays, places = collect([(q, i, 0) for q in inside for i in later])
            pieces = tuple(
                (
                    offsets[q] - p * half_rows,
                    tuple(places[i * len(later) : (i + 1) * len(later)]),
                )
                for i, q in enumerate(inside)
            )
            grad_query, grad_conv, state, packed = gate(
                p, half_rows, segments, groups, pieces, after(sums[p]), arrays, query_in, conv_out, decay, grad_query
            )
            last, gated[p] = packed, (grad_conv, state)
            states[p] = lax.all_to_all(packed, "ctx", 0, 0, tiled=True)
        elif s == "scan":
            last = scanned[p] = scan(p, segments, *gated[p], decay, residue)
        elif s == "fix":
            last = grad_input = fix(
                p, half_rows, segments, group, after(scanned[p]), states[p], decay, residue, toks, width, grad_input
            )
        else:
            route, part, _ = portions[p]
            rows, (blocks,) = width // part, blocks
            bit = bits[route[s]]
            wanted = [(p, i, block ^ bit) for block in blocks for i in range(s)]
            arrays, places = collect(wanted)
            items = tuple(
                (block ^ bit, offsets[p], rows, tuple(places[i * s : (i + 1) * s])) for i, block in enumerate(blocks)
            )
            if last is None:
                last, turned = first_send(items, width, place, out_weight, out_grad)
            else:
                last = send(items, True, width, after(place), out_weight, turned, arrays)
            arrived = lax.ppermute(last, "ch", [(i, i ^ bit) for i in range(size)])
            each = part_of(rows, len(blocks))
            for i, block in enumerate(blocks):
                received[p, s, block] = (arrived, i * rows, i * (rows // each), each)
    return grad_query, grad_input


def solution(mesh):
    placed = (
        P("ctx", "ch"),
        P(None, "ch"),
        P("ctx", "ch"),
        P("ctx", "ch"),
        P("ch", None),
        P("ch", None),
    )
    return jax.shard_map(
        local,
        mesh=mesh,
        in_specs=placed,
        out_specs=(P("ctx", "ch"), P("ctx", "ch")),
        check_vma=False,
    )
```

```python
import functools
import math

import jax
import jax.numpy as jnp
from jax import lax
from jax.experimental import pallas as pl
from jax.experimental.pallas import tpu as pltpu
from jax.sharding import PartitionSpec as P

PEAKS = 16
SPAN = 251 * math.log(2.0)
SHIFT = 125 * math.log(2.0)
STEP = 256
VMEM = 12 * 1024 * 1024
QUICK = pl.CostEstimate(flops=0, bytes_accessed=1024, transcendentals=0)

PORTIONS = (((0, 1, 2), 2, 0), ((0, 1, 2), 2, 1))
ORDER = (
    (0, 0, (6,)), (1, 0, (6,)), (0, 0, (4,)), (1, 0, (4,)), (0, 0, (0,)), (0, 1, (4,)), (0, 0, (2,)), (1, 1, (4,)),
    (1, 0, (2,)), (0, 2, (0,)), (0, 1, (0,)), (1, 0, (0,)), (1, 2, (0,)), (1, 1, (0,)), (0, "sum"), (0, "gate"),
    (0, "scan"), (1, "sum"), (1, "gate"), (0, "fix"), (1, "scan"), (1, "fix"),
)
WAITS = {(0, "sum"): ((0, 2, 0),), (0, "scan"): ((1, 2, 0),), (1, 0, (0,)): ((1, 1, 4),)}


def part_of(rows, blocks):
    return next(part for part in range(16, rows + 1, 16) if rows % part == 0 and rows // part * blocks <= PEAKS)


def step_of(rows):
    return next(step for step in (STEP, STEP // 2, rows) if rows % step == 0)


def encode(block, part):
    codes, peaks = [], []
    for i in range(block.shape[0] // part):
        piece = block[i * part : (i + 1) * part, :]
        size = jnp.abs(piece)
        peak = jnp.maximum(jnp.max(size, axis=0, keepdims=True) * 1.01, 1e-30)
        peak = peak.astype(jnp.bfloat16).astype(jnp.float32)
        code = jnp.exp(size * (SPAN / peak) - SHIFT)
        codes.append(jnp.where(piece < 0, -code, code))
        peaks.append(peak)
    return jnp.concatenate(codes, axis=0).astype(jnp.bfloat16), peaks


def put_peaks(peaks, out_ref):
    if len(peaks) < PEAKS:
        peaks = peaks + [jnp.zeros((PEAKS - len(peaks), peaks[0].shape[1]), jnp.float32)]
    out_ref[out_ref.shape[0] - PEAKS :, :] = jnp.concatenate(peaks, axis=0).astype(jnp.bfloat16)


def decode(ref, place, first, count):
    start, peak, part = place
    peaks = ref[ref.shape[0] - PEAKS :, :].astype(jnp.float32) * (1.0 / SPAN)
    blocks = []
    for i in range(first // part, -(-(first + count) // part)):
        low, high = max(first, i * part), min(first + count, (i + 1) * part)
        code = ref[start + low : start + high, :].astype(jnp.float32)
        size = (jnp.log(jnp.abs(code)) + SHIFT) * peaks[peak + i : peak + i + 1, :]
        blocks.append(jnp.where(code < 0, -size, size))
    return jnp.concatenate(blocks, axis=0)


def pinned(array):
    return pltpu.with_memory_space_constraint(array, pltpu.HBM)


def send_kernel(items, coded, width, near, place_ref, w_ref, turned_ref, *refs):
    near_refs, out_ref = refs[:near], refs[near]
    base, peaks = 0, []
    for block, offset, rows, sources in items:
        step = step_of(rows)
        first = (place_ref[0] ^ block) * width + offset
        for at in range(0, rows, step):
            total = jnp.dot(
                w_ref[pl.ds(pl.multiple_of(first + at, 16), step), :],
                turned_ref[...],
                preferred_element_type=jnp.float32,
            )
            for source, place in sources:
                total = total + decode(near_refs[source], place, at, step)
            if coded:
                total, more = encode(total, part_of(rows, len(items)))
                peaks += more
            out_ref[base + at : base + at + step, :] = total
        base += rows
    if coded:
        put_peaks(peaks, out_ref)


def send(items, coded, width, place, weight, turned, nears):
    toks = turned.shape[1]
    vmem = pl.BlockSpec(memory_space=pltpu.VMEM)
    count = sum(rows for _, _, rows, _ in items) + (PEAKS if coded else 0)
    return pl.pallas_call(
        functools.partial(send_kernel, items, coded, width, len(nears)),
        in_specs=[pl.BlockSpec(memory_space=pltpu.SMEM)] + [vmem] * (2 + len(nears)),
        out_specs=vmem,
        out_shape=jax.ShapeDtypeStruct((count, toks), jnp.bfloat16 if coded else jnp.float32),
        compiler_params=pltpu.CompilerParams(vmem_limit_bytes=VMEM),
        cost_estimate=QUICK,
    )(place, weight, turned, *nears)


def first_kernel(items, width, place_ref, w_hbm, g_hbm, out_ref, turned_ref, w_ref, g_ref, sems):
    copies = [pltpu.make_async_copy(g_hbm, g_ref, sems.at[0])]
    base = 0
    for block, offset, rows, _ in items:
        step = step_of(rows)
        first = pl.multiple_of((place_ref[0] ^ block) * width + offset, 16)
        for at in range(0, rows, step):
            copies.append(
                pltpu.make_async_copy(
                    w_hbm.at[pl.ds(first + at, step), :], w_ref.at[pl.ds(base + at, step), :], sems.at[len(copies)]
                )
            )
        base += rows
    for copy in copies:
        copy.start()
    copies[0].wait()
    turned_ref[...] = g_ref[...].T
    base, peaks, waits = 0, [], iter(copies[1:])
    for _, _, rows, _ in items:
        step = step_of(rows)
        for at in range(base, base + rows, step):
            next(waits).wait()
            total = jnp.dot(w_ref[at : at + step, :], turned_ref[...], preferred_element_type=jnp.float32)
            total, more = encode(total, part_of(rows, len(items)))
            peaks += more
            out_ref[at : at + step, :] = total
        base += rows
    put_peaks(peaks, out_ref)


def first_send(items, width, place, weight, grad):
    toks, depth = grad.shape
    vmem = pl.BlockSpec(memory_space=pltpu.VMEM)
    high = pl.BlockSpec(memory_space=pltpu.HBM)
    count = sum(rows for _, _, rows, _ in items)
    steps = sum(rows // step_of(rows) for _, _, rows, _ in items)
    return pl.pallas_call(
        functools.partial(first_kernel, items, width),
        in_specs=[pl.BlockSpec(memory_space=pltpu.SMEM), high, high],
        out_specs=(vmem, vmem),
        out_shape=(
            jax.ShapeDtypeStruct((count + PEAKS, toks), jnp.bfloat16),
            jax.ShapeDtypeStruct((depth, toks), jnp.bfloat16),
        ),
        scratch_shapes=[
            pltpu.VMEM((count, depth), jnp.bfloat16),
            pltpu.VMEM((toks, depth), jnp.bfloat16),
            pltpu.SemaphoreType.DMA((1 + steps,)),
        ],
        compiler_params=pltpu.CompilerParams(vmem_limit_bytes=VMEM),
        cost_estimate=QUICK,
    )(place, pinned(weight), pinned(grad))


def steps_back(count, body, state, unroll):
    def some(i, state):
        for j in range(unroll):
            state = body(count - 1 - (i * unroll + j), state)
        return state

    return lax.fori_loop(0, count // unroll, some, state)


def power(base, exponent):
    result = None
    while exponent:
        if exponent % 2:
            result = base if result is None else result * base
        base = base * base
        exponent //= 2
    return result


def segment_of(shape, segments):
    return lax.rem(lax.broadcasted_iota(jnp.int32, shape, 0), segments)


def rolled(value, by):
    by %= value.shape[0]
    return pltpu.roll(value, by, 0) if by else value


def gate_kernel(half, rows, segments, pieces, near, acc_ref, *refs):
    near_refs, refs = refs[:near], refs[near:]
    query_ref, conv_ref, decay_ref = refs[:3]
    out_hbm, gc_ref, state_ref, pack_ref, gq_ref, sem = refs[-6:]
    toks = query_ref.shape[0]
    modes, sublanes, lanes = state_ref.shape
    mine = slice(half * sublanes, (half + 1) * sublanes)
    for line in range(rows // lanes):
        mix = acc_ref[line * lanes : (line + 1) * lanes, :]
        first, sources = next(piece for piece in reversed(pieces) if piece[0] <= line * lanes)
        for source, place in sources:
            mix = mix + decode(near_refs[source], place, line * lanes - first, lanes)
        mix = mix.T
        at = slice(line * lanes, (line + 1) * lanes)
        full = slice(half * rows + line * lanes, half * rows + (line + 1) * lanes)
        gq_ref[:, at] = (mix * conv_ref[:, full].astype(jnp.float32)).astype(jnp.bfloat16)
        gc_ref[line * toks : (line + 1) * toks, :] = mix * query_ref[:, full].astype(jnp.float32)
    store = pltpu.make_async_copy(gq_ref, out_hbm.at[:, pl.ds(half * rows, rows)], sem)
    store.start()
    decay = [decay_ref[n, mine] for n in range(modes)]
    span = toks // segments

    def step(t, state):
        row = gc_ref[pl.ds(t, sublanes, stride=span), :]
        return tuple(decay[n] * state[n] + row for n in range(modes))

    zero = jnp.zeros((sublanes, lanes), jnp.float32)
    state = steps_back(span, step, (zero,) * modes, 8)
    segment = segment_of((sublanes, lanes), segments)
    whole = []
    for n in range(modes):
        state_ref[n] = state[n]
        total = state[n]
        if segments > 1:
            factor = jnp.where(segment < segments - 1, power(decay[n], span), 0.0)
            for _ in range(segments - 1):
                total = state[n] + factor * rolled(total, -1)
        whole.append(total)
    for m in range(modes // segments):
        packed = whole[m * segments]
        for j in range(1, segments):
            packed = jnp.where(segment == j, rolled(whole[m * segments + j], j), packed)
        for copy in range(pack_ref.shape[0]):
            pack_ref[copy, m] = packed
    store.wait()


def gate(half, rows, segments, copies, pieces, acc, nears, query_in, conv_out, decay, partial):
    toks, width = query_in.shape
    modes, sublanes, lanes = decay.shape
    sublanes = rows // lanes * segments
    vmem = pl.BlockSpec(memory_space=pltpu.VMEM)
    high = pl.BlockSpec(memory_space=pltpu.HBM)
    more = [] if partial is None else [partial]
    return pl.pallas_call(
        functools.partial(gate_kernel, half, rows, segments, pieces, len(nears)),
        in_specs=[vmem] * (4 + len(nears)) + [high] * len(more),
        out_specs=(high, vmem, vmem, vmem),
        out_shape=(
            jax.ShapeDtypeStruct((toks, width), jnp.bfloat16),
            jax.ShapeDtypeStruct((rows // lanes * toks, lanes), jnp.float32),
            jax.ShapeDtypeStruct((modes, sublanes, lanes), jnp.float32),
            jax.ShapeDtypeStruct((copies, modes // segments, sublanes, lanes), jnp.float32),
        ),
        scratch_shapes=[pltpu.VMEM((toks, rows), jnp.bfloat16), pltpu.SemaphoreType.DMA],
        input_output_aliases={4 + len(nears): 0} if more else {},
        compiler_params=pltpu.CompilerParams(vmem_limit_bytes=VMEM),
        cost_estimate=QUICK,
    )(acc, *nears, query_in, conv_out, decay, *more)


def summed(terms):
    while len(terms) > 1:
        terms = [terms[k] + terms[k + 1] if k + 1 < len(terms) else terms[k] for k in range(0, len(terms), 2)]
    return terms[0]


def scan_kernel(half, segments, gc_ref, state_ref, decay_ref, residue_ref, rows_ref):
    modes, sublanes, lanes = state_ref.shape
    mine = slice(half * sublanes, (half + 1) * sublanes)
    span = gc_ref.shape[0] // sublanes
    segment = segment_of((sublanes, lanes), segments)
    decay = [decay_ref[n, mine] for n in range(modes)]
    start = []
    for n in range(modes):
        total = jnp.zeros((sublanes, lanes), jnp.float32)
        if segments > 1:
            group = power(decay[n], span)
            for k in range(segments - 2, -1, -1):
                total = jnp.where(segment == k, rolled(state_ref[n] + group * total, -1), total)
        start.append(total)

    def step(t, state):
        at = pl.ds(t, sublanes, stride=span)
        row = gc_ref[at, :]
        state = tuple(decay[n] * state[n] + row for n in range(modes))
        rows_ref[at, :] = summed([residue_ref[n, mine] * state[n] for n in range(modes)])
        return state

    steps_back(span, step, tuple(start), 8)


def scan(half, segments, grad_conv, state, decay, residues):
    vmem = pl.BlockSpec(memory_space=pltpu.VMEM)
    return pl.pallas_call(
        functools.partial(scan_kernel, half, segments),
        in_specs=[vmem] * 4,
        out_specs=vmem,
        out_shape=jax.ShapeDtypeStruct(grad_conv.shape, jnp.float32),
        compiler_params=pltpu.CompilerParams(vmem_limit_bytes=VMEM),
        cost_estimate=QUICK,
    )(grad_conv, state, decay, residues)


def fix_kernel(half, segments, group_ref, rows_in_ref, states_ref, decay_ref, residue_ref, *refs):
    out_hbm, rows_ref, out_ref, sem = refs[-4:]
    toks, rows = out_ref.shape
    groups, _, sublanes, lanes = states_ref.shape
    modes = decay_ref.shape[0]
    mine = slice(half * sublanes, (half + 1) * sublanes)
    span = toks // segments
    segment = segment_of((sublanes, lanes), segments)
    decay = [decay_ref[n, mine] for n in range(modes)]
    start = []
    for n in range(modes):
        lap = power(decay[n], span)
        whole = power(lap, segments)
        m, j = divmod(n, segments)
        total = jnp.zeros((sublanes, lanes), jnp.float32)
        for group in range(groups - 1, 0, -1):
            state = rolled(states_ref[group, m], segments - 1 - j)
            total = jnp.where(group > group_ref[0], total * whole + state, total)
        for k in range(segments - 2, -1, -1):
            total = jnp.where(segment == k, rolled(lap * total, -1), total)
        start.append(residue_ref[n, mine] * total)

    def step(t, state):
        at = pl.ds(t, sublanes, stride=span)
        state = tuple(decay[n] * state[n] for n in range(modes))
        rows_ref[at, :] = rows_in_ref[at, :] + summed(list(state))
        return state

    steps_back(span, step, tuple(start), 8)
    for line in range(rows // lanes):
        out_ref[:, line * lanes : (line + 1) * lanes] = rows_ref[
            line * toks : (line + 1) * toks, :
        ].astype(jnp.bfloat16)
    store = pltpu.make_async_copy(out_ref, out_hbm.at[:, pl.ds(half * rows, rows)], sem)
    store.start()
    store.wait()


def fix(half, rows, segments, group, scanned, states, decay, residues, toks, width, partial):
    vmem = pl.BlockSpec(memory_space=pltpu.VMEM)
    high = pl.BlockSpec(memory_space=pltpu.HBM)
    more = [] if partial is None else [partial]
    return pl.pallas_call(
        functools.partial(fix_kernel, half, segments),
        in_specs=[pl.BlockSpec(memory_space=pltpu.SMEM)] + [vmem] * 4 + [high] * len(more),
        out_specs=high,
        out_shape=jax.ShapeDtypeStruct((toks, width), jnp.bfloat16),
        scratch_shapes=[
            pltpu.VMEM(scanned.shape, jnp.float32),
            pltpu.VMEM((toks, rows), jnp.bfloat16),
            pltpu.SemaphoreType.DMA,
        ],
        input_output_aliases={5: 0} if more else {},
        compiler_params=pltpu.CompilerParams(vmem_limit_bytes=VMEM),
        cost_estimate=QUICK,
    )(group, scanned, states, decay, residues, *more)


def local(out_grad, out_weight, query_in, conv_out, residues, decay_rates):
    toks, width = query_in.shape
    modes = decay_rates.shape[1]
    lanes = math.gcd(width, 128)
    size, groups = lax.axis_size("ch"), lax.axis_size("ctx")
    bits = [1 << i for i in range(size.bit_length() - 1)]
    place = jnp.reshape(lax.axis_index("ch"), (1,)).astype(jnp.int32)
    group = jnp.reshape(lax.axis_index("ctx"), (1,)).astype(jnp.int32)
    half_rows = width // 2
    lines = half_rows // lanes
    segments = 8 // lines
    by_mode = lambda values: jnp.repeat(values.T.reshape(modes, width // lanes, lanes), segments, axis=1)
    decay, residue = by_mode(decay_rates), by_mode(residues)

    portions, order, waits = PORTIONS, ORDER, WAITS
    if size != 8:
        waits = {}
        portions = ((tuple(range(len(bits))), 2, 0), (tuple(range(len(bits))), 2, 1))
        order = [
            (p, s, (block,))
            for p in range(2)
            for s, bit in enumerate(bits)
            for block in sorted(range(0, size, 2 * bit), reverse=True)
        ] + [(p, kind) for kind in ("sum", "gate", "scan", "fix") for p in range(2)]
    offsets = [sum(width // part for _, part, _ in portions[:p]) for p in range(len(portions))]

    received, sums, gated, scanned, states = {}, {}, {}, {}, {}
    grad_query = grad_input = last = None

    def after(value):
        return value if last is None else lax.optimization_barrier((value, last, *awaited))[0]

    def collect(wanted):
        arrays, places = [], []
        for key in wanted:
            array, *place = received[key]
            index = next((i for i, known in enumerate(arrays) if known is array), len(arrays))
            if index == len(arrays):
                arrays.append(array)
            places.append((index, tuple(place)))
        return arrays, places

    for p, s, *blocks in order:
        awaited = [received[key][0] for key in waits.get((p, s, *blocks), ())]
        inside = [q for q, (_, _, half) in enumerate(portions) if half == p]
        if s == "sum":
            arrays, places = collect([(q, 0, 0) for q in inside])
            items = tuple((0, offsets[q], width // portions[q][1], (at,)) for q, at in zip(inside, places))
            last = sums[p] = send(items, False, width, after(place), out_weight, turned, arrays)
        elif s == "gate":
            later = range(1, len(bits))
            arrays, places = collect([(q, i, 0) for q in inside for i in later])
            pieces = tuple(
                (
                    offsets[q] - p * half_rows,
                    tuple(places[i * len(later) : (i + 1) * len(later)]),
                )
                for i, q in enumerate(inside)
            )
            grad_query, grad_conv, state, packed = gate(
                p, half_rows, segments, groups, pieces, after(sums[p]), arrays, query_in, conv_out, decay, grad_query
            )
            last, gated[p] = packed, (grad_conv, state)
            states[p] = lax.all_to_all(packed, "ctx", 0, 0, tiled=True)
        elif s == "scan":
            last = scanned[p] = scan(p, segments, after(gated[p][0]), gated[p][1], decay, residue)
        elif s == "fix":
            last = grad_input = fix(
                p, half_rows, segments, group, after(scanned[p]), states[p], decay, residue, toks, width, grad_input
            )
        else:
            route, part, _ = portions[p]
            rows, (blocks,) = width // part, blocks
            bit = bits[route[s]]
            wanted = [(p, i, block ^ bit) for block in blocks for i in range(s)]
            arrays, places = collect(wanted)
            items = tuple(
                (block ^ bit, offsets[p], rows, tuple(places[i * s : (i + 1) * s])) for i, block in enumerate(blocks)
            )
            if last is None:
                last, turned = first_send(items, width, place, out_weight, out_grad)
            else:
                last = send(items, True, width, after(place), out_weight, turned, arrays)
            arrived = lax.ppermute(last, "ch", [(i, i ^ bit) for i in range(size)])
            each = part_of(rows, len(blocks))
            for i, block in enumerate(blocks):
                received[p, s, block] = (arrived, i * rows, i * (rows // each), each)
    return grad_query, grad_input


def solution(mesh):
    placed = (
        P("ctx", "ch"),
        P(None, "ch"),
        P("ctx", "ch"),
        P("ctx", "ch"),
        P("ch", None),
        P("ch", None),
    )
    return jax.shard_map(
        local,
        mesh=mesh,
        in_specs=placed,
        out_specs=(P("ctx", "ch"), P("ctx", "ch")),
        check_vma=False,
    )
```

```python
import functools
import math

import jax
import jax.numpy as jnp
from jax import lax
from jax.experimental import pallas as pl
from jax.experimental.pallas import tpu as pltpu
from jax.sharding import PartitionSpec as P

PEAKS = 16
SPAN = 251 * math.log(2.0)
SHIFT = 125 * math.log(2.0)
STEP = 256
VMEM = 24 * 1024 * 1024
QUICK = pl.CostEstimate(flops=0, bytes_accessed=1024, transcendentals=0)

PORTIONS = (((0, 1, 2), 2, 0), ((0, 1, 2), 2, 1))
ORDER = (
    ((1, 0, 6),), ((0, 0, 6),), ((1, 0, 4),), ((1, 0, 0),), ((0, 0, 2),), ((1, 1, 4),), ((0, 0, 4),), ((1, 0, 2),),
    ((0, 1, 4),), ((1, 2, 0),), ((0, 0, 0),), ((0, 1, 0),), ((0, 2, 0),), ((1, 1, 0),), ("sum", 0), ("gate", 0),
    ("sum", 1), ("gate", 1), ("scan", 1), ("fix", 1),
)
WAITS = {((1, 1, 0),): ((1, 2, 0),), ((0, 0, 0),): ((0, 1, 4),)}


def part_of(rows, blocks):
    return next(part for part in range(16, rows + 1, 16) if rows % part == 0 and rows // part * blocks <= PEAKS)


def step_of(rows):
    return next(step for step in (STEP, STEP // 2, rows) if rows % step == 0)


def encode(block, part):
    codes, peaks = [], []
    for i in range(block.shape[0] // part):
        piece = block[i * part : (i + 1) * part, :]
        size = jnp.abs(piece)
        peak = jnp.maximum(jnp.max(size, axis=0, keepdims=True) * 1.01, 1e-30)
        peak = peak.astype(jnp.bfloat16).astype(jnp.float32)
        code = jnp.exp(size * (SPAN / peak) - SHIFT)
        codes.append(jnp.where(piece < 0, -code, code))
        peaks.append(peak)
    return jnp.concatenate(codes, axis=0).astype(jnp.bfloat16), peaks


def put_peaks(peaks, out_ref):
    if len(peaks) < PEAKS:
        peaks = peaks + [jnp.zeros((PEAKS - len(peaks), peaks[0].shape[1]), jnp.float32)]
    out_ref[out_ref.shape[0] - PEAKS :, :] = jnp.concatenate(peaks, axis=0).astype(jnp.bfloat16)


def decode(ref, place, first, count):
    start, peak, part = place
    peaks = ref[ref.shape[0] - PEAKS :, :].astype(jnp.float32) * (1.0 / SPAN)
    blocks = []
    for i in range(first // part, -(-(first + count) // part)):
        low, high = max(first, i * part), min(first + count, (i + 1) * part)
        code = ref[start + low : start + high, :].astype(jnp.float32)
        size = (jnp.log(jnp.abs(code)) + SHIFT) * peaks[peak + i : peak + i + 1, :]
        blocks.append(jnp.where(code < 0, -size, size))
    return jnp.concatenate(blocks, axis=0)


def pinned(array):
    return pltpu.with_memory_space_constraint(array, pltpu.HBM)


def send_kernel(items, coded, width, near, place_ref, w_ref, turned_ref, *refs):
    near_refs, out_ref = refs[:near], refs[near]
    base, peaks = 0, []
    for block, offset, rows, sources in items:
        step = step_of(rows)
        first = (place_ref[0] ^ block) * width + offset
        for at in range(0, rows, step):
            total = jnp.dot(
                w_ref[pl.ds(pl.multiple_of(first + at, 16), step), :],
                turned_ref[...],
                preferred_element_type=jnp.float32,
            )
            for source, place in sources:
                total = total + decode(near_refs[source], place, at, step)
            if coded:
                total, more = encode(total, part_of(rows, len(items)))
                peaks += more
            out_ref[base + at : base + at + step, :] = total
        base += rows
    if coded:
        put_peaks(peaks, out_ref)


def send(items, coded, width, place, weight, turned, nears):
    toks = turned.shape[1]
    vmem = pl.BlockSpec(memory_space=pltpu.VMEM)
    count = sum(rows for _, _, rows, _ in items) + (PEAKS if coded else 0)
    return pl.pallas_call(
        functools.partial(send_kernel, items, coded, width, len(nears)),
        in_specs=[pl.BlockSpec(memory_space=pltpu.SMEM)] + [vmem] * (2 + len(nears)),
        out_specs=vmem,
        out_shape=jax.ShapeDtypeStruct((count, toks), jnp.bfloat16 if coded else jnp.float32),
        compiler_params=pltpu.CompilerParams(vmem_limit_bytes=VMEM),
        cost_estimate=QUICK,
    )(place, weight, turned, *nears)


def first_kernel(items, width, place_ref, w_hbm, g_hbm, out_ref, turned_ref, w_ref, g_ref, sems):
    copies = [pltpu.make_async_copy(g_hbm, g_ref, sems.at[0])]
    base = 0
    for block, offset, rows, _ in items:
        step = step_of(rows)
        first = pl.multiple_of((place_ref[0] ^ block) * width + offset, 16)
        for at in range(0, rows, step):
            copies.append(
                pltpu.make_async_copy(
                    w_hbm.at[pl.ds(first + at, step), :], w_ref.at[pl.ds(base + at, step), :], sems.at[len(copies)]
                )
            )
        base += rows
    for copy in copies:
        copy.start()
    copies[0].wait()
    turned_ref[...] = g_ref[...].T
    base, peaks, waits = 0, [], iter(copies[1:])
    for _, _, rows, _ in items:
        step = step_of(rows)
        for at in range(base, base + rows, step):
            next(waits).wait()
            total = jnp.dot(w_ref[at : at + step, :], turned_ref[...], preferred_element_type=jnp.float32)
            total, more = encode(total, part_of(rows, len(items)))
            peaks += more
            out_ref[at : at + step, :] = total
        base += rows
    put_peaks(peaks, out_ref)


def first_send(items, width, place, weight, grad):
    toks, depth = grad.shape
    vmem = pl.BlockSpec(memory_space=pltpu.VMEM)
    high = pl.BlockSpec(memory_space=pltpu.HBM)
    count = sum(rows for _, _, rows, _ in items)
    steps = sum(rows // step_of(rows) for _, _, rows, _ in items)
    return pl.pallas_call(
        functools.partial(first_kernel, items, width),
        in_specs=[pl.BlockSpec(memory_space=pltpu.SMEM), high, high],
        out_specs=(vmem, vmem),
        out_shape=(
            jax.ShapeDtypeStruct((count + PEAKS, toks), jnp.bfloat16),
            jax.ShapeDtypeStruct((depth, toks), jnp.bfloat16),
        ),
        scratch_shapes=[
            pltpu.VMEM((count, depth), jnp.bfloat16),
            pltpu.VMEM((toks, depth), jnp.bfloat16),
            pltpu.SemaphoreType.DMA((1 + steps,)),
        ],
        compiler_params=pltpu.CompilerParams(vmem_limit_bytes=VMEM),
        cost_estimate=QUICK,
    )(place, pinned(weight), pinned(grad))


def steps_back(count, body, state, unroll):
    def some(i, state):
        for j in range(unroll):
            state = body(count - 1 - (i * unroll + j), state)
        return state

    return lax.fori_loop(0, count // unroll, some, state)


def power(base, exponent):
    result = None
    while exponent:
        if exponent % 2:
            result = base if result is None else result * base
        base = base * base
        exponent //= 2
    return result


def segment_of(shape, segments):
    return lax.rem(lax.broadcasted_iota(jnp.int32, shape, 0), segments)


def rolled(value, by):
    by %= value.shape[0]
    return pltpu.roll(value, by, 0) if by else value


def gate_kernel(half, rows, segments, pieces, near, acc_ref, *refs):
    near_refs, refs = refs[:near], refs[near:]
    query_ref, conv_ref, decay_ref, other_ref = refs[:4]
    out_hbm, rows_ref, state_ref, pack_ref = refs[-7:-3] if half == 0 else refs[-6:-2]
    gq_ref, sem = refs[-2:]
    gc_ref = refs[-3] if half == 0 else rows_ref
    toks = query_ref.shape[0]
    modes, sublanes, lanes = state_ref.shape
    mine = slice(half * sublanes, (half + 1) * sublanes)
    for line in range(rows // lanes):
        mix = acc_ref[line * lanes : (line + 1) * lanes, :]
        first, sources = next(piece for piece in reversed(pieces) if piece[0] <= line * lanes)
        for source, place in sources:
            mix = mix + decode(near_refs[source], place, line * lanes - first, lanes)
        mix = mix.T
        at = slice(line * lanes, (line + 1) * lanes)
        full = slice(half * rows + line * lanes, half * rows + (line + 1) * lanes)
        gq_ref[:, at] = (mix * conv_ref[:, full].astype(jnp.float32)).astype(jnp.bfloat16)
        gc_ref[line * toks : (line + 1) * toks, :] = mix * query_ref[:, full].astype(jnp.float32)
    store = pltpu.make_async_copy(gq_ref, out_hbm.at[:, pl.ds(half * rows, rows)], sem)
    store.start()
    decay = [decay_ref[n, mine] for n in range(modes)]
    span = toks // segments

    def step(t, state):
        at = pl.ds(t, sublanes, stride=span)
        row = gc_ref[at, :]
        state = tuple(decay[n] * state[n] + row for n in range(modes))
        if half == 0:
            rows_ref[at, :] = summed([other_ref[n, mine] * state[n] for n in range(modes)])
        return state

    zero = jnp.zeros((sublanes, lanes), jnp.float32)
    state = steps_back(span, step, (zero,) * modes, 8)
    segment = segment_of((sublanes, lanes), segments)
    whole = []
    for n in range(modes):
        state_ref[n] = state[n]
        total = state[n]
        if segments > 1:
            factor = jnp.where(segment < segments - 1, power(decay[n], span), 0.0)
            for _ in range(segments - 1):
                total = state[n] + factor * rolled(total, -1)
        whole.append(total)
    packs = modes // segments
    for m in range(packs):
        packed = whole[m * segments]
        for j in range(1, segments):
            packed = jnp.where(segment == j, rolled(whole[m * segments + j], j), packed)
        if half == 0:
            pack_ref[m] = packed
        else:
            pack_ref[m] = other_ref[m]
            pack_ref[packs + m] = packed
    store.wait()


def gate(half, rows, segments, pieces, acc, nears, query_in, conv_out, decay, other, partial):
    toks, width = query_in.shape
    modes, _, lanes = decay.shape
    sublanes = rows // lanes * segments
    vmem = pl.BlockSpec(memory_space=pltpu.VMEM)
    high = pl.BlockSpec(memory_space=pltpu.HBM)
    more = [] if partial is None else [partial]
    lines = (rows // lanes * toks, lanes)
    return pl.pallas_call(
        functools.partial(gate_kernel, half, rows, segments, pieces, len(nears)),
        in_specs=[vmem] * (5 + len(nears)) + [high] * len(more),
        out_specs=(high, vmem, vmem, vmem),
        out_shape=(
            jax.ShapeDtypeStruct((toks, width), jnp.bfloat16),
            jax.ShapeDtypeStruct(lines, jnp.float32),
            jax.ShapeDtypeStruct((modes, sublanes, lanes), jnp.float32),
            jax.ShapeDtypeStruct(((1 + half) * modes // segments, sublanes, lanes), jnp.float32),
        ),
        scratch_shapes=([pltpu.VMEM(lines, jnp.float32)] if half == 0 else [])
        + [pltpu.VMEM((toks, rows), jnp.bfloat16), pltpu.SemaphoreType.DMA],
        input_output_aliases={5 + len(nears): 0} if more else {},
        compiler_params=pltpu.CompilerParams(vmem_limit_bytes=VMEM),
        cost_estimate=QUICK,
    )(acc, *nears, query_in, conv_out, decay, other, *more)


def summed(terms):
    while len(terms) > 1:
        terms = [terms[k] + terms[k + 1] if k + 1 < len(terms) else terms[k] for k in range(0, len(terms), 2)]
    return terms[0]


def scan_kernel(half, segments, gc_ref, state_ref, decay_ref, residue_ref, rows_ref):
    modes, sublanes, lanes = state_ref.shape
    mine = slice(half * sublanes, (half + 1) * sublanes)
    span = gc_ref.shape[0] // sublanes
    segment = segment_of((sublanes, lanes), segments)
    decay = [decay_ref[n, mine] for n in range(modes)]
    start = []
    for n in range(modes):
        total = jnp.zeros((sublanes, lanes), jnp.float32)
        if segments > 1:
            group = power(decay[n], span)
            for k in range(segments - 2, -1, -1):
                total = jnp.where(segment == k, rolled(state_ref[n] + group * total, -1), total)
        start.append(total)

    def step(t, state):
        at = pl.ds(t, sublanes, stride=span)
        row = gc_ref[at, :]
        state = tuple(decay[n] * state[n] + row for n in range(modes))
        rows_ref[at, :] = summed([residue_ref[n, mine] * state[n] for n in range(modes)])
        return state

    steps_back(span, step, tuple(start), 8)


def scan(half, segments, grad_conv, state, decay, residues):
    vmem = pl.BlockSpec(memory_space=pltpu.VMEM)
    return pl.pallas_call(
        functools.partial(scan_kernel, half, segments),
        in_specs=[vmem] * 4,
        out_specs=vmem,
        out_shape=jax.ShapeDtypeStruct(grad_conv.shape, jnp.float32),
        compiler_params=pltpu.CompilerParams(vmem_limit_bytes=VMEM),
        cost_estimate=QUICK,
    )(grad_conv, state, decay, residues)


def fix_kernel(segments, hops, *refs):
    scanned_refs, state_ref, later_refs = refs[:2], refs[2], refs[3 : 3 + hops]
    decay_ref, residue_ref, out_hbm, rows_ref, out_ref, sems = refs[3 + hops :]
    toks, width = out_ref.shape
    modes, sublanes, lanes = state_ref.shape
    packs = modes // segments
    rows = width // 2
    span = toks // segments
    segment = segment_of((sublanes, lanes), segments)
    stores = []
    for half in range(2):
        mine = slice(half * sublanes, (half + 1) * sublanes)
        decay = [decay_ref[n, mine] for n in range(modes)]
        start = []
        for n in range(modes):
            lap = power(decay[n], span)
            whole = power(lap, segments)
            m, j = divmod(n, segments)
            arrived = [rolled(ref[half * packs + m], segments - 1 - j) for ref in later_refs]
            total = arrived[-1]
            for state in reversed(arrived[:-1]):
                total = total * whole + state
            for k in range(segments - 2, -1, -1):
                brought = lap * total
                if half == 0:
                    brought = brought + state_ref[n]
                total = jnp.where(segment == k, rolled(brought, -1), total)
            start.append(residue_ref[n, mine] * total)

        def step(t, state, scanned_ref=scanned_refs[half], decay=decay):
            at = pl.ds(t, sublanes, stride=span)
            state = tuple(decay[n] * state[n] for n in range(modes))
            rows_ref[at, :] = scanned_ref[at, :] + summed(list(state))
            return state

        steps_back(span, step, tuple(start), 8)
        for line in range(rows // lanes):
            out_ref[:, half * rows + line * lanes : half * rows + (line + 1) * lanes] = rows_ref[
                line * toks : (line + 1) * toks, :
            ].astype(jnp.bfloat16)
        columns = pl.ds(half * rows, rows)
        stores.append(pltpu.make_async_copy(out_ref.at[:, columns], out_hbm.at[:, columns], sems.at[half]))
        stores[-1].start()
    for store in stores:
        store.wait()


def fix(segments, scanned, state, laters, decay, residues, toks, width):
    vmem = pl.BlockSpec(memory_space=pltpu.VMEM)
    return pl.pallas_call(
        functools.partial(fix_kernel, segments, len(laters)),
        in_specs=[vmem] * (5 + len(laters)),
        out_specs=pl.BlockSpec(memory_space=pltpu.HBM),
        out_shape=jax.ShapeDtypeStruct((toks, width), jnp.bfloat16),
        scratch_shapes=[
            pltpu.VMEM(scanned[0].shape, jnp.float32),
            pltpu.VMEM((toks, width), jnp.bfloat16),
            pltpu.SemaphoreType.DMA((2,)),
        ],
        compiler_params=pltpu.CompilerParams(vmem_limit_bytes=VMEM),
        cost_estimate=QUICK,
    )(*scanned, state, *laters, decay, residues)


def local(out_grad, out_weight, query_in, conv_out, residues, decay_rates):
    toks, width = query_in.shape
    modes = decay_rates.shape[1]
    lanes = math.gcd(width, 128)
    size, groups = lax.axis_size("ch"), lax.axis_size("ctx")
    bits = [1 << i for i in range(size.bit_length() - 1)]
    place = jnp.reshape(lax.axis_index("ch"), (1,)).astype(jnp.int32)
    half_rows = width // 2
    lines = half_rows // lanes
    segments = 8 // lines
    by_mode = lambda values: jnp.repeat(values.T.reshape(modes, width // lanes, lanes), segments, axis=1)
    decay, residue = by_mode(decay_rates), by_mode(residues)

    portions, order, waits = PORTIONS, ORDER, WAITS
    if size != 8:
        waits = {}
        portions = ((tuple(range(len(bits))), 2, 0), (tuple(range(len(bits))), 2, 1))
        order = [
            ((p, s, block),)
            for p in range(2)
            for s, bit in enumerate(bits)
            for block in sorted(range(0, size, 2 * bit), reverse=True)
        ] + [("sum", 0), ("gate", 0), ("sum", 1), ("gate", 1), ("scan", 1), ("fix", 1)]
    offsets = [sum(width // part for _, part, _ in portions[:p]) for p in range(len(portions))]

    received, sums, scanned, states, packed = {}, {}, {}, {}, {}
    grad_query = last = None

    def after(value):
        return value if last is None else lax.optimization_barrier((value, last, *awaited))[0]

    def collect(wanted):
        arrays, places = [], []
        for key in wanted:
            array, *place = received[key]
            index = next((i for i, known in enumerate(arrays) if known is array), len(arrays))
            if index == len(arrays):
                arrays.append(array)
            places.append((index, tuple(place)))
        return arrays, places

    for todo in order:
        awaited = [received[key][0] for key in waits.get(todo, ())]
        kind, half = todo if isinstance(todo[0], str) else ("send", None)
        inside = [q for q, (_, _, lies) in enumerate(portions) if lies == half]
        if kind == "send":
            arrays, items = [], []
            wanted, rows, bits_of = [], [], []
            for p, s, block in todo:
                route, share, _ = portions[p]
                bits_of.append(bits[route[s]])
                rows.append(width // share)
                wanted.append([(p, i, block ^ bits_of[-1]) for i in range(s)])
            bit, count = bits_of[0], len(todo)
            arrays, places = collect([key for keys in wanted for key in keys])
            places = iter(places)
            items = tuple(
                (block ^ bit, offsets[p], rows[i], tuple(next(places) for _ in wanted[i]))
                for i, (p, _, block) in enumerate(todo)
            )
            if last is None:
                last, turned = first_send(items, width, place, out_weight, out_grad)
            else:
                last = send(items, True, width, after(place), out_weight, turned, arrays)
            arrived = lax.ppermute(last, "ch", [(i, i ^ bit) for i in range(size)])
            start = peak = 0
            for i, key in enumerate(todo):
                part = part_of(rows[i], count)
                received[key] = (arrived, start, peak, part)
                start, peak = start + rows[i], peak + rows[i] // part
        elif kind == "sum":
            arrays, places = collect([(q, 0, 0) for q in inside])
            items = tuple((0, offsets[q], width // portions[q][1], (at,)) for q, at in zip(inside, places))
            last = sums[half] = send(items, False, width, after(place), out_weight, turned, arrays)
        elif kind == "gate":
            later = range(1, len(bits))
            arrays, places = collect([(q, i, 0) for q in inside for i in later])
            pieces = tuple(
                (offsets[q] - half * half_rows, tuple(places[i * len(later) : (i + 1) * len(later)]))
                for i, q in enumerate(inside)
            )
            other = residue if half == 0 else packed[0]
            grad_query, scanned[half], states[half], packed[half] = gate(
                half,
                half_rows,
                segments,
                pieces,
                after(sums[half]),
                arrays,
                query_in,
                conv_out,
                decay,
                other,
                grad_query,
            )
            last = packed[half]
        elif kind == "scan":
            groups = lax.axis_size("ctx")
            laters = [
                lax.ppermute(packed[1], "ctx", [(i, i - hop) for i in range(hop, groups)]) for hop in range(1, groups)
            ]
            scanned[1] = scan(1, segments, after(scanned[1]), states[1], decay, residue)
        else:
            grad_input = fix(
                segments, [scanned[0], scanned[1]], states[0], laters, decay, residue, toks, width
            )
    return grad_query, grad_input


def solution(mesh):
    placed = (
        P("ctx", "ch"),
        P(None, "ch"),
        P("ctx", "ch"),
        P("ctx", "ch"),
        P("ch", None),
        P("ch", None),
    )
    return jax.shard_map(
        local,
        mesh=mesh,
        in_specs=placed,
        out_specs=(P("ctx", "ch"), P("ctx", "ch")),
        check_vma=False,
    )
```

```python
import functools
import math

import jax
import jax.numpy as jnp
from jax import lax
from jax.experimental import pallas as pl
from jax.experimental.pallas import tpu as pltpu
from jax.sharding import PartitionSpec as P

PEAKS = 16
SPAN = 251 * math.log(2.0)
SHIFT = 125 * math.log(2.0)
STEP = 256
VMEM = 24 * 1024 * 1024
QUICK = pl.CostEstimate(flops=0, bytes_accessed=1024, transcendentals=0)

PORTIONS = (((0, 1, 2), 2, 0), ((0, 1, 2), 2, 1))
ORDER = (
    ((0, 0, 6),), ((1, 0, 0),), ((0, 0, 4),), ((1, 0, 6),), ((1, 0, 2),), ((1, 0, 4),), ((0, 0, 2),), ((0, 1, 4),),
    ((1, 1, 4),), ((0, 2, 0),), ((0, 0, 0),), ((0, 1, 0),), ((1, 2, 0),), ((1, 1, 0),), ("laps", None), ("sum", 0),
    ("sum", 1), ("gate", 0), ("gate", 1), ("scan", 1), ("fix", None),
)
WAITS = {
    ((1, 1, 0),): ((0, 2, 0),),
    ("sum", 0): ((0, 1, 0), (0, 0, 0)),
    ((1, 2, 0),): ((1, 1, 4),),
    ("gate", 1): ((1, 2, 0),),
}


def part_of(rows, blocks):
    return next(part for part in range(16, rows + 1, 16) if rows % part == 0 and rows // part * blocks <= PEAKS)


def step_of(rows):
    return next(step for step in (STEP, STEP // 2, rows) if rows % step == 0)


def encode(block, part):
    codes, peaks = [], []
    for i in range(block.shape[0] // part):
        piece = block[i * part : (i + 1) * part, :]
        size = jnp.abs(piece)
        peak = jnp.maximum(jnp.max(size, axis=0, keepdims=True) * 1.01, 1e-30)
        peak = peak.astype(jnp.bfloat16).astype(jnp.float32)
        code = jnp.exp(size * (SPAN / peak) - SHIFT)
        codes.append(jnp.where(piece < 0, -code, code))
        peaks.append(peak)
    return jnp.concatenate(codes, axis=0).astype(jnp.bfloat16), peaks


def put_peaks(peaks, out_ref):
    if len(peaks) < PEAKS:
        peaks = peaks + [jnp.zeros((PEAKS - len(peaks), peaks[0].shape[1]), jnp.float32)]
    out_ref[out_ref.shape[0] - PEAKS :, :] = jnp.concatenate(peaks, axis=0).astype(jnp.bfloat16)


def decode(ref, place, first, count):
    start, peak, part = place
    peaks = ref[ref.shape[0] - PEAKS :, :].astype(jnp.float32) * (1.0 / SPAN)
    blocks = []
    for i in range(first // part, -(-(first + count) // part)):
        low, high = max(first, i * part), min(first + count, (i + 1) * part)
        code = ref[start + low : start + high, :].astype(jnp.float32)
        size = (jnp.log(jnp.abs(code)) + SHIFT) * peaks[peak + i : peak + i + 1, :]
        blocks.append(jnp.where(code < 0, -size, size))
    return jnp.concatenate(blocks, axis=0)


def pinned(array):
    return pltpu.with_memory_space_constraint(array, pltpu.HBM)


def send_kernel(items, coded, width, near, place_ref, w_ref, turned_ref, *refs):
    near_refs, out_ref = refs[:near], refs[near]
    base, peaks = 0, []
    for block, offset, rows, sources in items:
        step = step_of(rows)
        first = (place_ref[0] ^ block) * width + offset
        for at in range(0, rows, step):
            total = jnp.dot(
                w_ref[pl.ds(pl.multiple_of(first + at, 16), step), :],
                turned_ref[...],
                preferred_element_type=jnp.float32,
            )
            for source, place in sources:
                total = total + decode(near_refs[source], place, at, step)
            if coded:
                total, more = encode(total, part_of(rows, len(items)))
                peaks += more
            out_ref[base + at : base + at + step, :] = total
        base += rows
    if coded:
        put_peaks(peaks, out_ref)


def send(items, coded, width, place, weight, turned, nears):
    toks = turned.shape[1]
    vmem = pl.BlockSpec(memory_space=pltpu.VMEM)
    count = sum(rows for _, _, rows, _ in items) + (PEAKS if coded else 0)
    return pl.pallas_call(
        functools.partial(send_kernel, items, coded, width, len(nears)),
        in_specs=[pl.BlockSpec(memory_space=pltpu.SMEM)] + [vmem] * (2 + len(nears)),
        out_specs=vmem,
        out_shape=jax.ShapeDtypeStruct((count, toks), jnp.bfloat16 if coded else jnp.float32),
        compiler_params=pltpu.CompilerParams(vmem_limit_bytes=VMEM),
        cost_estimate=QUICK,
    )(place, weight, turned, *nears)


def first_kernel(items, width, place_ref, w_hbm, g_hbm, out_ref, turned_ref, w_ref, g_ref, sems):
    copies = [pltpu.make_async_copy(g_hbm, g_ref, sems.at[0])]
    base = 0
    for block, offset, rows, _ in items:
        step = step_of(rows)
        first = pl.multiple_of((place_ref[0] ^ block) * width + offset, 16)
        for at in range(0, rows, step):
            copies.append(
                pltpu.make_async_copy(
                    w_hbm.at[pl.ds(first + at, step), :], w_ref.at[pl.ds(base + at, step), :], sems.at[len(copies)]
                )
            )
        base += rows
    for copy in copies:
        copy.start()
    copies[0].wait()
    turned_ref[...] = g_ref[...].T
    base, peaks, waits = 0, [], iter(copies[1:])
    for _, _, rows, _ in items:
        step = step_of(rows)
        for at in range(base, base + rows, step):
            next(waits).wait()
            total = jnp.dot(w_ref[at : at + step, :], turned_ref[...], preferred_element_type=jnp.float32)
            total, more = encode(total, part_of(rows, len(items)))
            peaks += more
            out_ref[at : at + step, :] = total
        base += rows
    put_peaks(peaks, out_ref)


def first_send(items, width, place, weight, grad):
    toks, depth = grad.shape
    vmem = pl.BlockSpec(memory_space=pltpu.VMEM)
    high = pl.BlockSpec(memory_space=pltpu.HBM)
    count = sum(rows for _, _, rows, _ in items)
    steps = sum(rows // step_of(rows) for _, _, rows, _ in items)
    return pl.pallas_call(
        functools.partial(first_kernel, items, width),
        in_specs=[pl.BlockSpec(memory_space=pltpu.SMEM), high, high],
        out_specs=(vmem, vmem),
        out_shape=(
            jax.ShapeDtypeStruct((count + PEAKS, toks), jnp.bfloat16),
            jax.ShapeDtypeStruct((depth, toks), jnp.bfloat16),
        ),
        scratch_shapes=[
            pltpu.VMEM((count, depth), jnp.bfloat16),
            pltpu.VMEM((toks, depth), jnp.bfloat16),
            pltpu.SemaphoreType.DMA((1 + steps,)),
        ],
        compiler_params=pltpu.CompilerParams(vmem_limit_bytes=VMEM),
        cost_estimate=QUICK,
    )(place, pinned(weight), pinned(grad))


def steps_back(count, body, state, unroll):
    def some(i, state):
        for j in range(unroll):
            state = body(count - 1 - (i * unroll + j), state)
        return state

    return lax.fori_loop(0, count // unroll, some, state)


def power(base, exponent):
    result = None
    while exponent:
        if exponent % 2:
            result = base if result is None else result * base
        base = base * base
        exponent //= 2
    return result


def segment_of(shape, segments):
    return lax.rem(lax.broadcasted_iota(jnp.int32, shape, 0), segments)


def rolled(value, by):
    by %= value.shape[0]
    return pltpu.roll(value, by, 0) if by else value


def gate_kernel(half, rows, segments, pieces, near, acc_ref, *refs):
    near_refs, refs = refs[:near], refs[near:]
    query_ref, conv_ref, decay_ref, lap_ref, other_ref = refs[:5]
    out_hbm, rows_ref, state_ref, pack_ref = refs[-7:-3] if half == 0 else refs[-6:-2]
    gq_ref, sem = refs[-2:]
    gc_ref = refs[-3] if half == 0 else rows_ref
    toks = query_ref.shape[0]
    modes, sublanes, lanes = state_ref.shape
    mine = slice(half * sublanes, (half + 1) * sublanes)
    for line in range(rows // lanes):
        mix = acc_ref[line * lanes : (line + 1) * lanes, :]
        first, sources = next(piece for piece in reversed(pieces) if piece[0] <= line * lanes)
        for source, place in sources:
            mix = mix + decode(near_refs[source], place, line * lanes - first, lanes)
        mix = mix.T
        at = slice(line * lanes, (line + 1) * lanes)
        full = slice(half * rows + line * lanes, half * rows + (line + 1) * lanes)
        gq_ref[:, at] = (mix * conv_ref[:, full].astype(jnp.float32)).astype(jnp.bfloat16)
        gc_ref[line * toks : (line + 1) * toks, :] = mix * query_ref[:, full].astype(jnp.float32)
    store = pltpu.make_async_copy(gq_ref, out_hbm.at[:, pl.ds(half * rows, rows)], sem)
    store.start()
    decay = [decay_ref[n, mine] for n in range(modes)]
    span = toks // segments

    def step(t, state):
        at = pl.ds(t, sublanes, stride=span)
        row = gc_ref[at, :]
        state = tuple(decay[n] * state[n] + row for n in range(modes))
        if half == 0:
            rows_ref[at, :] = summed([other_ref[n, mine] * state[n] for n in range(modes)])
        return state

    zero = jnp.zeros((sublanes, lanes), jnp.float32)
    state = steps_back(span, step, (zero,) * modes, 8)
    segment = segment_of((sublanes, lanes), segments)
    whole = []
    for n in range(modes):
        state_ref[n] = state[n]
        total = state[n]
        if segments > 1:
            factor = jnp.where(segment < segments - 1, lap_ref[n, mine], 0.0)
            for _ in range(segments - 1):
                total = state[n] + factor * rolled(total, -1)
        whole.append(total)
    packs = modes // segments
    for m in range(packs):
        packed = whole[m * segments]
        for j in range(1, segments):
            packed = jnp.where(segment == j, rolled(whole[m * segments + j], j), packed)
        if half == 0:
            pack_ref[m] = packed
        else:
            pack_ref[m] = other_ref[m]
            pack_ref[packs + m] = packed
    store.wait()


def gate(half, rows, segments, pieces, acc, nears, query_in, conv_out, decay, lap, other, partial):
    toks, width = query_in.shape
    modes, _, lanes = decay.shape
    sublanes = rows // lanes * segments
    vmem = pl.BlockSpec(memory_space=pltpu.VMEM)
    high = pl.BlockSpec(memory_space=pltpu.HBM)
    more = [] if partial is None else [partial]
    lines = (rows // lanes * toks, lanes)
    return pl.pallas_call(
        functools.partial(gate_kernel, half, rows, segments, pieces, len(nears)),
        in_specs=[vmem] * (6 + len(nears)) + [high] * len(more),
        out_specs=(high, vmem, vmem, vmem),
        out_shape=(
            jax.ShapeDtypeStruct((toks, width), jnp.bfloat16),
            jax.ShapeDtypeStruct(lines, jnp.float32),
            jax.ShapeDtypeStruct((modes, sublanes, lanes), jnp.float32),
            jax.ShapeDtypeStruct(((1 + half) * modes // segments, sublanes, lanes), jnp.float32),
        ),
        scratch_shapes=([pltpu.VMEM(lines, jnp.float32)] if half == 0 else [])
        + [pltpu.VMEM((toks, rows), jnp.bfloat16), pltpu.SemaphoreType.DMA],
        input_output_aliases={6 + len(nears): 0} if more else {},
        compiler_params=pltpu.CompilerParams(vmem_limit_bytes=VMEM),
        cost_estimate=QUICK,
    )(acc, *nears, query_in, conv_out, decay, lap, other, *more)


def summed(terms):
    while len(terms) > 1:
        terms = [terms[k] + terms[k + 1] if k + 1 < len(terms) else terms[k] for k in range(0, len(terms), 2)]
    return terms[0]


def scan_kernel(half, segments, gc_ref, state_ref, decay_ref, lap_ref, residue_ref, rows_ref):
    modes, sublanes, lanes = state_ref.shape
    mine = slice(half * sublanes, (half + 1) * sublanes)
    span = gc_ref.shape[0] // sublanes
    segment = segment_of((sublanes, lanes), segments)
    decay = [decay_ref[n, mine] for n in range(modes)]
    start = []
    for n in range(modes):
        total = jnp.zeros((sublanes, lanes), jnp.float32)
        if segments > 1:
            for k in range(segments - 2, -1, -1):
                total = jnp.where(segment == k, rolled(state_ref[n] + lap_ref[n, mine] * total, -1), total)
        start.append(total)

    def step(t, state):
        at = pl.ds(t, sublanes, stride=span)
        row = gc_ref[at, :]
        state = tuple(decay[n] * state[n] + row for n in range(modes))
        rows_ref[at, :] = summed([residue_ref[n, mine] * state[n] for n in range(modes)])
        return state

    steps_back(span, step, tuple(start), 8)


def scan(half, segments, grad_conv, state, decay, lap, residues):
    vmem = pl.BlockSpec(memory_space=pltpu.VMEM)
    return pl.pallas_call(
        functools.partial(scan_kernel, half, segments),
        in_specs=[vmem] * 5,
        out_specs=vmem,
        out_shape=jax.ShapeDtypeStruct(grad_conv.shape, jnp.float32),
        compiler_params=pltpu.CompilerParams(vmem_limit_bytes=VMEM),
        cost_estimate=QUICK,
    )(grad_conv, state, decay, lap, residues)


def laps_kernel(segments, span, decay_ref, lap_ref, wide_ref):
    modes, sublanes, lanes = decay_ref.shape
    sublanes //= 2
    packs = modes // segments
    segment = segment_of((sublanes, lanes), segments)
    for half in range(2):
        mine = slice(half * sublanes, (half + 1) * sublanes)
        for m in range(packs):
            packed = None
            for j in range(segments):
                lap = power(decay_ref[m * segments + j, mine], span)
                lap_ref[m * segments + j, mine] = lap
                wide = power(lap, segments)
                packed = wide if packed is None else jnp.where(segment == j, wide, packed)
            wide_ref[half * packs + m] = packed


def laps(segments, toks, decay):
    modes, sublanes, lanes = decay.shape
    vmem = pl.BlockSpec(memory_space=pltpu.VMEM)
    return pl.pallas_call(
        functools.partial(laps_kernel, segments, toks // segments),
        in_specs=[vmem],
        out_specs=(vmem, vmem),
        out_shape=(
            jax.ShapeDtypeStruct(decay.shape, jnp.float32),
            jax.ShapeDtypeStruct((2 * modes // segments, sublanes // 2, lanes), jnp.float32),
        ),
        compiler_params=pltpu.CompilerParams(vmem_limit_bytes=VMEM),
        cost_estimate=QUICK,
    )(decay)


def join_kernel(round_, group_ref, state_ref, arrived_ref, wide_ref, out_ref):
    earlier = (group_ref[0] >> round_) % 2 == 0
    for m in range(out_ref.shape[0]):
        wide = power(wide_ref[m], 1 << round_)
        mine, other = state_ref[m], arrived_ref[m]
        out_ref[m] = jnp.where(earlier, mine + wide * other, other + wide * mine)


def join(round_, group, state, arrived, wide):
    vmem = pl.BlockSpec(memory_space=pltpu.VMEM)
    return pl.pallas_call(
        functools.partial(join_kernel, round_),
        in_specs=[pl.BlockSpec(memory_space=pltpu.SMEM)] + [vmem] * 3,
        out_specs=vmem,
        out_shape=jax.ShapeDtypeStruct(state.shape, jnp.float32),
        compiler_params=pltpu.CompilerParams(vmem_limit_bytes=VMEM),
        cost_estimate=QUICK,
    )(group, state, arrived, wide)


def fix_kernel(segments, rounds, group_ref, *refs):
    scanned_refs, state_ref, arrived_refs = refs[:2], refs[2], refs[3 : 3 + rounds]
    decay_ref, lap_ref, wide_ref, residue_ref, out_hbm, rows_ref, out_ref, sems = refs[3 + rounds :]
    toks, width = out_ref.shape
    modes, sublanes, lanes = state_ref.shape
    packs = modes // segments
    rows = width // 2
    span = toks // segments
    segment = segment_of((sublanes, lanes), segments)
    earlier = [(group_ref[0] >> r) % 2 == 0 for r in range(rounds)]
    stores = []
    for half in range(2):
        mine = slice(half * sublanes, (half + 1) * sublanes)
        decay = [decay_ref[n, mine] for n in range(modes)]
        start = []
        for m in range(packs):
            brought = jnp.zeros((sublanes, lanes), jnp.float32)
            between = jnp.ones((sublanes, lanes), jnp.float32)
            for r in range(rounds):
                state = arrived_refs[r][half * packs + m]
                brought = jnp.where(earlier[r], brought + between * state, brought)
                if r + 1 < rounds:
                    between = jnp.where(earlier[r], between * power(wide_ref[half * packs + m], 1 << r), between)
            for j in range(segments):
                n = m * segments + j
                total = rolled(brought, segments - 1 - j)
                for k in range(segments - 2, -1, -1):
                    before = lap_ref[n, mine] * total
                    if half == 0:
                        before = before + state_ref[n]
                    total = jnp.where(segment == k, rolled(before, -1), total)
                start.append(residue_ref[n, mine] * total)

        def step(t, state, scanned_ref=scanned_refs[half], decay=decay):
            at = pl.ds(t, sublanes, stride=span)
            state = tuple(decay[n] * state[n] for n in range(modes))
            rows_ref[at, :] = scanned_ref[at, :] + summed(list(state))
            return state

        steps_back(span, step, tuple(start), 8)
        for line in range(rows // lanes):
            out_ref[:, half * rows + line * lanes : half * rows + (line + 1) * lanes] = rows_ref[
                line * toks : (line + 1) * toks, :
            ].astype(jnp.bfloat16)
        columns = pl.ds(half * rows, rows)
        stores.append(pltpu.make_async_copy(out_ref.at[:, columns], out_hbm.at[:, columns], sems.at[half]))
        stores[-1].start()
    for store in stores:
        store.wait()


def fix(segments, group, scanned, state, arrived, decay, lap, wide, residues, toks, width):
    vmem = pl.BlockSpec(memory_space=pltpu.VMEM)
    return pl.pallas_call(
        functools.partial(fix_kernel, segments, len(arrived)),
        in_specs=[pl.BlockSpec(memory_space=pltpu.SMEM)] + [vmem] * (7 + len(arrived)),
        out_specs=pl.BlockSpec(memory_space=pltpu.HBM),
        out_shape=jax.ShapeDtypeStruct((toks, width), jnp.bfloat16),
        scratch_shapes=[
            pltpu.VMEM(scanned[0].shape, jnp.float32),
            pltpu.VMEM((toks, width), jnp.bfloat16),
            pltpu.SemaphoreType.DMA((2,)),
        ],
        compiler_params=pltpu.CompilerParams(vmem_limit_bytes=VMEM),
        cost_estimate=QUICK,
    )(group, *scanned, state, *arrived, decay, lap, wide, residues)


def local(out_grad, out_weight, query_in, conv_out, residues, decay_rates):
    toks, width = query_in.shape
    modes = decay_rates.shape[1]
    lanes = math.gcd(width, 128)
    size, groups = lax.axis_size("ch"), lax.axis_size("ctx")
    bits = [1 << i for i in range(size.bit_length() - 1)]
    place = jnp.reshape(lax.axis_index("ch"), (1,)).astype(jnp.int32)
    group = jnp.reshape(lax.axis_index("ctx"), (1,)).astype(jnp.int32)
    half_rows = width // 2
    lines = half_rows // lanes
    segments = 8 // lines
    by_mode = lambda values: jnp.repeat(values.T.reshape(modes, width // lanes, lanes), segments, axis=1)
    decay, residue = by_mode(decay_rates), by_mode(residues)

    portions, order, waits = PORTIONS, ORDER, WAITS
    if size != 8:
        waits = {}
        portions = ((tuple(range(len(bits))), 2, 0), (tuple(range(len(bits))), 2, 1))
        order = [
            ((p, s, block),)
            for p in range(2)
            for s, bit in enumerate(bits)
            for block in sorted(range(0, size, 2 * bit), reverse=True)
        ] + [("laps", None), ("sum", 0), ("sum", 1), ("gate", 0), ("gate", 1), ("scan", 1), ("fix", None)]
    offsets = [sum(width // part for _, part, _ in portions[:p]) for p in range(len(portions))]

    received, sums, scanned, states, packed = {}, {}, {}, {}, {}
    grad_query = last = None

    def after(value):
        return value if last is None else lax.optimization_barrier((value, last, *awaited))[0]

    def collect(wanted):
        arrays, places = [], []
        for key in wanted:
            array, *place = received[key]
            index = next((i for i, known in enumerate(arrays) if known is array), len(arrays))
            if index == len(arrays):
                arrays.append(array)
            places.append((index, tuple(place)))
        return arrays, places

    for todo in order:
        awaited = [received[key][0] for key in waits.get(todo, ())]
        kind, half = todo if isinstance(todo[0], str) else ("send", None)
        inside = [q for q, (_, _, lies) in enumerate(portions) if lies == half]
        if kind == "send":
            arrays, items = [], []
            wanted, rows, bits_of = [], [], []
            for p, s, block in todo:
                route, share, _ = portions[p]
                bits_of.append(bits[route[s]])
                rows.append(width // share)
                wanted.append([(p, i, block ^ bits_of[-1]) for i in range(s)])
            bit, count = bits_of[0], len(todo)
            arrays, places = collect([key for keys in wanted for key in keys])
            places = iter(places)
            items = tuple(
                (block ^ bit, offsets[p], rows[i], tuple(next(places) for _ in wanted[i]))
                for i, (p, _, block) in enumerate(todo)
            )
            if last is None:
                last, turned = first_send(items, width, place, out_weight, out_grad)
            else:
                last = send(items, True, width, after(place), out_weight, turned, arrays)
            arrived = lax.ppermute(last, "ch", [(i, i ^ bit) for i in range(size)])
            start = peak = 0
            for i, key in enumerate(todo):
                part = part_of(rows[i], count)
                received[key] = (arrived, start, peak, part)
                start, peak = start + rows[i], peak + rows[i] // part
        elif kind == "laps":
            lap, wide = laps(segments, toks, after(decay))
            last = wide
        elif kind == "sum":
            items = tuple((0, offsets[q], width // portions[q][1], ()) for q in inside)
            last = sums[half] = send(items, False, width, after(place), out_weight, turned, [])
        elif kind == "gate":
            stages = range(len(bits))
            arrays, places = collect([(q, i, 0) for q in inside for i in stages])
            pieces = tuple(
                (offsets[q] - half * half_rows, tuple(places[i * len(stages) : (i + 1) * len(stages)]))
                for i, q in enumerate(inside)
            )
            other = residue if half == 0 else packed[0]
            grad_query, scanned[half], states[half], packed[half] = gate(
                half,
                half_rows,
                segments,
                pieces,
                after(sums[half]),
                arrays,
                query_in,
                conv_out,
                decay,
                lap,
                other,
                grad_query,
            )
            last = packed[half]
        elif kind == "scan":
            groups = lax.axis_size("ctx")
            swap = lambda array, round_: lax.ppermute(array, "ctx", [(i, i ^ (1 << round_)) for i in range(groups)])
            arrived = [swap(packed[1], 0)]
            last = scanned[1] = scan(1, segments, after(scanned[1]), states[1], decay, lap, residue)
            joined = packed[1]
            for round_ in range(1, groups.bit_length() - 1):
                joined = last = join(round_ - 1, after(group), joined, arrived[-1], wide)
                arrived.append(swap(joined, round_))
        else:
            grad_input = fix(
                segments, group, [scanned[0], scanned[1]], states[0], arrived, decay, lap, wide, residue, toks, width
            )
    return grad_query, grad_input


def solution(mesh):
    placed = (
        P("ctx", "ch"),
        P(None, "ch"),
        P("ctx", "ch"),
        P("ctx", "ch"),
        P("ch", None),
        P("ch", None),
    )
    return jax.shard_map(
        local,
        mesh=mesh,
        in_specs=placed,
        out_specs=(P("ctx", "ch"), P("ctx", "ch")),
        check_vma=False,
    )
```

```python
import functools
import math

import jax
import jax.numpy as jnp
from jax import lax
from jax.experimental import pallas as pl
from jax.experimental.pallas import tpu as pltpu
from jax.sharding import PartitionSpec as P

PEAKS = 16
SPAN = 251 * math.log(2.0)
SHIFT = 125 * math.log(2.0)
STEP = 256
PIECE = 128
VMEM = 24 * 1024 * 1024
QUICK = pl.CostEstimate(flops=0, bytes_accessed=1024, transcendentals=0)

PORTIONS = (((0, 1, 2), 2, 0), ((0, 1, 2), 2, 1))
ORDER = (
    ((0, 0, 6),), ((1, 0, 0),), ((0, 0, 4),), ((1, 0, 6),), ((1, 0, 2),), ((1, 0, 4),), ((0, 0, 2),), ((0, 1, 4),),
    ((1, 1, 4),), ((0, 2, 0),), ((0, 0, 0),), ((0, 1, 0),), ((1, 2, 0),), ((1, 1, 0),), ("laps", None), ("sum", 0),
    ("sum", 1), ("gate", 0), ("gate", 1), ("scan", 1), ("fix", None),
)
WAITS = {
    ((1, 1, 0),): ((0, 2, 0),),
    ("sum", 0): ((0, 1, 0), (0, 0, 0)),
    ((1, 2, 0),): ((1, 1, 4),),
    ("gate", 1): ((1, 2, 0),),
}


def part_of(rows, blocks):
    return next(part for part in range(16, rows + 1, 16) if rows % part == 0 and rows // part * blocks <= PEAKS)


def step_of(rows):
    return next(step for step in (STEP, STEP // 2, rows) if rows % step == 0)


def encode(block, part):
    codes, peaks = [], []
    for i in range(block.shape[0] // part):
        piece = block[i * part : (i + 1) * part, :]
        size = jnp.abs(piece)
        peak = jnp.maximum(jnp.max(size, axis=0, keepdims=True) * 1.01, 1e-30)
        peak = peak.astype(jnp.bfloat16).astype(jnp.float32)
        code = jnp.exp(size * (SPAN / peak) - SHIFT)
        codes.append(jnp.where(piece < 0, -code, code))
        peaks.append(peak)
    return jnp.concatenate(codes, axis=0).astype(jnp.bfloat16), peaks


def put_peaks(peaks, out_ref):
    if len(peaks) < PEAKS:
        peaks = peaks + [jnp.zeros((PEAKS - len(peaks), peaks[0].shape[1]), jnp.float32)]
    out_ref[out_ref.shape[0] - PEAKS :, :] = jnp.concatenate(peaks, axis=0).astype(jnp.bfloat16)


def decode(ref, place, first, count):
    start, peak, part = place
    peaks = ref[ref.shape[0] - PEAKS :, :].astype(jnp.float32) * (1.0 / SPAN)
    blocks = []
    for i in range(first // part, -(-(first + count) // part)):
        low, high = max(first, i * part), min(first + count, (i + 1) * part)
        code = ref[start + low : start + high, :].astype(jnp.float32)
        size = (jnp.log(jnp.abs(code)) + SHIFT) * peaks[peak + i : peak + i + 1, :]
        blocks.append(jnp.where(code < 0, -size, size))
    return jnp.concatenate(blocks, axis=0)


def pinned(array):
    return pltpu.with_memory_space_constraint(array, pltpu.HBM)


def send_kernel(items, coded, width, near, place_ref, w_ref, turned_ref, *refs):
    near_refs, out_ref = refs[:near], refs[near]
    base, peaks = 0, []
    for block, offset, rows, sources in items:
        step = step_of(rows)
        first = (place_ref[0] ^ block) * width + offset
        for at in range(0, rows, step):
            total = jnp.dot(
                w_ref[pl.ds(pl.multiple_of(first + at, 16), step), :],
                turned_ref[...],
                preferred_element_type=jnp.float32,
            )
            for source, place in sources:
                total = total + decode(near_refs[source], place, at, step)
            if coded:
                total, more = encode(total, part_of(rows, len(items)))
                peaks += more
            out_ref[base + at : base + at + step, :] = total
        base += rows
    if coded:
        put_peaks(peaks, out_ref)


def send(items, coded, width, place, weight, turned, nears):
    toks = turned.shape[1]
    vmem = pl.BlockSpec(memory_space=pltpu.VMEM)
    count = sum(rows for _, _, rows, _ in items) + (PEAKS if coded else 0)
    return pl.pallas_call(
        functools.partial(send_kernel, items, coded, width, len(nears)),
        in_specs=[pl.BlockSpec(memory_space=pltpu.SMEM)] + [vmem] * (2 + len(nears)),
        out_specs=vmem,
        out_shape=jax.ShapeDtypeStruct((count, toks), jnp.bfloat16 if coded else jnp.float32),
        compiler_params=pltpu.CompilerParams(vmem_limit_bytes=VMEM),
        cost_estimate=QUICK,
    )(place, weight, turned, *nears)


def first_kernel(items, width, place_ref, w_hbm, g_hbm, out_ref, turned_ref, w_ref, g_ref, sems):
    copies, toks = [], g_ref.shape[0]
    piece = math.gcd(toks, PIECE)
    for at in range(0, toks, piece):
        lines = pl.ds(at, piece)
        copies.append(pltpu.make_async_copy(g_hbm.at[lines, :], g_ref.at[lines, :], sems.at[len(copies)]))
    base, grads = 0, len(copies)
    for block, offset, rows, _ in items:
        step = math.gcd(rows, PIECE)
        first = pl.multiple_of((place_ref[0] ^ block) * width + offset, 16)
        for at in range(0, rows, step):
            copies.append(
                pltpu.make_async_copy(
                    w_hbm.at[pl.ds(first + at, step), :], w_ref.at[pl.ds(base + at, step), :], sems.at[len(copies)]
                )
            )
        base += rows
    for copy in copies:
        copy.start()
    for i, at in enumerate(range(0, toks, piece)):
        copies[i].wait()
        turned_ref[:, at : at + piece] = g_ref[at : at + piece, :].T
    base, peaks, waits = 0, [], iter(copies[grads:])
    for _, _, rows, _ in items:
        step = step_of(rows)
        for at in range(base, base + rows, step):
            for _ in range(step // math.gcd(rows, PIECE)):
                next(waits).wait()
            total = jnp.dot(w_ref[at : at + step, :], turned_ref[...], preferred_element_type=jnp.float32)
            total, more = encode(total, part_of(rows, len(items)))
            peaks += more
            out_ref[at : at + step, :] = total
        base += rows
    put_peaks(peaks, out_ref)


def first_send(items, width, place, weight, grad):
    toks, depth = grad.shape
    vmem = pl.BlockSpec(memory_space=pltpu.VMEM)
    high = pl.BlockSpec(memory_space=pltpu.HBM)
    count = sum(rows for _, _, rows, _ in items)
    steps = toks // math.gcd(toks, PIECE) + sum(rows // math.gcd(rows, PIECE) for _, _, rows, _ in items)
    return pl.pallas_call(
        functools.partial(first_kernel, items, width),
        in_specs=[pl.BlockSpec(memory_space=pltpu.SMEM), high, high],
        out_specs=(vmem, vmem),
        out_shape=(
            jax.ShapeDtypeStruct((count + PEAKS, toks), jnp.bfloat16),
            jax.ShapeDtypeStruct((depth, toks), jnp.bfloat16),
        ),
        scratch_shapes=[
            pltpu.VMEM((count, depth), jnp.bfloat16),
            pltpu.VMEM((toks, depth), jnp.bfloat16),
            pltpu.SemaphoreType.DMA((steps,)),
        ],
        compiler_params=pltpu.CompilerParams(vmem_limit_bytes=VMEM),
        cost_estimate=QUICK,
    )(place, pinned(weight), pinned(grad))


def steps_back(count, body, state, unroll):
    unroll = math.gcd(count, unroll)

    def some(i, state):
        for j in range(unroll):
            state = body(count - 1 - (i * unroll + j), state)
        return state

    return lax.fori_loop(0, count // unroll, some, state)


def power(base, exponent):
    result = None
    while exponent:
        if exponent % 2:
            result = base if result is None else result * base
        base = base * base
        exponent //= 2
    return result


def segment_of(shape, segments):
    return lax.rem(lax.broadcasted_iota(jnp.int32, shape, 0), segments)


def rolled(value, by):
    by %= value.shape[0]
    return pltpu.roll(value, by, 0) if by else value


def gate_kernel(half, rows, segments, pieces, near, acc_ref, *refs):
    near_refs, refs = refs[:near], refs[near:]
    query_ref, conv_ref, decay_ref, lap_ref, other_ref = refs[:5]
    out_hbm, rows_ref, state_ref, pack_ref = refs[-7:-3] if half == 0 else refs[-6:-2]
    gq_ref, sem = refs[-2:]
    gc_ref = refs[-3] if half == 0 else rows_ref
    toks = query_ref.shape[0]
    modes, sublanes, lanes = state_ref.shape
    mine = slice(half * sublanes, (half + 1) * sublanes)
    for line in range(rows // lanes):
        mix = acc_ref[line * lanes : (line + 1) * lanes, :]
        first, sources = next(piece for piece in reversed(pieces) if piece[0] <= line * lanes)
        for source, place in sources:
            mix = mix + decode(near_refs[source], place, line * lanes - first, lanes)
        mix = mix.T
        at = slice(line * lanes, (line + 1) * lanes)
        full = slice(half * rows + line * lanes, half * rows + (line + 1) * lanes)
        gq_ref[:, at] = (mix * conv_ref[:, full].astype(jnp.float32)).astype(jnp.bfloat16)
        gc_ref[line * toks : (line + 1) * toks, :] = mix * query_ref[:, full].astype(jnp.float32)
    store = pltpu.make_async_copy(gq_ref, out_hbm.at[:, pl.ds(half * rows, rows)], sem)
    store.start()
    decay = [decay_ref[n, mine] for n in range(modes)]
    span = toks // segments

    def step(t, state):
        at = pl.ds(t, sublanes, stride=span)
        row = gc_ref[at, :]
        state = tuple(decay[n] * state[n] + row for n in range(modes))
        if half == 0:
            rows_ref[at, :] = summed([other_ref[n, mine] * state[n] for n in range(modes)])
        return state

    zero = jnp.zeros((sublanes, lanes), jnp.float32)
    state = steps_back(span, step, (zero,) * modes, 16)
    segment = segment_of((sublanes, lanes), segments)
    whole = []
    for n in range(modes):
        state_ref[n] = state[n]
        total = state[n]
        if segments > 1:
            factor = jnp.where(segment < segments - 1, lap_ref[n, mine], 0.0)
            for _ in range(segments - 1):
                total = state[n] + factor * rolled(total, -1)
        whole.append(total)
    packs = modes // segments
    for m in range(packs):
        packed = whole[m * segments]
        for j in range(1, segments):
            packed = jnp.where(segment == j, rolled(whole[m * segments + j], j), packed)
        if half == 0:
            pack_ref[m] = packed
        else:
            pack_ref[m] = other_ref[m]
            pack_ref[packs + m] = packed
    store.wait()


def gate(half, rows, segments, pieces, acc, nears, query_in, conv_out, decay, lap, other, partial):
    toks, width = query_in.shape
    modes, _, lanes = decay.shape
    sublanes = rows // lanes * segments
    vmem = pl.BlockSpec(memory_space=pltpu.VMEM)
    high = pl.BlockSpec(memory_space=pltpu.HBM)
    more = [] if partial is None else [partial]
    lines = (rows // lanes * toks, lanes)
    return pl.pallas_call(
        functools.partial(gate_kernel, half, rows, segments, pieces, len(nears)),
        in_specs=[vmem] * (6 + len(nears)) + [high] * len(more),
        out_specs=(high, vmem, vmem, vmem),
        out_shape=(
            jax.ShapeDtypeStruct((toks, width), jnp.bfloat16),
            jax.ShapeDtypeStruct(lines, jnp.float32),
            jax.ShapeDtypeStruct((modes, sublanes, lanes), jnp.float32),
            jax.ShapeDtypeStruct(((1 + half) * modes // segments, sublanes, lanes), jnp.float32),
        ),
        scratch_shapes=([pltpu.VMEM(lines, jnp.float32)] if half == 0 else [])
        + [pltpu.VMEM((toks, rows), jnp.bfloat16), pltpu.SemaphoreType.DMA],
        input_output_aliases={6 + len(nears): 0} if more else {},
        compiler_params=pltpu.CompilerParams(vmem_limit_bytes=VMEM),
        cost_estimate=QUICK,
    )(acc, *nears, query_in, conv_out, decay, lap, other, *more)


def summed(terms):
    while len(terms) > 1:
        terms = [terms[k] + terms[k + 1] if k + 1 < len(terms) else terms[k] for k in range(0, len(terms), 2)]
    return terms[0]


def scan_kernel(half, segments, gc_ref, state_ref, decay_ref, lap_ref, residue_ref, rows_ref):
    modes, sublanes, lanes = state_ref.shape
    mine = slice(half * sublanes, (half + 1) * sublanes)
    span = gc_ref.shape[0] // sublanes
    segment = segment_of((sublanes, lanes), segments)
    decay = [decay_ref[n, mine] for n in range(modes)]
    start = []
    for n in range(modes):
        total = jnp.zeros((sublanes, lanes), jnp.float32)
        if segments > 1:
            for k in range(segments - 2, -1, -1):
                total = jnp.where(segment == k, rolled(state_ref[n] + lap_ref[n, mine] * total, -1), total)
        start.append(total)

    def step(t, state):
        at = pl.ds(t, sublanes, stride=span)
        row = gc_ref[at, :]
        state = tuple(decay[n] * state[n] + row for n in range(modes))
        rows_ref[at, :] = summed([residue_ref[n, mine] * state[n] for n in range(modes)])
        return state

    steps_back(span, step, tuple(start), 16)


def scan(half, segments, grad_conv, state, decay, lap, residues):
    vmem = pl.BlockSpec(memory_space=pltpu.VMEM)
    return pl.pallas_call(
        functools.partial(scan_kernel, half, segments),
        in_specs=[vmem] * 5,
        out_specs=vmem,
        out_shape=jax.ShapeDtypeStruct(grad_conv.shape, jnp.float32),
        compiler_params=pltpu.CompilerParams(vmem_limit_bytes=VMEM),
        cost_estimate=QUICK,
    )(grad_conv, state, decay, lap, residues)


def laps_kernel(segments, span, decay_ref, lap_ref, wide_ref):
    modes, sublanes, lanes = decay_ref.shape
    sublanes //= 2
    packs = modes // segments
    segment = segment_of((sublanes, lanes), segments)
    for half in range(2):
        mine = slice(half * sublanes, (half + 1) * sublanes)
        for m in range(packs):
            packed = None
            for j in range(segments):
                lap = power(decay_ref[m * segments + j, mine], span)
                lap_ref[m * segments + j, mine] = lap
                wide = power(lap, segments)
                packed = wide if packed is None else jnp.where(segment == j, wide, packed)
            wide_ref[half * packs + m] = packed


def laps(segments, toks, decay):
    modes, sublanes, lanes = decay.shape
    vmem = pl.BlockSpec(memory_space=pltpu.VMEM)
    return pl.pallas_call(
        functools.partial(laps_kernel, segments, toks // segments),
        in_specs=[vmem],
        out_specs=(vmem, vmem),
        out_shape=(
            jax.ShapeDtypeStruct(decay.shape, jnp.float32),
            jax.ShapeDtypeStruct((2 * modes // segments, sublanes // 2, lanes), jnp.float32),
        ),
        compiler_params=pltpu.CompilerParams(vmem_limit_bytes=VMEM),
        cost_estimate=QUICK,
    )(decay)


def join_kernel(round_, group_ref, state_ref, arrived_ref, wide_ref, out_ref):
    earlier = (group_ref[0] >> round_) % 2 == 0
    for m in range(out_ref.shape[0]):
        wide = power(wide_ref[m], 1 << round_)
        mine, other = state_ref[m], arrived_ref[m]
        out_ref[m] = jnp.where(earlier, mine + wide * other, other + wide * mine)


def join(round_, group, state, arrived, wide):
    vmem = pl.BlockSpec(memory_space=pltpu.VMEM)
    return pl.pallas_call(
        functools.partial(join_kernel, round_),
        in_specs=[pl.BlockSpec(memory_space=pltpu.SMEM)] + [vmem] * 3,
        out_specs=vmem,
        out_shape=jax.ShapeDtypeStruct(state.shape, jnp.float32),
        compiler_params=pltpu.CompilerParams(vmem_limit_bytes=VMEM),
        cost_estimate=QUICK,
    )(group, state, arrived, wide)


def fix_kernel(segments, rounds, group_ref, *refs):
    scanned_refs, state_ref, arrived_refs = refs[:2], refs[2], refs[3 : 3 + rounds]
    decay_ref, lap_ref, wide_ref, residue_ref, out_hbm, rows_ref, out_ref, sems = refs[3 + rounds :]
    toks, width = out_ref.shape
    modes, sublanes, lanes = state_ref.shape
    packs = modes // segments
    rows = width // 2
    span = toks // segments
    segment = segment_of((sublanes, lanes), segments)
    earlier = [(group_ref[0] >> r) % 2 == 0 for r in range(rounds)]
    stores = []
    for half in range(2):
        mine = slice(half * sublanes, (half + 1) * sublanes)
        decay = [decay_ref[n, mine] for n in range(modes)]
        start = []
        for m in range(packs):
            brought = jnp.zeros((sublanes, lanes), jnp.float32)
            between = jnp.ones((sublanes, lanes), jnp.float32)
            for r in range(rounds):
                state = arrived_refs[r][half * packs + m]
                brought = jnp.where(earlier[r], brought + between * state, brought)
                if r + 1 < rounds:
                    between = jnp.where(earlier[r], between * power(wide_ref[half * packs + m], 1 << r), between)
            for j in range(segments):
                n = m * segments + j
                total = rolled(brought, segments - 1 - j)
                for k in range(segments - 2, -1, -1):
                    before = lap_ref[n, mine] * total
                    if half == 0:
                        before = before + state_ref[n]
                    total = jnp.where(segment == k, rolled(before, -1), total)
                start.append(residue_ref[n, mine] * total)

        def step(t, state, scanned_ref=scanned_refs[half], decay=decay):
            at = pl.ds(t, sublanes, stride=span)
            state = tuple(decay[n] * state[n] for n in range(modes))
            rows_ref[at, :] = scanned_ref[at, :] + summed(list(state))
            return state

        steps_back(span, step, tuple(start), 16)
        for line in range(rows // lanes):
            out_ref[:, half * rows + line * lanes : half * rows + (line + 1) * lanes] = rows_ref[
                line * toks : (line + 1) * toks, :
            ].astype(jnp.bfloat16)
        columns = pl.ds(half * rows, rows)
        stores.append(pltpu.make_async_copy(out_ref.at[:, columns], out_hbm.at[:, columns], sems.at[half]))
        stores[-1].start()
    for store in stores:
        store.wait()


def fix(segments, group, scanned, state, arrived, decay, lap, wide, residues, toks, width):
    vmem = pl.BlockSpec(memory_space=pltpu.VMEM)
    return pl.pallas_call(
        functools.partial(fix_kernel, segments, len(arrived)),
        in_specs=[pl.BlockSpec(memory_space=pltpu.SMEM)] + [vmem] * (7 + len(arrived)),
        out_specs=pl.BlockSpec(memory_space=pltpu.HBM),
        out_shape=jax.ShapeDtypeStruct((toks, width), jnp.bfloat16),
        scratch_shapes=[
            pltpu.VMEM(scanned[0].shape, jnp.float32),
            pltpu.VMEM((toks, width), jnp.bfloat16),
            pltpu.SemaphoreType.DMA((2,)),
        ],
        compiler_params=pltpu.CompilerParams(vmem_limit_bytes=VMEM),
        cost_estimate=QUICK,
    )(group, *scanned, state, *arrived, decay, lap, wide, residues)


def local(out_grad, out_weight, query_in, conv_out, residues, decay_rates):
    toks, width = query_in.shape
    modes = decay_rates.shape[1]
    lanes = math.gcd(width, 128)
    size, groups = lax.axis_size("ch"), lax.axis_size("ctx")
    bits = [1 << i for i in range(size.bit_length() - 1)]
    place = jnp.reshape(lax.axis_index("ch"), (1,)).astype(jnp.int32)
    group = jnp.reshape(lax.axis_index("ctx"), (1,)).astype(jnp.int32)
    half_rows = width // 2
    lines = half_rows // lanes
    segments = 8 // lines
    by_mode = lambda values: jnp.repeat(values.T.reshape(modes, width // lanes, lanes), segments, axis=1)
    decay, residue = by_mode(decay_rates), by_mode(residues)

    portions, order, waits = PORTIONS, ORDER, WAITS
    if size != 8:
        waits = {}
        portions = ((tuple(range(len(bits))), 2, 0), (tuple(range(len(bits))), 2, 1))
        order = [
            ((p, s, block),)
            for p in range(2)
            for s, bit in enumerate(bits)
            for block in sorted(range(0, size, 2 * bit), reverse=True)
        ] + [("laps", None), ("sum", 0), ("sum", 1), ("gate", 0), ("gate", 1), ("scan", 1), ("fix", None)]
    offsets = [sum(width // part for _, part, _ in portions[:p]) for p in range(len(portions))]

    received, sums, scanned, states, packed = {}, {}, {}, {}, {}
    grad_query = last = None

    def after(value):
        return value if last is None else lax.optimization_barrier((value, last, *awaited))[0]

    def collect(wanted):
        arrays, places = [], []
        for key in wanted:
            array, *place = received[key]
            index = next((i for i, known in enumerate(arrays) if known is array), len(arrays))
            if index == len(arrays):
                arrays.append(array)
            places.append((index, tuple(place)))
        return arrays, places

    for todo in order:
        awaited = [received[key][0] for key in waits.get(todo, ())]
        kind, half = todo if isinstance(todo[0], str) else ("send", None)
        inside = [q for q, (_, _, lies) in enumerate(portions) if lies == half]
        if kind == "send":
            arrays, items = [], []
            wanted, rows, bits_of = [], [], []
            for p, s, block in todo:
                route, share, _ = portions[p]
                bits_of.append(bits[route[s]])
                rows.append(width // share)
                wanted.append([(p, i, block ^ bits_of[-1]) for i in range(s)])
            bit, count = bits_of[0], len(todo)
            arrays, places = collect([key for keys in wanted for key in keys])
            places = iter(places)
            items = tuple(
                (block ^ bit, offsets[p], rows[i], tuple(next(places) for _ in wanted[i]))
                for i, (p, _, block) in enumerate(todo)
            )
            if last is None:
                last, turned = first_send(items, width, place, out_weight, out_grad)
            else:
                last = send(items, True, width, after(place), out_weight, turned, arrays)
            arrived = lax.ppermute(last, "ch", [(i, i ^ bit) for i in range(size)])
            start = peak = 0
            for i, key in enumerate(todo):
                part = part_of(rows[i], count)
                received[key] = (arrived, start, peak, part)
                start, peak = start + rows[i], peak + rows[i] // part
        elif kind == "laps":
            lap, wide = laps(segments, toks, after(decay))
            last = wide
        elif kind == "sum":
            items = tuple((0, offsets[q], width // portions[q][1], ()) for q in inside)
            last = sums[half] = send(items, False, width, after(place), out_weight, turned, [])
        elif kind == "gate":
            stages = range(len(bits))
            arrays, places = collect([(q, i, 0) for q in inside for i in stages])
            pieces = tuple(
                (offsets[q] - half * half_rows, tuple(places[i * len(stages) : (i + 1) * len(stages)]))
                for i, q in enumerate(inside)
            )
            other = residue if half == 0 else packed[0]
            grad_query, scanned[half], states[half], packed[half] = gate(
                half,
                half_rows,
                segments,
                pieces,
                after(sums[half]),
                arrays,
                query_in,
                conv_out,
                decay,
                lap,
                other,
                grad_query,
            )
            last = packed[half]
        elif kind == "scan":
            groups = lax.axis_size("ctx")
            swap = lambda array, round_: lax.ppermute(array, "ctx", [(i, i ^ (1 << round_)) for i in range(groups)])
            arrived, joined = [swap(packed[1], 0)], packed[1]
            for round_ in range(1, groups.bit_length() - 1):
                joined = last = join(round_ - 1, after(group), joined, arrived[-1], wide)
                arrived.append(swap(joined, round_))
            scanned[1] = scan(1, segments, after(scanned[1]), states[1], decay, lap, residue)
        else:
            grad_input = fix(
                segments, group, [scanned[0], scanned[1]], states[0], arrived, decay, lap, wide, residue, toks, width
            )
    return grad_query, grad_input


def solution(mesh):
    placed = (
        P("ctx", "ch"),
        P(None, "ch"),
        P("ctx", "ch"),
        P("ctx", "ch"),
        P("ch", None),
        P("ch", None),
    )
    return jax.shard_map(
        local,
        mesh=mesh,
        in_specs=placed,
        out_specs=(P("ctx", "ch"), P("ctx", "ch")),
        check_vma=False,
    )
```

```python
import functools
import math

import jax
import jax.numpy as jnp
from jax import lax
from jax.experimental import pallas as pl
from jax.experimental.pallas import tpu as pltpu
from jax.sharding import PartitionSpec as P

PEAKS = 16
SPAN = 251 * math.log(2.0)
SHIFT = 125 * math.log(2.0)
STEP = 256
PIECE = 128
GAP = 8
VMEM = 24 * 1024 * 1024
QUICK = pl.CostEstimate(flops=0, bytes_accessed=1024, transcendentals=0)

PORTIONS = (((0, 1, 2), 2, 0), ((0, 1, 2), 2, 1))
ORDER = (
    ((0, 0, 6),), ((1, 0, 0),), ((0, 0, 4),), ((1, 0, 6),), ((1, 0, 2),), ((1, 0, 4),), ((0, 0, 2),), ((0, 1, 4),),
    ((1, 1, 4),), ((0, 2, 0),), ((0, 0, 0),), ((0, 1, 0),), ((1, 2, 0),), ((1, 1, 0),), ("laps", None), ("sum", 0),
    ("sum", 1), ("gate", 0), ("gate", 1), ("scan", 1), ("fix", None),
)
WAITS = {
    ((1, 1, 0),): ((0, 2, 0),),
    ("sum", 0): ((0, 1, 0), (0, 0, 0)),
    ((1, 2, 0),): ((1, 1, 4),),
    ("gate", 1): ((1, 2, 0),),
}


def part_of(rows, blocks):
    return next(part for part in range(16, rows + 1, 16) if rows % part == 0 and rows // part * blocks <= PEAKS)


def step_of(rows):
    return next(step for step in (STEP, STEP // 2, rows) if rows % step == 0)


def encode(block, part):
    codes, peaks = [], []
    for i in range(block.shape[0] // part):
        piece = block[i * part : (i + 1) * part, :]
        size = jnp.abs(piece)
        peak = jnp.maximum(jnp.max(size, axis=0, keepdims=True) * 1.01, 1e-30)
        peak = peak.astype(jnp.bfloat16).astype(jnp.float32)
        code = jnp.exp(size * (SPAN / peak) - SHIFT)
        codes.append(jnp.where(piece < 0, -code, code))
        peaks.append(peak)
    return jnp.concatenate(codes, axis=0).astype(jnp.bfloat16), peaks


def put_peaks(peaks, out_ref):
    if len(peaks) < PEAKS:
        peaks = peaks + [jnp.zeros((PEAKS - len(peaks), peaks[0].shape[1]), jnp.float32)]
    out_ref[out_ref.shape[0] - PEAKS :, :] = jnp.concatenate(peaks, axis=0).astype(jnp.bfloat16)


def decode(ref, place, first, count):
    start, peak, part = place
    peaks = ref[ref.shape[0] - PEAKS :, :].astype(jnp.float32) * (1.0 / SPAN)
    blocks = []
    for i in range(first // part, -(-(first + count) // part)):
        low, high = max(first, i * part), min(first + count, (i + 1) * part)
        code = ref[start + low : start + high, :].astype(jnp.float32)
        size = (jnp.log(jnp.abs(code)) + SHIFT) * peaks[peak + i : peak + i + 1, :]
        blocks.append(jnp.where(code < 0, -size, size))
    return jnp.concatenate(blocks, axis=0)


def pinned(array):
    return pltpu.with_memory_space_constraint(array, pltpu.HBM)


def send_kernel(items, coded, width, near, place_ref, w_ref, turned_ref, *refs):
    near_refs, out_ref = refs[:near], refs[near]
    base, peaks = 0, []
    for block, offset, rows, sources in items:
        step = step_of(rows)
        first = (place_ref[0] ^ block) * width + offset
        for at in range(0, rows, step):
            total = jnp.dot(
                w_ref[pl.ds(pl.multiple_of(first + at, 16), step), :],
                turned_ref[...],
                preferred_element_type=jnp.float32,
            )
            for source, place in sources:
                total = total + decode(near_refs[source], place, at, step)
            if coded:
                total, more = encode(total, part_of(rows, len(items)))
                peaks += more
            out_ref[base + at : base + at + step, :] = total
        base += rows
    if coded:
        put_peaks(peaks, out_ref)


def send(items, coded, width, place, weight, turned, nears):
    toks = turned.shape[1]
    vmem = pl.BlockSpec(memory_space=pltpu.VMEM)
    count = sum(rows for _, _, rows, _ in items) + (PEAKS if coded else 0)
    return pl.pallas_call(
        functools.partial(send_kernel, items, coded, width, len(nears)),
        in_specs=[pl.BlockSpec(memory_space=pltpu.SMEM)] + [vmem] * (2 + len(nears)),
        out_specs=vmem,
        out_shape=jax.ShapeDtypeStruct((count, toks), jnp.bfloat16 if coded else jnp.float32),
        compiler_params=pltpu.CompilerParams(vmem_limit_bytes=VMEM),
        cost_estimate=QUICK,
    )(place, weight, turned, *nears)


def first_kernel(items, width, place_ref, w_hbm, g_hbm, out_ref, turned_ref, w_ref, g_ref, sems):
    copies, toks = [], g_ref.shape[0]
    piece = math.gcd(toks, PIECE)
    for at in range(0, toks, piece):
        lines = pl.ds(at, piece)
        copies.append(pltpu.make_async_copy(g_hbm.at[lines, :], g_ref.at[lines, :], sems.at[len(copies)]))
    base, grads = 0, len(copies)
    for block, offset, rows, _ in items:
        step = math.gcd(rows, PIECE)
        first = pl.multiple_of((place_ref[0] ^ block) * width + offset, 16)
        for at in range(0, rows, step):
            copies.append(
                pltpu.make_async_copy(
                    w_hbm.at[pl.ds(first + at, step), :], w_ref.at[pl.ds(base + at, step), :], sems.at[len(copies)]
                )
            )
        base += rows
    for copy in copies:
        copy.start()
    for i, at in enumerate(range(0, toks, piece)):
        copies[i].wait()
        turned_ref[:, at : at + piece] = g_ref[at : at + piece, :].T
    base, peaks, waits = 0, [], iter(copies[grads:])
    for _, _, rows, _ in items:
        step = step_of(rows)
        for at in range(base, base + rows, step):
            for _ in range(step // math.gcd(rows, PIECE)):
                next(waits).wait()
            total = jnp.dot(w_ref[at : at + step, :], turned_ref[...], preferred_element_type=jnp.float32)
            total, more = encode(total, part_of(rows, len(items)))
            peaks += more
            out_ref[at : at + step, :] = total
        base += rows
    put_peaks(peaks, out_ref)


def first_send(items, width, place, weight, grad):
    toks, depth = grad.shape
    vmem = pl.BlockSpec(memory_space=pltpu.VMEM)
    high = pl.BlockSpec(memory_space=pltpu.HBM)
    count = sum(rows for _, _, rows, _ in items)
    steps = toks // math.gcd(toks, PIECE) + sum(rows // math.gcd(rows, PIECE) for _, _, rows, _ in items)
    return pl.pallas_call(
        functools.partial(first_kernel, items, width),
        in_specs=[pl.BlockSpec(memory_space=pltpu.SMEM), high, high],
        out_specs=(vmem, vmem),
        out_shape=(
            jax.ShapeDtypeStruct((count + PEAKS, toks), jnp.bfloat16),
            jax.ShapeDtypeStruct((depth, toks), jnp.bfloat16),
        ),
        scratch_shapes=[
            pltpu.VMEM((count, depth), jnp.bfloat16),
            pltpu.VMEM((toks, depth), jnp.bfloat16),
            pltpu.SemaphoreType.DMA((steps,)),
        ],
        compiler_params=pltpu.CompilerParams(vmem_limit_bytes=VMEM),
        cost_estimate=QUICK,
    )(place, pinned(weight), pinned(grad))


def steps_back(count, body, state, unroll):
    unroll = math.gcd(count, unroll)

    def some(i, state):
        for j in range(unroll):
            state = body(count - 1 - (i * unroll + j), state)
        return state

    return lax.fori_loop(0, count // unroll, some, state)


def power(base, exponent):
    result = None
    while exponent:
        if exponent % 2:
            result = base if result is None else result * base
        base = base * base
        exponent //= 2
    return result


def segment_of(shape, segments):
    return lax.rem(lax.broadcasted_iota(jnp.int32, shape, 0), segments)


def rolled(value, by):
    by %= value.shape[0]
    return pltpu.roll(value, by, 0) if by else value


def gate_kernel(half, rows, segments, pieces, near, acc_ref, *refs):
    near_refs, refs = refs[:near], refs[near:]
    query_ref, conv_ref, decay_ref, lap_ref, other_ref = refs[:5]
    out_hbm, rows_ref, state_ref, pack_ref = refs[-7:-3] if half == 0 else refs[-6:-2]
    gq_ref, sem = refs[-2:]
    gc_ref = refs[-3] if half == 0 else rows_ref
    toks = query_ref.shape[0]
    modes, sublanes, lanes = state_ref.shape
    mine = slice(half * sublanes, (half + 1) * sublanes)
    for line in range(rows // lanes):
        mix = acc_ref[line * lanes : (line + 1) * lanes, :]
        first, sources = next(piece for piece in reversed(pieces) if piece[0] <= line * lanes)
        for source, place in sources:
            mix = mix + decode(near_refs[source], place, line * lanes - first, lanes)
        mix = mix.T
        at = slice(line * lanes, (line + 1) * lanes)
        full = slice(half * rows + line * lanes, half * rows + (line + 1) * lanes)
        gq_ref[:, at] = (mix * conv_ref[:, full].astype(jnp.float32)).astype(jnp.bfloat16)
        gated = mix * query_ref[:, full].astype(jnp.float32)
        for k in range(segments):
            start = (line * segments + k) * (toks // segments + GAP)
            gc_ref[start : start + toks // segments, :] = gated[k * (toks // segments) : (k + 1) * (toks // segments), :]
    store = pltpu.make_async_copy(gq_ref, out_hbm.at[:, pl.ds(half * rows, rows)], sem)
    store.start()
    decay = [decay_ref[n, mine] for n in range(modes)]
    span = toks // segments

    def step(t, state):
        at = pl.ds(t, sublanes, stride=span + GAP)
        row = gc_ref[at, :]
        state = tuple(decay[n] * state[n] + row for n in range(modes))
        if half == 0:
            rows_ref[at, :] = summed([other_ref[n, mine] * state[n] for n in range(modes)])
        return state

    zero = jnp.zeros((sublanes, lanes), jnp.float32)
    state = steps_back(span, step, (zero,) * modes, 16)
    segment = segment_of((sublanes, lanes), segments)
    whole = []
    for n in range(modes):
        state_ref[n] = state[n]
        total = state[n]
        if segments > 1:
            factor = jnp.where(segment < segments - 1, lap_ref[n, mine], 0.0)
            for _ in range(segments - 1):
                total = state[n] + factor * rolled(total, -1)
        whole.append(total)
    packs = modes // segments
    for m in range(packs):
        packed = whole[m * segments]
        for j in range(1, segments):
            packed = jnp.where(segment == j, rolled(whole[m * segments + j], j), packed)
        if half == 0:
            pack_ref[m] = packed
        else:
            pack_ref[m] = other_ref[m]
            pack_ref[packs + m] = packed
    store.wait()


def gate(half, rows, segments, pieces, acc, nears, query_in, conv_out, decay, lap, other, partial):
    toks, width = query_in.shape
    modes, _, lanes = decay.shape
    sublanes = rows // lanes * segments
    vmem = pl.BlockSpec(memory_space=pltpu.VMEM)
    high = pl.BlockSpec(memory_space=pltpu.HBM)
    more = [] if partial is None else [partial]
    lines = (sublanes * (toks // segments + GAP), lanes)
    return pl.pallas_call(
        functools.partial(gate_kernel, half, rows, segments, pieces, len(nears)),
        in_specs=[vmem] * (6 + len(nears)) + [high] * len(more),
        out_specs=(high, vmem, vmem, vmem),
        out_shape=(
            jax.ShapeDtypeStruct((toks, width), jnp.bfloat16),
            jax.ShapeDtypeStruct(lines, jnp.float32),
            jax.ShapeDtypeStruct((modes, sublanes, lanes), jnp.float32),
            jax.ShapeDtypeStruct(((1 + half) * modes // segments, sublanes, lanes), jnp.float32),
        ),
        scratch_shapes=([pltpu.VMEM(lines, jnp.float32)] if half == 0 else [])
        + [pltpu.VMEM((toks, rows), jnp.bfloat16), pltpu.SemaphoreType.DMA],
        input_output_aliases={6 + len(nears): 0} if more else {},
        compiler_params=pltpu.CompilerParams(vmem_limit_bytes=VMEM),
        cost_estimate=QUICK,
    )(acc, *nears, query_in, conv_out, decay, lap, other, *more)


def summed(terms):
    while len(terms) > 1:
        terms = [terms[k] + terms[k + 1] if k + 1 < len(terms) else terms[k] for k in range(0, len(terms), 2)]
    return terms[0]


def scan_kernel(half, segments, gc_ref, state_ref, decay_ref, lap_ref, residue_ref, rows_ref):
    modes, sublanes, lanes = state_ref.shape
    mine = slice(half * sublanes, (half + 1) * sublanes)
    span = gc_ref.shape[0] // sublanes - GAP
    segment = segment_of((sublanes, lanes), segments)
    decay = [decay_ref[n, mine] for n in range(modes)]
    start = []
    for n in range(modes):
        total = jnp.zeros((sublanes, lanes), jnp.float32)
        if segments > 1:
            for k in range(segments - 2, -1, -1):
                total = jnp.where(segment == k, rolled(state_ref[n] + lap_ref[n, mine] * total, -1), total)
        start.append(total)

    def step(t, state):
        at = pl.ds(t, sublanes, stride=span + GAP)
        row = gc_ref[at, :]
        state = tuple(decay[n] * state[n] + row for n in range(modes))
        rows_ref[at, :] = summed([residue_ref[n, mine] * state[n] for n in range(modes)])
        return state

    steps_back(span, step, tuple(start), 16)


def scan(half, segments, grad_conv, state, decay, lap, residues):
    vmem = pl.BlockSpec(memory_space=pltpu.VMEM)
    return pl.pallas_call(
        functools.partial(scan_kernel, half, segments),
        in_specs=[vmem] * 5,
        out_specs=vmem,
        out_shape=jax.ShapeDtypeStruct(grad_conv.shape, jnp.float32),
        compiler_params=pltpu.CompilerParams(vmem_limit_bytes=VMEM),
        cost_estimate=QUICK,
    )(grad_conv, state, decay, lap, residues)


def laps_kernel(segments, span, decay_ref, lap_ref, wide_ref):
    modes, sublanes, lanes = decay_ref.shape
    sublanes //= 2
    packs = modes // segments
    segment = segment_of((sublanes, lanes), segments)
    for half in range(2):
        mine = slice(half * sublanes, (half + 1) * sublanes)
        for m in range(packs):
            packed = None
            for j in range(segments):
                lap = power(decay_ref[m * segments + j, mine], span)
                lap_ref[m * segments + j, mine] = lap
                wide = power(lap, segments)
                packed = wide if packed is None else jnp.where(segment == j, wide, packed)
            wide_ref[half * packs + m] = packed


def laps(segments, toks, decay):
    modes, sublanes, lanes = decay.shape
    vmem = pl.BlockSpec(memory_space=pltpu.VMEM)
    return pl.pallas_call(
        functools.partial(laps_kernel, segments, toks // segments),
        in_specs=[vmem],
        out_specs=(vmem, vmem),
        out_shape=(
            jax.ShapeDtypeStruct(decay.shape, jnp.float32),
            jax.ShapeDtypeStruct((2 * modes // segments, sublanes // 2, lanes), jnp.float32),
        ),
        compiler_params=pltpu.CompilerParams(vmem_limit_bytes=VMEM),
        cost_estimate=QUICK,
    )(decay)


def join_kernel(round_, group_ref, state_ref, arrived_ref, wide_ref, out_ref):
    earlier = (group_ref[0] >> round_) % 2 == 0
    for m in range(out_ref.shape[0]):
        wide = power(wide_ref[m], 1 << round_)
        mine, other = state_ref[m], arrived_ref[m]
        out_ref[m] = jnp.where(earlier, mine + wide * other, other + wide * mine)


def join(round_, group, state, arrived, wide):
    vmem = pl.BlockSpec(memory_space=pltpu.VMEM)
    return pl.pallas_call(
        functools.partial(join_kernel, round_),
        in_specs=[pl.BlockSpec(memory_space=pltpu.SMEM)] + [vmem] * 3,
        out_specs=vmem,
        out_shape=jax.ShapeDtypeStruct(state.shape, jnp.float32),
        compiler_params=pltpu.CompilerParams(vmem_limit_bytes=VMEM),
        cost_estimate=QUICK,
    )(group, state, arrived, wide)


def fix_kernel(segments, rounds, group_ref, *refs):
    scanned_refs, state_ref, arrived_refs = refs[:2], refs[2], refs[3 : 3 + rounds]
    decay_ref, lap_ref, wide_ref, residue_ref, out_hbm, rows_ref, out_ref, sems = refs[3 + rounds :]
    toks, width = out_ref.shape
    modes, sublanes, lanes = state_ref.shape
    packs = modes // segments
    rows = width // 2
    span = toks // segments
    segment = segment_of((sublanes, lanes), segments)
    earlier = [(group_ref[0] >> r) % 2 == 0 for r in range(rounds)]
    stores = []
    for half in range(2):
        mine = slice(half * sublanes, (half + 1) * sublanes)
        decay = [decay_ref[n, mine] for n in range(modes)]
        start = []
        for m in range(packs):
            brought = jnp.zeros((sublanes, lanes), jnp.float32)
            between = jnp.ones((sublanes, lanes), jnp.float32)
            for r in range(rounds):
                state = arrived_refs[r][half * packs + m]
                brought = jnp.where(earlier[r], brought + between * state, brought)
                if r + 1 < rounds:
                    between = jnp.where(earlier[r], between * power(wide_ref[half * packs + m], 1 << r), between)
            for j in range(segments):
                n = m * segments + j
                total = rolled(brought, segments - 1 - j)
                for k in range(segments - 2, -1, -1):
                    before = lap_ref[n, mine] * total
                    if half == 0:
                        before = before + state_ref[n]
                    total = jnp.where(segment == k, rolled(before, -1), total)
                start.append(residue_ref[n, mine] * total)

        def step(t, state, scanned_ref=scanned_refs[half], decay=decay):
            at = pl.ds(t, sublanes, stride=span + GAP)
            state = tuple(decay[n] * state[n] for n in range(modes))
            rows_ref[at, :] = scanned_ref[at, :] + summed(list(state))
            return state

        steps_back(span, step, tuple(start), 16)
        for line in range(rows // lanes):
            at = slice(half * rows + line * lanes, half * rows + (line + 1) * lanes)
            for k in range(segments):
                start = (line * segments + k) * (span + GAP)
                out_ref[k * span : (k + 1) * span, at] = rows_ref[start : start + span, :].astype(jnp.bfloat16)
        columns = pl.ds(half * rows, rows)
        stores.append(pltpu.make_async_copy(out_ref.at[:, columns], out_hbm.at[:, columns], sems.at[half]))
        stores[-1].start()
    for store in stores:
        store.wait()


def fix(segments, group, scanned, state, arrived, decay, lap, wide, residues, toks, width):
    vmem = pl.BlockSpec(memory_space=pltpu.VMEM)
    return pl.pallas_call(
        functools.partial(fix_kernel, segments, len(arrived)),
        in_specs=[pl.BlockSpec(memory_space=pltpu.SMEM)] + [vmem] * (7 + len(arrived)),
        out_specs=pl.BlockSpec(memory_space=pltpu.HBM),
        out_shape=jax.ShapeDtypeStruct((toks, width), jnp.bfloat16),
        scratch_shapes=[
            pltpu.VMEM(scanned[0].shape, jnp.float32),
            pltpu.VMEM((toks, width), jnp.bfloat16),
            pltpu.SemaphoreType.DMA((2,)),
        ],
        compiler_params=pltpu.CompilerParams(vmem_limit_bytes=VMEM),
        cost_estimate=QUICK,
    )(group, *scanned, state, *arrived, decay, lap, wide, residues)


def local(out_grad, out_weight, query_in, conv_out, residues, decay_rates):
    toks, width = query_in.shape
    modes = decay_rates.shape[1]
    lanes = math.gcd(width, 128)
    size, groups = lax.axis_size("ch"), lax.axis_size("ctx")
    bits = [1 << i for i in range(size.bit_length() - 1)]
    place = jnp.reshape(lax.axis_index("ch"), (1,)).astype(jnp.int32)
    group = jnp.reshape(lax.axis_index("ctx"), (1,)).astype(jnp.int32)
    half_rows = width // 2
    lines = half_rows // lanes
    segments = 8 // lines
    by_mode = lambda values: jnp.repeat(values.T.reshape(modes, width // lanes, lanes), segments, axis=1)
    decay, residue = by_mode(decay_rates), by_mode(residues)

    portions, order, waits = PORTIONS, ORDER, WAITS
    if size != 8:
        waits = {}
        portions = ((tuple(range(len(bits))), 2, 0), (tuple(range(len(bits))), 2, 1))
        order = [
            ((p, s, block),)
            for p in range(2)
            for s, bit in enumerate(bits)
            for block in sorted(range(0, size, 2 * bit), reverse=True)
        ] + [("laps", None), ("sum", 0), ("sum", 1), ("gate", 0), ("gate", 1), ("scan", 1), ("fix", None)]
    offsets = [sum(width // part for _, part, _ in portions[:p]) for p in range(len(portions))]

    received, sums, scanned, states, packed = {}, {}, {}, {}, {}
    grad_query = last = None

    def after(value):
        return value if last is None else lax.optimization_barrier((value, last, *awaited))[0]

    def collect(wanted):
        arrays, places = [], []
        for key in wanted:
            array, *place = received[key]
            index = next((i for i, known in enumerate(arrays) if known is array), len(arrays))
            if index == len(arrays):
                arrays.append(array)
            places.append((index, tuple(place)))
        return arrays, places

    for todo in order:
        awaited = [received[key][0] for key in waits.get(todo, ())]
        kind, half = todo if isinstance(todo[0], str) else ("send", None)
        inside = [q for q, (_, _, lies) in enumerate(portions) if lies == half]
        if kind == "send":
            arrays, items = [], []
            wanted, rows, bits_of = [], [], []
            for p, s, block in todo:
                route, share, _ = portions[p]
                bits_of.append(bits[route[s]])
                rows.append(width // share)
                wanted.append([(p, i, block ^ bits_of[-1]) for i in range(s)])
            bit, count = bits_of[0], len(todo)
            arrays, places = collect([key for keys in wanted for key in keys])
            places = iter(places)
            items = tuple(
                (block ^ bit, offsets[p], rows[i], tuple(next(places) for _ in wanted[i]))
                for i, (p, _, block) in enumerate(todo)
            )
            if last is None:
                last, turned = first_send(items, width, place, out_weight, out_grad)
            else:
                last = send(items, True, width, after(place), out_weight, turned, arrays)
            arrived = lax.ppermute(last, "ch", [(i, i ^ bit) for i in range(size)])
            start = peak = 0
            for i, key in enumerate(todo):
                part = part_of(rows[i], count)
                received[key] = (arrived, start, peak, part)
                start, peak = start + rows[i], peak + rows[i] // part
        elif kind == "laps":
            lap, wide = laps(segments, toks, after(decay))
            last = wide
        elif kind == "sum":
            items = tuple((0, offsets[q], width // portions[q][1], ()) for q in inside)
            last = sums[half] = send(items, False, width, after(place), out_weight, turned, [])
        elif kind == "gate":
            stages = range(len(bits))
            arrays, places = collect([(q, i, 0) for q in inside for i in stages])
            pieces = tuple(
                (offsets[q] - half * half_rows, tuple(places[i * len(stages) : (i + 1) * len(stages)]))
                for i, q in enumerate(inside)
            )
            other = residue if half == 0 else packed[0]
            grad_query, scanned[half], states[half], packed[half] = gate(
                half,
                half_rows,
                segments,
                pieces,
                after(sums[half]),
                arrays,
                query_in,
                conv_out,
                decay,
                lap,
                other,
                grad_query,
            )
            last = packed[half]
        elif kind == "scan":
            groups = lax.axis_size("ctx")
            swap = lambda array, round_: lax.ppermute(array, "ctx", [(i, i ^ (1 << round_)) for i in range(groups)])
            arrived, joined = [swap(packed[1], 0)], packed[1]
            for round_ in range(1, groups.bit_length() - 1):
                joined = last = join(round_ - 1, after(group), joined, arrived[-1], wide)
                arrived.append(swap(joined, round_))
            scanned[1] = scan(1, segments, after(scanned[1]), states[1], decay, lap, residue)
        else:
            grad_input = fix(
                segments, group, [scanned[0], scanned[1]], states[0], arrived, decay, lap, wide, residue, toks, width
            )
    return grad_query, grad_input


def solution(mesh):
    placed = (
        P("ctx", "ch"),
        P(None, "ch"),
        P("ctx", "ch"),
        P("ctx", "ch"),
        P("ch", None),
        P("ch", None),
    )
    return jax.shard_map(
        local,
        mesh=mesh,
        in_specs=placed,
        out_specs=(P("ctx", "ch"), P("ctx", "ch")),
        check_vma=False,
    )
```

```python
import functools
import math

import jax
import jax.numpy as jnp
from jax import lax
from jax.experimental import pallas as pl
from jax.experimental.pallas import tpu as pltpu
from jax.sharding import PartitionSpec as P

PEAKS = 16
SPAN = 251 * math.log(2.0)
SHIFT = 125 * math.log(2.0)
STEP = 256
PIECE = 128
GAP = 8
VMEM = 24 * 1024 * 1024
QUICK = pl.CostEstimate(flops=0, bytes_accessed=1024, transcendentals=0)

PORTIONS = (((0, 1, 2), 2, 0), ((0, 1, 2), 2, 1))
ORDER = (
    ((0, 0, 6),), ((1, 0, 0),), ((0, 0, 4),), ((1, 0, 6),), ((1, 0, 2),), ((1, 0, 4),), ((0, 0, 2),), ((0, 1, 4),),
    ((1, 1, 4),), ((0, 2, 0),), ((0, 0, 0),), ((0, 1, 0),), ((1, 2, 0),), ((1, 1, 0),), ("laps", None), ("sum", 0),
    ("sum", 1), ("gate", 0), ("gate", 1), ("scan", 1), ("fix", None),
)
WAITS = {
    ((1, 1, 0),): ((0, 2, 0),),
    ("sum", 0): ((0, 1, 0), (0, 0, 0)),
    ((1, 2, 0),): ((1, 1, 4),),
    ("gate", 1): ((1, 2, 0),),
}


def folds_of(toks):
    return toks // 128 if toks % 128 == 0 and PEAKS % (toks // 128) == 0 else 1


def part_of(rows, blocks, folds):
    return next(
        part for part in range(16, rows + 1, 16) if rows % part == 0 and rows // part * blocks * folds <= PEAKS
    )


def step_of(rows):
    return next(step for step in (STEP, STEP // 2, rows) if rows % step == 0)


def encode(block, part):
    codes, peaks = [], []
    for i in range(block.shape[0] // part):
        piece = block[i * part : (i + 1) * part, :]
        size = jnp.abs(piece)
        peak = jnp.maximum(jnp.max(size, axis=0, keepdims=True) * 1.01, 1e-30)
        peak = peak.astype(jnp.bfloat16).astype(jnp.float32)
        code = jnp.exp(size * (SPAN / peak) - SHIFT)
        codes.append(jnp.where(piece < 0, -code, code))
        peaks.append(peak)
    return jnp.concatenate(codes, axis=0).astype(jnp.bfloat16), peaks


def put(codes, out_ref, at):
    lanes = out_ref.shape[1]
    folds = codes.shape[1] // lanes
    rows = (out_ref.shape[0] - PEAKS) // folds
    for fold in range(folds):
        out_ref[fold * rows + at : fold * rows + at + codes.shape[0], :] = codes[:, fold * lanes : (fold + 1) * lanes]


def put_peaks(peaks, out_ref):
    lanes = out_ref.shape[1]
    peaks = [peak[:, at : at + lanes] for peak in peaks for at in range(0, peak.shape[1], lanes)]
    if len(peaks) < PEAKS:
        peaks.append(jnp.zeros((PEAKS - len(peaks), lanes), jnp.float32))
    out_ref[out_ref.shape[0] - PEAKS :, :] = jnp.concatenate(peaks, axis=0).astype(jnp.bfloat16)


def decode(ref, place, first, count, folds):
    start, peak, part = place
    rows = (ref.shape[0] - PEAKS) // folds
    peaks = ref[ref.shape[0] - PEAKS :, :].astype(jnp.float32) * (1.0 / SPAN)
    columns = []
    for fold in range(folds):
        blocks = []
        for i in range(first // part, -(-(first + count) // part)):
            low, high = max(first, i * part), min(first + count, (i + 1) * part)
            code = ref[fold * rows + start + low : fold * rows + start + high, :].astype(jnp.float32)
            at = (peak + i) * folds + fold
            size = (jnp.log(jnp.abs(code)) + SHIFT) * peaks[at : at + 1, :]
            blocks.append(jnp.where(code < 0, -size, size))
        columns.append(jnp.concatenate(blocks, axis=0))
    return jnp.concatenate(columns, axis=1)


def pinned(array):
    return pltpu.with_memory_space_constraint(array, pltpu.HBM)


def send_kernel(items, coded, width, near, place_ref, w_ref, turned_ref, *refs):
    near_refs, out_ref = refs[:near], refs[near]
    folds = folds_of(turned_ref.shape[1])
    base, peaks = 0, []
    for block, offset, rows, sources in items:
        step = step_of(rows)
        first = (place_ref[0] ^ block) * width + offset
        for at in range(0, rows, step):
            total = jnp.dot(
                w_ref[pl.ds(pl.multiple_of(first + at, 16), step), :],
                turned_ref[...],
                preferred_element_type=jnp.float32,
            )
            for source, place in sources:
                total = total + decode(near_refs[source], place, at, step, folds)
            if coded:
                total, more = encode(total, part_of(rows, len(items), folds))
                peaks += more
                put(total, out_ref, base + at)
            else:
                out_ref[base + at : base + at + step, :] = total
        base += rows
    if coded:
        put_peaks(peaks, out_ref)


def send(items, coded, width, place, weight, turned, nears):
    toks = turned.shape[1]
    vmem = pl.BlockSpec(memory_space=pltpu.VMEM)
    count = sum(rows for _, _, rows, _ in items)
    folds = folds_of(toks)
    shape = (folds * count + PEAKS, toks // folds) if coded else (count, toks)
    return pl.pallas_call(
        functools.partial(send_kernel, items, coded, width, len(nears)),
        in_specs=[pl.BlockSpec(memory_space=pltpu.SMEM)] + [vmem] * (2 + len(nears)),
        out_specs=vmem,
        out_shape=jax.ShapeDtypeStruct(shape, jnp.bfloat16 if coded else jnp.float32),
        compiler_params=pltpu.CompilerParams(vmem_limit_bytes=VMEM),
        cost_estimate=QUICK,
    )(place, weight, turned, *nears)


def first_kernel(items, width, place_ref, w_hbm, g_hbm, out_ref, turned_ref, w_ref, g_ref, sems):
    copies, toks = [], g_ref.shape[0]
    piece = math.gcd(toks, PIECE)
    for at in range(0, toks, piece):
        lines = pl.ds(at, piece)
        copies.append(pltpu.make_async_copy(g_hbm.at[lines, :], g_ref.at[lines, :], sems.at[len(copies)]))
    base, grads = 0, len(copies)
    for block, offset, rows, _ in items:
        step = math.gcd(rows, PIECE)
        first = pl.multiple_of((place_ref[0] ^ block) * width + offset, 16)
        for at in range(0, rows, step):
            copies.append(
                pltpu.make_async_copy(
                    w_hbm.at[pl.ds(first + at, step), :], w_ref.at[pl.ds(base + at, step), :], sems.at[len(copies)]
                )
            )
        base += rows
    for copy in copies:
        copy.start()
    for i, at in enumerate(range(0, toks, piece)):
        copies[i].wait()
        turned_ref[:, at : at + piece] = g_ref[at : at + piece, :].T
    base, peaks, waits = 0, [], iter(copies[grads:])
    for _, _, rows, _ in items:
        step = step_of(rows)
        for at in range(base, base + rows, step):
            for _ in range(step // math.gcd(rows, PIECE)):
                next(waits).wait()
            total = jnp.dot(w_ref[at : at + step, :], turned_ref[...], preferred_element_type=jnp.float32)
            total, more = encode(total, part_of(rows, len(items), folds_of(toks)))
            peaks += more
            put(total, out_ref, at)
        base += rows
    put_peaks(peaks, out_ref)


def first_send(items, width, place, weight, grad):
    toks, depth = grad.shape
    vmem = pl.BlockSpec(memory_space=pltpu.VMEM)
    high = pl.BlockSpec(memory_space=pltpu.HBM)
    count = sum(rows for _, _, rows, _ in items)
    folds = folds_of(toks)
    steps = toks // math.gcd(toks, PIECE) + sum(rows // math.gcd(rows, PIECE) for _, _, rows, _ in items)
    return pl.pallas_call(
        functools.partial(first_kernel, items, width),
        in_specs=[pl.BlockSpec(memory_space=pltpu.SMEM), high, high],
        out_specs=(vmem, vmem),
        out_shape=(
            jax.ShapeDtypeStruct((folds * count + PEAKS, toks // folds), jnp.bfloat16),
            jax.ShapeDtypeStruct((depth, toks), jnp.bfloat16),
        ),
        scratch_shapes=[
            pltpu.VMEM((count, depth), jnp.bfloat16),
            pltpu.VMEM((toks, depth), jnp.bfloat16),
            pltpu.SemaphoreType.DMA((steps,)),
        ],
        compiler_params=pltpu.CompilerParams(vmem_limit_bytes=VMEM),
        cost_estimate=QUICK,
    )(place, pinned(weight), pinned(grad))


def steps_back(count, body, state, unroll):
    unroll = math.gcd(count, unroll)

    def some(i, state):
        for j in range(unroll):
            state = body(count - 1 - (i * unroll + j), state)
        return state

    return lax.fori_loop(0, count // unroll, some, state)


def power(base, exponent):
    result = None
    while exponent:
        if exponent % 2:
            result = base if result is None else result * base
        base = base * base
        exponent //= 2
    return result


def segment_of(shape, segments):
    return lax.rem(lax.broadcasted_iota(jnp.int32, shape, 0), segments)


def rolled(value, by):
    by %= value.shape[0]
    return pltpu.roll(value, by, 0) if by else value


def gate_kernel(half, rows, segments, pieces, near, acc_ref, *refs):
    near_refs, refs = refs[:near], refs[near:]
    query_ref, conv_ref, decay_ref, lap_ref, other_ref = refs[:5]
    out_hbm, rows_ref, state_ref, pack_ref = refs[-7:-3] if half == 0 else refs[-6:-2]
    gq_ref, sem = refs[-2:]
    gc_ref = refs[-3] if half == 0 else rows_ref
    toks = query_ref.shape[0]
    modes, sublanes, lanes = state_ref.shape
    mine = slice(half * sublanes, (half + 1) * sublanes)
    for line in range(rows // lanes):
        mix = acc_ref[line * lanes : (line + 1) * lanes, :]
        first, sources = next(piece for piece in reversed(pieces) if piece[0] <= line * lanes)
        for source, place in sources:
            mix = mix + decode(near_refs[source], place, line * lanes - first, lanes, folds_of(toks))
        mix = mix.T
        at = slice(line * lanes, (line + 1) * lanes)
        full = slice(half * rows + line * lanes, half * rows + (line + 1) * lanes)
        gq_ref[:, at] = (mix * conv_ref[:, full].astype(jnp.float32)).astype(jnp.bfloat16)
        gated = mix * query_ref[:, full].astype(jnp.float32)
        for k in range(segments):
            start = (line * segments + k) * (toks // segments + GAP)
            gc_ref[start : start + toks // segments, :] = gated[k * (toks // segments) : (k + 1) * (toks // segments), :]
    store = pltpu.make_async_copy(gq_ref, out_hbm.at[:, pl.ds(half * rows, rows)], sem)
    store.start()
    decay = [decay_ref[n, mine] for n in range(modes)]
    span = toks // segments

    def step(t, state):
        at = pl.ds(t, sublanes, stride=span + GAP)
        row = gc_ref[at, :]
        state = tuple(decay[n] * state[n] + row for n in range(modes))
        if half == 0:
            rows_ref[at, :] = summed([other_ref[n, mine] * state[n] for n in range(modes)])
        return state

    zero = jnp.zeros((sublanes, lanes), jnp.float32)
    state = steps_back(span, step, (zero,) * modes, 16)
    segment = segment_of((sublanes, lanes), segments)
    whole = []
    for n in range(modes):
        state_ref[n] = state[n]
        total = state[n]
        if segments > 1:
            factor = jnp.where(segment < segments - 1, lap_ref[n, mine], 0.0)
            for _ in range(segments - 1):
                total = state[n] + factor * rolled(total, -1)
        whole.append(total)
    packs = modes // segments
    for m in range(packs):
        packed = whole[m * segments]
        for j in range(1, segments):
            packed = jnp.where(segment == j, rolled(whole[m * segments + j], j), packed)
        if half == 0:
            pack_ref[m] = packed
        else:
            pack_ref[m] = other_ref[m]
            pack_ref[packs + m] = packed
    store.wait()


def gate(half, rows, segments, pieces, acc, nears, query_in, conv_out, decay, lap, other, partial):
    toks, width = query_in.shape
    modes, _, lanes = decay.shape
    sublanes = rows // lanes * segments
    vmem = pl.BlockSpec(memory_space=pltpu.VMEM)
    high = pl.BlockSpec(memory_space=pltpu.HBM)
    more = [] if partial is None else [partial]
    lines = (sublanes * (toks // segments + GAP), lanes)
    return pl.pallas_call(
        functools.partial(gate_kernel, half, rows, segments, pieces, len(nears)),
        in_specs=[vmem] * (6 + len(nears)) + [high] * len(more),
        out_specs=(high, vmem, vmem, vmem),
        out_shape=(
            jax.ShapeDtypeStruct((toks, width), jnp.bfloat16),
            jax.ShapeDtypeStruct(lines, jnp.float32),
            jax.ShapeDtypeStruct((modes, sublanes, lanes), jnp.float32),
            jax.ShapeDtypeStruct(((1 + half) * modes // segments, sublanes, lanes), jnp.float32),
        ),
        scratch_shapes=([pltpu.VMEM(lines, jnp.float32)] if half == 0 else [])
        + [pltpu.VMEM((toks, rows), jnp.bfloat16), pltpu.SemaphoreType.DMA],
        input_output_aliases={6 + len(nears): 0} if more else {},
        compiler_params=pltpu.CompilerParams(vmem_limit_bytes=VMEM),
        cost_estimate=QUICK,
    )(acc, *nears, query_in, conv_out, decay, lap, other, *more)


def summed(terms):
    while len(terms) > 1:
        terms = [terms[k] + terms[k + 1] if k + 1 < len(terms) else terms[k] for k in range(0, len(terms), 2)]
    return terms[0]


def scan_kernel(half, segments, gc_ref, state_ref, decay_ref, lap_ref, residue_ref, rows_ref):
    modes, sublanes, lanes = state_ref.shape
    mine = slice(half * sublanes, (half + 1) * sublanes)
    span = gc_ref.shape[0] // sublanes - GAP
    segment = segment_of((sublanes, lanes), segments)
    decay = [decay_ref[n, mine] for n in range(modes)]
    start = []
    for n in range(modes):
        total = jnp.zeros((sublanes, lanes), jnp.float32)
        if segments > 1:
            for k in range(segments - 2, -1, -1):
                total = jnp.where(segment == k, rolled(state_ref[n] + lap_ref[n, mine] * total, -1), total)
        start.append(total)

    def step(t, state):
        at = pl.ds(t, sublanes, stride=span + GAP)
        row = gc_ref[at, :]
        state = tuple(decay[n] * state[n] + row for n in range(modes))
        rows_ref[at, :] = summed([residue_ref[n, mine] * state[n] for n in range(modes)])
        return state

    steps_back(span, step, tuple(start), 16)


def scan(half, segments, grad_conv, state, decay, lap, residues):
    vmem = pl.BlockSpec(memory_space=pltpu.VMEM)
    return pl.pallas_call(
        functools.partial(scan_kernel, half, segments),
        in_specs=[vmem] * 5,
        out_specs=vmem,
        out_shape=jax.ShapeDtypeStruct(grad_conv.shape, jnp.float32),
        compiler_params=pltpu.CompilerParams(vmem_limit_bytes=VMEM),
        cost_estimate=QUICK,
    )(grad_conv, state, decay, lap, residues)


def laps_kernel(segments, span, decay_ref, lap_ref, wide_ref):
    modes, sublanes, lanes = decay_ref.shape
    sublanes //= 2
    packs = modes // segments
    segment = segment_of((sublanes, lanes), segments)
    for half in range(2):
        mine = slice(half * sublanes, (half + 1) * sublanes)
        for m in range(packs):
            packed = None
            for j in range(segments):
                lap = power(decay_ref[m * segments + j, mine], span)
                lap_ref[m * segments + j, mine] = lap
                wide = power(lap, segments)
                packed = wide if packed is None else jnp.where(segment == j, wide, packed)
            wide_ref[half * packs + m] = packed


def laps(segments, toks, decay):
    modes, sublanes, lanes = decay.shape
    vmem = pl.BlockSpec(memory_space=pltpu.VMEM)
    return pl.pallas_call(
        functools.partial(laps_kernel, segments, toks // segments),
        in_specs=[vmem],
        out_specs=(vmem, vmem),
        out_shape=(
            jax.ShapeDtypeStruct(decay.shape, jnp.float32),
            jax.ShapeDtypeStruct((2 * modes // segments, sublanes // 2, lanes), jnp.float32),
        ),
        compiler_params=pltpu.CompilerParams(vmem_limit_bytes=VMEM),
        cost_estimate=QUICK,
    )(decay)


def states_in(ref, shape):
    if ref.shape == shape:
        return [ref[m] for m in range(shape[0])]
    packs, sublanes, _ = shape
    rows = decode(ref, (0, 0, part_of(packs * sublanes, 1, 1)), 0, packs * sublanes, 1)
    return [rows[m * sublanes : (m + 1) * sublanes, :] for m in range(packs)]


def join_kernel(round_, group_ref, state_ref, arrived_ref, wide_ref, out_ref, coded_ref):
    earlier = (group_ref[0] >> round_) % 2 == 0
    packs, sublanes, _ = state_ref.shape
    joined = []
    for m, other in enumerate(states_in(arrived_ref, state_ref.shape)):
        wide = power(wide_ref[m], 1 << round_)
        mine = state_ref[m]
        joined.append(jnp.where(earlier, mine + wide * other, other + wide * mine))
        out_ref[m] = joined[-1]
    codes, peaks = encode(jnp.concatenate(joined, axis=0), part_of(packs * sublanes, 1, 1))
    put(codes, coded_ref, 0)
    put_peaks(peaks, coded_ref)


def join(round_, group, state, arrived, wide):
    vmem = pl.BlockSpec(memory_space=pltpu.VMEM)
    packs, sublanes, lanes = state.shape
    return pl.pallas_call(
        functools.partial(join_kernel, round_),
        in_specs=[pl.BlockSpec(memory_space=pltpu.SMEM)] + [vmem] * 3,
        out_specs=(vmem, vmem),
        out_shape=(
            jax.ShapeDtypeStruct(state.shape, jnp.float32),
            jax.ShapeDtypeStruct((packs * sublanes + PEAKS, lanes), jnp.bfloat16),
        ),
        compiler_params=pltpu.CompilerParams(vmem_limit_bytes=VMEM),
        cost_estimate=QUICK,
    )(group, state, arrived, wide)


def fix_kernel(segments, rounds, group_ref, *refs):
    scanned_refs, state_ref, arrived_refs = refs[:2], refs[2], refs[3 : 3 + rounds]
    decay_ref, lap_ref, wide_ref, residue_ref, out_hbm, rows_ref, out_ref, sems = refs[3 + rounds :]
    toks, width = out_ref.shape
    modes, sublanes, lanes = state_ref.shape
    packs = modes // segments
    rows = width // 2
    span = toks // segments
    segment = segment_of((sublanes, lanes), segments)
    earlier = [(group_ref[0] >> r) % 2 == 0 for r in range(rounds)]
    arrived = [states_in(ref, (2 * packs, sublanes, lanes)) for ref in arrived_refs]
    stores = []
    for half in range(2):
        mine = slice(half * sublanes, (half + 1) * sublanes)
        decay = [decay_ref[n, mine] for n in range(modes)]
        start = []
        for m in range(packs):
            brought = jnp.zeros((sublanes, lanes), jnp.float32)
            between = jnp.ones((sublanes, lanes), jnp.float32)
            for r in range(rounds):
                state = arrived[r][half * packs + m]
                brought = jnp.where(earlier[r], brought + between * state, brought)
                if r + 1 < rounds:
                    between = jnp.where(earlier[r], between * power(wide_ref[half * packs + m], 1 << r), between)
            for j in range(segments):
                n = m * segments + j
                total = rolled(brought, segments - 1 - j)
                for k in range(segments - 2, -1, -1):
                    before = lap_ref[n, mine] * total
                    if half == 0:
                        before = before + state_ref[n]
                    total = jnp.where(segment == k, rolled(before, -1), total)
                start.append(residue_ref[n, mine] * total)

        def step(t, state, scanned_ref=scanned_refs[half], decay=decay):
            at = pl.ds(t, sublanes, stride=span + GAP)
            state = tuple(decay[n] * state[n] for n in range(modes))
            rows_ref[at, :] = scanned_ref[at, :] + summed(list(state))
            return state

        steps_back(span, step, tuple(start), 16)
        for line in range(rows // lanes):
            at = slice(half * rows + line * lanes, half * rows + (line + 1) * lanes)
            for k in range(segments):
                start = (line * segments + k) * (span + GAP)
                out_ref[k * span : (k + 1) * span, at] = rows_ref[start : start + span, :].astype(jnp.bfloat16)
        columns = pl.ds(half * rows, rows)
        stores.append(pltpu.make_async_copy(out_ref.at[:, columns], out_hbm.at[:, columns], sems.at[half]))
        stores[-1].start()
    for store in stores:
        store.wait()


def fix(segments, group, scanned, state, arrived, decay, lap, wide, residues, toks, width):
    vmem = pl.BlockSpec(memory_space=pltpu.VMEM)
    return pl.pallas_call(
        functools.partial(fix_kernel, segments, len(arrived)),
        in_specs=[pl.BlockSpec(memory_space=pltpu.SMEM)] + [vmem] * (7 + len(arrived)),
        out_specs=pl.BlockSpec(memory_space=pltpu.HBM),
        out_shape=jax.ShapeDtypeStruct((toks, width), jnp.bfloat16),
        scratch_shapes=[
            pltpu.VMEM(scanned[0].shape, jnp.float32),
            pltpu.VMEM((toks, width), jnp.bfloat16),
            pltpu.SemaphoreType.DMA((2,)),
        ],
        compiler_params=pltpu.CompilerParams(vmem_limit_bytes=VMEM),
        cost_estimate=QUICK,
    )(group, *scanned, state, *arrived, decay, lap, wide, residues)


def local(out_grad, out_weight, query_in, conv_out, residues, decay_rates):
    toks, width = query_in.shape
    modes = decay_rates.shape[1]
    lanes = math.gcd(width, 128)
    size, groups = lax.axis_size("ch"), lax.axis_size("ctx")
    bits = [1 << i for i in range(size.bit_length() - 1)]
    place = jnp.reshape(lax.axis_index("ch"), (1,)).astype(jnp.int32)
    group = jnp.reshape(lax.axis_index("ctx"), (1,)).astype(jnp.int32)
    half_rows = width // 2
    lines = half_rows // lanes
    segments = 8 // lines
    by_mode = lambda values: jnp.repeat(values.T.reshape(modes, width // lanes, lanes), segments, axis=1)
    decay, residue = by_mode(decay_rates), by_mode(residues)

    portions, order, waits = PORTIONS, ORDER, WAITS
    if size != 8:
        waits = {}
        portions = ((tuple(range(len(bits))), 2, 0), (tuple(range(len(bits))), 2, 1))
        order = [
            ((p, s, block),)
            for p in range(2)
            for s, bit in enumerate(bits)
            for block in sorted(range(0, size, 2 * bit), reverse=True)
        ] + [("laps", None), ("sum", 0), ("sum", 1), ("gate", 0), ("gate", 1), ("scan", 1), ("fix", None)]
    offsets = [sum(width // part for _, part, _ in portions[:p]) for p in range(len(portions))]

    received, sums, scanned, states, packed = {}, {}, {}, {}, {}
    grad_query = last = None

    def after(value):
        return value if last is None else lax.optimization_barrier((value, last, *awaited))[0]

    def collect(wanted):
        arrays, places = [], []
        for key in wanted:
            array, *place = received[key]
            index = next((i for i, known in enumerate(arrays) if known is array), len(arrays))
            if index == len(arrays):
                arrays.append(array)
            places.append((index, tuple(place)))
        return arrays, places

    for todo in order:
        awaited = [received[key][0] for key in waits.get(todo, ())]
        kind, half = todo if isinstance(todo[0], str) else ("send", None)
        inside = [q for q, (_, _, lies) in enumerate(portions) if lies == half]
        if kind == "send":
            arrays, items = [], []
            wanted, rows, bits_of = [], [], []
            for p, s, block in todo:
                route, share, _ = portions[p]
                bits_of.append(bits[route[s]])
                rows.append(width // share)
                wanted.append([(p, i, block ^ bits_of[-1]) for i in range(s)])
            bit, count = bits_of[0], len(todo)
            arrays, places = collect([key for keys in wanted for key in keys])
            places = iter(places)
            items = tuple(
                (block ^ bit, offsets[p], rows[i], tuple(next(places) for _ in wanted[i]))
                for i, (p, _, block) in enumerate(todo)
            )
            if last is None:
                last, turned = first_send(items, width, place, out_weight, out_grad)
            else:
                last = send(items, True, width, after(place), out_weight, turned, arrays)
            arrived = lax.ppermute(last, "ch", [(i, i ^ bit) for i in range(size)])
            start = peak = 0
            for i, key in enumerate(todo):
                part = part_of(rows[i], count, folds_of(toks))
                received[key] = (arrived, start, peak, part)
                start, peak = start + rows[i], peak + rows[i] // part
        elif kind == "laps":
            lap, wide = laps(segments, toks, after(decay))
            last = wide
        elif kind == "sum":
            items = tuple((0, offsets[q], width // portions[q][1], ()) for q in inside)
            last = sums[half] = send(items, False, width, after(place), out_weight, turned, [])
        elif kind == "gate":
            stages = range(len(bits))
            arrays, places = collect([(q, i, 0) for q in inside for i in stages])
            pieces = tuple(
                (offsets[q] - half * half_rows, tuple(places[i * len(stages) : (i + 1) * len(stages)]))
                for i, q in enumerate(inside)
            )
            other = residue if half == 0 else packed[0]
            grad_query, scanned[half], states[half], packed[half] = gate(
                half,
                half_rows,
                segments,
                pieces,
                after(sums[half]),
                arrays,
                query_in,
                conv_out,
                decay,
                lap,
                other,
                grad_query,
            )
            last = packed[half]
        elif kind == "scan":
            groups = lax.axis_size("ctx")
            swap = lambda array, round_: lax.ppermute(array, "ctx", [(i, i ^ (1 << round_)) for i in range(groups)])
            arrived, joined = [swap(packed[1], 0)], packed[1]
            for round_ in range(1, groups.bit_length() - 1):
                joined, last = join(round_ - 1, after(group), joined, arrived[-1], wide)
                arrived.append(swap(last, round_))
            scanned[1] = scan(1, segments, after(scanned[1]), states[1], decay, lap, residue)
        else:
            grad_input = fix(
                segments, group, [scanned[0], scanned[1]], states[0], arrived, decay, lap, wide, residue, toks, width
            )
    return grad_query, grad_input


def solution(mesh):
    placed = (
        P("ctx", "ch"),
        P(None, "ch"),
        P("ctx", "ch"),
        P("ctx", "ch"),
        P("ch", None),
        P("ch", None),
    )
    return jax.shard_map(
        local,
        mesh=mesh,
        in_specs=placed,
        out_specs=(P("ctx", "ch"), P("ctx", "ch")),
        check_vma=False,
    )
```

```python
import functools
import math

import jax
import jax.numpy as jnp
from jax import lax
from jax.experimental import pallas as pl
from jax.experimental.pallas import tpu as pltpu
from jax.sharding import PartitionSpec as P

PEAKS = 16
SPAN = 251 * math.log(2.0)
SHIFT = 125 * math.log(2.0)
STEP = 256
PIECE = 128
GAP = 8
VMEM = 24 * 1024 * 1024
QUICK = pl.CostEstimate(flops=0, bytes_accessed=1024, transcendentals=0)

PORTIONS = (((0, 1, 2), 4, 0), ((1, 0, 2), 4, 0), ((0, 1, 2), 4, 1), ((0, 1, 2), 4, 1))
ORDER = (
    ((0, 0, 6), (0, 0, 2)), ((1, 0, 5), (1, 0, 1)), ((2, 0, 2), (3, 0, 2)), ("sum", 1), ((2, 0, 6), (3, 0, 6)),
    ((2, 0, 4), (3, 0, 4)), ((1, 0, 4), (0, 1, 4)), ((1, 1, 4), (0, 0, 4)), ((2, 1, 4), (3, 1, 4)),
    ((1, 0, 0), (0, 1, 0)), ((0, 2, 0), (1, 2, 0)), ((2, 2, 0), (3, 2, 0)), ((1, 1, 0), (0, 0, 0)),
    ((2, 1, 0), (3, 1, 0)), ((2, 0, 0), (3, 0, 0)), ("laps", None), ("sum", 0), ("gate", 0), ("gate", 1), ("scan", 1),
    ("fix", None),
)
WAITS = {
    ((1, 0, 0), (0, 1, 0)): ((1, 0, 4),),
    ((2, 0, 0), (3, 0, 0)): ((0, 2, 0), (1, 0, 0)),
    ("gate", 1): ((2, 2, 0), (2, 1, 0)),
}


def folds_of(toks):
    return toks // 128 if toks % 128 == 0 and PEAKS % (toks // 128) == 0 else 1


def part_of(rows, blocks, folds):
    return next(
        part for part in range(16, rows + 1, 16) if rows % part == 0 and rows // part * blocks * folds <= PEAKS
    )


def step_of(rows):
    return next(step for step in (STEP, STEP // 2, rows) if rows % step == 0)


def encode(block, part):
    codes, peaks = [], []
    for i in range(block.shape[0] // part):
        piece = block[i * part : (i + 1) * part, :]
        size = jnp.abs(piece)
        peak = jnp.maximum(jnp.max(size, axis=0, keepdims=True) * 1.01, 1e-30)
        peak = peak.astype(jnp.bfloat16).astype(jnp.float32)
        code = jnp.exp(size * (SPAN / peak) - SHIFT)
        codes.append(jnp.where(piece < 0, -code, code))
        peaks.append(peak)
    return jnp.concatenate(codes, axis=0).astype(jnp.bfloat16), peaks


def put(codes, out_ref, at):
    lanes = out_ref.shape[1]
    folds = codes.shape[1] // lanes
    rows = (out_ref.shape[0] - PEAKS) // folds
    for fold in range(folds):
        out_ref[fold * rows + at : fold * rows + at + codes.shape[0], :] = codes[:, fold * lanes : (fold + 1) * lanes]


def put_peaks(peaks, out_ref):
    lanes = out_ref.shape[1]
    peaks = [peak[:, at : at + lanes] for peak in peaks for at in range(0, peak.shape[1], lanes)]
    if len(peaks) < PEAKS:
        peaks.append(jnp.zeros((PEAKS - len(peaks), lanes), jnp.float32))
    out_ref[out_ref.shape[0] - PEAKS :, :] = jnp.concatenate(peaks, axis=0).astype(jnp.bfloat16)


def decode(ref, place, first, count, folds):
    start, peak, part = place
    rows = (ref.shape[0] - PEAKS) // folds
    peaks = ref[ref.shape[0] - PEAKS :, :].astype(jnp.float32) * (1.0 / SPAN)
    columns = []
    for fold in range(folds):
        blocks = []
        for i in range(first // part, -(-(first + count) // part)):
            low, high = max(first, i * part), min(first + count, (i + 1) * part)
            code = ref[fold * rows + start + low : fold * rows + start + high, :].astype(jnp.float32)
            at = (peak + i) * folds + fold
            size = (jnp.log(jnp.abs(code)) + SHIFT) * peaks[at : at + 1, :]
            blocks.append(jnp.where(code < 0, -size, size))
        columns.append(jnp.concatenate(blocks, axis=0))
    return jnp.concatenate(columns, axis=1)


def pinned(array):
    return pltpu.with_memory_space_constraint(array, pltpu.HBM)


def send_kernel(items, coded, width, near, place_ref, w_ref, turned_ref, *refs):
    near_refs, out_ref = refs[:near], refs[near]
    folds = folds_of(turned_ref.shape[1])
    base, peaks = 0, []
    for block, offset, rows, sources in items:
        step = step_of(rows)
        first = (place_ref[0] ^ block) * width + offset
        for at in range(0, rows, step):
            total = jnp.dot(
                w_ref[pl.ds(pl.multiple_of(first + at, 16), step), :],
                turned_ref[...],
                preferred_element_type=jnp.float32,
            )
            for source, place in sources:
                total = total + decode(near_refs[source], place, at, step, folds)
            if coded:
                total, more = encode(total, part_of(rows, len(items), folds))
                peaks += more
                put(total, out_ref, base + at)
            else:
                out_ref[base + at : base + at + step, :] = total
        base += rows
    if coded:
        put_peaks(peaks, out_ref)


def send(items, coded, width, place, weight, turned, nears):
    toks = turned.shape[1]
    vmem = pl.BlockSpec(memory_space=pltpu.VMEM)
    count = sum(rows for _, _, rows, _ in items)
    folds = folds_of(toks)
    shape = (folds * count + PEAKS, toks // folds) if coded else (count, toks)
    return pl.pallas_call(
        functools.partial(send_kernel, items, coded, width, len(nears)),
        in_specs=[pl.BlockSpec(memory_space=pltpu.SMEM)] + [vmem] * (2 + len(nears)),
        out_specs=vmem,
        out_shape=jax.ShapeDtypeStruct(shape, jnp.bfloat16 if coded else jnp.float32),
        compiler_params=pltpu.CompilerParams(vmem_limit_bytes=VMEM),
        cost_estimate=QUICK,
    )(place, weight, turned, *nears)


def first_kernel(items, width, place_ref, w_hbm, g_hbm, out_ref, turned_ref, w_ref, g_ref, sems):
    copies, toks = [], g_ref.shape[0]
    piece = math.gcd(toks, PIECE)
    for at in range(0, toks, piece):
        lines = pl.ds(at, piece)
        copies.append(pltpu.make_async_copy(g_hbm.at[lines, :], g_ref.at[lines, :], sems.at[len(copies)]))
    base, grads = 0, len(copies)
    for block, offset, rows, _ in items:
        step = math.gcd(rows, PIECE)
        first = pl.multiple_of((place_ref[0] ^ block) * width + offset, 16)
        for at in range(0, rows, step):
            copies.append(
                pltpu.make_async_copy(
                    w_hbm.at[pl.ds(first + at, step), :], w_ref.at[pl.ds(base + at, step), :], sems.at[len(copies)]
                )
            )
        base += rows
    for copy in copies:
        copy.start()
    for i, at in enumerate(range(0, toks, piece)):
        copies[i].wait()
        turned_ref[:, at : at + piece] = g_ref[at : at + piece, :].T
    base, peaks, waits = 0, [], iter(copies[grads:])
    for _, _, rows, _ in items:
        step = step_of(rows)
        for at in range(base, base + rows, step):
            for _ in range(step // math.gcd(rows, PIECE)):
                next(waits).wait()
            total = jnp.dot(w_ref[at : at + step, :], turned_ref[...], preferred_element_type=jnp.float32)
            total, more = encode(total, part_of(rows, len(items), folds_of(toks)))
            peaks += more
            put(total, out_ref, at)
        base += rows
    put_peaks(peaks, out_ref)


def first_send(items, width, place, weight, grad):
    toks, depth = grad.shape
    vmem = pl.BlockSpec(memory_space=pltpu.VMEM)
    high = pl.BlockSpec(memory_space=pltpu.HBM)
    count = sum(rows for _, _, rows, _ in items)
    folds = folds_of(toks)
    steps = toks // math.gcd(toks, PIECE) + sum(rows // math.gcd(rows, PIECE) for _, _, rows, _ in items)
    return pl.pallas_call(
        functools.partial(first_kernel, items, width),
        in_specs=[pl.BlockSpec(memory_space=pltpu.SMEM), high, high],
        out_specs=(vmem, vmem),
        out_shape=(
            jax.ShapeDtypeStruct((folds * count + PEAKS, toks // folds), jnp.bfloat16),
            jax.ShapeDtypeStruct((depth, toks), jnp.bfloat16),
        ),
        scratch_shapes=[
            pltpu.VMEM((count, depth), jnp.bfloat16),
            pltpu.VMEM((toks, depth), jnp.bfloat16),
            pltpu.SemaphoreType.DMA((steps,)),
        ],
        compiler_params=pltpu.CompilerParams(vmem_limit_bytes=VMEM),
        cost_estimate=QUICK,
    )(place, pinned(weight), pinned(grad))


def steps_back(count, body, state, unroll):
    unroll = math.gcd(count, unroll)

    def some(i, state):
        for j in range(unroll):
            state = body(count - 1 - (i * unroll + j), state)
        return state

    return lax.fori_loop(0, count // unroll, some, state)


def power(base, exponent):
    result = None
    while exponent:
        if exponent % 2:
            result = base if result is None else result * base
        base = base * base
        exponent //= 2
    return result


def segment_of(shape, segments):
    return lax.rem(lax.broadcasted_iota(jnp.int32, shape, 0), segments)


def rolled(value, by):
    by %= value.shape[0]
    return pltpu.roll(value, by, 0) if by else value


def gate_kernel(half, rows, segments, pieces, near, acc_ref, *refs):
    near_refs, refs = refs[:near], refs[near:]
    query_ref, conv_ref, decay_ref, lap_ref, other_ref = refs[:5]
    out_hbm, rows_ref, state_ref, pack_ref = refs[-7:-3] if half == 0 else refs[-6:-2]
    gq_ref, sem = refs[-2:]
    gc_ref = refs[-3] if half == 0 else rows_ref
    toks = query_ref.shape[0]
    modes, sublanes, lanes = state_ref.shape
    mine = slice(half * sublanes, (half + 1) * sublanes)
    for line in range(rows // lanes):
        mix = acc_ref[line * lanes : (line + 1) * lanes, :]
        first, sources = next(piece for piece in reversed(pieces) if piece[0] <= line * lanes)
        for source, place in sources:
            mix = mix + decode(near_refs[source], place, line * lanes - first, lanes, folds_of(toks))
        mix = mix.T
        at = slice(line * lanes, (line + 1) * lanes)
        full = slice(half * rows + line * lanes, half * rows + (line + 1) * lanes)
        gq_ref[:, at] = (mix * conv_ref[:, full].astype(jnp.float32)).astype(jnp.bfloat16)
        gated = mix * query_ref[:, full].astype(jnp.float32)
        for k in range(segments):
            start = (line * segments + k) * (toks // segments + GAP)
            gc_ref[start : start + toks // segments, :] = gated[k * (toks // segments) : (k + 1) * (toks // segments), :]
    store = pltpu.make_async_copy(gq_ref, out_hbm.at[:, pl.ds(half * rows, rows)], sem)
    store.start()
    decay = [decay_ref[n, mine] for n in range(modes)]
    span = toks // segments

    def step(t, state):
        at = pl.ds(t, sublanes, stride=span + GAP)
        row = gc_ref[at, :]
        state = tuple(decay[n] * state[n] + row for n in range(modes))
        if half == 0:
            rows_ref[at, :] = summed([other_ref[n, mine] * state[n] for n in range(modes)])
        return state

    zero = jnp.zeros((sublanes, lanes), jnp.float32)
    state = steps_back(span, step, (zero,) * modes, 16)
    segment = segment_of((sublanes, lanes), segments)
    whole = []
    for n in range(modes):
        state_ref[n] = state[n]
        total = state[n]
        if segments > 1:
            factor = jnp.where(segment < segments - 1, lap_ref[n, mine], 0.0)
            for _ in range(segments - 1):
                total = state[n] + factor * rolled(total, -1)
        whole.append(total)
    packs = modes // segments
    for m in range(packs):
        packed = whole[m * segments]
        for j in range(1, segments):
            packed = jnp.where(segment == j, rolled(whole[m * segments + j], j), packed)
        if half == 0:
            pack_ref[m] = packed
        else:
            pack_ref[m] = other_ref[m]
            pack_ref[packs + m] = packed
    store.wait()


def gate(half, rows, segments, pieces, acc, nears, query_in, conv_out, decay, lap, other, partial):
    toks, width = query_in.shape
    modes, _, lanes = decay.shape
    sublanes = rows // lanes * segments
    vmem = pl.BlockSpec(memory_space=pltpu.VMEM)
    high = pl.BlockSpec(memory_space=pltpu.HBM)
    more = [] if partial is None else [partial]
    lines = (sublanes * (toks // segments + GAP), lanes)
    return pl.pallas_call(
        functools.partial(gate_kernel, half, rows, segments, pieces, len(nears)),
        in_specs=[vmem] * (6 + len(nears)) + [high] * len(more),
        out_specs=(high, vmem, vmem, vmem),
        out_shape=(
            jax.ShapeDtypeStruct((toks, width), jnp.bfloat16),
            jax.ShapeDtypeStruct(lines, jnp.float32),
            jax.ShapeDtypeStruct((modes, sublanes, lanes), jnp.float32),
            jax.ShapeDtypeStruct(((1 + half) * modes // segments, sublanes, lanes), jnp.float32),
        ),
        scratch_shapes=([pltpu.VMEM(lines, jnp.float32)] if half == 0 else [])
        + [pltpu.VMEM((toks, rows), jnp.bfloat16), pltpu.SemaphoreType.DMA],
        input_output_aliases={6 + len(nears): 0} if more else {},
        compiler_params=pltpu.CompilerParams(vmem_limit_bytes=VMEM),
        cost_estimate=QUICK,
    )(acc, *nears, query_in, conv_out, decay, lap, other, *more)


def summed(terms):
    while len(terms) > 1:
        terms = [terms[k] + terms[k + 1] if k + 1 < len(terms) else terms[k] for k in range(0, len(terms), 2)]
    return terms[0]


def scan_kernel(half, segments, gc_ref, state_ref, decay_ref, lap_ref, residue_ref, rows_ref):
    modes, sublanes, lanes = state_ref.shape
    mine = slice(half * sublanes, (half + 1) * sublanes)
    span = gc_ref.shape[0] // sublanes - GAP
    segment = segment_of((sublanes, lanes), segments)
    decay = [decay_ref[n, mine] for n in range(modes)]
    start = []
    for n in range(modes):
        total = jnp.zeros((sublanes, lanes), jnp.float32)
        if segments > 1:
            for k in range(segments - 2, -1, -1):
                total = jnp.where(segment == k, rolled(state_ref[n] + lap_ref[n, mine] * total, -1), total)
        start.append(total)

    def step(t, state):
        at = pl.ds(t, sublanes, stride=span + GAP)
        row = gc_ref[at, :]
        state = tuple(decay[n] * state[n] + row for n in range(modes))
        rows_ref[at, :] = summed([residue_ref[n, mine] * state[n] for n in range(modes)])
        return state

    steps_back(span, step, tuple(start), 16)


def scan(half, segments, grad_conv, state, decay, lap, residues):
    vmem = pl.BlockSpec(memory_space=pltpu.VMEM)
    return pl.pallas_call(
        functools.partial(scan_kernel, half, segments),
        in_specs=[vmem] * 5,
        out_specs=vmem,
        out_shape=jax.ShapeDtypeStruct(grad_conv.shape, jnp.float32),
        compiler_params=pltpu.CompilerParams(vmem_limit_bytes=VMEM),
        cost_estimate=QUICK,
    )(grad_conv, state, decay, lap, residues)


def laps_kernel(segments, span, decay_ref, lap_ref, wide_ref):
    modes, sublanes, lanes = decay_ref.shape
    sublanes //= 2
    packs = modes // segments
    segment = segment_of((sublanes, lanes), segments)
    for half in range(2):
        mine = slice(half * sublanes, (half + 1) * sublanes)
        for m in range(packs):
            packed = None
            for j in range(segments):
                lap = power(decay_ref[m * segments + j, mine], span)
                lap_ref[m * segments + j, mine] = lap
                wide = power(lap, segments)
                packed = wide if packed is None else jnp.where(segment == j, wide, packed)
            wide_ref[half * packs + m] = packed


def laps(segments, toks, decay):
    modes, sublanes, lanes = decay.shape
    vmem = pl.BlockSpec(memory_space=pltpu.VMEM)
    return pl.pallas_call(
        functools.partial(laps_kernel, segments, toks // segments),
        in_specs=[vmem],
        out_specs=(vmem, vmem),
        out_shape=(
            jax.ShapeDtypeStruct(decay.shape, jnp.float32),
            jax.ShapeDtypeStruct((2 * modes // segments, sublanes // 2, lanes), jnp.float32),
        ),
        compiler_params=pltpu.CompilerParams(vmem_limit_bytes=VMEM),
        cost_estimate=QUICK,
    )(decay)


def states_in(ref, shape):
    if ref.shape == shape:
        return [ref[m] for m in range(shape[0])]
    packs, sublanes, _ = shape
    rows = decode(ref, (0, 0, packs * sublanes // 2), 0, packs * sublanes, 1)
    return [rows[m * sublanes : (m + 1) * sublanes, :] for m in range(packs)]


def join_kernel(round_, group_ref, state_ref, arrived_ref, wide_ref, out_ref, coded_ref):
    earlier = (group_ref[0] >> round_) % 2 == 0
    packs, sublanes, _ = state_ref.shape
    joined = []
    for m, other in enumerate(states_in(arrived_ref, state_ref.shape)):
        wide = power(wide_ref[m], 1 << round_)
        mine = state_ref[m]
        joined.append(jnp.where(earlier, mine + wide * other, other + wide * mine))
        out_ref[m] = joined[-1]
    codes, peaks = encode(jnp.concatenate(joined, axis=0), packs * sublanes // 2)
    put(codes, coded_ref, 0)
    put_peaks(peaks, coded_ref)


def join(round_, group, state, arrived, wide):
    vmem = pl.BlockSpec(memory_space=pltpu.VMEM)
    packs, sublanes, lanes = state.shape
    return pl.pallas_call(
        functools.partial(join_kernel, round_),
        in_specs=[pl.BlockSpec(memory_space=pltpu.SMEM)] + [vmem] * 3,
        out_specs=(vmem, vmem),
        out_shape=(
            jax.ShapeDtypeStruct(state.shape, jnp.float32),
            jax.ShapeDtypeStruct((packs * sublanes + PEAKS, lanes), jnp.bfloat16),
        ),
        compiler_params=pltpu.CompilerParams(vmem_limit_bytes=VMEM),
        cost_estimate=QUICK,
    )(group, state, arrived, wide)


def fix_kernel(segments, rounds, group_ref, *refs):
    scanned_refs, state_ref, arrived_refs = refs[:2], refs[2], refs[3 : 3 + rounds]
    decay_ref, lap_ref, wide_ref, residue_ref, out_hbm, rows_ref, out_ref, sems = refs[3 + rounds :]
    toks, width = out_ref.shape
    modes, sublanes, lanes = state_ref.shape
    packs = modes // segments
    rows = width // 2
    span = toks // segments
    segment = segment_of((sublanes, lanes), segments)
    earlier = [(group_ref[0] >> r) % 2 == 0 for r in range(rounds)]
    arrived = [states_in(ref, (2 * packs, sublanes, lanes)) for ref in arrived_refs]
    stores = []
    for half in range(2):
        mine = slice(half * sublanes, (half + 1) * sublanes)
        decay = [decay_ref[n, mine] for n in range(modes)]
        start = []
        for m in range(packs):
            brought = jnp.zeros((sublanes, lanes), jnp.float32)
            between = jnp.ones((sublanes, lanes), jnp.float32)
            for r in range(rounds):
                state = arrived[r][half * packs + m]
                brought = jnp.where(earlier[r], brought + between * state, brought)
                if r + 1 < rounds:
                    between = jnp.where(earlier[r], between * power(wide_ref[half * packs + m], 1 << r), between)
            for j in range(segments):
                n = m * segments + j
                total = rolled(brought, segments - 1 - j)
                for k in range(segments - 2, -1, -1):
                    before = lap_ref[n, mine] * total
                    if half == 0:
                        before = before + state_ref[n]
                    total = jnp.where(segment == k, rolled(before, -1), total)
                start.append(residue_ref[n, mine] * total)

        def step(t, state, scanned_ref=scanned_refs[half], decay=decay):
            at = pl.ds(t, sublanes, stride=span + GAP)
            state = tuple(decay[n] * state[n] for n in range(modes))
            rows_ref[at, :] = scanned_ref[at, :] + summed(list(state))
            return state

        steps_back(span, step, tuple(start), 16)
        for line in range(rows // lanes):
            at = slice(half * rows + line * lanes, half * rows + (line + 1) * lanes)
            for k in range(segments):
                start = (line * segments + k) * (span + GAP)
                out_ref[k * span : (k + 1) * span, at] = rows_ref[start : start + span, :].astype(jnp.bfloat16)
        columns = pl.ds(half * rows, rows)
        stores.append(pltpu.make_async_copy(out_ref.at[:, columns], out_hbm.at[:, columns], sems.at[half]))
        stores[-1].start()
    for store in stores:
        store.wait()


def fix(segments, group, scanned, state, arrived, decay, lap, wide, residues, toks, width):
    vmem = pl.BlockSpec(memory_space=pltpu.VMEM)
    return pl.pallas_call(
        functools.partial(fix_kernel, segments, len(arrived)),
        in_specs=[pl.BlockSpec(memory_space=pltpu.SMEM)] + [vmem] * (7 + len(arrived)),
        out_specs=pl.BlockSpec(memory_space=pltpu.HBM),
        out_shape=jax.ShapeDtypeStruct((toks, width), jnp.bfloat16),
        scratch_shapes=[
            pltpu.VMEM(scanned[0].shape, jnp.float32),
            pltpu.VMEM((toks, width), jnp.bfloat16),
            pltpu.SemaphoreType.DMA((2,)),
        ],
        compiler_params=pltpu.CompilerParams(vmem_limit_bytes=VMEM),
        cost_estimate=QUICK,
    )(group, *scanned, state, *arrived, decay, lap, wide, residues)


def local(out_grad, out_weight, query_in, conv_out, residues, decay_rates):
    toks, width = query_in.shape
    modes = decay_rates.shape[1]
    lanes = math.gcd(width, 128)
    size, groups = lax.axis_size("ch"), lax.axis_size("ctx")
    bits = [1 << i for i in range(size.bit_length() - 1)]
    place = jnp.reshape(lax.axis_index("ch"), (1,)).astype(jnp.int32)
    group = jnp.reshape(lax.axis_index("ctx"), (1,)).astype(jnp.int32)
    half_rows = width // 2
    lines = half_rows // lanes
    segments = 8 // lines
    by_mode = lambda values: jnp.repeat(values.T.reshape(modes, width // lanes, lanes), segments, axis=1)
    decay, residue = by_mode(decay_rates), by_mode(residues)

    portions, order, waits = PORTIONS, ORDER, WAITS
    if size != 8:
        waits = {}
        portions = ((tuple(range(len(bits))), 2, 0), (tuple(range(len(bits))), 2, 1))
        order = [
            ((p, s, block),)
            for p in range(2)
            for s, bit in enumerate(bits)
            for block in sorted(range(0, size, 2 * bit), reverse=True)
        ] + [("laps", None), ("sum", 0), ("sum", 1), ("gate", 0), ("gate", 1), ("scan", 1), ("fix", None)]
    offsets = [sum(width // part for _, part, _ in portions[:p]) for p in range(len(portions))]

    received, sums, scanned, states, packed = {}, {}, {}, {}, {}
    grad_query = last = None

    def after(value):
        return value if last is None else lax.optimization_barrier((value, last, *awaited))[0]

    def collect(wanted):
        arrays, places = [], []
        for key in wanted:
            array, *place = received[key]
            index = next((i for i, known in enumerate(arrays) if known is array), len(arrays))
            if index == len(arrays):
                arrays.append(array)
            places.append((index, tuple(place)))
        return arrays, places

    for todo in order:
        awaited = [received[key][0] for key in waits.get(todo, ())]
        kind, half = todo if isinstance(todo[0], str) else ("send", None)
        inside = [q for q, (_, _, lies) in enumerate(portions) if lies == half]
        if kind == "send":
            arrays, items = [], []
            wanted, rows, bits_of = [], [], []
            for p, s, block in todo:
                route, share, _ = portions[p]
                bits_of.append(bits[route[s]])
                rows.append(width // share)
                wanted.append([(p, i, block ^ bits_of[-1]) for i in range(s)])
            bit, count = bits_of[0], len(todo)
            arrays, places = collect([key for keys in wanted for key in keys])
            places = iter(places)
            items = tuple(
                (block ^ bit, offsets[p], rows[i], tuple(next(places) for _ in wanted[i]))
                for i, (p, _, block) in enumerate(todo)
            )
            if last is None:
                last, turned = first_send(items, width, place, out_weight, out_grad)
            else:
                last = send(items, True, width, after(place), out_weight, turned, arrays)
            arrived = lax.ppermute(last, "ch", [(i, i ^ bit) for i in range(size)])
            start = peak = 0
            for i, key in enumerate(todo):
                part = part_of(rows[i], count, folds_of(toks))
                received[key] = (arrived, start, peak, part)
                start, peak = start + rows[i], peak + rows[i] // part
        elif kind == "laps":
            lap, wide = laps(segments, toks, after(decay))
            last = wide
        elif kind == "sum":
            items = tuple((0, offsets[q], width // portions[q][1], ()) for q in inside)
            last = sums[half] = send(items, False, width, after(place), out_weight, turned, [])
        elif kind == "gate":
            stages = range(len(bits))
            arrays, places = collect([(q, i, 0) for q in inside for i in stages])
            pieces = tuple(
                (offsets[q] - half * half_rows, tuple(places[i * len(stages) : (i + 1) * len(stages)]))
                for i, q in enumerate(inside)
            )
            other = residue if half == 0 else packed[0]
            grad_query, scanned[half], states[half], packed[half] = gate(
                half,
                half_rows,
                segments,
                pieces,
                after(sums[half]),
                arrays,
                query_in,
                conv_out,
                decay,
                lap,
                other,
                grad_query,
            )
            last = packed[half]
        elif kind == "scan":
            groups = lax.axis_size("ctx")
            swap = lambda array, round_: lax.ppermute(array, "ctx", [(i, i ^ (1 << round_)) for i in range(groups)])
            arrived, joined = [swap(packed[1], 0)], packed[1]
            for round_ in range(1, groups.bit_length() - 1):
                joined, last = join(round_ - 1, after(group), joined, arrived[-1], wide)
                arrived.append(swap(last, round_))
            scanned[1] = scan(1, segments, after(scanned[1]), states[1], decay, lap, residue)
        else:
            grad_input = fix(
                segments, group, [scanned[0], scanned[1]], states[0], arrived, decay, lap, wide, residue, toks, width
            )
    return grad_query, grad_input


def solution(mesh):
    placed = (
        P("ctx", "ch"),
        P(None, "ch"),
        P("ctx", "ch"),
        P("ctx", "ch"),
        P("ch", None),
        P("ch", None),
    )
    return jax.shard_map(
        local,
        mesh=mesh,
        in_specs=placed,
        out_specs=(P("ctx", "ch"), P("ctx", "ch")),
        check_vma=False,
    )
```

```python
import functools
import math

import jax
import jax.numpy as jnp
from jax import lax
from jax.experimental import pallas as pl
from jax.experimental.pallas import tpu as pltpu
from jax.sharding import PartitionSpec as P

PEAKS = 16
SPAN = 251 * math.log(2.0)
SHIFT = 125 * math.log(2.0)
STEP = 256
PIECE = 128
GAP = 8
VMEM = 24 * 1024 * 1024
QUICK = pl.CostEstimate(flops=0, bytes_accessed=1024, transcendentals=0)

PORTIONS = (((0, 1, 2), 4, 0), ((1, 0, 2), 4, 0), ((0, 1, 2), 4, 1), ((0, 1, 2), 4, 1))
ORDER = (
    ((0, 0, 6), (0, 0, 2)), ((1, 0, 5), (1, 0, 1)), ((2, 0, 2), (3, 0, 2)), ("sum", 1), ((2, 0, 6), (3, 0, 6)),
    ((2, 0, 4), (3, 0, 4)), ((1, 0, 4), (0, 1, 4)), ((1, 1, 4), (0, 0, 4)), ((2, 1, 4), (3, 1, 4)),
    ((1, 0, 0), (0, 1, 0)), ((0, 2, 0), (1, 2, 0)), ((2, 2, 0), (3, 2, 0)), ((1, 1, 0), (0, 0, 0)),
    ((2, 1, 0), (3, 1, 0)), ((2, 0, 0), (3, 0, 0)), ("laps", None), ("sum", 0), ("gate", 0), ("gate", 1), ("scan", 1),
    ("fix", None),
)
WAITS = {
    ((1, 0, 0), (0, 1, 0)): ((1, 0, 4),),
    ((2, 0, 0), (3, 0, 0)): ((0, 2, 0), (1, 0, 0)),
    ("gate", 1): ((2, 2, 0), (2, 1, 0)),
}


def folds_of(toks):
    return toks // 128 if toks % 128 == 0 and PEAKS % (toks // 128) == 0 else 1


def part_of(rows, blocks, folds):
    return next(
        part for part in range(16, rows + 1, 16) if rows % part == 0 and rows // part * blocks * folds <= PEAKS
    )


def step_of(rows):
    return next(step for step in (STEP, STEP // 2, rows) if rows % step == 0)


def encode(block, part):
    codes, peaks = [], []
    for i in range(block.shape[0] // part):
        piece = block[i * part : (i + 1) * part, :]
        size = jnp.abs(piece)
        peak = jnp.maximum(jnp.max(size, axis=0, keepdims=True) * 1.01, 1e-30)
        peak = peak.astype(jnp.bfloat16).astype(jnp.float32)
        code = jnp.exp(size * (SPAN / peak) - SHIFT)
        codes.append(jnp.where(piece < 0, -code, code))
        peaks.append(peak)
    return jnp.concatenate(codes, axis=0).astype(jnp.bfloat16), peaks


def put(codes, out_ref, at):
    lanes = out_ref.shape[1]
    folds = codes.shape[1] // lanes
    rows = (out_ref.shape[0] - PEAKS) // folds
    for fold in range(folds):
        out_ref[fold * rows + at : fold * rows + at + codes.shape[0], :] = codes[:, fold * lanes : (fold + 1) * lanes]


def put_peaks(peaks, out_ref):
    lanes = out_ref.shape[1]
    peaks = [peak[:, at : at + lanes] for peak in peaks for at in range(0, peak.shape[1], lanes)]
    if len(peaks) < PEAKS:
        peaks.append(jnp.zeros((PEAKS - len(peaks), lanes), jnp.float32))
    out_ref[out_ref.shape[0] - PEAKS :, :] = jnp.concatenate(peaks, axis=0).astype(jnp.bfloat16)


def decode(ref, place, first, count, folds):
    start, peak, part = place
    rows = (ref.shape[0] - PEAKS) // folds
    peaks = ref[ref.shape[0] - PEAKS :, :].astype(jnp.float32) * (1.0 / SPAN)
    columns = []
    for fold in range(folds):
        blocks = []
        for i in range(first // part, -(-(first + count) // part)):
            low, high = max(first, i * part), min(first + count, (i + 1) * part)
            code = ref[fold * rows + start + low : fold * rows + start + high, :].astype(jnp.float32)
            at = (peak + i) * folds + fold
            size = (jnp.log(jnp.abs(code)) + SHIFT) * peaks[at : at + 1, :]
            blocks.append(jnp.where(code < 0, -size, size))
        columns.append(jnp.concatenate(blocks, axis=0))
    return jnp.concatenate(columns, axis=1)


def pinned(array):
    return pltpu.with_memory_space_constraint(array, pltpu.HBM)


def send_kernel(items, coded, width, near, place_ref, w_ref, turned_ref, *refs):
    near_refs, out_ref = refs[:near], refs[near]
    folds = folds_of(turned_ref.shape[1])
    base, peaks = 0, []
    for block, offset, rows, sources in items:
        step = step_of(rows)
        first = (place_ref[0] ^ block) * width + offset
        for at in range(0, rows, step):
            total = jnp.dot(
                w_ref[pl.ds(pl.multiple_of(first + at, 16), step), :],
                turned_ref[...],
                preferred_element_type=jnp.float32,
            )
            for source, place in sources:
                total = total + decode(near_refs[source], place, at, step, folds)
            if coded:
                total, more = encode(total, part_of(rows, len(items), folds))
                peaks += more
                put(total, out_ref, base + at)
            else:
                out_ref[base + at : base + at + step, :] = total
        base += rows
    if coded:
        put_peaks(peaks, out_ref)


def send(items, coded, width, place, weight, turned, nears):
    toks = turned.shape[1]
    vmem = pl.BlockSpec(memory_space=pltpu.VMEM)
    count = sum(rows for _, _, rows, _ in items)
    folds = folds_of(toks)
    shape = (folds * count + PEAKS, toks // folds) if coded else (count, toks)
    return pl.pallas_call(
        functools.partial(send_kernel, items, coded, width, len(nears)),
        in_specs=[pl.BlockSpec(memory_space=pltpu.SMEM)] + [vmem] * (2 + len(nears)),
        out_specs=vmem,
        out_shape=jax.ShapeDtypeStruct(shape, jnp.bfloat16 if coded else jnp.float32),
        compiler_params=pltpu.CompilerParams(vmem_limit_bytes=VMEM),
        cost_estimate=QUICK,
    )(place, weight, turned, *nears)


def first_kernel(items, width, place_ref, w_hbm, g_hbm, out_ref, turned_ref, w_ref, g_ref, sems):
    copies, toks = [], g_ref.shape[0]
    piece = math.gcd(toks, PIECE)
    for at in range(0, toks, piece):
        lines = pl.ds(at, piece)
        copies.append(pltpu.make_async_copy(g_hbm.at[lines, :], g_ref.at[lines, :], sems.at[len(copies)]))
    base, grads = 0, len(copies)
    for block, offset, rows, _ in items:
        step = math.gcd(rows, PIECE)
        first = pl.multiple_of((place_ref[0] ^ block) * width + offset, 16)
        for at in range(0, rows, step):
            copies.append(
                pltpu.make_async_copy(
                    w_hbm.at[pl.ds(first + at, step), :], w_ref.at[pl.ds(base + at, step), :], sems.at[len(copies)]
                )
            )
        base += rows
    for copy in copies:
        copy.start()
    for i, at in enumerate(range(0, toks, piece)):
        copies[i].wait()
        turned_ref[:, at : at + piece] = g_ref[at : at + piece, :].T
    base, peaks, waits = 0, [], iter(copies[grads:])
    for _, _, rows, _ in items:
        step = step_of(rows)
        for at in range(base, base + rows, step):
            for _ in range(step // math.gcd(rows, PIECE)):
                next(waits).wait()
            total = jnp.dot(w_ref[at : at + step, :], turned_ref[...], preferred_element_type=jnp.float32)
            total, more = encode(total, part_of(rows, len(items), folds_of(toks)))
            peaks += more
            put(total, out_ref, at)
        base += rows
    put_peaks(peaks, out_ref)


def first_send(items, width, place, weight, grad):
    toks, depth = grad.shape
    vmem = pl.BlockSpec(memory_space=pltpu.VMEM)
    high = pl.BlockSpec(memory_space=pltpu.HBM)
    count = sum(rows for _, _, rows, _ in items)
    folds = folds_of(toks)
    steps = toks // math.gcd(toks, PIECE) + sum(rows // math.gcd(rows, PIECE) for _, _, rows, _ in items)
    return pl.pallas_call(
        functools.partial(first_kernel, items, width),
        in_specs=[pl.BlockSpec(memory_space=pltpu.SMEM), high, high],
        out_specs=(vmem, vmem),
        out_shape=(
            jax.ShapeDtypeStruct((folds * count + PEAKS, toks // folds), jnp.bfloat16),
            jax.ShapeDtypeStruct((depth, toks), jnp.bfloat16),
        ),
        scratch_shapes=[
            pltpu.VMEM((count, depth), jnp.bfloat16),
            pltpu.VMEM((toks, depth), jnp.bfloat16),
            pltpu.SemaphoreType.DMA((steps,)),
        ],
        compiler_params=pltpu.CompilerParams(vmem_limit_bytes=VMEM),
        cost_estimate=QUICK,
    )(place, pinned(weight), pinned(grad))


def steps_back(count, body, state, unroll):
    unroll = math.gcd(count, unroll)

    def some(i, state):
        for j in range(unroll):
            state = body(count - 1 - (i * unroll + j), state)
        return state

    return lax.fori_loop(0, count // unroll, some, state)


def power(base, exponent):
    result = None
    while exponent:
        if exponent % 2:
            result = base if result is None else result * base
        base = base * base
        exponent //= 2
    return result


def segment_of(shape, segments):
    return lax.rem(lax.broadcasted_iota(jnp.int32, shape, 0), segments)


def rolled(value, by):
    by %= value.shape[0]
    return pltpu.roll(value, by, 0) if by else value


def gate_kernel(half, rows, segments, pieces, near, acc_ref, *refs):
    near_refs, refs = refs[:near], refs[near:]
    query_ref, conv_ref, decay_ref, lap_ref, other_ref = refs[:5]
    out_hbm, rows_ref, state_ref, pack_ref = refs[-7:-3] if half == 0 else refs[-6:-2]
    gq_ref, sem = refs[-2:]
    gc_ref = refs[-3] if half == 0 else rows_ref
    toks = query_ref.shape[0]
    modes, sublanes, lanes = state_ref.shape
    mine = slice(half * sublanes, (half + 1) * sublanes)
    for line in range(rows // lanes):
        mix = acc_ref[line * lanes : (line + 1) * lanes, :]
        first, sources = next(piece for piece in reversed(pieces) if piece[0] <= line * lanes)
        for source, place in sources:
            mix = mix + decode(near_refs[source], place, line * lanes - first, lanes, folds_of(toks))
        mix = mix.T
        at = slice(line * lanes, (line + 1) * lanes)
        full = slice(half * rows + line * lanes, half * rows + (line + 1) * lanes)
        gq_ref[:, at] = (mix * conv_ref[:, full].astype(jnp.float32)).astype(jnp.bfloat16)
        gated = mix * query_ref[:, full].astype(jnp.float32)
        for k in range(segments):
            start = (line * segments + k) * (toks // segments + GAP)
            gc_ref[start : start + toks // segments, :] = gated[k * (toks // segments) : (k + 1) * (toks // segments), :]
    store = pltpu.make_async_copy(gq_ref, out_hbm.at[:, pl.ds(half * rows, rows)], sem)
    store.start()
    decay = [decay_ref[n, mine] for n in range(modes)]
    span = toks // segments

    def step(t, state):
        at = pl.ds(t, sublanes, stride=span + GAP)
        row = gc_ref[at, :]
        state = tuple(decay[n] * state[n] + row for n in range(modes))
        if half == 0:
            rows_ref[at, :] = summed([other_ref[n, mine] * state[n] for n in range(modes)])
        return state

    zero = jnp.zeros((sublanes, lanes), jnp.float32)
    state = steps_back(span, step, (zero,) * modes, 16)
    segment = segment_of((sublanes, lanes), segments)
    whole = []
    for n in range(modes):
        state_ref[n] = state[n]
        total = state[n]
        if segments > 1:
            factor = jnp.where(segment < segments - 1, lap_ref[n, mine], 0.0)
            for _ in range(segments - 1):
                total = state[n] + factor * rolled(total, -1)
        whole.append(total)
    packs = modes // segments
    for m in range(packs):
        packed = whole[m * segments]
        for j in range(1, segments):
            packed = jnp.where(segment == j, rolled(whole[m * segments + j], j), packed)
        if half == 0:
            pack_ref[m] = packed
        else:
            pack_ref[m] = other_ref[m]
            pack_ref[packs + m] = packed
    store.wait()


def gate(half, rows, segments, pieces, acc, nears, query_in, conv_out, decay, lap, other, partial):
    toks, width = query_in.shape
    modes, _, lanes = decay.shape
    sublanes = rows // lanes * segments
    vmem = pl.BlockSpec(memory_space=pltpu.VMEM)
    high = pl.BlockSpec(memory_space=pltpu.HBM)
    more = [] if partial is None else [partial]
    lines = (sublanes * (toks // segments + GAP), lanes)
    return pl.pallas_call(
        functools.partial(gate_kernel, half, rows, segments, pieces, len(nears)),
        in_specs=[vmem] * (6 + len(nears)) + [high] * len(more),
        out_specs=(high, vmem, vmem, vmem),
        out_shape=(
            jax.ShapeDtypeStruct((toks, width), jnp.bfloat16),
            jax.ShapeDtypeStruct(lines, jnp.float32),
            jax.ShapeDtypeStruct((modes, sublanes, lanes), jnp.float32),
            jax.ShapeDtypeStruct(((1 + half) * modes // segments, sublanes, lanes), jnp.float32),
        ),
        scratch_shapes=([pltpu.VMEM(lines, jnp.float32)] if half == 0 else [])
        + [pltpu.VMEM((toks, rows), jnp.bfloat16), pltpu.SemaphoreType.DMA],
        input_output_aliases={6 + len(nears): 0} if more else {},
        compiler_params=pltpu.CompilerParams(vmem_limit_bytes=VMEM),
        cost_estimate=QUICK,
    )(acc, *nears, query_in, conv_out, decay, lap, other, *more)


def summed(terms):
    while len(terms) > 1:
        terms = [terms[k] + terms[k + 1] if k + 1 < len(terms) else terms[k] for k in range(0, len(terms), 2)]
    return terms[0]


def scan_kernel(half, segments, gc_ref, state_ref, decay_ref, lap_ref, residue_ref, rows_ref):
    modes, sublanes, lanes = state_ref.shape
    mine = slice(half * sublanes, (half + 1) * sublanes)
    span = gc_ref.shape[0] // sublanes - GAP
    segment = segment_of((sublanes, lanes), segments)
    decay = [decay_ref[n, mine] for n in range(modes)]
    start = []
    for n in range(modes):
        total = jnp.zeros((sublanes, lanes), jnp.float32)
        if segments > 1:
            for k in range(segments - 2, -1, -1):
                total = jnp.where(segment == k, rolled(state_ref[n] + lap_ref[n, mine] * total, -1), total)
        start.append(total)

    def step(t, state):
        at = pl.ds(t, sublanes, stride=span + GAP)
        row = gc_ref[at, :]
        state = tuple(decay[n] * state[n] + row for n in range(modes))
        rows_ref[at, :] = summed([residue_ref[n, mine] * state[n] for n in range(modes)])
        return state

    steps_back(span, step, tuple(start), 16)


def scan(half, segments, grad_conv, state, decay, lap, residues):
    vmem = pl.BlockSpec(memory_space=pltpu.VMEM)
    return pl.pallas_call(
        functools.partial(scan_kernel, half, segments),
        in_specs=[vmem] * 5,
        out_specs=vmem,
        out_shape=jax.ShapeDtypeStruct(grad_conv.shape, jnp.float32),
        compiler_params=pltpu.CompilerParams(vmem_limit_bytes=VMEM),
        cost_estimate=QUICK,
    )(grad_conv, state, decay, lap, residues)


def laps_kernel(segments, span, decay_ref, lap_ref, wide_ref):
    modes, sublanes, lanes = decay_ref.shape
    sublanes //= 2
    packs = modes // segments
    segment = segment_of((sublanes, lanes), segments)
    for half in range(2):
        mine = slice(half * sublanes, (half + 1) * sublanes)
        for m in range(packs):
            packed = None
            for j in range(segments):
                lap = power(decay_ref[m * segments + j, mine], span)
                lap_ref[m * segments + j, mine] = lap
                wide = power(lap, segments)
                packed = wide if packed is None else jnp.where(segment == j, wide, packed)
            wide_ref[half * packs + m] = packed


def laps(segments, toks, decay):
    modes, sublanes, lanes = decay.shape
    vmem = pl.BlockSpec(memory_space=pltpu.VMEM)
    return pl.pallas_call(
        functools.partial(laps_kernel, segments, toks // segments),
        in_specs=[vmem],
        out_specs=(vmem, vmem),
        out_shape=(
            jax.ShapeDtypeStruct(decay.shape, jnp.float32),
            jax.ShapeDtypeStruct((2 * modes // segments, sublanes // 2, lanes), jnp.float32),
        ),
        compiler_params=pltpu.CompilerParams(vmem_limit_bytes=VMEM),
        cost_estimate=QUICK,
    )(decay)


def states_in(ref, shape):
    if ref.shape == shape:
        return [ref[m] for m in range(shape[0])]
    packs, sublanes, _ = shape
    rows = decode(ref, (0, 0, packs * sublanes // 2), 0, packs * sublanes, 1)
    return [rows[m * sublanes : (m + 1) * sublanes, :] for m in range(packs)]


def join_kernel(round_, group_ref, state_ref, arrived_ref, wide_ref, coded_ref, *out_refs):
    earlier = (group_ref[0] >> round_) % 2 == 0
    packs, sublanes, _ = state_ref.shape
    joined = []
    for m, other in enumerate(states_in(arrived_ref, state_ref.shape)):
        wide = power(wide_ref[m], 1 << round_)
        mine = state_ref[m]
        joined.append(jnp.where(earlier, mine + wide * other, other + wide * mine))
        for out_ref in out_refs:
            out_ref[m] = joined[-1]
    codes, peaks = encode(jnp.concatenate(joined, axis=0), packs * sublanes // 2)
    put(codes, coded_ref, 0)
    put_peaks(peaks, coded_ref)


def join(round_, group, state, arrived, wide, last):
    vmem = pl.BlockSpec(memory_space=pltpu.VMEM)
    packs, sublanes, lanes = state.shape
    return pl.pallas_call(
        functools.partial(join_kernel, round_),
        in_specs=[pl.BlockSpec(memory_space=pltpu.SMEM)] + [vmem] * 3,
        out_specs=[vmem] * (1 if last else 2),
        out_shape=[
            jax.ShapeDtypeStruct((packs * sublanes + PEAKS, lanes), jnp.bfloat16),
            jax.ShapeDtypeStruct(state.shape, jnp.float32),
        ][: 1 if last else 2],
        compiler_params=pltpu.CompilerParams(vmem_limit_bytes=VMEM),
        cost_estimate=QUICK,
    )(group, state, arrived, wide)


def fix_kernel(segments, rounds, group_ref, *refs):
    scanned_refs, state_ref, arrived_refs = refs[:2], refs[2], refs[3 : 3 + rounds]
    decay_ref, lap_ref, wide_ref, residue_ref, out_hbm, rows_ref, out_ref, sems = refs[3 + rounds :]
    toks, width = out_ref.shape
    modes, sublanes, lanes = state_ref.shape
    packs = modes // segments
    rows = width // 2
    span = toks // segments
    segment = segment_of((sublanes, lanes), segments)
    earlier = [(group_ref[0] >> r) % 2 == 0 for r in range(rounds)]
    arrived = [states_in(ref, (2 * packs, sublanes, lanes)) for ref in arrived_refs]
    stores = []
    for half in range(2):
        mine = slice(half * sublanes, (half + 1) * sublanes)
        decay = [decay_ref[n, mine] for n in range(modes)]
        start = []
        for m in range(packs):
            brought = jnp.zeros((sublanes, lanes), jnp.float32)
            between = jnp.ones((sublanes, lanes), jnp.float32)
            for r in range(rounds):
                state = arrived[r][half * packs + m]
                brought = jnp.where(earlier[r], brought + between * state, brought)
                if r + 1 < rounds:
                    between = jnp.where(earlier[r], between * power(wide_ref[half * packs + m], 1 << r), between)
            for j in range(segments):
                n = m * segments + j
                total = rolled(brought, segments - 1 - j)
                for k in range(segments - 2, -1, -1):
                    before = lap_ref[n, mine] * total
                    if half == 0:
                        before = before + state_ref[n]
                    total = jnp.where(segment == k, rolled(before, -1), total)
                start.append(residue_ref[n, mine] * total)

        def step(t, state, scanned_ref=scanned_refs[half], decay=decay):
            at = pl.ds(t, sublanes, stride=span + GAP)
            state = tuple(decay[n] * state[n] for n in range(modes))
            rows_ref[at, :] = scanned_ref[at, :] + summed(list(state))
            return state

        steps_back(span, step, tuple(start), 16)
        for line in range(rows // lanes):
            at = slice(half * rows + line * lanes, half * rows + (line + 1) * lanes)
            for k in range(segments):
                start = (line * segments + k) * (span + GAP)
                out_ref[k * span : (k + 1) * span, at] = rows_ref[start : start + span, :].astype(jnp.bfloat16)
        columns = pl.ds(half * rows, rows)
        stores.append(pltpu.make_async_copy(out_ref.at[:, columns], out_hbm.at[:, columns], sems.at[half]))
        stores[-1].start()
    for store in stores:
        store.wait()


def fix(segments, group, scanned, state, arrived, decay, lap, wide, residues, toks, width):
    vmem = pl.BlockSpec(memory_space=pltpu.VMEM)
    return pl.pallas_call(
        functools.partial(fix_kernel, segments, len(arrived)),
        in_specs=[pl.BlockSpec(memory_space=pltpu.SMEM)] + [vmem] * (7 + len(arrived)),
        out_specs=pl.BlockSpec(memory_space=pltpu.HBM),
        out_shape=jax.ShapeDtypeStruct((toks, width), jnp.bfloat16),
        scratch_shapes=[
            pltpu.VMEM(scanned[0].shape, jnp.float32),
            pltpu.VMEM((toks, width), jnp.bfloat16),
            pltpu.SemaphoreType.DMA((2,)),
        ],
        compiler_params=pltpu.CompilerParams(vmem_limit_bytes=VMEM),
        cost_estimate=QUICK,
    )(group, *scanned, state, *arrived, decay, lap, wide, residues)


def local(out_grad, out_weight, query_in, conv_out, residues, decay_rates):
    toks, width = query_in.shape
    modes = decay_rates.shape[1]
    lanes = math.gcd(width, 128)
    size, groups = lax.axis_size("ch"), lax.axis_size("ctx")
    bits = [1 << i for i in range(size.bit_length() - 1)]
    place = jnp.reshape(lax.axis_index("ch"), (1,)).astype(jnp.int32)
    group = jnp.reshape(lax.axis_index("ctx"), (1,)).astype(jnp.int32)
    half_rows = width // 2
    lines = half_rows // lanes
    segments = 8 // lines
    by_mode = lambda values: jnp.repeat(values.T.reshape(modes, width // lanes, lanes), segments, axis=1)
    decay, residue = by_mode(decay_rates), by_mode(residues)

    portions, order, waits = PORTIONS, ORDER, WAITS
    if size != 8:
        waits = {}
        portions = ((tuple(range(len(bits))), 2, 0), (tuple(range(len(bits))), 2, 1))
        order = [
            ((p, s, block),)
            for p in range(2)
            for s, bit in enumerate(bits)
            for block in sorted(range(0, size, 2 * bit), reverse=True)
        ] + [("laps", None), ("sum", 0), ("sum", 1), ("gate", 0), ("gate", 1), ("scan", 1), ("fix", None)]
    offsets = [sum(width // part for _, part, _ in portions[:p]) for p in range(len(portions))]

    received, sums, scanned, states, packed = {}, {}, {}, {}, {}
    grad_query = last = None

    def after(value):
        return value if last is None else lax.optimization_barrier((value, last, *awaited))[0]

    def collect(wanted):
        arrays, places = [], []
        for key in wanted:
            array, *place = received[key]
            index = next((i for i, known in enumerate(arrays) if known is array), len(arrays))
            if index == len(arrays):
                arrays.append(array)
            places.append((index, tuple(place)))
        return arrays, places

    for todo in order:
        awaited = [received[key][0] for key in waits.get(todo, ())]
        kind, half = todo if isinstance(todo[0], str) else ("send", None)
        inside = [q for q, (_, _, lies) in enumerate(portions) if lies == half]
        if kind == "send":
            arrays, items = [], []
            wanted, rows, bits_of = [], [], []
            for p, s, block in todo:
                route, share, _ = portions[p]
                bits_of.append(bits[route[s]])
                rows.append(width // share)
                wanted.append([(p, i, block ^ bits_of[-1]) for i in range(s)])
            bit, count = bits_of[0], len(todo)
            arrays, places = collect([key for keys in wanted for key in keys])
            places = iter(places)
            items = tuple(
                (block ^ bit, offsets[p], rows[i], tuple(next(places) for _ in wanted[i]))
                for i, (p, _, block) in enumerate(todo)
            )
            if last is None:
                last, turned = first_send(items, width, place, out_weight, out_grad)
            else:
                last = send(items, True, width, after(place), out_weight, turned, arrays)
            arrived = lax.ppermute(last, "ch", [(i, i ^ bit) for i in range(size)])
            start = peak = 0
            for i, key in enumerate(todo):
                part = part_of(rows[i], count, folds_of(toks))
                received[key] = (arrived, start, peak, part)
                start, peak = start + rows[i], peak + rows[i] // part
        elif kind == "laps":
            lap, wide = laps(segments, toks, after(decay))
            last = wide
        elif kind == "sum":
            items = tuple((0, offsets[q], width // portions[q][1], ()) for q in inside)
            last = sums[half] = send(items, False, width, after(place), out_weight, turned, [])
        elif kind == "gate":
            stages = range(len(bits))
            arrays, places = collect([(q, i, 0) for q in inside for i in stages])
            pieces = tuple(
                (offsets[q] - half * half_rows, tuple(places[i * len(stages) : (i + 1) * len(stages)]))
                for i, q in enumerate(inside)
            )
            other = residue if half == 0 else packed[0]
            grad_query, scanned[half], states[half], packed[half] = gate(
                half,
                half_rows,
                segments,
                pieces,
                after(sums[half]),
                arrays,
                query_in,
                conv_out,
                decay,
                lap,
                other,
                grad_query,
            )
            last = packed[half]
        elif kind == "scan":
            groups = lax.axis_size("ctx")
            swap = lambda array, round_: lax.ppermute(array, "ctx", [(i, i ^ (1 << round_)) for i in range(groups)])
            arrived, joined = [swap(packed[1], 0)], packed[1]
            rounds = groups.bit_length() - 1
            for round_ in range(1, rounds):
                last, *joined = join(round_ - 1, after(group), joined, arrived[-1], wide, round_ + 1 == rounds)
                joined = joined[0] if joined else None
                arrived.append(swap(last, round_))
            scanned[1] = scan(1, segments, after(scanned[1]), states[1], decay, lap, residue)
        else:
            grad_input = fix(
                segments, group, [scanned[0], scanned[1]], states[0], arrived, decay, lap, wide, residue, toks, width
            )
    return grad_query, grad_input


def solution(mesh):
    placed = (
        P("ctx", "ch"),
        P(None, "ch"),
        P("ctx", "ch"),
        P("ctx", "ch"),
        P("ch", None),
        P("ch", None),
    )
    return jax.shard_map(
        local,
        mesh=mesh,
        in_specs=placed,
        out_specs=(P("ctx", "ch"), P("ctx", "ch")),
        check_vma=False,
    )
```

```python
import functools
import math

import jax
import jax.numpy as jnp
from jax import lax
from jax.experimental import pallas as pl
from jax.experimental.pallas import tpu as pltpu
from jax.sharding import PartitionSpec as P

PEAKS = 16
SPAN = 251 * math.log(2.0)
SHIFT = 125 * math.log(2.0)
STEP = 256
PIECE = 128
GAP = 8
VMEM = 24 * 1024 * 1024
QUICK = pl.CostEstimate(flops=0, bytes_accessed=1024, transcendentals=0)

PORTIONS = (((0, 1, 2), 4, 0), ((1, 0, 2), 4, 0), ((0, 1, 2), 4, 1), ((0, 1, 2), 4, 1))
ORDER = (
    ((0, 0, 6), (0, 0, 2)),
    ((1, 0, 5), (1, 0, 1)),
    ("sum", 1),
    ((2, 0, 2), (3, 0, 2)),
    ((2, 0, 6), (3, 0, 6)),
    ((2, 0, 4), (3, 0, 4)),
    ((1, 0, 4), (0, 1, 4)),
    ((1, 1, 4), (0, 0, 4)),
    ((2, 1, 4), (3, 1, 4)),
    ((1, 0, 0), (0, 1, 0)),
    ((0, 2, 0), (1, 2, 0)),
    ((2, 2, 0), (3, 2, 0)),
    ((1, 1, 0), (0, 0, 0)),
    ((2, 1, 0), (3, 1, 0)),
    ((2, 0, 0), (3, 0, 0)),
    ("sum", 0),
    ("laps", None),
    ("gate", 0),
    ("gate", 1),
    ("scan", 1),
    ("fix", None),
)
WAITS = {
    ((1, 0, 0), (0, 1, 0)): ((1, 0, 4),),
    ("gate", 0): ((0, 2, 0), (1, 0, 0)),
    ("gate", 1): ((2, 2, 0), (2, 1, 0)),
}


def folds_of(toks):
    return toks // 128 if toks % 128 == 0 and PEAKS % (toks // 128) == 0 else 1


def part_of(rows, blocks, folds):
    return next(
        part for part in range(16, rows + 1, 16) if rows % part == 0 and rows // part * blocks * folds <= PEAKS
    )


def step_of(rows):
    return next(step for step in (STEP, STEP // 2, rows) if rows % step == 0)


def encode(block, part):
    codes, peaks = [], []
    for i in range(block.shape[0] // part):
        piece = block[i * part : (i + 1) * part, :]
        size = jnp.abs(piece)
        peak = jnp.maximum(jnp.max(size, axis=0, keepdims=True) * 1.01, 1e-30)
        peak = peak.astype(jnp.bfloat16).astype(jnp.float32)
        code = jnp.exp(size * (SPAN / peak) - SHIFT)
        codes.append(jnp.where(piece < 0, -code, code))
        peaks.append(peak)
    return jnp.concatenate(codes, axis=0).astype(jnp.bfloat16), peaks


def put(codes, out_ref, at):
    lanes = out_ref.shape[1]
    folds = codes.shape[1] // lanes
    rows = (out_ref.shape[0] - PEAKS) // folds
    for fold in range(folds):
        out_ref[fold * rows + at : fold * rows + at + codes.shape[0], :] = codes[:, fold * lanes : (fold + 1) * lanes]


def put_peaks(peaks, out_ref):
    lanes = out_ref.shape[1]
    peaks = [peak[:, at : at + lanes] for peak in peaks for at in range(0, peak.shape[1], lanes)]
    if len(peaks) < PEAKS:
        peaks.append(jnp.zeros((PEAKS - len(peaks), lanes), jnp.float32))
    out_ref[out_ref.shape[0] - PEAKS :, :] = jnp.concatenate(peaks, axis=0).astype(jnp.bfloat16)


def decode(ref, place, first, count, folds):
    start, peak, part = place
    rows = (ref.shape[0] - PEAKS) // folds
    peaks = ref[ref.shape[0] - PEAKS :, :].astype(jnp.float32) * (1.0 / SPAN)
    columns = []
    for fold in range(folds):
        blocks = []
        for i in range(first // part, -(-(first + count) // part)):
            low, high = max(first, i * part), min(first + count, (i + 1) * part)
            code = ref[fold * rows + start + low : fold * rows + start + high, :].astype(jnp.float32)
            at = (peak + i) * folds + fold
            size = (jnp.log(jnp.abs(code)) + SHIFT) * peaks[at : at + 1, :]
            blocks.append(jnp.where(code < 0, -size, size))
        columns.append(jnp.concatenate(blocks, axis=0))
    return jnp.concatenate(columns, axis=1)


def pinned(array):
    return pltpu.with_memory_space_constraint(array, pltpu.HBM)


def send_kernel(items, coded, width, near, place_ref, w_ref, turned_ref, *refs):
    near_refs, out_ref = refs[:near], refs[near]
    folds = folds_of(turned_ref.shape[1])
    base, peaks = 0, []
    for block, offset, rows, sources in items:
        step = step_of(rows)
        first = (place_ref[0] ^ block) * width + offset
        for at in range(0, rows, step):
            total = jnp.dot(
                w_ref[pl.ds(pl.multiple_of(first + at, 16), step), :],
                turned_ref[...],
                preferred_element_type=jnp.float32,
            )
            for source, place in sources:
                total = total + decode(near_refs[source], place, at, step, folds)
            if coded:
                total, more = encode(total, part_of(rows, len(items), folds))
                peaks += more
                put(total, out_ref, base + at)
            else:
                out_ref[base + at : base + at + step, :] = total
        base += rows
    if coded:
        put_peaks(peaks, out_ref)


def send(items, coded, width, place, weight, turned, nears):
    toks = turned.shape[1]
    vmem = pl.BlockSpec(memory_space=pltpu.VMEM)
    count = sum(rows for _, _, rows, _ in items)
    folds = folds_of(toks)
    shape = (folds * count + PEAKS, toks // folds) if coded else (count, toks)
    return pl.pallas_call(
        functools.partial(send_kernel, items, coded, width, len(nears)),
        in_specs=[pl.BlockSpec(memory_space=pltpu.SMEM)] + [vmem] * (2 + len(nears)),
        out_specs=vmem,
        out_shape=jax.ShapeDtypeStruct(shape, jnp.bfloat16 if coded else jnp.float32),
        compiler_params=pltpu.CompilerParams(vmem_limit_bytes=VMEM),
        cost_estimate=QUICK,
    )(place, weight, turned, *nears)


def first_kernel(items, width, place_ref, w_hbm, g_hbm, out_ref, turned_ref, w_ref, g_ref, sems):
    copies, toks = [], g_ref.shape[0]
    piece = math.gcd(toks, PIECE)
    for at in range(0, toks, piece):
        lines = pl.ds(at, piece)
        copies.append(pltpu.make_async_copy(g_hbm.at[lines, :], g_ref.at[lines, :], sems.at[len(copies)]))
    base, grads = 0, len(copies)
    for block, offset, rows, _ in items:
        step = math.gcd(rows, PIECE)
        first = pl.multiple_of((place_ref[0] ^ block) * width + offset, 16)
        for at in range(0, rows, step):
            copies.append(
                pltpu.make_async_copy(
                    w_hbm.at[pl.ds(first + at, step), :], w_ref.at[pl.ds(base + at, step), :], sems.at[len(copies)]
                )
            )
        base += rows
    for copy in copies:
        copy.start(priority=1)
    for i, at in enumerate(range(0, toks, piece)):
        copies[i].wait()
        turned_ref[:, at : at + piece] = g_ref[at : at + piece, :].T
    base, peaks, waits = 0, [], iter(copies[grads:])
    for _, _, rows, _ in items:
        step = step_of(rows)
        for at in range(base, base + rows, step):
            for _ in range(step // math.gcd(rows, PIECE)):
                next(waits).wait()
            total = jnp.dot(w_ref[at : at + step, :], turned_ref[...], preferred_element_type=jnp.float32)
            total, more = encode(total, part_of(rows, len(items), folds_of(toks)))
            peaks += more
            put(total, out_ref, at)
        base += rows
    put_peaks(peaks, out_ref)


def first_send(items, width, place, weight, grad):
    toks, depth = grad.shape
    vmem = pl.BlockSpec(memory_space=pltpu.VMEM)
    high = pl.BlockSpec(memory_space=pltpu.HBM)
    count = sum(rows for _, _, rows, _ in items)
    folds = folds_of(toks)
    steps = toks // math.gcd(toks, PIECE) + sum(rows // math.gcd(rows, PIECE) for _, _, rows, _ in items)
    return pl.pallas_call(
        functools.partial(first_kernel, items, width),
        in_specs=[pl.BlockSpec(memory_space=pltpu.SMEM), high, high],
        out_specs=(vmem, vmem),
        out_shape=(
            jax.ShapeDtypeStruct((folds * count + PEAKS, toks // folds), jnp.bfloat16),
            jax.ShapeDtypeStruct((depth, toks), jnp.bfloat16),
        ),
        scratch_shapes=[
            pltpu.VMEM((count, depth), jnp.bfloat16),
            pltpu.VMEM((toks, depth), jnp.bfloat16),
            pltpu.SemaphoreType.DMA((steps,)),
        ],
        compiler_params=pltpu.CompilerParams(vmem_limit_bytes=VMEM),
        cost_estimate=QUICK,
    )(place, pinned(weight), pinned(grad))


def steps_back(count, body, state, unroll):
    unroll = math.gcd(count, unroll)

    def some(i, state):
        for j in range(unroll):
            state = body(count - 1 - (i * unroll + j), state)
        return state

    return lax.fori_loop(0, count // unroll, some, state)


def power(base, exponent):
    result = None
    while exponent:
        if exponent % 2:
            result = base if result is None else result * base
        base = base * base
        exponent //= 2
    return result


def segment_of(shape, segments):
    return lax.rem(lax.broadcasted_iota(jnp.int32, shape, 0), segments)


def rolled(value, by):
    by %= value.shape[0]
    return pltpu.roll(value, by, 0) if by else value


def gate_kernel(half, rows, segments, pieces, near, acc_ref, *refs):
    near_refs, refs = refs[:near], refs[near:]
    query_ref, conv_ref, decay_ref, lap_ref, other_ref = refs[:5]
    out_hbm, rows_ref, state_ref, pack_ref = refs[-7:-3] if half == 0 else refs[-6:-2]
    gq_ref, sem = refs[-2:]
    gc_ref = refs[-3] if half == 0 else rows_ref
    toks = query_ref.shape[0]
    modes, sublanes, lanes = state_ref.shape
    mine = slice(half * sublanes, (half + 1) * sublanes)
    for line in range(rows // lanes):
        mix = acc_ref[line * lanes : (line + 1) * lanes, :]
        first, sources = next(piece for piece in reversed(pieces) if piece[0] <= line * lanes)
        for source, place in sources:
            mix = mix + decode(near_refs[source], place, line * lanes - first, lanes, folds_of(toks))
        mix = mix.T
        at = slice(line * lanes, (line + 1) * lanes)
        full = slice(half * rows + line * lanes, half * rows + (line + 1) * lanes)
        gq_ref[:, at] = (mix * conv_ref[:, full].astype(jnp.float32)).astype(jnp.bfloat16)
        gated = mix * query_ref[:, full].astype(jnp.float32)
        for k in range(segments):
            start = (line * segments + k) * (toks // segments + GAP)
            gc_ref[start : start + toks // segments, :] = gated[k * (toks // segments) : (k + 1) * (toks // segments), :]
    store = pltpu.make_async_copy(gq_ref, out_hbm.at[:, pl.ds(half * rows, rows)], sem)
    store.start()
    decay = [decay_ref[n, mine] for n in range(modes)]
    span = toks // segments

    def step(t, state):
        at = pl.ds(t, sublanes, stride=span + GAP)
        row = gc_ref[at, :]
        state = tuple(decay[n] * state[n] + row for n in range(modes))
        if half == 0:
            rows_ref[at, :] = summed([other_ref[n, mine] * state[n] for n in range(modes)])
        return state

    zero = jnp.zeros((sublanes, lanes), jnp.float32)
    state = steps_back(span, step, (zero,) * modes, 16)
    segment = segment_of((sublanes, lanes), segments)
    whole = []
    for n in range(modes):
        state_ref[n] = state[n]
        total = state[n]
        if segments > 1:
            factor = jnp.where(segment < segments - 1, lap_ref[n, mine], 0.0)
            for _ in range(segments - 1):
                total = state[n] + factor * rolled(total, -1)
        whole.append(total)
    packs = modes // segments
    for m in range(packs):
        packed = whole[m * segments]
        for j in range(1, segments):
            packed = jnp.where(segment == j, rolled(whole[m * segments + j], j), packed)
        if half == 0:
            pack_ref[m] = packed
        else:
            pack_ref[m] = other_ref[m]
            pack_ref[packs + m] = packed
    store.wait()


def gate(half, rows, segments, pieces, acc, nears, query_in, conv_out, decay, lap, other, partial):
    toks, width = query_in.shape
    modes, _, lanes = decay.shape
    sublanes = rows // lanes * segments
    vmem = pl.BlockSpec(memory_space=pltpu.VMEM)
    high = pl.BlockSpec(memory_space=pltpu.HBM)
    more = [] if partial is None else [partial]
    lines = (sublanes * (toks // segments + GAP), lanes)
    return pl.pallas_call(
        functools.partial(gate_kernel, half, rows, segments, pieces, len(nears)),
        in_specs=[vmem] * (6 + len(nears)) + [high] * len(more),
        out_specs=(high, vmem, vmem, vmem),
        out_shape=(
            jax.ShapeDtypeStruct((toks, width), jnp.bfloat16),
            jax.ShapeDtypeStruct(lines, jnp.float32),
            jax.ShapeDtypeStruct((modes, sublanes, lanes), jnp.float32),
            jax.ShapeDtypeStruct(((1 + half) * modes // segments, sublanes, lanes), jnp.float32),
        ),
        scratch_shapes=([pltpu.VMEM(lines, jnp.float32)] if half == 0 else [])
        + [pltpu.VMEM((toks, rows), jnp.bfloat16), pltpu.SemaphoreType.DMA],
        input_output_aliases={6 + len(nears): 0} if more else {},
        compiler_params=pltpu.CompilerParams(vmem_limit_bytes=VMEM),
        cost_estimate=QUICK,
    )(acc, *nears, query_in, conv_out, decay, lap, other, *more)


def summed(terms):
    while len(terms) > 1:
        terms = [terms[k] + terms[k + 1] if k + 1 < len(terms) else terms[k] for k in range(0, len(terms), 2)]
    return terms[0]


def scan_kernel(half, segments, gc_ref, state_ref, decay_ref, lap_ref, residue_ref, rows_ref):
    modes, sublanes, lanes = state_ref.shape
    mine = slice(half * sublanes, (half + 1) * sublanes)
    span = gc_ref.shape[0] // sublanes - GAP
    segment = segment_of((sublanes, lanes), segments)
    decay = [decay_ref[n, mine] for n in range(modes)]
    start = []
    for n in range(modes):
        total = jnp.zeros((sublanes, lanes), jnp.float32)
        if segments > 1:
            for k in range(segments - 2, -1, -1):
                total = jnp.where(segment == k, rolled(state_ref[n] + lap_ref[n, mine] * total, -1), total)
        start.append(total)

    def step(t, state):
        at = pl.ds(t, sublanes, stride=span + GAP)
        row = gc_ref[at, :]
        state = tuple(decay[n] * state[n] + row for n in range(modes))
        rows_ref[at, :] = summed([residue_ref[n, mine] * state[n] for n in range(modes)])
        return state

    steps_back(span, step, tuple(start), 16)


def scan(half, segments, grad_conv, state, decay, lap, residues):
    vmem = pl.BlockSpec(memory_space=pltpu.VMEM)
    return pl.pallas_call(
        functools.partial(scan_kernel, half, segments),
        in_specs=[vmem] * 5,
        out_specs=vmem,
        out_shape=jax.ShapeDtypeStruct(grad_conv.shape, jnp.float32),
        compiler_params=pltpu.CompilerParams(vmem_limit_bytes=VMEM),
        cost_estimate=QUICK,
    )(grad_conv, state, decay, lap, residues)


def laps_kernel(segments, span, decay_ref, lap_ref, wide_ref):
    modes, sublanes, lanes = decay_ref.shape
    sublanes //= 2
    packs = modes // segments
    segment = segment_of((sublanes, lanes), segments)
    for half in range(2):
        mine = slice(half * sublanes, (half + 1) * sublanes)
        for m in range(packs):
            packed = None
            for j in range(segments):
                lap = power(decay_ref[m * segments + j, mine], span)
                lap_ref[m * segments + j, mine] = lap
                wide = power(lap, segments)
                packed = wide if packed is None else jnp.where(segment == j, wide, packed)
            wide_ref[half * packs + m] = packed


def laps(segments, toks, decay):
    modes, sublanes, lanes = decay.shape
    vmem = pl.BlockSpec(memory_space=pltpu.VMEM)
    return pl.pallas_call(
        functools.partial(laps_kernel, segments, toks // segments),
        in_specs=[vmem],
        out_specs=(vmem, vmem),
        out_shape=(
            jax.ShapeDtypeStruct(decay.shape, jnp.float32),
            jax.ShapeDtypeStruct((2 * modes // segments, sublanes // 2, lanes), jnp.float32),
        ),
        compiler_params=pltpu.CompilerParams(vmem_limit_bytes=VMEM),
        cost_estimate=QUICK,
    )(decay)


def states_in(ref, shape):
    if ref.shape == shape:
        return [ref[m] for m in range(shape[0])]
    packs, sublanes, _ = shape
    rows = decode(ref, (0, 0, packs * sublanes // 2), 0, packs * sublanes, 1)
    return [rows[m * sublanes : (m + 1) * sublanes, :] for m in range(packs)]


def join_kernel(round_, group_ref, state_ref, arrived_ref, wide_ref, coded_ref, *out_refs):
    earlier = (group_ref[0] >> round_) % 2 == 0
    packs, sublanes, _ = state_ref.shape
    joined = []
    for m, other in enumerate(states_in(arrived_ref, state_ref.shape)):
        wide = power(wide_ref[m], 1 << round_)
        mine = state_ref[m]
        joined.append(jnp.where(earlier, mine + wide * other, other + wide * mine))
        for out_ref in out_refs:
            out_ref[m] = joined[-1]
    codes, peaks = encode(jnp.concatenate(joined, axis=0), packs * sublanes // 2)
    put(codes, coded_ref, 0)
    put_peaks(peaks, coded_ref)


def join(round_, group, state, arrived, wide, last):
    vmem = pl.BlockSpec(memory_space=pltpu.VMEM)
    packs, sublanes, lanes = state.shape
    return pl.pallas_call(
        functools.partial(join_kernel, round_),
        in_specs=[pl.BlockSpec(memory_space=pltpu.SMEM)] + [vmem] * 3,
        out_specs=[vmem] * (1 if last else 2),
        out_shape=[
            jax.ShapeDtypeStruct((packs * sublanes + PEAKS, lanes), jnp.bfloat16),
            jax.ShapeDtypeStruct(state.shape, jnp.float32),
        ][: 1 if last else 2],
        compiler_params=pltpu.CompilerParams(vmem_limit_bytes=VMEM),
        cost_estimate=QUICK,
    )(group, state, arrived, wide)


def fix_kernel(segments, rounds, group_ref, *refs):
    scanned_refs, state_ref, arrived_refs = refs[:2], refs[2], refs[3 : 3 + rounds]
    decay_ref, lap_ref, wide_ref, residue_ref, out_hbm, rows_ref, out_ref, sems = refs[3 + rounds :]
    toks, width = out_ref.shape
    modes, sublanes, lanes = state_ref.shape
    packs = modes // segments
    rows = width // 2
    span = toks // segments
    segment = segment_of((sublanes, lanes), segments)
    earlier = [(group_ref[0] >> r) % 2 == 0 for r in range(rounds)]
    arrived = [states_in(ref, (2 * packs, sublanes, lanes)) for ref in arrived_refs]
    stores = []
    for half in range(2):
        mine = slice(half * sublanes, (half + 1) * sublanes)
        decay = [decay_ref[n, mine] for n in range(modes)]
        start = []
        for m in range(packs):
            brought = jnp.zeros((sublanes, lanes), jnp.float32)
            between = jnp.ones((sublanes, lanes), jnp.float32)
            for r in range(rounds):
                state = arrived[r][half * packs + m]
                brought = jnp.where(earlier[r], brought + between * state, brought)
                if r + 1 < rounds:
                    between = jnp.where(earlier[r], between * power(wide_ref[half * packs + m], 1 << r), between)
            for j in range(segments):
                n = m * segments + j
                total = rolled(brought, segments - 1 - j)
                for k in range(segments - 2, -1, -1):
                    before = lap_ref[n, mine] * total
                    if half == 0:
                        before = before + state_ref[n]
                    total = jnp.where(segment == k, rolled(before, -1), total)
                start.append(residue_ref[n, mine] * total)

        def step(t, state, scanned_ref=scanned_refs[half], decay=decay):
            at = pl.ds(t, sublanes, stride=span + GAP)
            state = tuple(decay[n] * state[n] for n in range(modes))
            rows_ref[at, :] = scanned_ref[at, :] + summed(list(state))
            return state

        steps_back(span, step, tuple(start), 16)
        for line in range(rows // lanes):
            at = slice(half * rows + line * lanes, half * rows + (line + 1) * lanes)
            for k in range(segments):
                start = (line * segments + k) * (span + GAP)
                out_ref[k * span : (k + 1) * span, at] = rows_ref[start : start + span, :].astype(jnp.bfloat16)
        columns = pl.ds(half * rows, rows)
        stores.append(pltpu.make_async_copy(out_ref.at[:, columns], out_hbm.at[:, columns], sems.at[half]))
        stores[-1].start()
    for store in stores:
        store.wait()


def fix(segments, group, scanned, state, arrived, decay, lap, wide, residues, toks, width):
    vmem = pl.BlockSpec(memory_space=pltpu.VMEM)
    return pl.pallas_call(
        functools.partial(fix_kernel, segments, len(arrived)),
        in_specs=[pl.BlockSpec(memory_space=pltpu.SMEM)] + [vmem] * (7 + len(arrived)),
        out_specs=pl.BlockSpec(memory_space=pltpu.HBM),
        out_shape=jax.ShapeDtypeStruct((toks, width), jnp.bfloat16),
        scratch_shapes=[
            pltpu.VMEM(scanned[0].shape, jnp.float32),
            pltpu.VMEM((toks, width), jnp.bfloat16),
            pltpu.SemaphoreType.DMA((2,)),
        ],
        compiler_params=pltpu.CompilerParams(vmem_limit_bytes=VMEM),
        cost_estimate=QUICK,
    )(group, *scanned, state, *arrived, decay, lap, wide, residues)


def local(out_grad, out_weight, query_in, conv_out, residues, decay_rates):
    toks, width = query_in.shape
    modes = decay_rates.shape[1]
    lanes = math.gcd(width, 128)
    size, groups = lax.axis_size("ch"), lax.axis_size("ctx")
    bits = [1 << i for i in range(size.bit_length() - 1)]
    place = jnp.reshape(lax.axis_index("ch"), (1,)).astype(jnp.int32)
    group = jnp.reshape(lax.axis_index("ctx"), (1,)).astype(jnp.int32)
    half_rows = width // 2
    lines = half_rows // lanes
    segments = 8 // lines
    by_mode = lambda values: jnp.repeat(values.T.reshape(modes, width // lanes, lanes), segments, axis=1)
    decay, residue = by_mode(decay_rates), by_mode(residues)

    portions, order, waits = PORTIONS, ORDER, WAITS
    if size != 8:
        waits = {}
        portions = ((tuple(range(len(bits))), 2, 0), (tuple(range(len(bits))), 2, 1))
        order = [
            ((p, s, block),)
            for p in range(2)
            for s, bit in enumerate(bits)
            for block in sorted(range(0, size, 2 * bit), reverse=True)
        ] + [("laps", None), ("sum", 0), ("sum", 1), ("gate", 0), ("gate", 1), ("scan", 1), ("fix", None)]
    offsets = [sum(width // part for _, part, _ in portions[:p]) for p in range(len(portions))]

    received, sums, scanned, states, packed = {}, {}, {}, {}, {}
    grad_query = last = None

    def after(value):
        return value if last is None else lax.optimization_barrier((value, last, *awaited))[0]

    def collect(wanted):
        arrays, places = [], []
        for key in wanted:
            array, *place = received[key]
            index = next((i for i, known in enumerate(arrays) if known is array), len(arrays))
            if index == len(arrays):
                arrays.append(array)
            places.append((index, tuple(place)))
        return arrays, places

    for todo in order:
        awaited = [received[key][0] for key in waits.get(todo, ())]
        kind, half = todo if isinstance(todo[0], str) else ("send", None)
        inside = [q for q, (_, _, lies) in enumerate(portions) if lies == half]
        if kind == "send":
            arrays, items = [], []
            wanted, rows, bits_of = [], [], []
            for p, s, block in todo:
                route, share, _ = portions[p]
                bits_of.append(bits[route[s]])
                rows.append(width // share)
                wanted.append([(p, i, block ^ bits_of[-1]) for i in range(s)])
            bit, count = bits_of[0], len(todo)
            arrays, places = collect([key for keys in wanted for key in keys])
            places = iter(places)
            items = tuple(
                (block ^ bit, offsets[p], rows[i], tuple(next(places) for _ in wanted[i]))
                for i, (p, _, block) in enumerate(todo)
            )
            if last is None:
                last, turned = first_send(items, width, place, out_weight, out_grad)
            else:
                last = send(items, True, width, after(place), out_weight, turned, arrays)
            arrived = lax.ppermute(last, "ch", [(i, i ^ bit) for i in range(size)])
            start = peak = 0
            for i, key in enumerate(todo):
                part = part_of(rows[i], count, folds_of(toks))
                received[key] = (arrived, start, peak, part)
                start, peak = start + rows[i], peak + rows[i] // part
        elif kind == "laps":
            lap, wide = laps(segments, toks, after(decay))
            last = wide
        elif kind == "sum":
            items = tuple((0, offsets[q], width // portions[q][1], ()) for q in inside)
            last = sums[half] = send(items, False, width, after(place), out_weight, turned, [])
        elif kind == "gate":
            stages = range(len(bits))
            arrays, places = collect([(q, i, 0) for q in inside for i in stages])
            pieces = tuple(
                (offsets[q] - half * half_rows, tuple(places[i * len(stages) : (i + 1) * len(stages)]))
                for i, q in enumerate(inside)
            )
            other = residue if half == 0 else packed[0]
            grad_query, scanned[half], states[half], packed[half] = gate(
                half,
                half_rows,
                segments,
                pieces,
                after(sums[half]),
                arrays,
                query_in,
                conv_out,
                decay,
                lap,
                other,
                grad_query,
            )
            last = packed[half]
        elif kind == "scan":
            groups = lax.axis_size("ctx")
            swap = lambda array, round_: lax.ppermute(array, "ctx", [(i, i ^ (1 << round_)) for i in range(groups)])
            arrived, joined = [swap(packed[1], 0)], packed[1]
            rounds = groups.bit_length() - 1
            for round_ in range(1, rounds):
                last, *joined = join(round_ - 1, after(group), joined, arrived[-1], wide, round_ + 1 == rounds)
                joined = joined[0] if joined else None
                arrived.append(swap(last, round_))
            scanned[1] = scan(1, segments, after(scanned[1]), states[1], decay, lap, residue)
        else:
            grad_input = fix(
                segments, group, [scanned[0], scanned[1]], states[0], arrived, decay, lap, wide, residue, toks, width
            )
    return grad_query, grad_input


def solution(mesh):
    placed = (
        P("ctx", "ch"),
        P(None, "ch"),
        P("ctx", "ch"),
        P("ctx", "ch"),
        P("ch", None),
        P("ch", None),
    )
    return jax.shard_map(
        local,
        mesh=mesh,
        in_specs=placed,
        out_specs=(P("ctx", "ch"), P("ctx", "ch")),
        check_vma=False,
    )
```

```python
import functools
import math

import jax
import jax.numpy as jnp
from jax import lax
from jax.experimental import pallas as pl
from jax.experimental.pallas import tpu as pltpu
from jax.sharding import PartitionSpec as P

PEAKS = 16
SPAN = 251 * math.log(2.0)
SHIFT = 125 * math.log(2.0)
STEP = 256
PIECE = 128
GAP = 8
VMEM = 24 * 1024 * 1024
QUICK = pl.CostEstimate(flops=0, bytes_accessed=1024, transcendentals=0)

PORTIONS = (((0, 1, 2), 4, 0), ((1, 0, 2), 4, 0), ((0, 1, 2), 4, 1), ((0, 1, 2), 4, 1))
ORDER = (
    ((0, 0, 6), (0, 0, 2)), ("both", ((1, 0, 5), (1, 0, 1)), ((2, 0, 6), (3, 0, 6))), ("sum", 1), ((2, 0, 2), (3, 0, 2)),
    ((2, 0, 4), (3, 0, 4)), ((1, 0, 4), (0, 1, 4)), ((1, 1, 4), (0, 0, 4)), ((2, 1, 4), (3, 1, 4)),
    ((1, 0, 0), (0, 1, 0)), ((0, 2, 0), (1, 2, 0)), ((2, 2, 0), (3, 2, 0)), ((1, 1, 0), (0, 0, 0)),
    ((2, 1, 0), (3, 1, 0)), ((2, 0, 0), (3, 0, 0)), ("sum", 0), ("laps", None), ("gate", 0), ("gate", 1), ("scan", 1),
    ("fix", None),
)
WAITS = {
    ((1, 0, 0), (0, 1, 0)): ((1, 0, 4),),
    ("gate", 0): ((0, 2, 0), (1, 0, 0)),
    ("gate", 1): ((2, 2, 0), (2, 1, 0)),
}


def folds_of(toks):
    return toks // 128 if toks % 128 == 0 and PEAKS % (toks // 128) == 0 else 1


def part_of(rows, blocks, folds):
    return next(
        part for part in range(16, rows + 1, 16) if rows % part == 0 and rows // part * blocks * folds <= PEAKS
    )


def step_of(rows):
    return next(step for step in (STEP, STEP // 2, rows) if rows % step == 0)


def encode(block, part):
    codes, peaks = [], []
    for i in range(block.shape[0] // part):
        piece = block[i * part : (i + 1) * part, :]
        size = jnp.abs(piece)
        peak = jnp.maximum(jnp.max(size, axis=0, keepdims=True) * 1.01, 1e-30)
        peak = peak.astype(jnp.bfloat16).astype(jnp.float32)
        code = jnp.exp(size * (SPAN / peak) - SHIFT)
        codes.append(jnp.where(piece < 0, -code, code))
        peaks.append(peak)
    return jnp.concatenate(codes, axis=0).astype(jnp.bfloat16), peaks


def put(codes, out_ref, at):
    lanes = out_ref.shape[1]
    folds = codes.shape[1] // lanes
    rows = (out_ref.shape[0] - PEAKS) // folds
    for fold in range(folds):
        out_ref[fold * rows + at : fold * rows + at + codes.shape[0], :] = codes[:, fold * lanes : (fold + 1) * lanes]


def put_peaks(peaks, out_ref):
    lanes = out_ref.shape[1]
    peaks = [peak[:, at : at + lanes] for peak in peaks for at in range(0, peak.shape[1], lanes)]
    if len(peaks) < PEAKS:
        peaks.append(jnp.zeros((PEAKS - len(peaks), lanes), jnp.float32))
    out_ref[out_ref.shape[0] - PEAKS :, :] = jnp.concatenate(peaks, axis=0).astype(jnp.bfloat16)


def decode(ref, place, first, count, folds):
    start, peak, part = place
    rows = (ref.shape[0] - PEAKS) // folds
    peaks = ref[ref.shape[0] - PEAKS :, :].astype(jnp.float32) * (1.0 / SPAN)
    columns = []
    for fold in range(folds):
        blocks = []
        for i in range(first // part, -(-(first + count) // part)):
            low, high = max(first, i * part), min(first + count, (i + 1) * part)
            code = ref[fold * rows + start + low : fold * rows + start + high, :].astype(jnp.float32)
            at = (peak + i) * folds + fold
            size = (jnp.log(jnp.abs(code)) + SHIFT) * peaks[at : at + 1, :]
            blocks.append(jnp.where(code < 0, -size, size))
        columns.append(jnp.concatenate(blocks, axis=0))
    return jnp.concatenate(columns, axis=1)


def pinned(array):
    return pltpu.with_memory_space_constraint(array, pltpu.HBM)


def send_kernel(items, coded, width, near, place_ref, w_ref, turned_ref, *refs):
    near_refs, out_ref = refs[:near], refs[near]
    folds = folds_of(turned_ref.shape[1])
    base, peaks = 0, []
    for block, offset, rows, sources in items:
        step = step_of(rows)
        first = (place_ref[0] ^ block) * width + offset
        for at in range(0, rows, step):
            total = jnp.dot(
                w_ref[pl.ds(pl.multiple_of(first + at, 16), step), :],
                turned_ref[...],
                preferred_element_type=jnp.float32,
            )
            for source, place in sources:
                total = total + decode(near_refs[source], place, at, step, folds)
            if coded:
                total, more = encode(total, part_of(rows, len(items), folds))
                peaks += more
                put(total, out_ref, base + at)
            else:
                out_ref[base + at : base + at + step, :] = total
        base += rows
    if coded:
        put_peaks(peaks, out_ref)


def send(items, coded, width, place, weight, turned, nears):
    toks = turned.shape[1]
    vmem = pl.BlockSpec(memory_space=pltpu.VMEM)
    count = sum(rows for _, _, rows, _ in items)
    folds = folds_of(toks)
    shape = (folds * count + PEAKS, toks // folds) if coded else (count, toks)
    return pl.pallas_call(
        functools.partial(send_kernel, items, coded, width, len(nears)),
        in_specs=[pl.BlockSpec(memory_space=pltpu.SMEM)] + [vmem] * (2 + len(nears)),
        out_specs=vmem,
        out_shape=jax.ShapeDtypeStruct(shape, jnp.bfloat16 if coded else jnp.float32),
        compiler_params=pltpu.CompilerParams(vmem_limit_bytes=VMEM),
        cost_estimate=QUICK,
    )(place, weight, turned, *nears)


def early_kernel(messages, width, turns, place_ref, w_hbm, g_ref, *refs):
    out_refs, refs = refs[: len(messages)], refs[len(messages) :]
    w_ref, sems = refs[-2:]
    turned_ref = refs[0] if turns else g_ref
    depth, toks = turned_ref.shape
    copies, waits = [], []
    if turns:
        piece = math.gcd(toks, PIECE)
        for at in range(0, toks, piece):
            lines = pl.ds(at, piece)
            copies.append(pltpu.make_async_copy(g_ref.at[lines, :], refs[1].at[lines, :], sems.at[len(copies)]))
    grads, base = len(copies), 0
    for items in messages:
        for block, offset, rows, _ in items:
            step = math.gcd(rows, PIECE)
            first = pl.multiple_of((place_ref[0] ^ block) * width + offset, 16)
            for at in range(0, rows, step):
                copies.append(
                    pltpu.make_async_copy(
                        w_hbm.at[pl.ds(first + at, step), :], w_ref.at[pl.ds(base + at, step), :], sems.at[len(copies)]
                    )
                )
            base += rows
    for copy in copies:
        copy.start(priority=1)
    for i in range(grads):
        copies[i].wait()
        turned_ref[:, i * piece : (i + 1) * piece] = refs[1][i * piece : (i + 1) * piece, :].T
    waits, base = iter(copies[grads:]), 0
    for items, out_ref in zip(messages, out_refs):
        start, peaks = base, []
        for _, _, rows, _ in items:
            step = step_of(rows)
            for at in range(base, base + rows, step):
                for _ in range(step // math.gcd(rows, PIECE)):
                    next(waits).wait()
                total = jnp.dot(w_ref[at : at + step, :], turned_ref[...], preferred_element_type=jnp.float32)
                total, more = encode(total, part_of(rows, len(items), folds_of(toks)))
                peaks += more
                put(total, out_ref, at - start)
            base += rows
        put_peaks(peaks, out_ref)


def early_send(messages, width, place, weight, grad, turns):
    toks, depth = grad.shape if turns else grad.shape[::-1]
    vmem = pl.BlockSpec(memory_space=pltpu.VMEM)
    high = pl.BlockSpec(memory_space=pltpu.HBM)
    counts = [sum(rows for _, _, rows, _ in items) for items in messages]
    folds = folds_of(toks)
    steps = sum(rows // math.gcd(rows, PIECE) for items in messages for _, _, rows, _ in items)
    steps += toks // math.gcd(toks, PIECE) if turns else 0
    coded = [jax.ShapeDtypeStruct((folds * count + PEAKS, toks // folds), jnp.bfloat16) for count in counts]
    return pl.pallas_call(
        functools.partial(early_kernel, messages, width, turns),
        in_specs=[pl.BlockSpec(memory_space=pltpu.SMEM), high, high if turns else vmem],
        out_specs=[vmem] * (len(messages) + turns),
        out_shape=coded + [jax.ShapeDtypeStruct((depth, toks), jnp.bfloat16)] * turns,
        scratch_shapes=[pltpu.VMEM((toks, depth), jnp.bfloat16)] * turns
        + [pltpu.VMEM((sum(counts), depth), jnp.bfloat16), pltpu.SemaphoreType.DMA((steps,))],
        compiler_params=pltpu.CompilerParams(vmem_limit_bytes=VMEM),
        cost_estimate=QUICK,
    )(place, pinned(weight), pinned(grad) if turns else grad)


def steps_back(count, body, state, unroll):
    unroll = math.gcd(count, unroll)

    def some(i, state):
        for j in range(unroll):
            state = body(count - 1 - (i * unroll + j), state)
        return state

    return lax.fori_loop(0, count // unroll, some, state)


def power(base, exponent):
    result = None
    while exponent:
        if exponent % 2:
            result = base if result is None else result * base
        base = base * base
        exponent //= 2
    return result


def segment_of(shape, segments):
    return lax.rem(lax.broadcasted_iota(jnp.int32, shape, 0), segments)


def rolled(value, by):
    by %= value.shape[0]
    return pltpu.roll(value, by, 0) if by else value


def gate_kernel(half, rows, segments, pieces, near, acc_ref, *refs):
    near_refs, refs = refs[:near], refs[near:]
    query_ref, conv_ref, decay_ref, lap_ref, other_ref = refs[:5]
    out_hbm, rows_ref, state_ref, pack_ref = refs[-7:-3] if half == 0 else refs[-6:-2]
    gq_ref, sem = refs[-2:]
    gc_ref = refs[-3] if half == 0 else rows_ref
    toks = query_ref.shape[0]
    modes, sublanes, lanes = state_ref.shape
    mine = slice(half * sublanes, (half + 1) * sublanes)
    for line in range(rows // lanes):
        mix = acc_ref[line * lanes : (line + 1) * lanes, :]
        first, sources = next(piece for piece in reversed(pieces) if piece[0] <= line * lanes)
        for source, place in sources:
            mix = mix + decode(near_refs[source], place, line * lanes - first, lanes, folds_of(toks))
        mix = mix.T
        at = slice(line * lanes, (line + 1) * lanes)
        full = slice(half * rows + line * lanes, half * rows + (line + 1) * lanes)
        gq_ref[:, at] = (mix * conv_ref[:, full].astype(jnp.float32)).astype(jnp.bfloat16)
        gated = mix * query_ref[:, full].astype(jnp.float32)
        for k in range(segments):
            start = (line * segments + k) * (toks // segments + GAP)
            gc_ref[start : start + toks // segments, :] = gated[k * (toks // segments) : (k + 1) * (toks // segments), :]
    store = pltpu.make_async_copy(gq_ref, out_hbm.at[:, pl.ds(half * rows, rows)], sem)
    store.start()
    decay = [decay_ref[n, mine] for n in range(modes)]
    span = toks // segments

    def step(t, state):
        at = pl.ds(t, sublanes, stride=span + GAP)
        row = gc_ref[at, :]
        state = tuple(decay[n] * state[n] + row for n in range(modes))
        if half == 0:
            rows_ref[at, :] = summed([other_ref[n, mine] * state[n] for n in range(modes)])
        return state

    zero = jnp.zeros((sublanes, lanes), jnp.float32)
    state = steps_back(span, step, (zero,) * modes, 16)
    segment = segment_of((sublanes, lanes), segments)
    whole = []
    for n in range(modes):
        state_ref[n] = state[n]
        total = state[n]
        if segments > 1:
            factor = jnp.where(segment < segments - 1, lap_ref[n, mine], 0.0)
            for _ in range(segments - 1):
                total = state[n] + factor * rolled(total, -1)
        whole.append(total)
    packs = modes // segments
    for m in range(packs):
        packed = whole[m * segments]
        for j in range(1, segments):
            packed = jnp.where(segment == j, rolled(whole[m * segments + j], j), packed)
        if half == 0:
            pack_ref[m] = packed
        else:
            pack_ref[m] = other_ref[m]
            pack_ref[packs + m] = packed
    store.wait()


def gate(half, rows, segments, pieces, acc, nears, query_in, conv_out, decay, lap, other, partial):
    toks, width = query_in.shape
    modes, _, lanes = decay.shape
    sublanes = rows // lanes * segments
    vmem = pl.BlockSpec(memory_space=pltpu.VMEM)
    high = pl.BlockSpec(memory_space=pltpu.HBM)
    more = [] if partial is None else [partial]
    lines = (sublanes * (toks // segments + GAP), lanes)
    return pl.pallas_call(
        functools.partial(gate_kernel, half, rows, segments, pieces, len(nears)),
        in_specs=[vmem] * (6 + len(nears)) + [high] * len(more),
        out_specs=(high, vmem, vmem, vmem),
        out_shape=(
            jax.ShapeDtypeStruct((toks, width), jnp.bfloat16),
            jax.ShapeDtypeStruct(lines, jnp.float32),
            jax.ShapeDtypeStruct((modes, sublanes, lanes), jnp.float32),
            jax.ShapeDtypeStruct(((1 + half) * modes // segments, sublanes, lanes), jnp.float32),
        ),
        scratch_shapes=([pltpu.VMEM(lines, jnp.float32)] if half == 0 else [])
        + [pltpu.VMEM((toks, rows), jnp.bfloat16), pltpu.SemaphoreType.DMA],
        input_output_aliases={6 + len(nears): 0} if more else {},
        compiler_params=pltpu.CompilerParams(vmem_limit_bytes=VMEM),
        cost_estimate=QUICK,
    )(acc, *nears, query_in, conv_out, decay, lap, other, *more)


def summed(terms):
    while len(terms) > 1:
        terms = [terms[k] + terms[k + 1] if k + 1 < len(terms) else terms[k] for k in range(0, len(terms), 2)]
    return terms[0]


def scan_kernel(half, segments, gc_ref, state_ref, decay_ref, lap_ref, residue_ref, rows_ref):
    modes, sublanes, lanes = state_ref.shape
    mine = slice(half * sublanes, (half + 1) * sublanes)
    span = gc_ref.shape[0] // sublanes - GAP
    segment = segment_of((sublanes, lanes), segments)
    decay = [decay_ref[n, mine] for n in range(modes)]
    start = []
    for n in range(modes):
        total = jnp.zeros((sublanes, lanes), jnp.float32)
        if segments > 1:
            for k in range(segments - 2, -1, -1):
                total = jnp.where(segment == k, rolled(state_ref[n] + lap_ref[n, mine] * total, -1), total)
        start.append(total)

    def step(t, state):
        at = pl.ds(t, sublanes, stride=span + GAP)
        row = gc_ref[at, :]
        state = tuple(decay[n] * state[n] + row for n in range(modes))
        rows_ref[at, :] = summed([residue_ref[n, mine] * state[n] for n in range(modes)])
        return state

    steps_back(span, step, tuple(start), 16)


def scan(half, segments, grad_conv, state, decay, lap, residues):
    vmem = pl.BlockSpec(memory_space=pltpu.VMEM)
    return pl.pallas_call(
        functools.partial(scan_kernel, half, segments),
        in_specs=[vmem] * 5,
        out_specs=vmem,
        out_shape=jax.ShapeDtypeStruct(grad_conv.shape, jnp.float32),
        compiler_params=pltpu.CompilerParams(vmem_limit_bytes=VMEM),
        cost_estimate=QUICK,
    )(grad_conv, state, decay, lap, residues)


def laps_kernel(segments, span, decay_ref, lap_ref, wide_ref):
    modes, sublanes, lanes = decay_ref.shape
    sublanes //= 2
    packs = modes // segments
    segment = segment_of((sublanes, lanes), segments)
    for half in range(2):
        mine = slice(half * sublanes, (half + 1) * sublanes)
        for m in range(packs):
            packed = None
            for j in range(segments):
                lap = power(decay_ref[m * segments + j, mine], span)
                lap_ref[m * segments + j, mine] = lap
                wide = power(lap, segments)
                packed = wide if packed is None else jnp.where(segment == j, wide, packed)
            wide_ref[half * packs + m] = packed


def laps(segments, toks, decay):
    modes, sublanes, lanes = decay.shape
    vmem = pl.BlockSpec(memory_space=pltpu.VMEM)
    return pl.pallas_call(
        functools.partial(laps_kernel, segments, toks // segments),
        in_specs=[vmem],
        out_specs=(vmem, vmem),
        out_shape=(
            jax.ShapeDtypeStruct(decay.shape, jnp.float32),
            jax.ShapeDtypeStruct((2 * modes // segments, sublanes // 2, lanes), jnp.float32),
        ),
        compiler_params=pltpu.CompilerParams(vmem_limit_bytes=VMEM),
        cost_estimate=QUICK,
    )(decay)


def states_in(ref, shape):
    if ref.shape == shape:
        return [ref[m] for m in range(shape[0])]
    packs, sublanes, _ = shape
    rows = decode(ref, (0, 0, packs * sublanes // 2), 0, packs * sublanes, 1)
    return [rows[m * sublanes : (m + 1) * sublanes, :] for m in range(packs)]


def join_kernel(round_, group_ref, state_ref, arrived_ref, wide_ref, coded_ref, *out_refs):
    earlier = (group_ref[0] >> round_) % 2 == 0
    packs, sublanes, _ = state_ref.shape
    joined = []
    for m, other in enumerate(states_in(arrived_ref, state_ref.shape)):
        wide = power(wide_ref[m], 1 << round_)
        mine = state_ref[m]
        joined.append(jnp.where(earlier, mine + wide * other, other + wide * mine))
        for out_ref in out_refs:
            out_ref[m] = joined[-1]
    codes, peaks = encode(jnp.concatenate(joined, axis=0), packs * sublanes // 2)
    put(codes, coded_ref, 0)
    put_peaks(peaks, coded_ref)


def join(round_, group, state, arrived, wide, last):
    vmem = pl.BlockSpec(memory_space=pltpu.VMEM)
    packs, sublanes, lanes = state.shape
    return pl.pallas_call(
        functools.partial(join_kernel, round_),
        in_specs=[pl.BlockSpec(memory_space=pltpu.SMEM)] + [vmem] * 3,
        out_specs=[vmem] * (1 if last else 2),
        out_shape=[
            jax.ShapeDtypeStruct((packs * sublanes + PEAKS, lanes), jnp.bfloat16),
            jax.ShapeDtypeStruct(state.shape, jnp.float32),
        ][: 1 if last else 2],
        compiler_params=pltpu.CompilerParams(vmem_limit_bytes=VMEM),
        cost_estimate=QUICK,
    )(group, state, arrived, wide)


def fix_kernel(segments, rounds, group_ref, *refs):
    scanned_refs, state_ref, arrived_refs = refs[:2], refs[2], refs[3 : 3 + rounds]
    decay_ref, lap_ref, wide_ref, residue_ref, out_hbm, rows_ref, out_ref, sems = refs[3 + rounds :]
    toks, width = out_ref.shape
    modes, sublanes, lanes = state_ref.shape
    packs = modes // segments
    rows = width // 2
    span = toks // segments
    segment = segment_of((sublanes, lanes), segments)
    earlier = [(group_ref[0] >> r) % 2 == 0 for r in range(rounds)]
    arrived = [states_in(ref, (2 * packs, sublanes, lanes)) for ref in arrived_refs]
    stores = []
    for half in range(2):
        mine = slice(half * sublanes, (half + 1) * sublanes)
        decay = [decay_ref[n, mine] for n in range(modes)]
        start = []
        for m in range(packs):
            brought = jnp.zeros((sublanes, lanes), jnp.float32)
            between = jnp.ones((sublanes, lanes), jnp.float32)
            for r in range(rounds):
                state = arrived[r][half * packs + m]
                brought = jnp.where(earlier[r], brought + between * state, brought)
                if r + 1 < rounds:
                    between = jnp.where(earlier[r], between * power(wide_ref[half * packs + m], 1 << r), between)
            for j in range(segments):
                n = m * segments + j
                total = rolled(brought, segments - 1 - j)
                for k in range(segments - 2, -1, -1):
                    before = lap_ref[n, mine] * total
                    if half == 0:
                        before = before + state_ref[n]
                    total = jnp.where(segment == k, rolled(before, -1), total)
                start.append(residue_ref[n, mine] * total)

        def step(t, state, scanned_ref=scanned_refs[half], decay=decay):
            at = pl.ds(t, sublanes, stride=span + GAP)
            state = tuple(decay[n] * state[n] for n in range(modes))
            rows_ref[at, :] = scanned_ref[at, :] + summed(list(state))
            return state

        steps_back(span, step, tuple(start), 16)
        for line in range(rows // lanes):
            at = slice(half * rows + line * lanes, half * rows + (line + 1) * lanes)
            for k in range(segments):
                start = (line * segments + k) * (span + GAP)
                out_ref[k * span : (k + 1) * span, at] = rows_ref[start : start + span, :].astype(jnp.bfloat16)
        columns = pl.ds(half * rows, rows)
        stores.append(pltpu.make_async_copy(out_ref.at[:, columns], out_hbm.at[:, columns], sems.at[half]))
        stores[-1].start()
    for store in stores:
        store.wait()


def fix(segments, group, scanned, state, arrived, decay, lap, wide, residues, toks, width):
    vmem = pl.BlockSpec(memory_space=pltpu.VMEM)
    return pl.pallas_call(
        functools.partial(fix_kernel, segments, len(arrived)),
        in_specs=[pl.BlockSpec(memory_space=pltpu.SMEM)] + [vmem] * (7 + len(arrived)),
        out_specs=pl.BlockSpec(memory_space=pltpu.HBM),
        out_shape=jax.ShapeDtypeStruct((toks, width), jnp.bfloat16),
        scratch_shapes=[
            pltpu.VMEM(scanned[0].shape, jnp.float32),
            pltpu.VMEM((toks, width), jnp.bfloat16),
            pltpu.SemaphoreType.DMA((2,)),
        ],
        compiler_params=pltpu.CompilerParams(vmem_limit_bytes=VMEM),
        cost_estimate=QUICK,
    )(group, *scanned, state, *arrived, decay, lap, wide, residues)


def local(out_grad, out_weight, query_in, conv_out, residues, decay_rates):
    toks, width = query_in.shape
    modes = decay_rates.shape[1]
    lanes = math.gcd(width, 128)
    size, groups = lax.axis_size("ch"), lax.axis_size("ctx")
    bits = [1 << i for i in range(size.bit_length() - 1)]
    place = jnp.reshape(lax.axis_index("ch"), (1,)).astype(jnp.int32)
    group = jnp.reshape(lax.axis_index("ctx"), (1,)).astype(jnp.int32)
    half_rows = width // 2
    lines = half_rows // lanes
    segments = 8 // lines
    by_mode = lambda values: jnp.repeat(values.T.reshape(modes, width // lanes, lanes), segments, axis=1)
    decay, residue = by_mode(decay_rates), by_mode(residues)

    portions, order, waits = PORTIONS, ORDER, WAITS
    if size != 8:
        waits = {}
        portions = ((tuple(range(len(bits))), 2, 0), (tuple(range(len(bits))), 2, 1))
        order = [
            ((p, s, block),)
            for p in range(2)
            for s, bit in enumerate(bits)
            for block in sorted(range(0, size, 2 * bit), reverse=True)
        ] + [("laps", None), ("sum", 0), ("sum", 1), ("gate", 0), ("gate", 1), ("scan", 1), ("fix", None)]
    offsets = [sum(width // part for _, part, _ in portions[:p]) for p in range(len(portions))]

    received, sums, scanned, states, packed = {}, {}, {}, {}, {}
    grad_query = last = None

    def after(value):
        return value if last is None else lax.optimization_barrier((value, last, *awaited))[0]

    def collect(wanted):
        arrays, places = [], []
        for key in wanted:
            array, *place = received[key]
            index = next((i for i, known in enumerate(arrays) if known is array), len(arrays))
            if index == len(arrays):
                arrays.append(array)
            places.append((index, tuple(place)))
        return arrays, places

    for todo in order:
        awaited = [received[key][0] for key in waits.get(todo, ())]
        kind, half = todo[:2] if isinstance(todo[0], str) else ("send", None)
        inside = [q for q, (_, _, lies) in enumerate(portions) if lies == half]
        if kind in ("send", "both"):
            messages = todo[1:] if kind == "both" else (todo,)
            bit_of = lambda key: bits[portions[key[0]][0][key[1]]]
            arrays, planned = [], []
            for message in messages:
                wanted = [[(p, i, block ^ bit_of((p, s, block))) for i in range(s)] for p, s, block in message]
                arrays, places = collect([key for keys in wanted for key in keys])
                places = iter(places)
                planned.append(
                    tuple(
                        (block ^ bit_of((p, s, block)), offsets[p], width // portions[p][1], tuple(next(places) for _ in keys))
                        for (p, s, block), keys in zip(message, wanted)
                    )
                )
            if last is None:
                *payloads, turned = early_send(planned, width, place, out_weight, out_grad, True)
            elif kind == "both":
                payloads = early_send(planned, width, after(place), out_weight, turned, False)
            else:
                payloads = [send(planned[0], True, width, after(place), out_weight, turned, arrays)]
            last = payloads[0]
            for message, items, payload in zip(messages, planned, payloads):
                bit = bit_of(message[0])
                arrived = lax.ppermute(payload, "ch", [(i, i ^ bit) for i in range(size)])
                start = peak = 0
                for key, (_, _, rows, _) in zip(message, items):
                    part = part_of(rows, len(items), folds_of(toks))
                    received[key] = (arrived, start, peak, part)
                    start, peak = start + rows, peak + rows // part
        elif kind == "laps":
            lap, wide = laps(segments, toks, after(decay))
            last = wide
        elif kind == "sum":
            items = tuple((0, offsets[q], width // portions[q][1], ()) for q in inside)
            last = sums[half] = send(items, False, width, after(place), out_weight, turned, [])
        elif kind == "gate":
            stages = range(len(bits))
            arrays, places = collect([(q, i, 0) for q in inside for i in stages])
            pieces = tuple(
                (offsets[q] - half * half_rows, tuple(places[i * len(stages) : (i + 1) * len(stages)]))
                for i, q in enumerate(inside)
            )
            other = residue if half == 0 else packed[0]
            grad_query, scanned[half], states[half], packed[half] = gate(
                half,
                half_rows,
                segments,
                pieces,
                after(sums[half]),
                arrays,
                query_in,
                conv_out,
                decay,
                lap,
                other,
                grad_query,
            )
            last = packed[half]
        elif kind == "scan":
            groups = lax.axis_size("ctx")
            swap = lambda array, round_: lax.ppermute(array, "ctx", [(i, i ^ (1 << round_)) for i in range(groups)])
            arrived, joined = [swap(packed[1], 0)], packed[1]
            rounds = groups.bit_length() - 1
            for round_ in range(1, rounds):
                last, *joined = join(round_ - 1, after(group), joined, arrived[-1], wide, round_ + 1 == rounds)
                joined = joined[0] if joined else None
                arrived.append(swap(last, round_))
            scanned[1] = scan(1, segments, after(scanned[1]), states[1], decay, lap, residue)
        else:
            grad_input = fix(
                segments, group, [scanned[0], scanned[1]], states[0], arrived, decay, lap, wide, residue, toks, width
            )
    return grad_query, grad_input


def solution(mesh):
    placed = (
        P("ctx", "ch"),
        P(None, "ch"),
        P("ctx", "ch"),
        P("ctx", "ch"),
        P("ch", None),
        P("ch", None),
    )
    return jax.shard_map(
        local,
        mesh=mesh,
        in_specs=placed,
        out_specs=(P("ctx", "ch"), P("ctx", "ch")),
        check_vma=False,
    )
```

```python
import functools
import math

import jax
import jax.numpy as jnp
from jax import lax
from jax.experimental import pallas as pl
from jax.experimental.pallas import tpu as pltpu
from jax.sharding import PartitionSpec as P

PEAKS = 16
SPAN = 251 * math.log(2.0)
SHIFT = 125 * math.log(2.0)
STEP = 256
PIECE = 128
GAP = 8
VMEM = 24 * 1024 * 1024
QUICK = pl.CostEstimate(flops=0, bytes_accessed=1024, transcendentals=0)

PORTIONS = (((0, 1, 2), 4, 0), ((1, 0, 2), 4, 0), ((0, 1, 2), 4, 1), ((0, 1, 2), 4, 1))
ORDER = (
    ((0, 0, 6), (0, 0, 2)), ("both", ((1, 0, 5), (1, 0, 1))), ((2, 0, 6), (3, 0, 6)), ((2, 0, 4), (3, 0, 4)), ("sum", 1), ((2, 0, 2), (3, 0, 2)),
    ((1, 0, 4), (0, 1, 4)), ((1, 1, 4), (0, 0, 4)), ((2, 1, 4), (3, 1, 4)),
    ((1, 0, 0), (0, 1, 0)), ((0, 2, 0), (1, 2, 0)), ((2, 2, 0), (3, 2, 0)), ((1, 1, 0), (0, 0, 0)),
    ((2, 1, 0), (3, 1, 0)), ((2, 0, 0), (3, 0, 0)), ("sum", 0), ("laps", None), ("gate", 0), ("gate", 1), ("scan", 1),
    ("fix", None),
)
WAITS = {
    ((1, 0, 0), (0, 1, 0)): ((1, 0, 4),),
    ("gate", 0): ((0, 2, 0), (1, 0, 0)),
    ("gate", 1): ((2, 2, 0), (2, 1, 0)),
}


def folds_of(toks):
    return toks // 128 if toks % 128 == 0 and PEAKS % (toks // 128) == 0 else 1


def part_of(rows, blocks, folds):
    return next(
        part for part in range(16, rows + 1, 16) if rows % part == 0 and rows // part * blocks * folds <= PEAKS
    )


def step_of(rows):
    return next(step for step in (STEP, STEP // 2, rows) if rows % step == 0)


def encode(block, part):
    codes, peaks = [], []
    for i in range(block.shape[0] // part):
        piece = block[i * part : (i + 1) * part, :]
        size = jnp.abs(piece)
        peak = jnp.maximum(jnp.max(size, axis=0, keepdims=True) * 1.01, 1e-30)
        peak = peak.astype(jnp.bfloat16).astype(jnp.float32)
        code = jnp.exp(size * (SPAN / peak) - SHIFT)
        codes.append(jnp.where(piece < 0, -code, code))
        peaks.append(peak)
    return jnp.concatenate(codes, axis=0).astype(jnp.bfloat16), peaks


def put(codes, out_ref, at):
    lanes = out_ref.shape[1]
    folds = codes.shape[1] // lanes
    rows = (out_ref.shape[0] - PEAKS) // folds
    for fold in range(folds):
        out_ref[fold * rows + at : fold * rows + at + codes.shape[0], :] = codes[:, fold * lanes : (fold + 1) * lanes]


def put_peaks(peaks, out_ref):
    lanes = out_ref.shape[1]
    peaks = [peak[:, at : at + lanes] for peak in peaks for at in range(0, peak.shape[1], lanes)]
    if len(peaks) < PEAKS:
        peaks.append(jnp.zeros((PEAKS - len(peaks), lanes), jnp.float32))
    out_ref[out_ref.shape[0] - PEAKS :, :] = jnp.concatenate(peaks, axis=0).astype(jnp.bfloat16)


def decode(ref, place, first, count, folds):
    start, peak, part = place
    rows = (ref.shape[0] - PEAKS) // folds
    peaks = ref[ref.shape[0] - PEAKS :, :].astype(jnp.float32) * (1.0 / SPAN)
    columns = []
    for fold in range(folds):
        blocks = []
        for i in range(first // part, -(-(first + count) // part)):
            low, high = max(first, i * part), min(first + count, (i + 1) * part)
            code = ref[fold * rows + start + low : fold * rows + start + high, :].astype(jnp.float32)
            at = (peak + i) * folds + fold
            size = (jnp.log(jnp.abs(code)) + SHIFT) * peaks[at : at + 1, :]
            blocks.append(jnp.where(code < 0, -size, size))
        columns.append(jnp.concatenate(blocks, axis=0))
    return jnp.concatenate(columns, axis=1)


def pinned(array):
    return pltpu.with_memory_space_constraint(array, pltpu.HBM)


def send_kernel(items, coded, width, near, place_ref, w_ref, turned_ref, *refs):
    near_refs, out_ref = refs[:near], refs[near]
    folds = folds_of(turned_ref.shape[1])
    base, peaks = 0, []
    for block, offset, rows, sources in items:
        step = step_of(rows)
        first = (place_ref[0] ^ block) * width + offset
        for at in range(0, rows, step):
            total = jnp.dot(
                w_ref[pl.ds(pl.multiple_of(first + at, 16), step), :],
                turned_ref[...],
                preferred_element_type=jnp.float32,
            )
            for source, place in sources:
                total = total + decode(near_refs[source], place, at, step, folds)
            if coded:
                total, more = encode(total, part_of(rows, len(items), folds))
                peaks += more
                put(total, out_ref, base + at)
            else:
                out_ref[base + at : base + at + step, :] = total
        base += rows
    if coded:
        put_peaks(peaks, out_ref)


def send(items, coded, width, place, weight, turned, nears):
    toks = turned.shape[1]
    vmem = pl.BlockSpec(memory_space=pltpu.VMEM)
    count = sum(rows for _, _, rows, _ in items)
    folds = folds_of(toks)
    shape = (folds * count + PEAKS, toks // folds) if coded else (count, toks)
    return pl.pallas_call(
        functools.partial(send_kernel, items, coded, width, len(nears)),
        in_specs=[pl.BlockSpec(memory_space=pltpu.SMEM)] + [vmem] * (2 + len(nears)),
        out_specs=vmem,
        out_shape=jax.ShapeDtypeStruct(shape, jnp.bfloat16 if coded else jnp.float32),
        compiler_params=pltpu.CompilerParams(vmem_limit_bytes=VMEM),
        cost_estimate=QUICK,
    )(place, weight, turned, *nears)


def early_kernel(messages, width, turns, place_ref, w_hbm, g_ref, *refs):
    out_refs, refs = refs[: len(messages)], refs[len(messages) :]
    w_ref, sems = refs[-2:]
    turned_ref = refs[0] if turns else g_ref
    depth, toks = turned_ref.shape
    copies, waits = [], []
    if turns:
        piece = math.gcd(toks, PIECE)
        for at in range(0, toks, piece):
            lines = pl.ds(at, piece)
            copies.append(pltpu.make_async_copy(g_ref.at[lines, :], refs[1].at[lines, :], sems.at[len(copies)]))
    grads, base = len(copies), 0
    for items in messages:
        for block, offset, rows, _ in items:
            step = math.gcd(rows, PIECE)
            first = pl.multiple_of((place_ref[0] ^ block) * width + offset, 16)
            for at in range(0, rows, step):
                copies.append(
                    pltpu.make_async_copy(
                        w_hbm.at[pl.ds(first + at, step), :], w_ref.at[pl.ds(base + at, step), :], sems.at[len(copies)]
                    )
                )
            base += rows
    for copy in copies:
        copy.start(priority=1)
    for i in range(grads):
        copies[i].wait()
        turned_ref[:, i * piece : (i + 1) * piece] = refs[1][i * piece : (i + 1) * piece, :].T
    waits, base = iter(copies[grads:]), 0
    for items, out_ref in zip(messages, out_refs):
        start, peaks = base, []
        for _, _, rows, _ in items:
            step = step_of(rows)
            for at in range(base, base + rows, step):
                for _ in range(step // math.gcd(rows, PIECE)):
                    next(waits).wait()
                total = jnp.dot(w_ref[at : at + step, :], turned_ref[...], preferred_element_type=jnp.float32)
                total, more = encode(total, part_of(rows, len(items), folds_of(toks)))
                peaks += more
                put(total, out_ref, at - start)
            base += rows
        put_peaks(peaks, out_ref)


def early_send(messages, width, place, weight, grad, turns):
    toks, depth = grad.shape if turns else grad.shape[::-1]
    vmem = pl.BlockSpec(memory_space=pltpu.VMEM)
    high = pl.BlockSpec(memory_space=pltpu.HBM)
    counts = [sum(rows for _, _, rows, _ in items) for items in messages]
    folds = folds_of(toks)
    steps = sum(rows // math.gcd(rows, PIECE) for items in messages for _, _, rows, _ in items)
    steps += toks // math.gcd(toks, PIECE) if turns else 0
    coded = [jax.ShapeDtypeStruct((folds * count + PEAKS, toks // folds), jnp.bfloat16) for count in counts]
    return pl.pallas_call(
        functools.partial(early_kernel, messages, width, turns),
        in_specs=[pl.BlockSpec(memory_space=pltpu.SMEM), high, high if turns else vmem],
        out_specs=[vmem] * (len(messages) + turns),
        out_shape=coded + [jax.ShapeDtypeStruct((depth, toks), jnp.bfloat16)] * turns,
        scratch_shapes=[pltpu.VMEM((toks, depth), jnp.bfloat16)] * turns
        + [pltpu.VMEM((sum(counts), depth), jnp.bfloat16), pltpu.SemaphoreType.DMA((steps,))],
        compiler_params=pltpu.CompilerParams(vmem_limit_bytes=VMEM),
        cost_estimate=QUICK,
    )(place, pinned(weight), pinned(grad) if turns else grad)


def steps_back(count, body, state, unroll):
    unroll = math.gcd(count, unroll)

    def some(i, state):
        for j in range(unroll):
            state = body(count - 1 - (i * unroll + j), state)
        return state

    return lax.fori_loop(0, count // unroll, some, state)


def power(base, exponent):
    result = None
    while exponent:
        if exponent % 2:
            result = base if result is None else result * base
        base = base * base
        exponent //= 2
    return result


def segment_of(shape, segments):
    return lax.rem(lax.broadcasted_iota(jnp.int32, shape, 0), segments)


def rolled(value, by):
    by %= value.shape[0]
    return pltpu.roll(value, by, 0) if by else value


def gate_kernel(half, rows, segments, pieces, near, acc_ref, *refs):
    near_refs, refs = refs[:near], refs[near:]
    query_ref, conv_ref, decay_ref, lap_ref, other_ref = refs[:5]
    out_hbm, rows_ref, state_ref, pack_ref = refs[-7:-3] if half == 0 else refs[-6:-2]
    gq_ref, sem = refs[-2:]
    gc_ref = refs[-3] if half == 0 else rows_ref
    toks = query_ref.shape[0]
    modes, sublanes, lanes = state_ref.shape
    mine = slice(half * sublanes, (half + 1) * sublanes)
    for line in range(rows // lanes):
        mix = acc_ref[line * lanes : (line + 1) * lanes, :]
        first, sources = next(piece for piece in reversed(pieces) if piece[0] <= line * lanes)
        for source, place in sources:
            mix = mix + decode(near_refs[source], place, line * lanes - first, lanes, folds_of(toks))
        mix = mix.T
        at = slice(line * lanes, (line + 1) * lanes)
        full = slice(half * rows + line * lanes, half * rows + (line + 1) * lanes)
        gq_ref[:, at] = (mix * conv_ref[:, full].astype(jnp.float32)).astype(jnp.bfloat16)
        gated = mix * query_ref[:, full].astype(jnp.float32)
        for k in range(segments):
            start = (line * segments + k) * (toks // segments + GAP)
            gc_ref[start : start + toks // segments, :] = gated[k * (toks // segments) : (k + 1) * (toks // segments), :]
    store = pltpu.make_async_copy(gq_ref, out_hbm.at[:, pl.ds(half * rows, rows)], sem)
    store.start()
    decay = [decay_ref[n, mine] for n in range(modes)]
    span = toks // segments

    def step(t, state):
        at = pl.ds(t, sublanes, stride=span + GAP)
        row = gc_ref[at, :]
        state = tuple(decay[n] * state[n] + row for n in range(modes))
        if half == 0:
            rows_ref[at, :] = summed([other_ref[n, mine] * state[n] for n in range(modes)])
        return state

    zero = jnp.zeros((sublanes, lanes), jnp.float32)
    state = steps_back(span, step, (zero,) * modes, 16)
    segment = segment_of((sublanes, lanes), segments)
    whole = []
    for n in range(modes):
        state_ref[n] = state[n]
        total = state[n]
        if segments > 1:
            factor = jnp.where(segment < segments - 1, lap_ref[n, mine], 0.0)
            for _ in range(segments - 1):
                total = state[n] + factor * rolled(total, -1)
        whole.append(total)
    packs = modes // segments
    for m in range(packs):
        packed = whole[m * segments]
        for j in range(1, segments):
            packed = jnp.where(segment == j, rolled(whole[m * segments + j], j), packed)
        if half == 0:
            pack_ref[m] = packed
        else:
            pack_ref[m] = other_ref[m]
            pack_ref[packs + m] = packed
    store.wait()


def gate(half, rows, segments, pieces, acc, nears, query_in, conv_out, decay, lap, other, partial):
    toks, width = query_in.shape
    modes, _, lanes = decay.shape
    sublanes = rows // lanes * segments
    vmem = pl.BlockSpec(memory_space=pltpu.VMEM)
    high = pl.BlockSpec(memory_space=pltpu.HBM)
    more = [] if partial is None else [partial]
    lines = (sublanes * (toks // segments + GAP), lanes)
    return pl.pallas_call(
        functools.partial(gate_kernel, half, rows, segments, pieces, len(nears)),
        in_specs=[vmem] * (6 + len(nears)) + [high] * len(more),
        out_specs=(high, vmem, vmem, vmem),
        out_shape=(
            jax.ShapeDtypeStruct((toks, width), jnp.bfloat16),
            jax.ShapeDtypeStruct(lines, jnp.float32),
            jax.ShapeDtypeStruct((modes, sublanes, lanes), jnp.float32),
            jax.ShapeDtypeStruct(((1 + half) * modes // segments, sublanes, lanes), jnp.float32),
        ),
        scratch_shapes=([pltpu.VMEM(lines, jnp.float32)] if half == 0 else [])
        + [pltpu.VMEM((toks, rows), jnp.bfloat16), pltpu.SemaphoreType.DMA],
        input_output_aliases={6 + len(nears): 0} if more else {},
        compiler_params=pltpu.CompilerParams(vmem_limit_bytes=VMEM),
        cost_estimate=QUICK,
    )(acc, *nears, query_in, conv_out, decay, lap, other, *more)


def summed(terms):
    while len(terms) > 1:
        terms = [terms[k] + terms[k + 1] if k + 1 < len(terms) else terms[k] for k in range(0, len(terms), 2)]
    return terms[0]


def scan_kernel(half, segments, gc_ref, state_ref, decay_ref, lap_ref, residue_ref, rows_ref):
    modes, sublanes, lanes = state_ref.shape
    mine = slice(half * sublanes, (half + 1) * sublanes)
    span = gc_ref.shape[0] // sublanes - GAP
    segment = segment_of((sublanes, lanes), segments)
    decay = [decay_ref[n, mine] for n in range(modes)]
    start = []
    for n in range(modes):
        total = jnp.zeros((sublanes, lanes), jnp.float32)
        if segments > 1:
            for k in range(segments - 2, -1, -1):
                total = jnp.where(segment == k, rolled(state_ref[n] + lap_ref[n, mine] * total, -1), total)
        start.append(total)

    def step(t, state):
        at = pl.ds(t, sublanes, stride=span + GAP)
        row = gc_ref[at, :]
        state = tuple(decay[n] * state[n] + row for n in range(modes))
        rows_ref[at, :] = summed([residue_ref[n, mine] * state[n] for n in range(modes)])
        return state

    steps_back(span, step, tuple(start), 16)


def scan(half, segments, grad_conv, state, decay, lap, residues):
    vmem = pl.BlockSpec(memory_space=pltpu.VMEM)
    return pl.pallas_call(
        functools.partial(scan_kernel, half, segments),
        in_specs=[vmem] * 5,
        out_specs=vmem,
        out_shape=jax.ShapeDtypeStruct(grad_conv.shape, jnp.float32),
        compiler_params=pltpu.CompilerParams(vmem_limit_bytes=VMEM),
        cost_estimate=QUICK,
    )(grad_conv, state, decay, lap, residues)


def laps_kernel(segments, span, decay_ref, lap_ref, wide_ref):
    modes, sublanes, lanes = decay_ref.shape
    sublanes //= 2
    packs = modes // segments
    segment = segment_of((sublanes, lanes), segments)
    for half in range(2):
        mine = slice(half * sublanes, (half + 1) * sublanes)
        for m in range(packs):
            packed = None
            for j in range(segments):
                lap = power(decay_ref[m * segments + j, mine], span)
                lap_ref[m * segments + j, mine] = lap
                wide = power(lap, segments)
                packed = wide if packed is None else jnp.where(segment == j, wide, packed)
            wide_ref[half * packs + m] = packed


def laps(segments, toks, decay):
    modes, sublanes, lanes = decay.shape
    vmem = pl.BlockSpec(memory_space=pltpu.VMEM)
    return pl.pallas_call(
        functools.partial(laps_kernel, segments, toks // segments),
        in_specs=[vmem],
        out_specs=(vmem, vmem),
        out_shape=(
            jax.ShapeDtypeStruct(decay.shape, jnp.float32),
            jax.ShapeDtypeStruct((2 * modes // segments, sublanes // 2, lanes), jnp.float32),
        ),
        compiler_params=pltpu.CompilerParams(vmem_limit_bytes=VMEM),
        cost_estimate=QUICK,
    )(decay)


def states_in(ref, shape):
    if ref.shape == shape:
        return [ref[m] for m in range(shape[0])]
    packs, sublanes, _ = shape
    rows = decode(ref, (0, 0, packs * sublanes // 2), 0, packs * sublanes, 1)
    return [rows[m * sublanes : (m + 1) * sublanes, :] for m in range(packs)]


def join_kernel(round_, group_ref, state_ref, arrived_ref, wide_ref, coded_ref, *out_refs):
    earlier = (group_ref[0] >> round_) % 2 == 0
    packs, sublanes, _ = state_ref.shape
    joined = []
    for m, other in enumerate(states_in(arrived_ref, state_ref.shape)):
        wide = power(wide_ref[m], 1 << round_)
        mine = state_ref[m]
        joined.append(jnp.where(earlier, mine + wide * other, other + wide * mine))
        for out_ref in out_refs:
            out_ref[m] = joined[-1]
    codes, peaks = encode(jnp.concatenate(joined, axis=0), packs * sublanes // 2)
    put(codes, coded_ref, 0)
    put_peaks(peaks, coded_ref)


def join(round_, group, state, arrived, wide, last):
    vmem = pl.BlockSpec(memory_space=pltpu.VMEM)
    packs, sublanes, lanes = state.shape
    return pl.pallas_call(
        functools.partial(join_kernel, round_),
        in_specs=[pl.BlockSpec(memory_space=pltpu.SMEM)] + [vmem] * 3,
        out_specs=[vmem] * (1 if last else 2),
        out_shape=[
            jax.ShapeDtypeStruct((packs * sublanes + PEAKS, lanes), jnp.bfloat16),
            jax.ShapeDtypeStruct(state.shape, jnp.float32),
        ][: 1 if last else 2],
        compiler_params=pltpu.CompilerParams(vmem_limit_bytes=VMEM),
        cost_estimate=QUICK,
    )(group, state, arrived, wide)


def fix_kernel(segments, rounds, group_ref, *refs):
    scanned_refs, state_ref, arrived_refs = refs[:2], refs[2], refs[3 : 3 + rounds]
    decay_ref, lap_ref, wide_ref, residue_ref, out_hbm, rows_ref, out_ref, sems = refs[3 + rounds :]
    toks, width = out_ref.shape
    modes, sublanes, lanes = state_ref.shape
    packs = modes // segments
    rows = width // 2
    span = toks // segments
    segment = segment_of((sublanes, lanes), segments)
    earlier = [(group_ref[0] >> r) % 2 == 0 for r in range(rounds)]
    arrived = [states_in(ref, (2 * packs, sublanes, lanes)) for ref in arrived_refs]
    stores = []
    for half in range(2):
        mine = slice(half * sublanes, (half + 1) * sublanes)
        decay = [decay_ref[n, mine] for n in range(modes)]
        start = []
        for m in range(packs):
            brought = jnp.zeros((sublanes, lanes), jnp.float32)
            between = jnp.ones((sublanes, lanes), jnp.float32)
            for r in range(rounds):
                state = arrived[r][half * packs + m]
                brought = jnp.where(earlier[r], brought + between * state, brought)
                if r + 1 < rounds:
                    between = jnp.where(earlier[r], between * power(wide_ref[half * packs + m], 1 << r), between)
            for j in range(segments):
                n = m * segments + j
                total = rolled(brought, segments - 1 - j)
                for k in range(segments - 2, -1, -1):
                    before = lap_ref[n, mine] * total
                    if half == 0:
                        before = before + state_ref[n]
                    total = jnp.where(segment == k, rolled(before, -1), total)
                start.append(residue_ref[n, mine] * total)

        def step(t, state, scanned_ref=scanned_refs[half], decay=decay):
            at = pl.ds(t, sublanes, stride=span + GAP)
            state = tuple(decay[n] * state[n] for n in range(modes))
            rows_ref[at, :] = scanned_ref[at, :] + summed(list(state))
            return state

        steps_back(span, step, tuple(start), 16)
        for line in range(rows // lanes):
            at = slice(half * rows + line * lanes, half * rows + (line + 1) * lanes)
            for k in range(segments):
                start = (line * segments + k) * (span + GAP)
                out_ref[k * span : (k + 1) * span, at] = rows_ref[start : start + span, :].astype(jnp.bfloat16)
        columns = pl.ds(half * rows, rows)
        stores.append(pltpu.make_async_copy(out_ref.at[:, columns], out_hbm.at[:, columns], sems.at[half]))
        stores[-1].start()
    for store in stores:
        store.wait()


def fix(segments, group, scanned, state, arrived, decay, lap, wide, residues, toks, width):
    vmem = pl.BlockSpec(memory_space=pltpu.VMEM)
    return pl.pallas_call(
        functools.partial(fix_kernel, segments, len(arrived)),
        in_specs=[pl.BlockSpec(memory_space=pltpu.SMEM)] + [vmem] * (7 + len(arrived)),
        out_specs=pl.BlockSpec(memory_space=pltpu.HBM),
        out_shape=jax.ShapeDtypeStruct((toks, width), jnp.bfloat16),
        scratch_shapes=[
            pltpu.VMEM(scanned[0].shape, jnp.float32),
            pltpu.VMEM((toks, width), jnp.bfloat16),
            pltpu.SemaphoreType.DMA((2,)),
        ],
        compiler_params=pltpu.CompilerParams(vmem_limit_bytes=VMEM),
        cost_estimate=QUICK,
    )(group, *scanned, state, *arrived, decay, lap, wide, residues)


def local(out_grad, out_weight, query_in, conv_out, residues, decay_rates):
    toks, width = query_in.shape
    modes = decay_rates.shape[1]
    lanes = math.gcd(width, 128)
    size, groups = lax.axis_size("ch"), lax.axis_size("ctx")
    bits = [1 << i for i in range(size.bit_length() - 1)]
    place = jnp.reshape(lax.axis_index("ch"), (1,)).astype(jnp.int32)
    group = jnp.reshape(lax.axis_index("ctx"), (1,)).astype(jnp.int32)
    half_rows = width // 2
    lines = half_rows // lanes
    segments = 8 // lines
    by_mode = lambda values: jnp.repeat(values.T.reshape(modes, width // lanes, lanes), segments, axis=1)
    decay, residue = by_mode(decay_rates), by_mode(residues)

    portions, order, waits = PORTIONS, ORDER, WAITS
    if size != 8:
        waits = {}
        portions = ((tuple(range(len(bits))), 2, 0), (tuple(range(len(bits))), 2, 1))
        order = [
            ((p, s, block),)
            for p in range(2)
            for s, bit in enumerate(bits)
            for block in sorted(range(0, size, 2 * bit), reverse=True)
        ] + [("laps", None), ("sum", 0), ("sum", 1), ("gate", 0), ("gate", 1), ("scan", 1), ("fix", None)]
    offsets = [sum(width // part for _, part, _ in portions[:p]) for p in range(len(portions))]

    received, sums, scanned, states, packed = {}, {}, {}, {}, {}
    grad_query = last = None

    def after(value):
        return value if last is None else lax.optimization_barrier((value, last, *awaited))[0]

    def collect(wanted):
        arrays, places = [], []
        for key in wanted:
            array, *place = received[key]
            index = next((i for i, known in enumerate(arrays) if known is array), len(arrays))
            if index == len(arrays):
                arrays.append(array)
            places.append((index, tuple(place)))
        return arrays, places

    for todo in order:
        awaited = [received[key][0] for key in waits.get(todo, ())]
        kind, half = todo[:2] if isinstance(todo[0], str) else ("send", None)
        inside = [q for q, (_, _, lies) in enumerate(portions) if lies == half]
        if kind in ("send", "both"):
            messages = todo[1:] if kind == "both" else (todo,)
            bit_of = lambda key: bits[portions[key[0]][0][key[1]]]
            arrays, planned = [], []
            for message in messages:
                wanted = [[(p, i, block ^ bit_of((p, s, block))) for i in range(s)] for p, s, block in message]
                arrays, places = collect([key for keys in wanted for key in keys])
                places = iter(places)
                planned.append(
                    tuple(
                        (block ^ bit_of((p, s, block)), offsets[p], width // portions[p][1], tuple(next(places) for _ in keys))
                        for (p, s, block), keys in zip(message, wanted)
                    )
                )
            if last is None:
                *payloads, turned = early_send(planned, width, place, out_weight, out_grad, True)
            elif kind == "both":
                payloads = early_send(planned, width, after(place), out_weight, turned, False)
            else:
                payloads = [send(planned[0], True, width, after(place), out_weight, turned, arrays)]
            last = payloads[0]
            for message, items, payload in zip(messages, planned, payloads):
                bit = bit_of(message[0])
                arrived = lax.ppermute(payload, "ch", [(i, i ^ bit) for i in range(size)])
                start = peak = 0
                for key, (_, _, rows, _) in zip(message, items):
                    part = part_of(rows, len(items), folds_of(toks))
                    received[key] = (arrived, start, peak, part)
                    start, peak = start + rows, peak + rows // part
        elif kind == "laps":
            lap, wide = laps(segments, toks, after(decay))
            last = wide
        elif kind == "sum":
            items = tuple((0, offsets[q], width // portions[q][1], ()) for q in inside)
            last = sums[half] = send(items, False, width, after(place), out_weight, turned, [])
        elif kind == "gate":
            stages = range(len(bits))
            arrays, places = collect([(q, i, 0) for q in inside for i in stages])
            pieces = tuple(
                (offsets[q] - half * half_rows, tuple(places[i * len(stages) : (i + 1) * len(stages)]))
                for i, q in enumerate(inside)
            )
            other = residue if half == 0 else packed[0]
            grad_query, scanned[half], states[half], packed[half] = gate(
                half,
                half_rows,
                segments,
                pieces,
                after(sums[half]),
                arrays,
                query_in,
                conv_out,
                decay,
                lap,
                other,
                grad_query,
            )
            last = packed[half]
        elif kind == "scan":
            groups = lax.axis_size("ctx")
            swap = lambda array, round_: lax.ppermute(array, "ctx", [(i, i ^ (1 << round_)) for i in range(groups)])
            arrived, joined = [swap(packed[1], 0)], packed[1]
            rounds = groups.bit_length() - 1
            for round_ in range(1, rounds):
                last, *joined = join(round_ - 1, after(group), joined, arrived[-1], wide, round_ + 1 == rounds)
                joined = joined[0] if joined else None
                arrived.append(swap(last, round_))
            scanned[1] = scan(1, segments, after(scanned[1]), states[1], decay, lap, residue)
        else:
            grad_input = fix(
                segments, group, [scanned[0], scanned[1]], states[0], arrived, decay, lap, wide, residue, toks, width
            )
    return grad_query, grad_input


def solution(mesh):
    placed = (
        P("ctx", "ch"),
        P(None, "ch"),
        P("ctx", "ch"),
        P("ctx", "ch"),
        P("ch", None),
        P("ch", None),
    )
    return jax.shard_map(
        local,
        mesh=mesh,
        in_specs=placed,
        out_specs=(P("ctx", "ch"), P("ctx", "ch")),
        check_vma=False,
    )
```

```python
import functools
import math

import jax
import jax.numpy as jnp
from jax import lax
from jax.experimental import pallas as pl
from jax.experimental.pallas import tpu as pltpu
from jax.sharding import PartitionSpec as P

PEAKS = 16
SPAN = 251 * math.log(2.0)
SHIFT = 125 * math.log(2.0)
STEP = 256
PIECE = 128
GAP = 8
VMEM = 24 * 1024 * 1024
QUICK = pl.CostEstimate(flops=0, bytes_accessed=1024, transcendentals=0)

PORTIONS = (((0, 1, 2), 4, 0), ((1, 0, 2), 4, 0), ((0, 1, 2), 4, 1), ((0, 1, 2), 4, 1))
ORDER = (
    ((0, 0, 6), (0, 0, 2)), ("both", ((1, 0, 5), (1, 0, 1))), ((2, 0, 6), (3, 0, 6)), ((2, 0, 4), (3, 0, 4)),
    ("sum", 1), ((2, 0, 2), (3, 0, 2)), ((1, 0, 4), (0, 1, 4)), ((1, 1, 4), (0, 0, 4)), ((2, 1, 4), (3, 1, 4)),
    ((1, 0, 0), (0, 1, 0)), ((0, 2, 0), (1, 2, 0)), ((2, 2, 0), (3, 2, 0)), ((1, 1, 0), (0, 0, 0)),
    ((2, 1, 0), (3, 1, 0)), ((2, 0, 0), (3, 0, 0)), ("sum", 0), ("laps", None), ("gate", 0), ("add", 1), ("gate", 1),
    ("scan", 1), ("fix", None),
)
WAITS = {
    ((1, 0, 0), (0, 1, 0)): ((1, 0, 4),),
    ("gate", 0): ((0, 2, 0), (1, 0, 0)),
    ("gate", 1): ((2, 1, 0),),
}


def folds_of(toks):
    return toks // 128 if toks % 128 == 0 and PEAKS % (toks // 128) == 0 else 1


def part_of(rows, blocks, folds):
    return next(
        part for part in range(16, rows + 1, 16) if rows % part == 0 and rows // part * blocks * folds <= PEAKS
    )


def step_of(rows):
    return next(step for step in (STEP, STEP // 2, rows) if rows % step == 0)


def encode(block, part):
    codes, peaks = [], []
    for i in range(block.shape[0] // part):
        piece = block[i * part : (i + 1) * part, :]
        size = jnp.abs(piece)
        peak = jnp.maximum(jnp.max(size, axis=0, keepdims=True) * 1.01, 1e-30)
        peak = peak.astype(jnp.bfloat16).astype(jnp.float32)
        code = jnp.exp(size * (SPAN / peak) - SHIFT)
        codes.append(jnp.where(piece < 0, -code, code))
        peaks.append(peak)
    return jnp.concatenate(codes, axis=0).astype(jnp.bfloat16), peaks


def put(codes, out_ref, at):
    lanes = out_ref.shape[1]
    folds = codes.shape[1] // lanes
    rows = (out_ref.shape[0] - PEAKS) // folds
    for fold in range(folds):
        out_ref[fold * rows + at : fold * rows + at + codes.shape[0], :] = codes[:, fold * lanes : (fold + 1) * lanes]


def put_peaks(peaks, out_ref):
    lanes = out_ref.shape[1]
    peaks = [peak[:, at : at + lanes] for peak in peaks for at in range(0, peak.shape[1], lanes)]
    if len(peaks) < PEAKS:
        peaks.append(jnp.zeros((PEAKS - len(peaks), lanes), jnp.float32))
    out_ref[out_ref.shape[0] - PEAKS :, :] = jnp.concatenate(peaks, axis=0).astype(jnp.bfloat16)


def decode(ref, place, first, count, folds):
    start, peak, part = place
    rows = (ref.shape[0] - PEAKS) // folds
    peaks = ref[ref.shape[0] - PEAKS :, :].astype(jnp.float32) * (1.0 / SPAN)
    columns = []
    for fold in range(folds):
        blocks = []
        for i in range(first // part, -(-(first + count) // part)):
            low, high = max(first, i * part), min(first + count, (i + 1) * part)
            code = ref[fold * rows + start + low : fold * rows + start + high, :].astype(jnp.float32)
            at = (peak + i) * folds + fold
            size = (jnp.log(jnp.abs(code)) + SHIFT) * peaks[at : at + 1, :]
            blocks.append(jnp.where(code < 0, -size, size))
        columns.append(jnp.concatenate(blocks, axis=0))
    return jnp.concatenate(columns, axis=1)


def pinned(array):
    return pltpu.with_memory_space_constraint(array, pltpu.HBM)


def send_kernel(items, coded, width, near, place_ref, w_ref, turned_ref, *refs):
    near_refs, out_ref = refs[:near], refs[near]
    folds = folds_of(turned_ref.shape[1])
    base, peaks = 0, []
    for block, offset, rows, sources in items:
        step = step_of(rows)
        first = (place_ref[0] ^ block) * width + offset
        for at in range(0, rows, step):
            total = jnp.dot(
                w_ref[pl.ds(pl.multiple_of(first + at, 16), step), :],
                turned_ref[...],
                preferred_element_type=jnp.float32,
            )
            for source, place in sources:
                total = total + decode(near_refs[source], place, at, step, folds)
            if coded:
                total, more = encode(total, part_of(rows, len(items), folds))
                peaks += more
                put(total, out_ref, base + at)
            else:
                out_ref[base + at : base + at + step, :] = total
        base += rows
    if coded:
        put_peaks(peaks, out_ref)


def send(items, coded, width, place, weight, turned, nears):
    toks = turned.shape[1]
    vmem = pl.BlockSpec(memory_space=pltpu.VMEM)
    count = sum(rows for _, _, rows, _ in items)
    folds = folds_of(toks)
    shape = (folds * count + PEAKS, toks // folds) if coded else (count, toks)
    return pl.pallas_call(
        functools.partial(send_kernel, items, coded, width, len(nears)),
        in_specs=[pl.BlockSpec(memory_space=pltpu.SMEM)] + [vmem] * (2 + len(nears)),
        out_specs=vmem,
        out_shape=jax.ShapeDtypeStruct(shape, jnp.bfloat16 if coded else jnp.float32),
        compiler_params=pltpu.CompilerParams(vmem_limit_bytes=VMEM),
        cost_estimate=QUICK,
    )(place, weight, turned, *nears)


def early_kernel(messages, width, turns, place_ref, w_hbm, g_ref, *refs):
    out_refs, refs = refs[: len(messages)], refs[len(messages) :]
    w_ref, sems = refs[-2:]
    turned_ref = refs[0] if turns else g_ref
    depth, toks = turned_ref.shape
    copies, waits = [], []
    if turns:
        piece = math.gcd(toks, PIECE)
        for at in range(0, toks, piece):
            lines = pl.ds(at, piece)
            copies.append(pltpu.make_async_copy(g_ref.at[lines, :], refs[1].at[lines, :], sems.at[len(copies)]))
    grads, base = len(copies), 0
    for items in messages:
        for block, offset, rows, _ in items:
            step = math.gcd(rows, PIECE)
            first = pl.multiple_of((place_ref[0] ^ block) * width + offset, 16)
            for at in range(0, rows, step):
                copies.append(
                    pltpu.make_async_copy(
                        w_hbm.at[pl.ds(first + at, step), :], w_ref.at[pl.ds(base + at, step), :], sems.at[len(copies)]
                    )
                )
            base += rows
    for copy in copies:
        copy.start(priority=1)
    for i in range(grads):
        copies[i].wait()
        turned_ref[:, i * piece : (i + 1) * piece] = refs[1][i * piece : (i + 1) * piece, :].T
    waits, base = iter(copies[grads:]), 0
    for items, out_ref in zip(messages, out_refs):
        start, peaks = base, []
        for _, _, rows, _ in items:
            step = step_of(rows)
            for at in range(base, base + rows, step):
                for _ in range(step // math.gcd(rows, PIECE)):
                    next(waits).wait()
                total = jnp.dot(w_ref[at : at + step, :], turned_ref[...], preferred_element_type=jnp.float32)
                total, more = encode(total, part_of(rows, len(items), folds_of(toks)))
                peaks += more
                put(total, out_ref, at - start)
            base += rows
        put_peaks(peaks, out_ref)


def early_send(messages, width, place, weight, grad, turns):
    toks, depth = grad.shape if turns else grad.shape[::-1]
    vmem = pl.BlockSpec(memory_space=pltpu.VMEM)
    high = pl.BlockSpec(memory_space=pltpu.HBM)
    counts = [sum(rows for _, _, rows, _ in items) for items in messages]
    folds = folds_of(toks)
    steps = sum(rows // math.gcd(rows, PIECE) for items in messages for _, _, rows, _ in items)
    steps += toks // math.gcd(toks, PIECE) if turns else 0
    coded = [jax.ShapeDtypeStruct((folds * count + PEAKS, toks // folds), jnp.bfloat16) for count in counts]
    return pl.pallas_call(
        functools.partial(early_kernel, messages, width, turns),
        in_specs=[pl.BlockSpec(memory_space=pltpu.SMEM), high, high if turns else vmem],
        out_specs=[vmem] * (len(messages) + turns),
        out_shape=coded + [jax.ShapeDtypeStruct((depth, toks), jnp.bfloat16)] * turns,
        scratch_shapes=[pltpu.VMEM((toks, depth), jnp.bfloat16)] * turns
        + [pltpu.VMEM((sum(counts), depth), jnp.bfloat16), pltpu.SemaphoreType.DMA((steps,))],
        compiler_params=pltpu.CompilerParams(vmem_limit_bytes=VMEM),
        cost_estimate=QUICK,
    )(place, pinned(weight), pinned(grad) if turns else grad)


def add_kernel(pieces, near, acc_ref, *refs):
    near_refs, out_ref = refs[:near], refs[near]
    toks = acc_ref.shape[1]
    for first, rows, sources in pieces:
        total = acc_ref[first : first + rows, :]
        for source, place in sources:
            total = total + decode(near_refs[source], place, 0, rows, folds_of(toks))
        out_ref[first : first + rows, :] = total


def add(pieces, acc, nears):
    vmem = pl.BlockSpec(memory_space=pltpu.VMEM)
    return pl.pallas_call(
        functools.partial(add_kernel, pieces, len(nears)),
        in_specs=[vmem] * (1 + len(nears)),
        out_specs=vmem,
        out_shape=jax.ShapeDtypeStruct(acc.shape, jnp.float32),
        compiler_params=pltpu.CompilerParams(vmem_limit_bytes=VMEM),
        cost_estimate=QUICK,
    )(acc, *nears)


def steps_back(count, body, state, unroll, base=0):
    unroll = math.gcd(count, unroll)

    def some(i, state):
        for j in range(unroll):
            state = body(base + count - 1 - (i * unroll + j), state)
        return state

    return lax.fori_loop(0, count // unroll, some, state)


def power(base, exponent):
    result = None
    while exponent:
        if exponent % 2:
            result = base if result is None else result * base
        base = base * base
        exponent //= 2
    return result


def segment_of(shape, segments):
    return lax.rem(lax.broadcasted_iota(jnp.int32, shape, 0), segments)


def rolled(value, by):
    by %= value.shape[0]
    return pltpu.roll(value, by, 0) if by else value


def gate_kernel(half, rows, segments, pieces, near, acc_ref, *refs):
    near_refs, refs = refs[:near], refs[near:]
    query_ref, conv_ref, decay_ref, lap_ref, other_ref = refs[:5]
    out_hbm, rows_ref, state_ref, pack_ref = refs[-7:-3] if half == 0 else refs[-6:-2]
    gq_ref, sem = refs[-2:]
    gc_ref = refs[-3] if half == 0 else rows_ref
    toks = query_ref.shape[0]
    modes, sublanes, lanes = state_ref.shape
    mine = slice(half * sublanes, (half + 1) * sublanes)
    for line in range(rows // lanes):
        mix = acc_ref[line * lanes : (line + 1) * lanes, :]
        first, sources = next(piece for piece in reversed(pieces) if piece[0] <= line * lanes)
        for source, place in sources:
            mix = mix + decode(near_refs[source], place, line * lanes - first, lanes, folds_of(toks))
        mix = mix.T
        at = slice(line * lanes, (line + 1) * lanes)
        full = slice(half * rows + line * lanes, half * rows + (line + 1) * lanes)
        gq_ref[:, at] = (mix * conv_ref[:, full].astype(jnp.float32)).astype(jnp.bfloat16)
        gated = mix * query_ref[:, full].astype(jnp.float32)
        for k in range(segments):
            start = (line * segments + k) * (toks // segments + GAP)
            gc_ref[start : start + toks // segments, :] = gated[k * (toks // segments) : (k + 1) * (toks // segments), :]
    store = pltpu.make_async_copy(gq_ref, out_hbm.at[:, pl.ds(half * rows, rows)], sem)
    store.start()
    decay = [decay_ref[n, mine] for n in range(modes)]
    span = toks // segments

    def step(t, state):
        at = pl.ds(t, sublanes, stride=span + GAP)
        row = gc_ref[at, :]
        state = tuple(decay[n] * state[n] + row for n in range(modes))
        if half == 0:
            rows_ref[at, :] = summed([other_ref[n, mine] * state[n] for n in range(modes)])
        return state

    zero = jnp.zeros((sublanes, lanes), jnp.float32)
    state = steps_back(span, step, (zero,) * modes, 16)
    segment = segment_of((sublanes, lanes), segments)
    whole = []
    for n in range(modes):
        state_ref[n] = state[n]
        total = state[n]
        if segments > 1:
            factor = jnp.where(segment < segments - 1, lap_ref[n, mine], 0.0)
            for _ in range(segments - 1):
                total = state[n] + factor * rolled(total, -1)
        whole.append(total)
    packs = modes // segments
    for m in range(packs):
        packed = whole[m * segments]
        for j in range(1, segments):
            packed = jnp.where(segment == j, rolled(whole[m * segments + j], j), packed)
        if half == 0:
            pack_ref[m] = packed
        else:
            pack_ref[m] = other_ref[m]
            pack_ref[packs + m] = packed
    store.wait()


def gate(half, rows, segments, pieces, acc, nears, query_in, conv_out, decay, lap, other, partial):
    toks, width = query_in.shape
    modes, _, lanes = decay.shape
    sublanes = rows // lanes * segments
    vmem = pl.BlockSpec(memory_space=pltpu.VMEM)
    high = pl.BlockSpec(memory_space=pltpu.HBM)
    more = [] if partial is None else [partial]
    lines = (sublanes * (toks // segments + GAP), lanes)
    return pl.pallas_call(
        functools.partial(gate_kernel, half, rows, segments, pieces, len(nears)),
        in_specs=[vmem] * (6 + len(nears)) + [high] * len(more),
        out_specs=(high, vmem, vmem, vmem),
        out_shape=(
            jax.ShapeDtypeStruct((toks, width), jnp.bfloat16),
            jax.ShapeDtypeStruct(lines, jnp.float32),
            jax.ShapeDtypeStruct((modes, sublanes, lanes), jnp.float32),
            jax.ShapeDtypeStruct(((1 + half) * modes // segments, sublanes, lanes), jnp.float32),
        ),
        scratch_shapes=([pltpu.VMEM(lines, jnp.float32)] if half == 0 else [])
        + [pltpu.VMEM((toks, rows), jnp.bfloat16), pltpu.SemaphoreType.DMA],
        input_output_aliases={6 + len(nears): 0} if more else {},
        compiler_params=pltpu.CompilerParams(vmem_limit_bytes=VMEM),
        cost_estimate=QUICK,
    )(acc, *nears, query_in, conv_out, decay, lap, other, *more)


def summed(terms):
    while len(terms) > 1:
        terms = [terms[k] + terms[k + 1] if k + 1 < len(terms) else terms[k] for k in range(0, len(terms), 2)]
    return terms[0]


def scan_kernel(half, segments, gc_ref, state_ref, decay_ref, lap_ref, residue_ref, rows_ref):
    modes, sublanes, lanes = state_ref.shape
    mine = slice(half * sublanes, (half + 1) * sublanes)
    span = gc_ref.shape[0] // sublanes - GAP
    segment = segment_of((sublanes, lanes), segments)
    decay = [decay_ref[n, mine] for n in range(modes)]
    start = []
    for n in range(modes):
        total = jnp.zeros((sublanes, lanes), jnp.float32)
        if segments > 1:
            for k in range(segments - 2, -1, -1):
                total = jnp.where(segment == k, rolled(state_ref[n] + lap_ref[n, mine] * total, -1), total)
        start.append(total)

    def step(t, state):
        at = pl.ds(t, sublanes, stride=span + GAP)
        row = gc_ref[at, :]
        state = tuple(decay[n] * state[n] + row for n in range(modes))
        rows_ref[at, :] = summed([residue_ref[n, mine] * state[n] for n in range(modes)])
        return state

    steps_back(span, step, tuple(start), 16)


def scan(half, segments, grad_conv, state, decay, lap, residues):
    vmem = pl.BlockSpec(memory_space=pltpu.VMEM)
    return pl.pallas_call(
        functools.partial(scan_kernel, half, segments),
        in_specs=[vmem] * 5,
        out_specs=vmem,
        out_shape=jax.ShapeDtypeStruct(grad_conv.shape, jnp.float32),
        compiler_params=pltpu.CompilerParams(vmem_limit_bytes=VMEM),
        cost_estimate=QUICK,
    )(grad_conv, state, decay, lap, residues)


def laps_kernel(segments, span, decay_ref, lap_ref, wide_ref):
    modes, sublanes, lanes = decay_ref.shape
    sublanes //= 2
    packs = modes // segments
    segment = segment_of((sublanes, lanes), segments)
    for half in range(2):
        mine = slice(half * sublanes, (half + 1) * sublanes)
        for m in range(packs):
            packed = None
            for j in range(segments):
                lap = power(decay_ref[m * segments + j, mine], span)
                lap_ref[m * segments + j, mine] = lap
                wide = power(lap, segments)
                packed = wide if packed is None else jnp.where(segment == j, wide, packed)
            wide_ref[half * packs + m] = packed


def laps(segments, toks, decay):
    modes, sublanes, lanes = decay.shape
    vmem = pl.BlockSpec(memory_space=pltpu.VMEM)
    return pl.pallas_call(
        functools.partial(laps_kernel, segments, toks // segments),
        in_specs=[vmem],
        out_specs=(vmem, vmem),
        out_shape=(
            jax.ShapeDtypeStruct(decay.shape, jnp.float32),
            jax.ShapeDtypeStruct((2 * modes // segments, sublanes // 2, lanes), jnp.float32),
        ),
        compiler_params=pltpu.CompilerParams(vmem_limit_bytes=VMEM),
        cost_estimate=QUICK,
    )(decay)


def states_in(ref, shape):
    if ref.shape == shape:
        return [ref[m] for m in range(shape[0])]
    packs, sublanes, _ = shape
    rows = decode(ref, (0, 0, packs * sublanes // 2), 0, packs * sublanes, 1)
    return [rows[m * sublanes : (m + 1) * sublanes, :] for m in range(packs)]


def join_kernel(round_, group_ref, state_ref, arrived_ref, wide_ref, coded_ref, *out_refs):
    earlier = (group_ref[0] >> round_) % 2 == 0
    packs, sublanes, _ = state_ref.shape
    joined = []
    for m, other in enumerate(states_in(arrived_ref, state_ref.shape)):
        wide = power(wide_ref[m], 1 << round_)
        mine = state_ref[m]
        joined.append(jnp.where(earlier, mine + wide * other, other + wide * mine))
        for out_ref in out_refs:
            out_ref[m] = joined[-1]
    codes, peaks = encode(jnp.concatenate(joined, axis=0), packs * sublanes // 2)
    put(codes, coded_ref, 0)
    put_peaks(peaks, coded_ref)


def join(round_, group, state, arrived, wide, last):
    vmem = pl.BlockSpec(memory_space=pltpu.VMEM)
    packs, sublanes, lanes = state.shape
    return pl.pallas_call(
        functools.partial(join_kernel, round_),
        in_specs=[pl.BlockSpec(memory_space=pltpu.SMEM)] + [vmem] * 3,
        out_specs=[vmem] * (1 if last else 2),
        out_shape=[
            jax.ShapeDtypeStruct((packs * sublanes + PEAKS, lanes), jnp.bfloat16),
            jax.ShapeDtypeStruct(state.shape, jnp.float32),
        ][: 1 if last else 2],
        compiler_params=pltpu.CompilerParams(vmem_limit_bytes=VMEM),
        cost_estimate=QUICK,
    )(group, state, arrived, wide)


def fix_kernel(segments, rounds, group_ref, *refs):
    scanned_refs, state_ref, arrived_refs = refs[:2], refs[2], refs[3 : 3 + rounds]
    decay_ref, lap_ref, wide_ref, residue_ref, out_hbm, rows_ref, out_ref, sems = refs[3 + rounds :]
    toks, width = out_ref.shape
    modes, sublanes, lanes = state_ref.shape
    packs = modes // segments
    rows = width // 2
    span = toks // segments
    segment = segment_of((sublanes, lanes), segments)
    earlier = [(group_ref[0] >> r) % 2 == 0 for r in range(rounds)]
    arrived = [states_in(ref, (2 * packs, sublanes, lanes)) for ref in arrived_refs]
    stores = []
    for half in range(2):
        mine = slice(half * sublanes, (half + 1) * sublanes)
        decay = [decay_ref[n, mine] for n in range(modes)]
        start = []
        for m in range(packs):
            brought = jnp.zeros((sublanes, lanes), jnp.float32)
            between = jnp.ones((sublanes, lanes), jnp.float32)
            for r in range(rounds):
                state = arrived[r][half * packs + m]
                brought = jnp.where(earlier[r], brought + between * state, brought)
                if r + 1 < rounds:
                    between = jnp.where(earlier[r], between * power(wide_ref[half * packs + m], 1 << r), between)
            for j in range(segments):
                n = m * segments + j
                total = rolled(brought, segments - 1 - j)
                for k in range(segments - 2, -1, -1):
                    before = lap_ref[n, mine] * total
                    if half == 0:
                        before = before + state_ref[n]
                    total = jnp.where(segment == k, rolled(before, -1), total)
                start.append(residue_ref[n, mine] * total)

        def step(t, state, scanned_ref=scanned_refs[half], decay=decay):
            at = pl.ds(t, sublanes, stride=span + GAP)
            state = tuple(decay[n] * state[n] for n in range(modes))
            rows_ref[at, :] = scanned_ref[at, :] + summed(list(state))
            return state

        state, columns = tuple(start), pl.ds(half * rows, rows)
        for base in (span // 2, 0):
            state = steps_back(span // 2, step, state, 16, base)
            for k in range(segments):
                for line in range(rows // lanes):
                    at = slice(half * rows + line * lanes, half * rows + (line + 1) * lanes)
                    first = (line * segments + k) * (span + GAP) + base
                    out_ref[k * span + base : k * span + base + span // 2, at] = rows_ref[
                        first : first + span // 2, :
                    ].astype(jnp.bfloat16)
                lines = pl.ds(k * span + base, span // 2)
                stores.append(
                    pltpu.make_async_copy(
                        out_ref.at[lines, columns], out_hbm.at[lines, columns], sems.at[len(stores)]
                    )
                )
                stores[-1].start()
    for store in stores:
        store.wait()


def fix(segments, group, scanned, state, arrived, decay, lap, wide, residues, toks, width):
    vmem = pl.BlockSpec(memory_space=pltpu.VMEM)
    return pl.pallas_call(
        functools.partial(fix_kernel, segments, len(arrived)),
        in_specs=[pl.BlockSpec(memory_space=pltpu.SMEM)] + [vmem] * (7 + len(arrived)),
        out_specs=pl.BlockSpec(memory_space=pltpu.HBM),
        out_shape=jax.ShapeDtypeStruct((toks, width), jnp.bfloat16),
        scratch_shapes=[
            pltpu.VMEM(scanned[0].shape, jnp.float32),
            pltpu.VMEM((toks, width), jnp.bfloat16),
            pltpu.SemaphoreType.DMA((4 * segments,)),
        ],
        compiler_params=pltpu.CompilerParams(vmem_limit_bytes=VMEM),
        cost_estimate=QUICK,
    )(group, *scanned, state, *arrived, decay, lap, wide, residues)


def local(out_grad, out_weight, query_in, conv_out, residues, decay_rates):
    toks, width = query_in.shape
    modes = decay_rates.shape[1]
    lanes = math.gcd(width, 128)
    size, groups = lax.axis_size("ch"), lax.axis_size("ctx")
    bits = [1 << i for i in range(size.bit_length() - 1)]
    place = jnp.reshape(lax.axis_index("ch"), (1,)).astype(jnp.int32)
    group = jnp.reshape(lax.axis_index("ctx"), (1,)).astype(jnp.int32)
    half_rows = width // 2
    lines = half_rows // lanes
    segments = 8 // lines
    by_mode = lambda values: jnp.repeat(values.T.reshape(modes, width // lanes, lanes), segments, axis=1)
    decay, residue = by_mode(decay_rates), by_mode(residues)

    portions, order, waits = PORTIONS, ORDER, WAITS
    if size != 8:
        waits = {}
        portions = ((tuple(range(len(bits))), 2, 0), (tuple(range(len(bits))), 2, 1))
        order = [
            ((p, s, block),)
            for p in range(2)
            for s, bit in enumerate(bits)
            for block in sorted(range(0, size, 2 * bit), reverse=True)
        ] + [("laps", None), ("sum", 0), ("sum", 1), ("gate", 0), ("gate", 1), ("scan", 1), ("fix", None)]
    offsets = [sum(width // part for _, part, _ in portions[:p]) for p in range(len(portions))]

    received, sums, scanned, states, packed = {}, {}, {}, {}, {}
    grad_query = last = None
    added = set()

    def after(value):
        return value if last is None else lax.optimization_barrier((value, last, *awaited))[0]

    def collect(wanted):
        arrays, places = [], []
        for key in wanted:
            array, *place = received[key]
            index = next((i for i, known in enumerate(arrays) if known is array), len(arrays))
            if index == len(arrays):
                arrays.append(array)
            places.append((index, tuple(place)))
        return arrays, places

    for todo in order:
        awaited = [received[key][0] for key in waits.get(todo, ())]
        kind, half = todo[:2] if isinstance(todo[0], str) else ("send", None)
        inside = [q for q, (_, _, lies) in enumerate(portions) if lies == half]
        if kind in ("send", "both"):
            messages = todo[1:] if kind == "both" else (todo,)
            bit_of = lambda key: bits[portions[key[0]][0][key[1]]]
            arrays, planned = [], []
            for message in messages:
                wanted = [[(p, i, block ^ bit_of((p, s, block))) for i in range(s)] for p, s, block in message]
                arrays, places = collect([key for keys in wanted for key in keys])
                places = iter(places)
                planned.append(
                    tuple(
                        (block ^ bit_of((p, s, block)), offsets[p], width // portions[p][1], tuple(next(places) for _ in keys))
                        for (p, s, block), keys in zip(message, wanted)
                    )
                )
            if last is None:
                *payloads, turned = early_send(planned, width, place, out_weight, out_grad, True)
            elif kind == "both":
                payloads = early_send(planned, width, after(place), out_weight, turned, False)
            else:
                payloads = [send(planned[0], True, width, after(place), out_weight, turned, arrays)]
            last = payloads[0]
            for message, items, payload in zip(messages, planned, payloads):
                bit = bit_of(message[0])
                arrived = lax.ppermute(payload, "ch", [(i, i ^ bit) for i in range(size)])
                start = peak = 0
                for key, (_, _, rows, _) in zip(message, items):
                    part = part_of(rows, len(items), folds_of(toks))
                    received[key] = (arrived, start, peak, part)
                    start, peak = start + rows, peak + rows // part
        elif kind == "laps":
            lap, wide = laps(segments, toks, after(decay))
            last = wide
        elif kind == "sum":
            items = tuple((0, offsets[q], width // portions[q][1], ()) for q in inside)
            last = sums[half] = send(items, False, width, after(place), out_weight, turned, [])
        elif kind == "add":
            arrays, places = collect([(q, len(bits) - 1, 0) for q in inside])
            pieces = tuple(
                (offsets[q] - half * half_rows, width // portions[q][1], (at,)) for q, at in zip(inside, places)
            )
            last = sums[half] = add(pieces, after(sums[half]), arrays)
            added.add(half)
        elif kind == "gate":
            stages = range(len(bits) - (half in added))
            arrays, places = collect([(q, i, 0) for q in inside for i in stages])
            pieces = tuple(
                (offsets[q] - half * half_rows, tuple(places[i * len(stages) : (i + 1) * len(stages)]))
                for i, q in enumerate(inside)
            )
            other = residue if half == 0 else packed[0]
            grad_query, scanned[half], states[half], packed[half] = gate(
                half,
                half_rows,
                segments,
                pieces,
                after(sums[half]),
                arrays,
                query_in,
                conv_out,
                decay,
                lap,
                other,
                grad_query,
            )
            last = packed[half]
        elif kind == "scan":
            groups = lax.axis_size("ctx")
            swap = lambda array, round_: lax.ppermute(array, "ctx", [(i, i ^ (1 << round_)) for i in range(groups)])
            arrived, joined = [swap(packed[1], 0)], packed[1]
            rounds = groups.bit_length() - 1
            for round_ in range(1, rounds):
                last, *joined = join(round_ - 1, after(group), joined, arrived[-1], wide, round_ + 1 == rounds)
                joined = joined[0] if joined else None
                arrived.append(swap(last, round_))
            scanned[1] = scan(1, segments, after(scanned[1]), states[1], decay, lap, residue)
        else:
            grad_input = fix(
                segments, group, [scanned[0], scanned[1]], states[0], arrived, decay, lap, wide, residue, toks, width
            )
    return grad_query, grad_input


def solution(mesh):
    placed = (
        P("ctx", "ch"),
        P(None, "ch"),
        P("ctx", "ch"),
        P("ctx", "ch"),
        P("ch", None),
        P("ch", None),
    )
    return jax.shard_map(
        local,
        mesh=mesh,
        in_specs=placed,
        out_specs=(P("ctx", "ch"), P("ctx", "ch")),
        check_vma=False,
    )
```

```python
import functools
import math

import jax
import jax.numpy as jnp
from jax import lax
from jax.experimental import pallas as pl
from jax.experimental.pallas import tpu as pltpu
from jax.sharding import PartitionSpec as P

PEAKS = 16
SPAN = 251 * math.log(2.0)
SHIFT = 125 * math.log(2.0)
STEP = 256
PIECE = 128
GAP = 8
VMEM = 24 * 1024 * 1024
QUICK = pl.CostEstimate(flops=0, bytes_accessed=1024, transcendentals=0)

PORTIONS = (((0, 1, 2), 4, 0), ((1, 0, 2), 4, 0), ((0, 1, 2), 4, 1), ((0, 1, 2), 4, 1))
ORDER = (
    ((0, 0, 6), (0, 0, 2)), ("both", ((1, 0, 5), (1, 0, 1))), ((2, 0, 6), (3, 0, 6)), ((2, 0, 4), (3, 0, 4)),
    ("sum", 1), ((2, 0, 2), (3, 0, 2)), ((1, 0, 4), (0, 1, 4)), ((1, 1, 4), (0, 0, 4)), ((2, 1, 4), (3, 1, 4)),
    ((1, 0, 0), (0, 1, 0)), ((0, 2, 0), (1, 2, 0)), ((2, 2, 0), (3, 2, 0)), ((1, 1, 0), (0, 0, 0)),
    ((2, 1, 0), (3, 1, 0)), ((2, 0, 0), (3, 0, 0)), ("sum", 0), ("laps", None), ("gate", 0), ("add", 1), ("gate", 1),
    ("scan", 1), ("fix", None),
)
WAITS = {
    ((1, 0, 0), (0, 1, 0)): ((1, 0, 4),),
    ("gate", 0): ((0, 2, 0), (1, 0, 0)),
    ("gate", 1): ((2, 1, 0),),
}


def folds_of(toks):
    return toks // 128 if toks % 128 == 0 and PEAKS % (toks // 128) == 0 else 1


def part_of(rows, blocks, folds):
    return next(
        part for part in range(16, rows + 1, 16) if rows % part == 0 and rows // part * blocks * folds <= PEAKS
    )


def step_of(rows):
    return next(step for step in (STEP, STEP // 2, rows) if rows % step == 0)


def encode(block, part):
    codes, peaks = [], []
    for i in range(block.shape[0] // part):
        piece = block[i * part : (i + 1) * part, :]
        size = jnp.abs(piece)
        peak = jnp.maximum(jnp.max(size, axis=0, keepdims=True) * 1.01, 1e-30)
        peak = peak.astype(jnp.bfloat16).astype(jnp.float32)
        code = jnp.exp(size * (SPAN / peak) - SHIFT)
        codes.append(jnp.where(piece < 0, -code, code))
        peaks.append(peak)
    return jnp.concatenate(codes, axis=0).astype(jnp.bfloat16), peaks


def put(codes, out_ref, at):
    lanes = out_ref.shape[1]
    folds = codes.shape[1] // lanes
    rows = (out_ref.shape[0] - PEAKS) // folds
    for fold in range(folds):
        out_ref[fold * rows + at : fold * rows + at + codes.shape[0], :] = codes[:, fold * lanes : (fold + 1) * lanes]


def put_peaks(peaks, out_ref):
    lanes = out_ref.shape[1]
    peaks = [peak[:, at : at + lanes] for peak in peaks for at in range(0, peak.shape[1], lanes)]
    if len(peaks) < PEAKS:
        peaks.append(jnp.zeros((PEAKS - len(peaks), lanes), jnp.float32))
    out_ref[out_ref.shape[0] - PEAKS :, :] = jnp.concatenate(peaks, axis=0).astype(jnp.bfloat16)


def decode(ref, place, first, count, folds):
    start, peak, part = place
    rows = (ref.shape[0] - PEAKS) // folds
    peaks = ref[ref.shape[0] - PEAKS :, :].astype(jnp.float32) * (1.0 / SPAN)
    columns = []
    for fold in range(folds):
        blocks = []
        for i in range(first // part, -(-(first + count) // part)):
            low, high = max(first, i * part), min(first + count, (i + 1) * part)
            code = ref[fold * rows + start + low : fold * rows + start + high, :].astype(jnp.float32)
            at = (peak + i) * folds + fold
            size = (jnp.log(jnp.abs(code)) + SHIFT) * peaks[at : at + 1, :]
            blocks.append(jnp.where(code < 0, -size, size))
        columns.append(jnp.concatenate(blocks, axis=0))
    return jnp.concatenate(columns, axis=1)


def pinned(array):
    return pltpu.with_memory_space_constraint(array, pltpu.HBM)


def send_kernel(items, coded, width, near, place_ref, w_ref, turned_ref, *refs):
    near_refs, out_ref = refs[:near], refs[near]
    folds = folds_of(turned_ref.shape[1])
    base, peaks = 0, []
    for block, offset, rows, sources in items:
        step = step_of(rows)
        first = (place_ref[0] ^ block) * width + offset
        for at in range(0, rows, step):
            total = jnp.dot(
                w_ref[pl.ds(pl.multiple_of(first + at, 16), step), :],
                turned_ref[...],
                preferred_element_type=jnp.float32,
            )
            for source, place in sources:
                total = total + decode(near_refs[source], place, at, step, folds)
            if coded:
                total, more = encode(total, part_of(rows, len(items), folds))
                peaks += more
                put(total, out_ref, base + at)
            else:
                out_ref[base + at : base + at + step, :] = total
        base += rows
    if coded:
        put_peaks(peaks, out_ref)


def send(items, coded, width, place, weight, turned, nears):
    toks = turned.shape[1]
    vmem = pl.BlockSpec(memory_space=pltpu.VMEM)
    count = sum(rows for _, _, rows, _ in items)
    folds = folds_of(toks)
    shape = (folds * count + PEAKS, toks // folds) if coded else (count, toks)
    return pl.pallas_call(
        functools.partial(send_kernel, items, coded, width, len(nears)),
        in_specs=[pl.BlockSpec(memory_space=pltpu.SMEM)] + [vmem] * (2 + len(nears)),
        out_specs=vmem,
        out_shape=jax.ShapeDtypeStruct(shape, jnp.bfloat16 if coded else jnp.float32),
        compiler_params=pltpu.CompilerParams(vmem_limit_bytes=VMEM),
        cost_estimate=QUICK,
    )(place, weight, turned, *nears)


def early_kernel(messages, width, turns, place_ref, w_hbm, g_ref, *refs):
    out_refs, refs = refs[: len(messages)], refs[len(messages) :]
    w_ref, sems = refs[-2:]
    turned_ref = refs[0] if turns else g_ref
    depth, toks = turned_ref.shape
    copies, waits = [], []
    if turns:
        piece = math.gcd(toks, PIECE)
        for at in range(0, toks, piece):
            lines = pl.ds(at, piece)
            copies.append(pltpu.make_async_copy(g_ref.at[lines, :], refs[1].at[lines, :], sems.at[len(copies)]))
    grads, base = len(copies), 0
    for items in messages:
        for block, offset, rows, _ in items:
            step = math.gcd(rows, PIECE)
            first = pl.multiple_of((place_ref[0] ^ block) * width + offset, 16)
            for at in range(0, rows, step):
                copies.append(
                    pltpu.make_async_copy(
                        w_hbm.at[pl.ds(first + at, step), :], w_ref.at[pl.ds(base + at, step), :], sems.at[len(copies)]
                    )
                )
            base += rows
    for copy in copies:
        copy.start(priority=1)
    for i in range(grads):
        copies[i].wait()
        turned_ref[:, i * piece : (i + 1) * piece] = refs[1][i * piece : (i + 1) * piece, :].T
    waits, base = iter(copies[grads:]), 0
    for items, out_ref in zip(messages, out_refs):
        start, peaks = base, []
        for _, _, rows, _ in items:
            step = step_of(rows)
            for at in range(base, base + rows, step):
                for _ in range(step // math.gcd(rows, PIECE)):
                    next(waits).wait()
                total = jnp.dot(w_ref[at : at + step, :], turned_ref[...], preferred_element_type=jnp.float32)
                total, more = encode(total, part_of(rows, len(items), folds_of(toks)))
                peaks += more
                put(total, out_ref, at - start)
            base += rows
        put_peaks(peaks, out_ref)


def early_send(messages, width, place, weight, grad, turns):
    toks, depth = grad.shape if turns else grad.shape[::-1]
    vmem = pl.BlockSpec(memory_space=pltpu.VMEM)
    high = pl.BlockSpec(memory_space=pltpu.HBM)
    counts = [sum(rows for _, _, rows, _ in items) for items in messages]
    folds = folds_of(toks)
    steps = sum(rows // math.gcd(rows, PIECE) for items in messages for _, _, rows, _ in items)
    steps += toks // math.gcd(toks, PIECE) if turns else 0
    coded = [jax.ShapeDtypeStruct((folds * count + PEAKS, toks // folds), jnp.bfloat16) for count in counts]
    return pl.pallas_call(
        functools.partial(early_kernel, messages, width, turns),
        in_specs=[pl.BlockSpec(memory_space=pltpu.SMEM), high, high if turns else vmem],
        out_specs=[vmem] * (len(messages) + turns),
        out_shape=coded + [jax.ShapeDtypeStruct((depth, toks), jnp.bfloat16)] * turns,
        scratch_shapes=[pltpu.VMEM((toks, depth), jnp.bfloat16)] * turns
        + [pltpu.VMEM((sum(counts), depth), jnp.bfloat16), pltpu.SemaphoreType.DMA((steps,))],
        compiler_params=pltpu.CompilerParams(vmem_limit_bytes=VMEM),
        cost_estimate=QUICK,
    )(place, pinned(weight), pinned(grad) if turns else grad)


def add_kernel(pieces, near, acc_ref, *refs):
    near_refs, out_ref = refs[:near], refs[near]
    toks = acc_ref.shape[1]
    for first, rows, sources in pieces:
        total = acc_ref[first : first + rows, :]
        for source, place in sources:
            total = total + decode(near_refs[source], place, 0, rows, folds_of(toks))
        out_ref[first : first + rows, :] = total


def add(pieces, acc, nears):
    vmem = pl.BlockSpec(memory_space=pltpu.VMEM)
    return pl.pallas_call(
        functools.partial(add_kernel, pieces, len(nears)),
        in_specs=[vmem] * (1 + len(nears)),
        out_specs=vmem,
        out_shape=jax.ShapeDtypeStruct(acc.shape, jnp.float32),
        compiler_params=pltpu.CompilerParams(vmem_limit_bytes=VMEM),
        cost_estimate=QUICK,
    )(acc, *nears)


def steps_back(count, body, state, unroll, base=0):
    unroll = math.gcd(count, unroll)

    def some(i, state):
        for j in range(unroll):
            state = body(base + count - 1 - (i * unroll + j), state)
        return state

    return lax.fori_loop(0, count // unroll, some, state)


def power(base, exponent):
    result = None
    while exponent:
        if exponent % 2:
            result = base if result is None else result * base
        base = base * base
        exponent //= 2
    return result


def segment_of(shape, segments):
    return lax.rem(lax.broadcasted_iota(jnp.int32, shape, 0), segments)


def rolled(value, by):
    by %= value.shape[0]
    return pltpu.roll(value, by, 0) if by else value


def gate_kernel(half, rows, segments, pieces, near, acc_ref, *refs):
    near_refs, refs = refs[:near], refs[near:]
    query_ref, conv_ref, decay_ref, lap_ref, other_ref = refs[:5]
    out_hbm, rows_ref, state_ref, pack_ref = refs[-7:-3] if half == 0 else refs[-6:-2]
    gq_ref, sem = refs[-2:]
    gc_ref = refs[-3] if half == 0 else rows_ref
    toks = query_ref.shape[0]
    modes, sublanes, lanes = state_ref.shape
    mine = slice(half * sublanes, (half + 1) * sublanes)
    for line in range(rows // lanes):
        mix = acc_ref[line * lanes : (line + 1) * lanes, :]
        first, sources = next(piece for piece in reversed(pieces) if piece[0] <= line * lanes)
        for source, place in sources:
            mix = mix + decode(near_refs[source], place, line * lanes - first, lanes, folds_of(toks))
        mix = mix.T
        at = slice(line * lanes, (line + 1) * lanes)
        full = slice(half * rows + line * lanes, half * rows + (line + 1) * lanes)
        gq_ref[:, at] = (mix * conv_ref[:, full].astype(jnp.float32)).astype(jnp.bfloat16)
        gated = mix * query_ref[:, full].astype(jnp.float32)
        for k in range(segments):
            start = (line * segments + k) * (toks // segments + GAP)
            gc_ref[start : start + toks // segments, :] = gated[k * (toks // segments) : (k + 1) * (toks // segments), :]
    store = pltpu.make_async_copy(gq_ref, out_hbm.at[:, pl.ds(half * rows, rows)], sem)
    store.start()
    decay = [decay_ref[n, mine] for n in range(modes)]
    span = toks // segments

    def step(t, state):
        at = pl.ds(t, sublanes, stride=span + GAP)
        row = gc_ref[at, :]
        state = tuple(decay[n] * state[n] + row for n in range(modes))
        if half == 0:
            rows_ref[at, :] = summed([other_ref[n, mine] * state[n] for n in range(modes)])
        return state

    zero = jnp.zeros((sublanes, lanes), jnp.float32)
    state = steps_back(span, step, (zero,) * modes, 16)
    segment = segment_of((sublanes, lanes), segments)
    whole = []
    for n in range(modes):
        state_ref[n] = state[n]
        total = state[n]
        if segments > 1:
            factor = jnp.where(segment < segments - 1, lap_ref[n, mine], 0.0)
            for _ in range(segments - 1):
                total = state[n] + factor * rolled(total, -1)
        whole.append(total)
    packs = modes // segments
    for m in range(packs):
        packed = whole[m * segments]
        for j in range(1, segments):
            packed = jnp.where(segment == j, rolled(whole[m * segments + j], j), packed)
        if half == 0:
            pack_ref[m] = packed
        else:
            pack_ref[m] = other_ref[m]
            pack_ref[packs + m] = packed
    store.wait()


def gate(half, rows, segments, pieces, acc, nears, query_in, conv_out, decay, lap, other, partial):
    toks, width = query_in.shape
    modes, _, lanes = decay.shape
    sublanes = rows // lanes * segments
    vmem = pl.BlockSpec(memory_space=pltpu.VMEM)
    high = pl.BlockSpec(memory_space=pltpu.HBM)
    more = [] if partial is None else [partial]
    lines = (sublanes * (toks // segments + GAP), lanes)
    return pl.pallas_call(
        functools.partial(gate_kernel, half, rows, segments, pieces, len(nears)),
        in_specs=[vmem] * (6 + len(nears)) + [high] * len(more),
        out_specs=(high, vmem, vmem, vmem),
        out_shape=(
            jax.ShapeDtypeStruct((toks, width), jnp.bfloat16),
            jax.ShapeDtypeStruct(lines, jnp.float32),
            jax.ShapeDtypeStruct((modes, sublanes, lanes), jnp.float32),
            jax.ShapeDtypeStruct(((1 + half) * modes // segments, sublanes, lanes), jnp.float32),
        ),
        scratch_shapes=([pltpu.VMEM(lines, jnp.float32)] if half == 0 else [])
        + [pltpu.VMEM((toks, rows), jnp.bfloat16), pltpu.SemaphoreType.DMA],
        input_output_aliases={6 + len(nears): 0} if more else {},
        compiler_params=pltpu.CompilerParams(vmem_limit_bytes=VMEM),
        cost_estimate=QUICK,
    )(acc, *nears, query_in, conv_out, decay, lap, other, *more)


def summed(terms):
    while len(terms) > 1:
        terms = [terms[k] + terms[k + 1] if k + 1 < len(terms) else terms[k] for k in range(0, len(terms), 2)]
    return terms[0]


def scan_kernel(half, segments, gc_ref, state_ref, decay_ref, lap_ref, residue_ref, rows_ref):
    modes, sublanes, lanes = state_ref.shape
    mine = slice(half * sublanes, (half + 1) * sublanes)
    span = gc_ref.shape[0] // sublanes - GAP
    segment = segment_of((sublanes, lanes), segments)
    decay = [decay_ref[n, mine] for n in range(modes)]
    start = []
    for n in range(modes):
        total = jnp.zeros((sublanes, lanes), jnp.float32)
        if segments > 1:
            for k in range(segments - 2, -1, -1):
                total = jnp.where(segment == k, rolled(state_ref[n] + lap_ref[n, mine] * total, -1), total)
        start.append(total)

    def step(t, state):
        at = pl.ds(t, sublanes, stride=span + GAP)
        row = gc_ref[at, :]
        state = tuple(decay[n] * state[n] + row for n in range(modes))
        rows_ref[at, :] = summed([residue_ref[n, mine] * state[n] for n in range(modes)])
        return state

    steps_back(span, step, tuple(start), 8)


def scan(half, segments, grad_conv, state, decay, lap, residues):
    vmem = pl.BlockSpec(memory_space=pltpu.VMEM)
    return pl.pallas_call(
        functools.partial(scan_kernel, half, segments),
        in_specs=[vmem] * 5,
        out_specs=vmem,
        out_shape=jax.ShapeDtypeStruct(grad_conv.shape, jnp.float32),
        compiler_params=pltpu.CompilerParams(vmem_limit_bytes=VMEM),
        cost_estimate=QUICK,
    )(grad_conv, state, decay, lap, residues)


def laps_kernel(segments, span, decay_ref, lap_ref, wide_ref):
    modes, sublanes, lanes = decay_ref.shape
    sublanes //= 2
    packs = modes // segments
    segment = segment_of((sublanes, lanes), segments)
    for half in range(2):
        mine = slice(half * sublanes, (half + 1) * sublanes)
        for m in range(packs):
            packed = None
            for j in range(segments):
                lap = power(decay_ref[m * segments + j, mine], span)
                lap_ref[m * segments + j, mine] = lap
                wide = power(lap, segments)
                packed = wide if packed is None else jnp.where(segment == j, wide, packed)
            wide_ref[half * packs + m] = packed


def laps(segments, toks, decay):
    modes, sublanes, lanes = decay.shape
    vmem = pl.BlockSpec(memory_space=pltpu.VMEM)
    return pl.pallas_call(
        functools.partial(laps_kernel, segments, toks // segments),
        in_specs=[vmem],
        out_specs=(vmem, vmem),
        out_shape=(
            jax.ShapeDtypeStruct(decay.shape, jnp.float32),
            jax.ShapeDtypeStruct((2 * modes // segments, sublanes // 2, lanes), jnp.float32),
        ),
        compiler_params=pltpu.CompilerParams(vmem_limit_bytes=VMEM),
        cost_estimate=QUICK,
    )(decay)


def states_in(ref, shape):
    if ref.shape == shape:
        return [ref[m] for m in range(shape[0])]
    packs, sublanes, _ = shape
    rows = decode(ref, (0, 0, packs * sublanes // 2), 0, packs * sublanes, 1)
    return [rows[m * sublanes : (m + 1) * sublanes, :] for m in range(packs)]


def join_kernel(round_, group_ref, state_ref, arrived_ref, wide_ref, coded_ref, *out_refs):
    earlier = (group_ref[0] >> round_) % 2 == 0
    packs, sublanes, _ = state_ref.shape
    joined = []
    for m, other in enumerate(states_in(arrived_ref, state_ref.shape)):
        wide = power(wide_ref[m], 1 << round_)
        mine = state_ref[m]
        joined.append(jnp.where(earlier, mine + wide * other, other + wide * mine))
        for out_ref in out_refs:
            out_ref[m] = joined[-1]
    codes, peaks = encode(jnp.concatenate(joined, axis=0), packs * sublanes // 2)
    put(codes, coded_ref, 0)
    put_peaks(peaks, coded_ref)


def join(round_, group, state, arrived, wide, last):
    vmem = pl.BlockSpec(memory_space=pltpu.VMEM)
    packs, sublanes, lanes = state.shape
    return pl.pallas_call(
        functools.partial(join_kernel, round_),
        in_specs=[pl.BlockSpec(memory_space=pltpu.SMEM)] + [vmem] * 3,
        out_specs=[vmem] * (1 if last else 2),
        out_shape=[
            jax.ShapeDtypeStruct((packs * sublanes + PEAKS, lanes), jnp.bfloat16),
            jax.ShapeDtypeStruct(state.shape, jnp.float32),
        ][: 1 if last else 2],
        compiler_params=pltpu.CompilerParams(vmem_limit_bytes=VMEM),
        cost_estimate=QUICK,
    )(group, state, arrived, wide)


def fix_kernel(segments, rounds, group_ref, *refs):
    scanned_refs, state_ref, arrived_refs = refs[:2], refs[2], refs[3 : 3 + rounds]
    decay_ref, lap_ref, wide_ref, residue_ref, out_hbm, rows_ref, out_ref, sems = refs[3 + rounds :]
    toks, width = out_ref.shape
    modes, sublanes, lanes = state_ref.shape
    packs = modes // segments
    rows = width // 2
    span = toks // segments
    segment = segment_of((sublanes, lanes), segments)
    earlier = [(group_ref[0] >> r) % 2 == 0 for r in range(rounds)]
    arrived = [states_in(ref, (2 * packs, sublanes, lanes)) for ref in arrived_refs]
    stores = []
    for half in range(2):
        mine = slice(half * sublanes, (half + 1) * sublanes)
        decay = [decay_ref[n, mine] for n in range(modes)]
        start = []
        for m in range(packs):
            brought = jnp.zeros((sublanes, lanes), jnp.float32)
            between = jnp.ones((sublanes, lanes), jnp.float32)
            for r in range(rounds):
                state = arrived[r][half * packs + m]
                brought = jnp.where(earlier[r], brought + between * state, brought)
                if r + 1 < rounds:
                    between = jnp.where(earlier[r], between * power(wide_ref[half * packs + m], 1 << r), between)
            for j in range(segments):
                n = m * segments + j
                total = rolled(brought, segments - 1 - j)
                for k in range(segments - 2, -1, -1):
                    before = lap_ref[n, mine] * total
                    if half == 0:
                        before = before + state_ref[n]
                    total = jnp.where(segment == k, rolled(before, -1), total)
                start.append(residue_ref[n, mine] * total)

        def step(t, state, scanned_ref=scanned_refs[half], decay=decay):
            at = pl.ds(t, sublanes, stride=span + GAP)
            state = tuple(decay[n] * state[n] for n in range(modes))
            rows_ref[at, :] = scanned_ref[at, :] + summed(list(state))
            return state

        state, columns = tuple(start), pl.ds(half * rows, rows)
        for base in (span // 2, 0):
            state = steps_back(span // 2, step, state, 8, base)
            for k in range(segments):
                for line in range(rows // lanes):
                    at = slice(half * rows + line * lanes, half * rows + (line + 1) * lanes)
                    first = (line * segments + k) * (span + GAP) + base
                    out_ref[k * span + base : k * span + base + span // 2, at] = rows_ref[
                        first : first + span // 2, :
                    ].astype(jnp.bfloat16)
                lines = pl.ds(k * span + base, span // 2)
                stores.append(
                    pltpu.make_async_copy(
                        out_ref.at[lines, columns], out_hbm.at[lines, columns], sems.at[len(stores)]
                    )
                )
                stores[-1].start()
    for store in stores:
        store.wait()


def fix(segments, group, scanned, state, arrived, decay, lap, wide, residues, toks, width):
    vmem = pl.BlockSpec(memory_space=pltpu.VMEM)
    return pl.pallas_call(
        functools.partial(fix_kernel, segments, len(arrived)),
        in_specs=[pl.BlockSpec(memory_space=pltpu.SMEM)] + [vmem] * (7 + len(arrived)),
        out_specs=pl.BlockSpec(memory_space=pltpu.HBM),
        out_shape=jax.ShapeDtypeStruct((toks, width), jnp.bfloat16),
        scratch_shapes=[
            pltpu.VMEM(scanned[0].shape, jnp.float32),
            pltpu.VMEM((toks, width), jnp.bfloat16),
            pltpu.SemaphoreType.DMA((4 * segments,)),
        ],
        compiler_params=pltpu.CompilerParams(vmem_limit_bytes=VMEM),
        cost_estimate=QUICK,
    )(group, *scanned, state, *arrived, decay, lap, wide, residues)


def local(out_grad, out_weight, query_in, conv_out, residues, decay_rates):
    toks, width = query_in.shape
    modes = decay_rates.shape[1]
    lanes = math.gcd(width, 128)
    size, groups = lax.axis_size("ch"), lax.axis_size("ctx")
    bits = [1 << i for i in range(size.bit_length() - 1)]
    place = jnp.reshape(lax.axis_index("ch"), (1,)).astype(jnp.int32)
    group = jnp.reshape(lax.axis_index("ctx"), (1,)).astype(jnp.int32)
    half_rows = width // 2
    lines = half_rows // lanes
    segments = 8 // lines
    by_mode = lambda values: jnp.repeat(values.T.reshape(modes, width // lanes, lanes), segments, axis=1)
    decay, residue = by_mode(decay_rates), by_mode(residues)

    portions, order, waits = PORTIONS, ORDER, WAITS
    if size != 8:
        waits = {}
        portions = ((tuple(range(len(bits))), 2, 0), (tuple(range(len(bits))), 2, 1))
        order = [
            ((p, s, block),)
            for p in range(2)
            for s, bit in enumerate(bits)
            for block in sorted(range(0, size, 2 * bit), reverse=True)
        ] + [("laps", None), ("sum", 0), ("sum", 1), ("gate", 0), ("gate", 1), ("scan", 1), ("fix", None)]
    offsets = [sum(width // part for _, part, _ in portions[:p]) for p in range(len(portions))]

    received, sums, scanned, states, packed = {}, {}, {}, {}, {}
    grad_query = last = None
    added = set()

    def after(value):
        return value if last is None else lax.optimization_barrier((value, last, *awaited))[0]

    def collect(wanted):
        arrays, places = [], []
        for key in wanted:
            array, *place = received[key]
            index = next((i for i, known in enumerate(arrays) if known is array), len(arrays))
            if index == len(arrays):
                arrays.append(array)
            places.append((index, tuple(place)))
        return arrays, places

    for todo in order:
        awaited = [received[key][0] for key in waits.get(todo, ())]
        kind, half = todo[:2] if isinstance(todo[0], str) else ("send", None)
        inside = [q for q, (_, _, lies) in enumerate(portions) if lies == half]
        if kind in ("send", "both"):
            messages = todo[1:] if kind == "both" else (todo,)
            bit_of = lambda key: bits[portions[key[0]][0][key[1]]]
            arrays, planned = [], []
            for message in messages:
                wanted = [[(p, i, block ^ bit_of((p, s, block))) for i in range(s)] for p, s, block in message]
                arrays, places = collect([key for keys in wanted for key in keys])
                places = iter(places)
                planned.append(
                    tuple(
                        (block ^ bit_of((p, s, block)), offsets[p], width // portions[p][1], tuple(next(places) for _ in keys))
                        for (p, s, block), keys in zip(message, wanted)
                    )
                )
            if last is None:
                *payloads, turned = early_send(planned, width, place, out_weight, out_grad, True)
            elif kind == "both":
                payloads = early_send(planned, width, after(place), out_weight, turned, False)
            else:
                payloads = [send(planned[0], True, width, after(place), out_weight, turned, arrays)]
            last = payloads[0]
            for message, items, payload in zip(messages, planned, payloads):
                bit = bit_of(message[0])
                arrived = lax.ppermute(payload, "ch", [(i, i ^ bit) for i in range(size)])
                start = peak = 0
                for key, (_, _, rows, _) in zip(message, items):
                    part = part_of(rows, len(items), folds_of(toks))
                    received[key] = (arrived, start, peak, part)
                    start, peak = start + rows, peak + rows // part
        elif kind == "laps":
            lap, wide = laps(segments, toks, after(decay))
            last = wide
        elif kind == "sum":
            items = tuple((0, offsets[q], width // portions[q][1], ()) for q in inside)
            last = sums[half] = send(items, False, width, after(place), out_weight, turned, [])
        elif kind == "add":
            arrays, places = collect([(q, len(bits) - 1, 0) for q in inside])
            pieces = tuple(
                (offsets[q] - half * half_rows, width // portions[q][1], (at,)) for q, at in zip(inside, places)
            )
            last = sums[half] = add(pieces, after(sums[half]), arrays)
            added.add(half)
        elif kind == "gate":
            stages = range(len(bits) - (half in added))
            arrays, places = collect([(q, i, 0) for q in inside for i in stages])
            pieces = tuple(
                (offsets[q] - half * half_rows, tuple(places[i * len(stages) : (i + 1) * len(stages)]))
                for i, q in enumerate(inside)
            )
            other = residue if half == 0 else packed[0]
            grad_query, scanned[half], states[half], packed[half] = gate(
                half,
                half_rows,
                segments,
                pieces,
                after(sums[half]),
                arrays,
                query_in,
                conv_out,
                decay,
                lap,
                other,
                grad_query,
            )
            last = packed[half]
        elif kind == "scan":
            groups = lax.axis_size("ctx")
            swap = lambda array, round_: lax.ppermute(array, "ctx", [(i, i ^ (1 << round_)) for i in range(groups)])
            arrived, joined = [swap(packed[1], 0)], packed[1]
            rounds = groups.bit_length() - 1
            for round_ in range(1, rounds):
                last, *joined = join(round_ - 1, after(group), joined, arrived[-1], wide, round_ + 1 == rounds)
                joined = joined[0] if joined else None
                arrived.append(swap(last, round_))
            scanned[1] = scan(1, segments, after(scanned[1]), states[1], decay, lap, residue)
        else:
            grad_input = fix(
                segments, group, [scanned[0], scanned[1]], states[0], arrived, decay, lap, wide, residue, toks, width
            )
    return grad_query, grad_input


def solution(mesh):
    placed = (
        P("ctx", "ch"),
        P(None, "ch"),
        P("ctx", "ch"),
        P("ctx", "ch"),
        P("ch", None),
        P("ch", None),
    )
    return jax.shard_map(
        local,
        mesh=mesh,
        in_specs=placed,
        out_specs=(P("ctx", "ch"), P("ctx", "ch")),
        check_vma=False,
    )
```

```python
import functools
import math

import jax
import jax.numpy as jnp
from jax import lax
from jax.experimental import pallas as pl
from jax.experimental.pallas import tpu as pltpu
from jax.sharding import PartitionSpec as P

PEAKS = 16
SPAN = 251 * math.log(2.0)
SHIFT = 125 * math.log(2.0)
STEP = 256
PIECE = 128
GAP = 8
VMEM = 24 * 1024 * 1024
QUICK = pl.CostEstimate(flops=0, bytes_accessed=1024, transcendentals=0)

PORTIONS = (((0, 1, 2), 4, 0), ((1, 0, 2), 4, 0), ((0, 1, 2), 4, 1), ((0, 1, 2), 4, 1))
ORDER = (
    ((0, 0, 6), (0, 0, 2)), ("both", ((1, 0, 5), (1, 0, 1))), ((2, 0, 6), (3, 0, 6)), ((2, 0, 4), (3, 0, 4)),
    ("sum", 1), ((2, 0, 2), (3, 0, 2)), ((1, 0, 4), (0, 1, 4)), ((1, 1, 4), (0, 0, 4)), ((2, 1, 4), (3, 1, 4)),
    ((1, 0, 0), (0, 1, 0)), ((0, 2, 0), (1, 2, 0)), ((2, 2, 0), (3, 2, 0)), ((1, 1, 0), (0, 0, 0)),
    ((2, 1, 0), (3, 1, 0)), ((2, 0, 0), (3, 0, 0)), ("sum", 0), ("laps", None), ("gate", 0), ("add", 1), ("gate", 1),
    ("scan", 1), ("fix", None),
)
WAITS = {
    ((1, 0, 0), (0, 1, 0)): ((1, 0, 4),),
    ("gate", 0): ((0, 2, 0), (1, 0, 0)),
    ("gate", 1): ((2, 1, 0),),
}


def folds_of(toks):
    return toks // 128 if toks % 128 == 0 and PEAKS % (toks // 128) == 0 else 1


def part_of(rows, blocks, folds):
    return next(
        part for part in range(16, rows + 1, 16) if rows % part == 0 and rows // part * blocks * folds <= PEAKS
    )


def step_of(rows):
    return next(step for step in (STEP, STEP // 2, rows) if rows % step == 0)


def encode(block, part):
    codes, peaks = [], []
    for i in range(block.shape[0] // part):
        piece = block[i * part : (i + 1) * part, :]
        size = jnp.abs(piece)
        peak = jnp.maximum(jnp.max(size, axis=0, keepdims=True) * 1.01, 1e-30)
        peak = peak.astype(jnp.bfloat16).astype(jnp.float32)
        code = jnp.exp(size * (SPAN / peak) - SHIFT)
        codes.append(jnp.where(piece < 0, -code, code))
        peaks.append(peak)
    return jnp.concatenate(codes, axis=0).astype(jnp.bfloat16), peaks


def put(codes, out_ref, at):
    lanes = out_ref.shape[1]
    folds = codes.shape[1] // lanes
    rows = (out_ref.shape[0] - PEAKS) // folds
    for fold in range(folds):
        out_ref[fold * rows + at : fold * rows + at + codes.shape[0], :] = codes[:, fold * lanes : (fold + 1) * lanes]


def put_peaks(peaks, out_ref):
    lanes = out_ref.shape[1]
    peaks = [peak[:, at : at + lanes] for peak in peaks for at in range(0, peak.shape[1], lanes)]
    if len(peaks) < PEAKS:
        peaks.append(jnp.zeros((PEAKS - len(peaks), lanes), jnp.float32))
    out_ref[out_ref.shape[0] - PEAKS :, :] = jnp.concatenate(peaks, axis=0).astype(jnp.bfloat16)


def decode(ref, place, first, count, folds):
    start, peak, part = place
    rows = (ref.shape[0] - PEAKS) // folds
    peaks = ref[ref.shape[0] - PEAKS :, :].astype(jnp.float32) * (1.0 / SPAN)
    columns = []
    for fold in range(folds):
        blocks = []
        for i in range(first // part, -(-(first + count) // part)):
            low, high = max(first, i * part), min(first + count, (i + 1) * part)
            code = ref[fold * rows + start + low : fold * rows + start + high, :].astype(jnp.float32)
            at = (peak + i) * folds + fold
            size = (jnp.log(jnp.abs(code)) + SHIFT) * peaks[at : at + 1, :]
            blocks.append(jnp.where(code < 0, -size, size))
        columns.append(jnp.concatenate(blocks, axis=0))
    return jnp.concatenate(columns, axis=1)


def pinned(array):
    return pltpu.with_memory_space_constraint(array, pltpu.HBM)


def send_kernel(items, coded, width, near, place_ref, w_ref, turned_ref, *refs):
    near_refs, out_ref = refs[:near], refs[near]
    folds = folds_of(turned_ref.shape[1])
    base, peaks = 0, []
    for block, offset, rows, sources in items:
        step = step_of(rows)
        first = (place_ref[0] ^ block) * width + offset
        for at in range(0, rows, step):
            total = jnp.dot(
                w_ref[pl.ds(pl.multiple_of(first + at, 16), step), :],
                turned_ref[...],
                preferred_element_type=jnp.float32,
            )
            for source, place in sources:
                total = total + decode(near_refs[source], place, at, step, folds)
            if coded:
                total, more = encode(total, part_of(rows, len(items), folds))
                peaks += more
                put(total, out_ref, base + at)
            else:
                out_ref[base + at : base + at + step, :] = total
        base += rows
    if coded:
        put_peaks(peaks, out_ref)


def send(items, coded, width, place, weight, turned, nears):
    toks = turned.shape[1]
    vmem = pl.BlockSpec(memory_space=pltpu.VMEM)
    count = sum(rows for _, _, rows, _ in items)
    folds = folds_of(toks)
    shape = (folds * count + PEAKS, toks // folds) if coded else (count, toks)
    return pl.pallas_call(
        functools.partial(send_kernel, items, coded, width, len(nears)),
        in_specs=[pl.BlockSpec(memory_space=pltpu.SMEM)] + [vmem] * (2 + len(nears)),
        out_specs=vmem,
        out_shape=jax.ShapeDtypeStruct(shape, jnp.bfloat16 if coded else jnp.float32),
        compiler_params=pltpu.CompilerParams(vmem_limit_bytes=VMEM),
        cost_estimate=QUICK,
    )(place, weight, turned, *nears)


def early_kernel(messages, width, turns, place_ref, w_hbm, g_ref, *refs):
    out_refs, refs = refs[: len(messages)], refs[len(messages) :]
    w_ref, sems = refs[-2:]
    turned_ref = refs[0] if turns else g_ref
    depth, toks = turned_ref.shape
    copies, waits = [], []
    if turns:
        piece = math.gcd(toks, PIECE)
        for at in range(0, toks, piece):
            lines = pl.ds(at, piece)
            copies.append(pltpu.make_async_copy(g_ref.at[lines, :], refs[1].at[lines, :], sems.at[len(copies)]))
    grads, base = len(copies), 0
    for items in messages:
        for block, offset, rows, _ in items:
            step = math.gcd(rows, PIECE)
            first = pl.multiple_of((place_ref[0] ^ block) * width + offset, 16)
            for at in range(0, rows, step):
                copies.append(
                    pltpu.make_async_copy(
                        w_hbm.at[pl.ds(first + at, step), :], w_ref.at[pl.ds(base + at, step), :], sems.at[len(copies)]
                    )
                )
            base += rows
    for copy in copies:
        copy.start(priority=1)
    for i in range(grads):
        copies[i].wait()
        turned_ref[:, i * piece : (i + 1) * piece] = refs[1][i * piece : (i + 1) * piece, :].T
    waits, base = iter(copies[grads:]), 0
    for items, out_ref in zip(messages, out_refs):
        start, peaks = base, []
        for _, _, rows, _ in items:
            step = step_of(rows)
            for at in range(base, base + rows, step):
                for _ in range(step // math.gcd(rows, PIECE)):
                    next(waits).wait()
                total = jnp.dot(w_ref[at : at + step, :], turned_ref[...], preferred_element_type=jnp.float32)
                total, more = encode(total, part_of(rows, len(items), folds_of(toks)))
                peaks += more
                put(total, out_ref, at - start)
            base += rows
        put_peaks(peaks, out_ref)


def early_send(messages, width, place, weight, grad, turns):
    toks, depth = grad.shape if turns else grad.shape[::-1]
    vmem = pl.BlockSpec(memory_space=pltpu.VMEM)
    high = pl.BlockSpec(memory_space=pltpu.HBM)
    counts = [sum(rows for _, _, rows, _ in items) for items in messages]
    folds = folds_of(toks)
    steps = sum(rows // math.gcd(rows, PIECE) for items in messages for _, _, rows, _ in items)
    steps += toks // math.gcd(toks, PIECE) if turns else 0
    coded = [jax.ShapeDtypeStruct((folds * count + PEAKS, toks // folds), jnp.bfloat16) for count in counts]
    return pl.pallas_call(
        functools.partial(early_kernel, messages, width, turns),
        in_specs=[pl.BlockSpec(memory_space=pltpu.SMEM), high, high if turns else vmem],
        out_specs=[vmem] * (len(messages) + turns),
        out_shape=coded + [jax.ShapeDtypeStruct((depth, toks), jnp.bfloat16)] * turns,
        scratch_shapes=[pltpu.VMEM((toks, depth), jnp.bfloat16)] * turns
        + [pltpu.VMEM((sum(counts), depth), jnp.bfloat16), pltpu.SemaphoreType.DMA((steps,))],
        compiler_params=pltpu.CompilerParams(vmem_limit_bytes=VMEM),
        cost_estimate=QUICK,
    )(place, pinned(weight), pinned(grad) if turns else grad)


def add_kernel(pieces, near, acc_ref, *refs):
    near_refs, out_ref = refs[:near], refs[near]
    toks = acc_ref.shape[1]
    for first, rows, sources in pieces:
        total = acc_ref[first : first + rows, :]
        for source, place in sources:
            total = total + decode(near_refs[source], place, 0, rows, folds_of(toks))
        out_ref[first : first + rows, :] = total


def add(pieces, acc, nears):
    vmem = pl.BlockSpec(memory_space=pltpu.VMEM)
    return pl.pallas_call(
        functools.partial(add_kernel, pieces, len(nears)),
        in_specs=[vmem] * (1 + len(nears)),
        out_specs=vmem,
        out_shape=jax.ShapeDtypeStruct(acc.shape, jnp.float32),
        compiler_params=pltpu.CompilerParams(vmem_limit_bytes=VMEM),
        cost_estimate=QUICK,
    )(acc, *nears)


def steps_back(count, body, state, unroll, base=0):
    unroll = math.gcd(count, unroll)

    def some(i, state):
        for j in range(unroll):
            state = body(base + count - 1 - (i * unroll + j), state)
        return state

    return lax.fori_loop(0, count // unroll, some, state)


def power(base, exponent):
    result = None
    while exponent:
        if exponent % 2:
            result = base if result is None else result * base
        base = base * base
        exponent //= 2
    return result


def segment_of(shape, segments):
    return lax.rem(lax.broadcasted_iota(jnp.int32, shape, 0), segments)


def rolled(value, by):
    by %= value.shape[0]
    return pltpu.roll(value, by, 0) if by else value


def gate_kernel(half, rows, segments, pieces, near, acc_ref, *refs):
    near_refs, refs = refs[:near], refs[near:]
    query_ref, conv_ref, decay_ref, lap_ref, other_ref = refs[:5]
    out_hbm, rows_ref, state_ref, pack_ref = refs[-7:-3] if half == 0 else refs[-6:-2]
    gq_ref, sem = refs[-2:]
    gc_ref = refs[-3] if half == 0 else rows_ref
    toks = query_ref.shape[0]
    modes, sublanes, lanes = state_ref.shape
    mine = slice(half * sublanes, (half + 1) * sublanes)
    for line in range(rows // lanes):
        mix = acc_ref[line * lanes : (line + 1) * lanes, :]
        first, sources = next(piece for piece in reversed(pieces) if piece[0] <= line * lanes)
        for source, place in sources:
            mix = mix + decode(near_refs[source], place, line * lanes - first, lanes, folds_of(toks))
        mix = mix.T
        at = slice(line * lanes, (line + 1) * lanes)
        full = slice(half * rows + line * lanes, half * rows + (line + 1) * lanes)
        gq_ref[:, at] = (mix * conv_ref[:, full].astype(jnp.float32)).astype(jnp.bfloat16)
        gated = mix * query_ref[:, full].astype(jnp.float32)
        for k in range(segments):
            start = (line * segments + k) * (toks // segments + GAP)
            gc_ref[start : start + toks // segments, :] = gated[k * (toks // segments) : (k + 1) * (toks // segments), :]
    store = pltpu.make_async_copy(gq_ref, out_hbm.at[:, pl.ds(half * rows, rows)], sem)
    store.start()
    decay = [decay_ref[n, mine] for n in range(modes)]
    span = toks // segments

    def step(t, state):
        at = pl.ds(t, sublanes, stride=span + GAP)
        row = gc_ref[at, :]
        state = tuple(decay[n] * state[n] + row for n in range(modes))
        if half == 0:
            rows_ref[at, :] = summed([other_ref[n, mine] * state[n] for n in range(modes)])
        return state

    zero = jnp.zeros((sublanes, lanes), jnp.float32)
    state = steps_back(span, step, (zero,) * modes, 16)
    segment = segment_of((sublanes, lanes), segments)
    whole = []
    for n in range(modes):
        state_ref[n] = state[n]
        total = state[n]
        if segments > 1:
            factor = jnp.where(segment < segments - 1, lap_ref[n, mine], 0.0)
            for _ in range(segments - 1):
                total = state[n] + factor * rolled(total, -1)
        whole.append(total)
    packs = modes // segments
    for m in range(packs):
        packed = whole[m * segments]
        for j in range(1, segments):
            packed = jnp.where(segment == j, rolled(whole[m * segments + j], j), packed)
        if half == 0:
            pack_ref[m] = packed
        else:
            pack_ref[m] = other_ref[m]
            pack_ref[packs + m] = packed
    store.wait()


def gate(half, rows, segments, pieces, acc, nears, query_in, conv_out, decay, lap, other, partial):
    toks, width = query_in.shape
    modes, _, lanes = decay.shape
    sublanes = rows // lanes * segments
    vmem = pl.BlockSpec(memory_space=pltpu.VMEM)
    high = pl.BlockSpec(memory_space=pltpu.HBM)
    more = [] if partial is None else [partial]
    lines = ((sublanes + 1) * (toks // segments + GAP), lanes)
    return pl.pallas_call(
        functools.partial(gate_kernel, half, rows, segments, pieces, len(nears)),
        in_specs=[vmem] * (6 + len(nears)) + [high] * len(more),
        out_specs=(high, vmem, vmem, vmem),
        out_shape=(
            jax.ShapeDtypeStruct((toks, width), jnp.bfloat16),
            jax.ShapeDtypeStruct(lines, jnp.float32),
            jax.ShapeDtypeStruct((modes, sublanes, lanes), jnp.float32),
            jax.ShapeDtypeStruct(((1 + half) * modes // segments, sublanes, lanes), jnp.float32),
        ),
        scratch_shapes=([pltpu.VMEM(lines, jnp.float32)] if half == 0 else [])
        + [pltpu.VMEM((toks, rows), jnp.bfloat16), pltpu.SemaphoreType.DMA],
        input_output_aliases={6 + len(nears): 0} if more else {},
        compiler_params=pltpu.CompilerParams(vmem_limit_bytes=VMEM),
        cost_estimate=QUICK,
    )(acc, *nears, query_in, conv_out, decay, lap, other, *more)


def summed(terms):
    while len(terms) > 1:
        terms = [terms[k] + terms[k + 1] if k + 1 < len(terms) else terms[k] for k in range(0, len(terms), 2)]
    return terms[0]


def scan_kernel(half, segments, gc_ref, state_ref, decay_ref, lap_ref, residue_ref, rows_ref):
    modes, sublanes, lanes = state_ref.shape
    mine = slice(half * sublanes, (half + 1) * sublanes)
    span = gc_ref.shape[0] // (sublanes + 1) - GAP
    segment = segment_of((sublanes, lanes), segments)
    decay = [decay_ref[n, mine] for n in range(modes)]
    start = []
    for n in range(modes):
        total = jnp.zeros((sublanes, lanes), jnp.float32)
        if segments > 1:
            for k in range(segments - 2, -1, -1):
                total = jnp.where(segment == k, rolled(state_ref[n] + lap_ref[n, mine] * total, -1), total)
        start.append(total)

    def step(t, state):
        at = pl.ds(t, sublanes, stride=span + GAP)
        row = gc_ref[at, :]
        state = tuple(decay[n] * state[n] + row for n in range(modes))
        rows_ref[at, :] = summed([residue_ref[n, mine] * state[n] for n in range(modes)])
        return state

    steps_back(span, step, tuple(start), 8)


def scan(half, segments, grad_conv, state, decay, lap, residues):
    vmem = pl.BlockSpec(memory_space=pltpu.VMEM)
    return pl.pallas_call(
        functools.partial(scan_kernel, half, segments),
        in_specs=[vmem] * 5,
        out_specs=vmem,
        out_shape=jax.ShapeDtypeStruct(grad_conv.shape, jnp.float32),
        compiler_params=pltpu.CompilerParams(vmem_limit_bytes=VMEM),
        cost_estimate=QUICK,
    )(grad_conv, state, decay, lap, residues)


def laps_kernel(segments, span, decay_ref, lap_ref, wide_ref):
    modes, sublanes, lanes = decay_ref.shape
    sublanes //= 2
    packs = modes // segments
    segment = segment_of((sublanes, lanes), segments)
    for half in range(2):
        mine = slice(half * sublanes, (half + 1) * sublanes)
        for m in range(packs):
            packed = None
            for j in range(segments):
                lap = power(decay_ref[m * segments + j, mine], span)
                lap_ref[m * segments + j, mine] = lap
                wide = power(lap, segments)
                packed = wide if packed is None else jnp.where(segment == j, wide, packed)
            wide_ref[half * packs + m] = packed


def laps(segments, toks, decay):
    modes, sublanes, lanes = decay.shape
    vmem = pl.BlockSpec(memory_space=pltpu.VMEM)
    return pl.pallas_call(
        functools.partial(laps_kernel, segments, toks // segments),
        in_specs=[vmem],
        out_specs=(vmem, vmem),
        out_shape=(
            jax.ShapeDtypeStruct(decay.shape, jnp.float32),
            jax.ShapeDtypeStruct((2 * modes // segments, sublanes // 2, lanes), jnp.float32),
        ),
        compiler_params=pltpu.CompilerParams(vmem_limit_bytes=VMEM),
        cost_estimate=QUICK,
    )(decay)


def states_in(ref, shape):
    if ref.shape == shape:
        return [ref[m] for m in range(shape[0])]
    packs, sublanes, _ = shape
    rows = decode(ref, (0, 0, packs * sublanes // 2), 0, packs * sublanes, 1)
    return [rows[m * sublanes : (m + 1) * sublanes, :] for m in range(packs)]


def join_kernel(round_, group_ref, state_ref, arrived_ref, wide_ref, coded_ref, *out_refs):
    earlier = (group_ref[0] >> round_) % 2 == 0
    packs, sublanes, _ = state_ref.shape
    joined = []
    for m, other in enumerate(states_in(arrived_ref, state_ref.shape)):
        wide = power(wide_ref[m], 1 << round_)
        mine = state_ref[m]
        joined.append(jnp.where(earlier, mine + wide * other, other + wide * mine))
        for out_ref in out_refs:
            out_ref[m] = joined[-1]
    codes, peaks = encode(jnp.concatenate(joined, axis=0), packs * sublanes // 2)
    put(codes, coded_ref, 0)
    put_peaks(peaks, coded_ref)


def join(round_, group, state, arrived, wide, last):
    vmem = pl.BlockSpec(memory_space=pltpu.VMEM)
    packs, sublanes, lanes = state.shape
    return pl.pallas_call(
        functools.partial(join_kernel, round_),
        in_specs=[pl.BlockSpec(memory_space=pltpu.SMEM)] + [vmem] * 3,
        out_specs=[vmem] * (1 if last else 2),
        out_shape=[
            jax.ShapeDtypeStruct((packs * sublanes + PEAKS, lanes), jnp.bfloat16),
            jax.ShapeDtypeStruct(state.shape, jnp.float32),
        ][: 1 if last else 2],
        compiler_params=pltpu.CompilerParams(vmem_limit_bytes=VMEM),
        cost_estimate=QUICK,
    )(group, state, arrived, wide)


def fix_kernel(segments, rounds, group_ref, *refs):
    scanned_refs, state_ref, arrived_refs = refs[:2], refs[2], refs[3 : 3 + rounds]
    decay_ref, lap_ref, wide_ref, residue_ref, out_hbm, rows_ref, out_ref, sems = refs[3 + rounds :]
    toks, width = out_ref.shape
    modes, sublanes, lanes = state_ref.shape
    packs = modes // segments
    rows = width // 2
    span = toks // segments
    segment = segment_of((sublanes, lanes), segments)
    earlier = [(group_ref[0] >> r) % 2 == 0 for r in range(rounds)]
    arrived = [states_in(ref, (2 * packs, sublanes, lanes)) for ref in arrived_refs]
    stores = []
    for half in range(2):
        mine = slice(half * sublanes, (half + 1) * sublanes)
        decay = [decay_ref[n, mine] for n in range(modes)]
        start = []
        for m in range(packs):
            brought = jnp.zeros((sublanes, lanes), jnp.float32)
            between = jnp.ones((sublanes, lanes), jnp.float32)
            for r in range(rounds):
                state = arrived[r][half * packs + m]
                brought = jnp.where(earlier[r], brought + between * state, brought)
                if r + 1 < rounds:
                    between = jnp.where(earlier[r], between * power(wide_ref[half * packs + m], 1 << r), between)
            for j in range(segments):
                n = m * segments + j
                total = rolled(brought, segments - 1 - j)
                for k in range(segments - 2, -1, -1):
                    before = lap_ref[n, mine] * total
                    if half == 0:
                        before = before + state_ref[n]
                    total = jnp.where(segment == k, rolled(before, -1), total)
                start.append(residue_ref[n, mine] * total)

        def step(t, state, scanned_ref=scanned_refs[half], decay=decay):
            at = pl.ds(t, sublanes, stride=span + GAP)
            state = tuple(decay[n] * state[n] for n in range(modes))
            rows_ref[at, :] = scanned_ref[at, :] + summed(list(state))
            return state

        state, columns = tuple(start), pl.ds(half * rows, rows)
        for base in (span // 2, 0):
            state = steps_back(span // 2, step, state, 8, base)
            for k in range(segments):
                for line in range(rows // lanes):
                    at = slice(half * rows + line * lanes, half * rows + (line + 1) * lanes)
                    first = (line * segments + k) * (span + GAP) + base
                    out_ref[k * span + base : k * span + base + span // 2, at] = rows_ref[
                        first : first + span // 2, :
                    ].astype(jnp.bfloat16)
                lines = pl.ds(k * span + base, span // 2)
                stores.append(
                    pltpu.make_async_copy(
                        out_ref.at[lines, columns], out_hbm.at[lines, columns], sems.at[len(stores)]
                    )
                )
                stores[-1].start()
    for store in stores:
        store.wait()


def fix(segments, group, scanned, state, arrived, decay, lap, wide, residues, toks, width):
    vmem = pl.BlockSpec(memory_space=pltpu.VMEM)
    return pl.pallas_call(
        functools.partial(fix_kernel, segments, len(arrived)),
        in_specs=[pl.BlockSpec(memory_space=pltpu.SMEM)] + [vmem] * (7 + len(arrived)),
        out_specs=pl.BlockSpec(memory_space=pltpu.HBM),
        out_shape=jax.ShapeDtypeStruct((toks, width), jnp.bfloat16),
        scratch_shapes=[
            pltpu.VMEM(scanned[0].shape, jnp.float32),
            pltpu.VMEM((toks, width), jnp.bfloat16),
            pltpu.SemaphoreType.DMA((4 * segments,)),
        ],
        compiler_params=pltpu.CompilerParams(vmem_limit_bytes=VMEM),
        cost_estimate=QUICK,
    )(group, *scanned, state, *arrived, decay, lap, wide, residues)


def local(out_grad, out_weight, query_in, conv_out, residues, decay_rates):
    toks, width = query_in.shape
    modes = decay_rates.shape[1]
    lanes = math.gcd(width, 128)
    size, groups = lax.axis_size("ch"), lax.axis_size("ctx")
    bits = [1 << i for i in range(size.bit_length() - 1)]
    place = jnp.reshape(lax.axis_index("ch"), (1,)).astype(jnp.int32)
    group = jnp.reshape(lax.axis_index("ctx"), (1,)).astype(jnp.int32)
    half_rows = width // 2
    lines = half_rows // lanes
    segments = 8 // lines
    by_mode = lambda values: jnp.repeat(values.T.reshape(modes, width // lanes, lanes), segments, axis=1)
    decay, residue = by_mode(decay_rates), by_mode(residues)

    portions, order, waits = PORTIONS, ORDER, WAITS
    if size != 8:
        waits = {}
        portions = ((tuple(range(len(bits))), 2, 0), (tuple(range(len(bits))), 2, 1))
        order = [
            ((p, s, block),)
            for p in range(2)
            for s, bit in enumerate(bits)
            for block in sorted(range(0, size, 2 * bit), reverse=True)
        ] + [("laps", None), ("sum", 0), ("sum", 1), ("gate", 0), ("gate", 1), ("scan", 1), ("fix", None)]
    offsets = [sum(width // part for _, part, _ in portions[:p]) for p in range(len(portions))]

    received, sums, scanned, states, packed = {}, {}, {}, {}, {}
    grad_query = last = None
    added = set()

    def after(value):
        return value if last is None else lax.optimization_barrier((value, last, *awaited))[0]

    def collect(wanted):
        arrays, places = [], []
        for key in wanted:
            array, *place = received[key]
            index = next((i for i, known in enumerate(arrays) if known is array), len(arrays))
            if index == len(arrays):
                arrays.append(array)
            places.append((index, tuple(place)))
        return arrays, places

    for todo in order:
        awaited = [received[key][0] for key in waits.get(todo, ())]
        kind, half = todo[:2] if isinstance(todo[0], str) else ("send", None)
        inside = [q for q, (_, _, lies) in enumerate(portions) if lies == half]
        if kind in ("send", "both"):
            messages = todo[1:] if kind == "both" else (todo,)
            bit_of = lambda key: bits[portions[key[0]][0][key[1]]]
            arrays, planned = [], []
            for message in messages:
                wanted = [[(p, i, block ^ bit_of((p, s, block))) for i in range(s)] for p, s, block in message]
                arrays, places = collect([key for keys in wanted for key in keys])
                places = iter(places)
                planned.append(
                    tuple(
                        (block ^ bit_of((p, s, block)), offsets[p], width // portions[p][1], tuple(next(places) for _ in keys))
                        for (p, s, block), keys in zip(message, wanted)
                    )
                )
            if last is None:
                *payloads, turned = early_send(planned, width, place, out_weight, out_grad, True)
            elif kind == "both":
                payloads = early_send(planned, width, after(place), out_weight, turned, False)
            else:
                payloads = [send(planned[0], True, width, after(place), out_weight, turned, arrays)]
            last = payloads[0]
            for message, items, payload in zip(messages, planned, payloads):
                bit = bit_of(message[0])
                arrived = lax.ppermute(payload, "ch", [(i, i ^ bit) for i in range(size)])
                start = peak = 0
                for key, (_, _, rows, _) in zip(message, items):
                    part = part_of(rows, len(items), folds_of(toks))
                    received[key] = (arrived, start, peak, part)
                    start, peak = start + rows, peak + rows // part
        elif kind == "laps":
            lap, wide = laps(segments, toks, after(decay))
            last = wide
        elif kind == "sum":
            items = tuple((0, offsets[q], width // portions[q][1], ()) for q in inside)
            last = sums[half] = send(items, False, width, after(place), out_weight, turned, [])
        elif kind == "add":
            arrays, places = collect([(q, len(bits) - 1, 0) for q in inside])
            pieces = tuple(
                (offsets[q] - half * half_rows, width // portions[q][1], (at,)) for q, at in zip(inside, places)
            )
            last = sums[half] = add(pieces, after(sums[half]), arrays)
            added.add(half)
        elif kind == "gate":
            stages = range(len(bits) - (half in added))
            arrays, places = collect([(q, i, 0) for q in inside for i in stages])
            pieces = tuple(
                (offsets[q] - half * half_rows, tuple(places[i * len(stages) : (i + 1) * len(stages)]))
                for i, q in enumerate(inside)
            )
            other = residue if half == 0 else packed[0]
            grad_query, scanned[half], states[half], packed[half] = gate(
                half,
                half_rows,
                segments,
                pieces,
                after(sums[half]),
                arrays,
                query_in,
                conv_out,
                decay,
                lap,
                other,
                grad_query,
            )
            last = packed[half]
        elif kind == "scan":
            groups = lax.axis_size("ctx")
            swap = lambda array, round_: lax.ppermute(array, "ctx", [(i, i ^ (1 << round_)) for i in range(groups)])
            arrived, joined = [swap(packed[1], 0)], packed[1]
            rounds = groups.bit_length() - 1
            for round_ in range(1, rounds):
                last, *joined = join(round_ - 1, after(group), joined, arrived[-1], wide, round_ + 1 == rounds)
                joined = joined[0] if joined else None
                arrived.append(swap(last, round_))
            scanned[1] = scan(1, segments, after(scanned[1]), states[1], decay, lap, residue)
        else:
            grad_input = fix(
                segments, group, [scanned[0], scanned[1]], states[0], arrived, decay, lap, wide, residue, toks, width
            )
    return grad_query, grad_input


def solution(mesh):
    placed = (
        P("ctx", "ch"),
        P(None, "ch"),
        P("ctx", "ch"),
        P("ctx", "ch"),
        P("ch", None),
        P("ch", None),
    )
    return jax.shard_map(
        local,
        mesh=mesh,
        in_specs=placed,
        out_specs=(P("ctx", "ch"), P("ctx", "ch")),
        check_vma=False,
    )
```

```python
import functools
import math

import jax
import jax.numpy as jnp
from jax import lax
from jax.experimental import pallas as pl
from jax.experimental.pallas import tpu as pltpu
from jax.sharding import PartitionSpec as P

PEAKS = 16
SPAN = 251 * math.log(2.0)
SHIFT = 125 * math.log(2.0)
STEP = 256
PIECE = 128
GAP = 8
VMEM = 24 * 1024 * 1024
QUICK = pl.CostEstimate(flops=0, bytes_accessed=1024, transcendentals=0)

PORTIONS = (((0, 1, 2), 4, 0), ((1, 0, 2), 4, 0), ((0, 1, 2), 4, 1), ((0, 1, 2), 4, 1))
ORDER = (
    ((0, 0, 6), (0, 0, 2)), ("both", ((1, 0, 5), (1, 0, 1))), ((2, 0, 6), (3, 0, 6)), ((2, 0, 4), (3, 0, 4)),
    ("sum", 1), ((2, 0, 2), (3, 0, 2)), ((1, 0, 4), (0, 1, 4)), ((1, 1, 4), (0, 0, 4)), ((2, 1, 4), (3, 1, 4)),
    ((1, 0, 0), (0, 1, 0)), ((0, 2, 0), (1, 2, 0)), ((2, 2, 0), (3, 2, 0)), ((1, 1, 0), (0, 0, 0)),
    ((2, 1, 0), (3, 1, 0)), ((2, 0, 0), (3, 0, 0)), ("sum", 0), ("laps", None), ("gate", 0), ("add", 1), ("gate", 1),
    ("scan", 1), ("fix", None),
)
WAITS = {
    ((1, 0, 0), (0, 1, 0)): ((1, 0, 4),),
    ("gate", 0): ((0, 2, 0), (1, 0, 0)),
    ("gate", 1): ((2, 1, 0),),
}


def folds_of(toks):
    return toks // 128 if toks % 128 == 0 and PEAKS % (toks // 128) == 0 else 1


def part_of(rows, blocks, folds):
    return next(
        part for part in range(16, rows + 1, 16) if rows % part == 0 and rows // part * blocks * folds <= PEAKS
    )


def step_of(rows):
    return next(step for step in (STEP, STEP // 2, rows) if rows % step == 0)


def encode(block, part):
    codes, peaks = [], []
    for i in range(block.shape[0] // part):
        piece = block[i * part : (i + 1) * part, :]
        size = jnp.abs(piece)
        peak = jnp.maximum(jnp.max(size, axis=0, keepdims=True) * 1.01, 1e-30)
        peak = peak.astype(jnp.bfloat16).astype(jnp.float32)
        code = jnp.exp(size * (SPAN / peak) - SHIFT)
        codes.append(jnp.where(piece < 0, -code, code))
        peaks.append(peak)
    return jnp.concatenate(codes, axis=0).astype(jnp.bfloat16), peaks


def put(codes, out_ref, at):
    lanes = out_ref.shape[1]
    folds = codes.shape[1] // lanes
    rows = (out_ref.shape[0] - PEAKS) // folds
    for fold in range(folds):
        out_ref[fold * rows + at : fold * rows + at + codes.shape[0], :] = codes[:, fold * lanes : (fold + 1) * lanes]


def put_peaks(peaks, out_ref):
    lanes = out_ref.shape[1]
    peaks = [peak[:, at : at + lanes] for peak in peaks for at in range(0, peak.shape[1], lanes)]
    if len(peaks) < PEAKS:
        peaks.append(jnp.zeros((PEAKS - len(peaks), lanes), jnp.float32))
    out_ref[out_ref.shape[0] - PEAKS :, :] = jnp.concatenate(peaks, axis=0).astype(jnp.bfloat16)


def decode(ref, place, first, count, folds):
    start, peak, part = place
    rows = (ref.shape[0] - PEAKS) // folds
    peaks = ref[ref.shape[0] - PEAKS :, :].astype(jnp.float32) * (1.0 / SPAN)
    columns = []
    for fold in range(folds):
        blocks = []
        for i in range(first // part, -(-(first + count) // part)):
            low, high = max(first, i * part), min(first + count, (i + 1) * part)
            code = ref[fold * rows + start + low : fold * rows + start + high, :].astype(jnp.float32)
            at = (peak + i) * folds + fold
            size = (jnp.log(jnp.abs(code)) + SHIFT) * peaks[at : at + 1, :]
            blocks.append(jnp.where(code < 0, -size, size))
        columns.append(jnp.concatenate(blocks, axis=0))
    return jnp.concatenate(columns, axis=1)


def pinned(array):
    return pltpu.with_memory_space_constraint(array, pltpu.HBM)


def send_kernel(items, coded, width, near, place_ref, w_ref, turned_ref, *refs):
    near_refs, out_ref = refs[:near], refs[near]
    folds = folds_of(turned_ref.shape[1])
    base, peaks = 0, []
    for block, offset, rows, sources in items:
        step = step_of(rows)
        first = (place_ref[0] ^ block) * width + offset
        for at in range(0, rows, step):
            total = jnp.dot(
                w_ref[pl.ds(pl.multiple_of(first + at, 16), step), :],
                turned_ref[...],
                preferred_element_type=jnp.float32,
            )
            for source, place in sources:
                total = total + decode(near_refs[source], place, at, step, folds)
            if coded:
                total, more = encode(total, part_of(rows, len(items), folds))
                peaks += more
                put(total, out_ref, base + at)
            else:
                out_ref[base + at : base + at + step, :] = total
        base += rows
    if coded:
        put_peaks(peaks, out_ref)


def send(items, coded, width, place, weight, turned, nears):
    toks = turned.shape[1]
    vmem = pl.BlockSpec(memory_space=pltpu.VMEM)
    count = sum(rows for _, _, rows, _ in items)
    folds = folds_of(toks)
    shape = (folds * count + PEAKS, toks // folds) if coded else (count, toks)
    return pl.pallas_call(
        functools.partial(send_kernel, items, coded, width, len(nears)),
        in_specs=[pl.BlockSpec(memory_space=pltpu.SMEM)] + [vmem] * (2 + len(nears)),
        out_specs=vmem,
        out_shape=jax.ShapeDtypeStruct(shape, jnp.bfloat16 if coded else jnp.float32),
        compiler_params=pltpu.CompilerParams(vmem_limit_bytes=VMEM),
        cost_estimate=QUICK,
    )(place, weight, turned, *nears)


def early_kernel(messages, width, turns, place_ref, w_hbm, g_ref, *refs):
    out_refs, refs = refs[: len(messages)], refs[len(messages) :]
    w_ref, sems = refs[-2:]
    turned_ref = refs[0] if turns else g_ref
    depth, toks = turned_ref.shape
    copies, waits = [], []
    if turns:
        piece = math.gcd(toks, PIECE)
        for at in range(0, toks, piece):
            lines = pl.ds(at, piece)
            copies.append(pltpu.make_async_copy(g_ref.at[lines, :], refs[1].at[lines, :], sems.at[len(copies)]))
    grads, base = len(copies), 0
    for items in messages:
        for block, offset, rows, _ in items:
            step = math.gcd(rows, PIECE)
            first = pl.multiple_of((place_ref[0] ^ block) * width + offset, 16)
            for at in range(0, rows, step):
                copies.append(
                    pltpu.make_async_copy(
                        w_hbm.at[pl.ds(first + at, step), :], w_ref.at[pl.ds(base + at, step), :], sems.at[len(copies)]
                    )
                )
            base += rows
    for copy in copies:
        copy.start(priority=1)
    for i in range(grads):
        copies[i].wait()
        turned_ref[:, i * piece : (i + 1) * piece] = refs[1][i * piece : (i + 1) * piece, :].T
    waits, base = iter(copies[grads:]), 0
    for items, out_ref in zip(messages, out_refs):
        start, peaks = base, []
        for _, _, rows, _ in items:
            step = step_of(rows)
            for at in range(base, base + rows, step):
                for _ in range(step // math.gcd(rows, PIECE)):
                    next(waits).wait()
                total = jnp.dot(w_ref[at : at + step, :], turned_ref[...], preferred_element_type=jnp.float32)
                total, more = encode(total, part_of(rows, len(items), folds_of(toks)))
                peaks += more
                put(total, out_ref, at - start)
            base += rows
        put_peaks(peaks, out_ref)


def early_send(messages, width, place, weight, grad, turns):
    toks, depth = grad.shape if turns else grad.shape[::-1]
    vmem = pl.BlockSpec(memory_space=pltpu.VMEM)
    high = pl.BlockSpec(memory_space=pltpu.HBM)
    counts = [sum(rows for _, _, rows, _ in items) for items in messages]
    folds = folds_of(toks)
    steps = sum(rows // math.gcd(rows, PIECE) for items in messages for _, _, rows, _ in items)
    steps += toks // math.gcd(toks, PIECE) if turns else 0
    coded = [jax.ShapeDtypeStruct((folds * count + PEAKS, toks // folds), jnp.bfloat16) for count in counts]
    return pl.pallas_call(
        functools.partial(early_kernel, messages, width, turns),
        in_specs=[pl.BlockSpec(memory_space=pltpu.SMEM), high, high if turns else vmem],
        out_specs=[vmem] * (len(messages) + turns),
        out_shape=coded + [jax.ShapeDtypeStruct((depth, toks), jnp.bfloat16)] * turns,
        scratch_shapes=[pltpu.VMEM((toks, depth), jnp.bfloat16)] * turns
        + [pltpu.VMEM((sum(counts), depth), jnp.bfloat16), pltpu.SemaphoreType.DMA((steps,))],
        compiler_params=pltpu.CompilerParams(vmem_limit_bytes=VMEM),
        cost_estimate=QUICK,
    )(place, pinned(weight), pinned(grad) if turns else grad)


def add_kernel(pieces, near, acc_ref, *refs):
    near_refs, out_ref = refs[:near], refs[near]
    toks = acc_ref.shape[1]
    for first, rows, sources in pieces:
        total = acc_ref[first : first + rows, :]
        for source, place in sources:
            total = total + decode(near_refs[source], place, 0, rows, folds_of(toks))
        out_ref[first : first + rows, :] = total


def add(pieces, acc, nears):
    vmem = pl.BlockSpec(memory_space=pltpu.VMEM)
    return pl.pallas_call(
        functools.partial(add_kernel, pieces, len(nears)),
        in_specs=[vmem] * (1 + len(nears)),
        out_specs=vmem,
        out_shape=jax.ShapeDtypeStruct(acc.shape, jnp.float32),
        compiler_params=pltpu.CompilerParams(vmem_limit_bytes=VMEM),
        cost_estimate=QUICK,
    )(acc, *nears)


def steps_back(count, body, state, unroll, base=0):
    unroll = math.gcd(count, unroll)

    def some(i, state):
        for j in range(unroll):
            state = body(base + count - 1 - (i * unroll + j), state)
        return state

    return lax.fori_loop(0, count // unroll, some, state)


def power(base, exponent):
    result = None
    while exponent:
        if exponent % 2:
            result = base if result is None else result * base
        base = base * base
        exponent //= 2
    return result


def segment_of(shape, segments):
    return lax.rem(lax.broadcasted_iota(jnp.int32, shape, 0), segments)


def rolled(value, by):
    by %= value.shape[0]
    return pltpu.roll(value, by, 0) if by else value


def gate_kernel(half, rows, segments, pieces, near, acc_ref, *refs):
    near_refs, refs = refs[:near], refs[near:]
    query_ref, conv_ref, decay_ref, lap_ref, other_ref = refs[:5]
    out_hbm, rows_ref, state_ref, pack_ref = refs[-7:-3] if half == 0 else refs[-6:-2]
    gq_ref, sem = refs[-2:]
    gc_ref = refs[-3] if half == 0 else rows_ref
    toks = query_ref.shape[0]
    modes, sublanes, lanes = state_ref.shape
    mine = slice(half * sublanes, (half + 1) * sublanes)
    for line in range(rows // lanes):
        mix = acc_ref[line * lanes : (line + 1) * lanes, :]
        first, sources = next(piece for piece in reversed(pieces) if piece[0] <= line * lanes)
        for source, place in sources:
            mix = mix + decode(near_refs[source], place, line * lanes - first, lanes, folds_of(toks))
        mix = mix.T
        at = slice(line * lanes, (line + 1) * lanes)
        full = slice(half * rows + line * lanes, half * rows + (line + 1) * lanes)
        gq_ref[:, at] = (mix * conv_ref[:, full].astype(jnp.float32)).astype(jnp.bfloat16)
        gated = mix * query_ref[:, full].astype(jnp.float32)
        for k in range(segments):
            start = (line * segments + k) * (toks // segments + GAP)
            gc_ref[start : start + toks // segments, :] = gated[k * (toks // segments) : (k + 1) * (toks // segments), :]
    store = pltpu.make_async_copy(gq_ref, out_hbm.at[:, pl.ds(half * rows, rows)], sem)
    store.start()
    decay = [decay_ref[n, mine] for n in range(modes)]
    span = toks // segments

    def step(t, state):
        at = pl.ds(t, sublanes, stride=span + GAP)
        row = gc_ref[at, :]
        state = tuple(decay[n] * state[n] + row for n in range(modes))
        if half == 0:
            rows_ref[at, :] = summed([other_ref[n, mine] * state[n] for n in range(modes)])
        return state

    zero = jnp.zeros((sublanes, lanes), jnp.float32)
    state = steps_back(span, step, (zero,) * modes, 8)
    segment = segment_of((sublanes, lanes), segments)
    whole = []
    for n in range(modes):
        state_ref[n] = state[n]
        total = state[n]
        if segments > 1:
            factor = jnp.where(segment < segments - 1, lap_ref[n, mine], 0.0)
            for _ in range(segments - 1):
                total = state[n] + factor * rolled(total, -1)
        whole.append(total)
    packs = modes // segments
    for m in range(packs):
        packed = whole[m * segments]
        for j in range(1, segments):
            packed = jnp.where(segment == j, rolled(whole[m * segments + j], j), packed)
        if half == 0:
            pack_ref[m] = packed
        else:
            pack_ref[m] = other_ref[m]
            pack_ref[packs + m] = packed
    store.wait()


def gate(half, rows, segments, pieces, acc, nears, query_in, conv_out, decay, lap, other, partial):
    toks, width = query_in.shape
    modes, _, lanes = decay.shape
    sublanes = rows // lanes * segments
    vmem = pl.BlockSpec(memory_space=pltpu.VMEM)
    high = pl.BlockSpec(memory_space=pltpu.HBM)
    more = [] if partial is None else [partial]
    lines = ((sublanes + 1) * (toks // segments + GAP), lanes)
    return pl.pallas_call(
        functools.partial(gate_kernel, half, rows, segments, pieces, len(nears)),
        in_specs=[vmem] * (6 + len(nears)) + [high] * len(more),
        out_specs=(high, vmem, vmem, vmem),
        out_shape=(
            jax.ShapeDtypeStruct((toks, width), jnp.bfloat16),
            jax.ShapeDtypeStruct(lines, jnp.float32),
            jax.ShapeDtypeStruct((modes, sublanes, lanes), jnp.float32),
            jax.ShapeDtypeStruct(((1 + half) * modes // segments, sublanes, lanes), jnp.float32),
        ),
        scratch_shapes=([pltpu.VMEM(lines, jnp.float32)] if half == 0 else [])
        + [pltpu.VMEM((toks, rows), jnp.bfloat16), pltpu.SemaphoreType.DMA],
        input_output_aliases={6 + len(nears): 0} if more else {},
        compiler_params=pltpu.CompilerParams(vmem_limit_bytes=VMEM),
        cost_estimate=QUICK,
    )(acc, *nears, query_in, conv_out, decay, lap, other, *more)


def summed(terms):
    while len(terms) > 1:
        terms = [terms[k] + terms[k + 1] if k + 1 < len(terms) else terms[k] for k in range(0, len(terms), 2)]
    return terms[0]


def scan_kernel(half, segments, gc_ref, state_ref, decay_ref, lap_ref, residue_ref, rows_ref):
    modes, sublanes, lanes = state_ref.shape
    mine = slice(half * sublanes, (half + 1) * sublanes)
    span = gc_ref.shape[0] // (sublanes + 1) - GAP
    segment = segment_of((sublanes, lanes), segments)
    decay = [decay_ref[n, mine] for n in range(modes)]
    start = []
    for n in range(modes):
        total = jnp.zeros((sublanes, lanes), jnp.float32)
        if segments > 1:
            for k in range(segments - 2, -1, -1):
                total = jnp.where(segment == k, rolled(state_ref[n] + lap_ref[n, mine] * total, -1), total)
        start.append(total)

    def step(t, state):
        at = pl.ds(t, sublanes, stride=span + GAP)
        row = gc_ref[at, :]
        state = tuple(decay[n] * state[n] + row for n in range(modes))
        rows_ref[at, :] = summed([residue_ref[n, mine] * state[n] for n in range(modes)])
        return state

    steps_back(span, step, tuple(start), 8)


def scan(half, segments, grad_conv, state, decay, lap, residues):
    vmem = pl.BlockSpec(memory_space=pltpu.VMEM)
    return pl.pallas_call(
        functools.partial(scan_kernel, half, segments),
        in_specs=[vmem] * 5,
        out_specs=vmem,
        out_shape=jax.ShapeDtypeStruct(grad_conv.shape, jnp.float32),
        compiler_params=pltpu.CompilerParams(vmem_limit_bytes=VMEM),
        cost_estimate=QUICK,
    )(grad_conv, state, decay, lap, residues)


def laps_kernel(segments, span, decay_ref, lap_ref, wide_ref):
    modes, sublanes, lanes = decay_ref.shape
    sublanes //= 2
    packs = modes // segments
    segment = segment_of((sublanes, lanes), segments)
    for half in range(2):
        mine = slice(half * sublanes, (half + 1) * sublanes)
        for m in range(packs):
            packed = None
            for j in range(segments):
                lap = power(decay_ref[m * segments + j, mine], span)
                lap_ref[m * segments + j, mine] = lap
                wide = power(lap, segments)
                packed = wide if packed is None else jnp.where(segment == j, wide, packed)
            wide_ref[half * packs + m] = packed


def laps(segments, toks, decay):
    modes, sublanes, lanes = decay.shape
    vmem = pl.BlockSpec(memory_space=pltpu.VMEM)
    return pl.pallas_call(
        functools.partial(laps_kernel, segments, toks // segments),
        in_specs=[vmem],
        out_specs=(vmem, vmem),
        out_shape=(
            jax.ShapeDtypeStruct(decay.shape, jnp.float32),
            jax.ShapeDtypeStruct((2 * modes // segments, sublanes // 2, lanes), jnp.float32),
        ),
        compiler_params=pltpu.CompilerParams(vmem_limit_bytes=VMEM),
        cost_estimate=QUICK,
    )(decay)


def states_in(ref, shape):
    if ref.shape == shape:
        return [ref[m] for m in range(shape[0])]
    packs, sublanes, _ = shape
    rows = decode(ref, (0, 0, packs * sublanes // 2), 0, packs * sublanes, 1)
    return [rows[m * sublanes : (m + 1) * sublanes, :] for m in range(packs)]


def join_kernel(round_, group_ref, state_ref, arrived_ref, wide_ref, coded_ref, *out_refs):
    earlier = (group_ref[0] >> round_) % 2 == 0
    packs, sublanes, _ = state_ref.shape
    joined = []
    for m, other in enumerate(states_in(arrived_ref, state_ref.shape)):
        wide = power(wide_ref[m], 1 << round_)
        mine = state_ref[m]
        joined.append(jnp.where(earlier, mine + wide * other, other + wide * mine))
        for out_ref in out_refs:
            out_ref[m] = joined[-1]
    codes, peaks = encode(jnp.concatenate(joined, axis=0), packs * sublanes // 2)
    put(codes, coded_ref, 0)
    put_peaks(peaks, coded_ref)


def join(round_, group, state, arrived, wide, last):
    vmem = pl.BlockSpec(memory_space=pltpu.VMEM)
    packs, sublanes, lanes = state.shape
    return pl.pallas_call(
        functools.partial(join_kernel, round_),
        in_specs=[pl.BlockSpec(memory_space=pltpu.SMEM)] + [vmem] * 3,
        out_specs=[vmem] * (1 if last else 2),
        out_shape=[
            jax.ShapeDtypeStruct((packs * sublanes + PEAKS, lanes), jnp.bfloat16),
            jax.ShapeDtypeStruct(state.shape, jnp.float32),
        ][: 1 if last else 2],
        compiler_params=pltpu.CompilerParams(vmem_limit_bytes=VMEM),
        cost_estimate=QUICK,
    )(group, state, arrived, wide)


def fix_kernel(segments, rounds, group_ref, *refs):
    scanned_refs, state_ref, arrived_refs = refs[:2], refs[2], refs[3 : 3 + rounds]
    decay_ref, lap_ref, wide_ref, residue_ref, out_hbm, rows_ref, out_ref, sems = refs[3 + rounds :]
    toks, width = out_ref.shape
    modes, sublanes, lanes = state_ref.shape
    packs = modes // segments
    rows = width // 2
    span = toks // segments
    segment = segment_of((sublanes, lanes), segments)
    earlier = [(group_ref[0] >> r) % 2 == 0 for r in range(rounds)]
    arrived = [states_in(ref, (2 * packs, sublanes, lanes)) for ref in arrived_refs]
    stores = []
    for half in range(2):
        mine = slice(half * sublanes, (half + 1) * sublanes)
        decay = [decay_ref[n, mine] for n in range(modes)]
        start = []
        for m in range(packs):
            brought = jnp.zeros((sublanes, lanes), jnp.float32)
            between = jnp.ones((sublanes, lanes), jnp.float32)
            for r in range(rounds):
                state = arrived[r][half * packs + m]
                brought = jnp.where(earlier[r], brought + between * state, brought)
                if r + 1 < rounds:
                    between = jnp.where(earlier[r], between * power(wide_ref[half * packs + m], 1 << r), between)
            for j in range(segments):
                n = m * segments + j
                total = rolled(brought, segments - 1 - j)
                for k in range(segments - 2, -1, -1):
                    before = lap_ref[n, mine] * total
                    if half == 0:
                        before = before + state_ref[n]
                    total = jnp.where(segment == k, rolled(before, -1), total)
                start.append(residue_ref[n, mine] * total)

        def step(t, state, scanned_ref=scanned_refs[half], decay=decay):
            at = pl.ds(t, sublanes, stride=span + GAP)
            state = tuple(decay[n] * state[n] for n in range(modes))
            rows_ref[at, :] = scanned_ref[at, :] + summed(list(state))
            return state

        state, columns = tuple(start), pl.ds(half * rows, rows)
        for base in (span // 2, 0):
            state = steps_back(span // 2, step, state, 8, base)
            for k in range(segments):
                for line in range(rows // lanes):
                    at = slice(half * rows + line * lanes, half * rows + (line + 1) * lanes)
                    first = (line * segments + k) * (span + GAP) + base
                    out_ref[k * span + base : k * span + base + span // 2, at] = rows_ref[
                        first : first + span // 2, :
                    ].astype(jnp.bfloat16)
                lines = pl.ds(k * span + base, span // 2)
                stores.append(
                    pltpu.make_async_copy(
                        out_ref.at[lines, columns], out_hbm.at[lines, columns], sems.at[len(stores)]
                    )
                )
                stores[-1].start()
    for store in stores:
        store.wait()


def fix(segments, group, scanned, state, arrived, decay, lap, wide, residues, toks, width):
    vmem = pl.BlockSpec(memory_space=pltpu.VMEM)
    return pl.pallas_call(
        functools.partial(fix_kernel, segments, len(arrived)),
        in_specs=[pl.BlockSpec(memory_space=pltpu.SMEM)] + [vmem] * (7 + len(arrived)),
        out_specs=pl.BlockSpec(memory_space=pltpu.HBM),
        out_shape=jax.ShapeDtypeStruct((toks, width), jnp.bfloat16),
        scratch_shapes=[
            pltpu.VMEM(scanned[0].shape, jnp.float32),
            pltpu.VMEM((toks, width), jnp.bfloat16),
            pltpu.SemaphoreType.DMA((4 * segments,)),
        ],
        compiler_params=pltpu.CompilerParams(vmem_limit_bytes=VMEM),
        cost_estimate=QUICK,
    )(group, *scanned, state, *arrived, decay, lap, wide, residues)


def local(out_grad, out_weight, query_in, conv_out, residues, decay_rates):
    toks, width = query_in.shape
    modes = decay_rates.shape[1]
    lanes = math.gcd(width, 128)
    size, groups = lax.axis_size("ch"), lax.axis_size("ctx")
    bits = [1 << i for i in range(size.bit_length() - 1)]
    place = jnp.reshape(lax.axis_index("ch"), (1,)).astype(jnp.int32)
    group = jnp.reshape(lax.axis_index("ctx"), (1,)).astype(jnp.int32)
    half_rows = width // 2
    lines = half_rows // lanes
    segments = 8 // lines
    by_mode = lambda values: jnp.repeat(values.T.reshape(modes, width // lanes, lanes), segments, axis=1)
    decay, residue = by_mode(decay_rates), by_mode(residues)

    portions, order, waits = PORTIONS, ORDER, WAITS
    if size != 8:
        waits = {}
        portions = ((tuple(range(len(bits))), 2, 0), (tuple(range(len(bits))), 2, 1))
        order = [
            ((p, s, block),)
            for p in range(2)
            for s, bit in enumerate(bits)
            for block in sorted(range(0, size, 2 * bit), reverse=True)
        ] + [("laps", None), ("sum", 0), ("sum", 1), ("gate", 0), ("gate", 1), ("scan", 1), ("fix", None)]
    offsets = [sum(width // part for _, part, _ in portions[:p]) for p in range(len(portions))]

    received, sums, scanned, states, packed = {}, {}, {}, {}, {}
    grad_query = last = None
    added = set()

    def after(value):
        return value if last is None else lax.optimization_barrier((value, last, *awaited))[0]

    def collect(wanted):
        arrays, places = [], []
        for key in wanted:
            array, *place = received[key]
            index = next((i for i, known in enumerate(arrays) if known is array), len(arrays))
            if index == len(arrays):
                arrays.append(array)
            places.append((index, tuple(place)))
        return arrays, places

    for todo in order:
        awaited = [received[key][0] for key in waits.get(todo, ())]
        kind, half = todo[:2] if isinstance(todo[0], str) else ("send", None)
        inside = [q for q, (_, _, lies) in enumerate(portions) if lies == half]
        if kind in ("send", "both"):
            messages = todo[1:] if kind == "both" else (todo,)
            bit_of = lambda key: bits[portions[key[0]][0][key[1]]]
            arrays, planned = [], []
            for message in messages:
                wanted = [[(p, i, block ^ bit_of((p, s, block))) for i in range(s)] for p, s, block in message]
                arrays, places = collect([key for keys in wanted for key in keys])
                places = iter(places)
                planned.append(
                    tuple(
                        (block ^ bit_of((p, s, block)), offsets[p], width // portions[p][1], tuple(next(places) for _ in keys))
                        for (p, s, block), keys in zip(message, wanted)
                    )
                )
            if last is None:
                *payloads, turned = early_send(planned, width, place, out_weight, out_grad, True)
            elif kind == "both":
                payloads = early_send(planned, width, after(place), out_weight, turned, False)
            else:
                payloads = [send(planned[0], True, width, after(place), out_weight, turned, arrays)]
            last = payloads[0]
            for message, items, payload in zip(messages, planned, payloads):
                bit = bit_of(message[0])
                arrived = lax.ppermute(payload, "ch", [(i, i ^ bit) for i in range(size)])
                start = peak = 0
                for key, (_, _, rows, _) in zip(message, items):
                    part = part_of(rows, len(items), folds_of(toks))
                    received[key] = (arrived, start, peak, part)
                    start, peak = start + rows, peak + rows // part
        elif kind == "laps":
            lap, wide = laps(segments, toks, after(decay))
            last = wide
        elif kind == "sum":
            items = tuple((0, offsets[q], width // portions[q][1], ()) for q in inside)
            last = sums[half] = send(items, False, width, after(place), out_weight, turned, [])
        elif kind == "add":
            arrays, places = collect([(q, len(bits) - 1, 0) for q in inside])
            pieces = tuple(
                (offsets[q] - half * half_rows, width // portions[q][1], (at,)) for q, at in zip(inside, places)
            )
            last = sums[half] = add(pieces, after(sums[half]), arrays)
            added.add(half)
        elif kind == "gate":
            stages = range(len(bits) - (half in added))
            arrays, places = collect([(q, i, 0) for q in inside for i in stages])
            pieces = tuple(
                (offsets[q] - half * half_rows, tuple(places[i * len(stages) : (i + 1) * len(stages)]))
                for i, q in enumerate(inside)
            )
            other = residue if half == 0 else packed[0]
            grad_query, scanned[half], states[half], packed[half] = gate(
                half,
                half_rows,
                segments,
                pieces,
                after(sums[half]),
                arrays,
                query_in,
                conv_out,
                decay,
                lap,
                other,
                grad_query,
            )
            last = packed[half]
        elif kind == "scan":
            groups = lax.axis_size("ctx")
            swap = lambda array, round_: lax.ppermute(array, "ctx", [(i, i ^ (1 << round_)) for i in range(groups)])
            arrived, joined = [swap(packed[1], 0)], packed[1]
            rounds = groups.bit_length() - 1
            for round_ in range(1, rounds):
                last, *joined = join(round_ - 1, after(group), joined, arrived[-1], wide, round_ + 1 == rounds)
                joined = joined[0] if joined else None
                arrived.append(swap(last, round_))
            scanned[1] = scan(1, segments, after(scanned[1]), states[1], decay, lap, residue)
        else:
            grad_input = fix(
                segments, group, [scanned[0], scanned[1]], states[0], arrived, decay, lap, wide, residue, toks, width
            )
    return grad_query, grad_input


def solution(mesh):
    placed = (
        P("ctx", "ch"),
        P(None, "ch"),
        P("ctx", "ch"),
        P("ctx", "ch"),
        P("ch", None),
        P("ch", None),
    )
    return jax.shard_map(
        local,
        mesh=mesh,
        in_specs=placed,
        out_specs=(P("ctx", "ch"), P("ctx", "ch")),
        check_vma=False,
    )
```
